32 devices in a mesh: dp: 8 (over z, x), expert: 4 (over y, core).
Axes of the slice: x: 2, y: 2, z: 4, core: 2. Of those that a mesh axis runs over, the one named last changes fastest.
Arguments:
- tokens: bfloat16 [16384, 1024], P(('dp', 'expert')), may hold values from -6 to 6
- cotangent: bfloat16 [16384, 1024], P(('dp', 'expert')), may hold values from -6 to 6
- gain_attn: float32 [1024], replicated, may hold values from 0.5 to 1.5
- w_query: bfloat16 [1024, 1024], replicated, may hold values from -0.1875 to 0.1875
- w_key: bfloat16 [1024, 1024], replicated, may hold values from -0.1875 to 0.1875
- w_value: bfloat16 [1024, 1024], replicated, may hold values from -0.1875 to 0.1875
- w_out: bfloat16 [1024, 1024], replicated, may hold values from -1.5 to 1.5
- rel_bias: float32 [32, 16], replicated, may hold values from -3 to 3
- gain_moe: float32 [1024], replicated, may hold values from 0.5 to 1.5
- w_router: bfloat16 [1024, 4], replicated, may hold values from -0.09375 to 0.09375
- w_gate: bfloat16 [4, 1024, 2816], P('expert'), may hold values from -0.1875 to 0.1875
- w_up: bfloat16 [4, 1024, 2816], P('expert'), may hold values from -0.1875 to 0.1875
- w_down: bfloat16 [4, 2816, 1024], P('expert'), may hold values from -0.4375 to 0.4375
- segments: int32 [32, 512], P(('dp', 'expert')), may hold values from 0 to 7, never falling along the last dimension, each value on 1 to 256 neighbouring positions
- routes: int32 [16384, 2], P(('dp', 'expert')), may hold values from 0 to 3, all different within a row; in each aligned block of 512 rows (0 to 511, 512 to 1023, ...) at most 320 rows name the same one
Outputs:
- layer_out: bfloat16 [16384, 1024], P(('dp', 'expert'))
- token_grad: float32 [16384, 1024], P(('dp', 'expert'))
- query_grad: float32 [1024, 1024], P(('dp', 'expert'))
- key_grad: float32 [1024, 1024], P(('dp', 'expert'))
- value_grad: float32 [1024, 1024], P(('dp', 'expert'))
- out_grad: float32 [1024, 1024], P(('dp', 'expert'))
- gain_attn_grad: float32 [1024], P(('dp', 'expert'))
- gain_moe_grad: float32 [1024], P(('dp', 'expert'))
- bias_grad: float32 [512], P(('dp', 'expert'))
- router_grad: float32 [1024, 4], P(('dp', 'expert'))
- gate_grad: float32 [4, 1024, 2816], P('expert', 'dp')
- up_grad: float32 [4, 1024, 2816], P('expert', 'dp')
- down_grad: float32 [4, 2816, 1024], P('expert', 'dp')
The draws below stay inside these ranges and needn't reach their ends.
Inputs may be any that keep to these rules, and one draw needn't show every extreme that they name: `routes`: in each aligned block of 512 rows (the rows of one device) every expert is named by at most 320 rows, and in some blocks one expert by exactly 320; a token's two experts differ. `segments`: within each sequence the document numbers never fall; a document has at most 256 tokens, and some document exactly that many.
All inputs are finite; a program needn't handle non-finite values.
Results may differ from the reference program's by a relative error of at most 0.015.
Values may be sent and summed in bfloat16 or wider, within the bound.
No kernel may reach another device: no remote copies, remote signals or barrier semaphores. Data moves between devices by JAX's collectives and lax.ppermute only.
A program may use at most 256 MiB of HBM per device.

```python
import math
import jax
import jax.numpy as jnp
import numpy as np
from jax import lax

D = 1024
HEADS = 16
HEAD_DIM = 64
FF = 2816
BUCKETS = 32
TOK_DEV = 512
EXPERTS = 4
CAP = 320
SEQS = 32
TOKENS = 16384


def with_spikes(values, key, source, target, blocks, factor):
    def block_of(dim):
        return (jnp.arange(values.shape[dim]) // (values.shape[dim] // blocks)).reshape((-1,) + (1,) * (values.ndim - 1 - dim))

    near = jax.random.permutation(key, blocks)[block_of(target)]
    far = (block_of(target) + blocks // 2) % blocks
    return jnp.where((block_of(source) == near) | (block_of(source) == far), factor * values, values)


def levels(stream_key, extent, cuts, low, high):
    loudness = 1.0
    for dim, parts in cuts:
        steps = jax.random.uniform(jax.random.fold_in(jax.random.fold_in(stream_key, 6), dim), (parts,), jnp.float32, low / len(cuts), high / len(cuts))
        loudness = loudness * jnp.repeat(jnp.exp(steps), extent[dim] // parts).reshape((-1,) + (1,) * (len(extent) - 1 - dim))
    return loudness


def split_up(count, total, bound, skew):
    loads = [(1 << 20) // math.isqrt(grade ** skew) + 1 for grade in range(2, count + 1)]
    spare, given = total - bound - (count - 1), [1] * (count - 1)
    while spare > 0:
        candidates = [i for i in range(count - 1) if given[i] < bound]
        mass, left = sum([loads[i] for i in candidates]), spare
        for i in candidates:
            addition = min(bound - given[i], max(1, left * loads[i] // mass), spare)
            given[i] = given[i] + addition
            spare = spare - addition
    return np.array([bound] + given)


def uneven_parts(stream_key, count, total, bound, lean):
    if count == 2:
        one = jax.random.randint(stream_key, (), max(1, total - bound), min(bound, total - 1) + 1)
        return jnp.stack([one, total - one])
    lengths = jnp.asarray(split_up(count, total, bound, lean), jnp.int32)
    couples = (count - 1) // 2
    source_of, receiver = lengths[1:1 + 2 * couples:2], lengths[2:2 + 2 * couples:2]
    room = jnp.minimum(source_of - 1, bound - receiver)
    moved = jax.random.randint(jax.random.fold_in(stream_key, 1), (couples,), 0, 1 << 20) % (room + 1)
    lengths = lengths.at[1:1 + 2 * couples:2].set(source_of - moved).at[2:2 + 2 * couples:2].set(receiver + moved)
    return lengths[jax.random.permutation(jax.random.fold_in(stream_key, 2), count)]


def assign_block(rng, own, number, rows, amount, top, most, skew):
    sequence = jax.random.permutation(rng, amount)
    packed, usual = portions_of(amount, rows * top, most, skew, True), portions_of(amount, rows * top, most, skew, False)
    places = jnp.arange(amount)

    def named(sizes, rotation):
        used = int((sizes > 0).sum())
        fixed = max(1, used // 4)
        shifted = fixed + (places - fixed + rotation * (used - fixed)) % max(1, amount - fixed)
        return jnp.zeros((amount,), jnp.int32).at[sequence[jnp.where(places < fixed, places, shifted)]].set(jnp.asarray(sizes, jnp.int32))

    sizes = jnp.where(number % 4 == 0, named(packed, number // 4), named(usual, number - number // 4 - 1))
    mixed = jax.random.permutation(jax.random.fold_in(own, 3), amount)
    giver, receiver = mixed[0:amount // 2 * 2:2], mixed[1:amount // 2 * 2:2]
    room = jnp.minimum(sizes[giver] - 1, most - sizes[receiver]) // 2
    room = jnp.where((giver == sequence[0]) | (receiver == sequence[0]) | (sizes[receiver] == 0), 0, jnp.maximum(room, 0))
    shifted = jax.random.randint(jax.random.fold_in(own, 4), (amount // 2,), 0, 1 << 20) % (room + 1)
    sizes = sizes.at[giver].add(-shifted).at[receiver].add(shifted)
    members = jnp.searchsorted(jnp.cumsum(sizes), jnp.arange(rows * top), side="right").astype(jnp.int32)
    listing = members.reshape(top, rows).T
    listing = listing[jax.random.permutation(jax.random.fold_in(own, 1), rows)]
    rotation = jax.random.randint(jax.random.fold_in(own, 2), (rows, 1), 0, top)
    return jnp.take_along_axis(listing, (jnp.arange(top)[None, :] + rotation) % top, axis=1)


def portions_of(amount, total, limit, slope, full):
    weights = [(1 << 20) // math.isqrt(rank ** slope) + 1 for rank in range(1, amount + 1)]
    largest = limit if full else min(limit, max(-(-total // amount), total * weights[0] // sum(weights)))
    least = 1 if total - largest >= amount - 1 else 0
    counts, spare = [largest] + [least] * (amount - 1), total - largest - least * (amount - 1)
    while spare > 0:
        movable = [i for i in range(1, amount) if counts[i] < largest] or [i for i in range(1, amount) if counts[i] < limit]
        whole, left = sum([weights[i] for i in movable]), spare
        for i in movable:
            extra = min(limit - counts[i], max(1, left * weights[i] // whole), spare)
            counts[i] = counts[i] + extra
            spare = spare - extra
    return np.array(counts)


def noise(key, extent, width, bound, split=(), kind=jnp.bfloat16):
    values = width * jax.random.normal(key, extent, jnp.float32)
    if split:
        values = values * levels(key, extent, split, -0.22, 0.18)
    return jnp.clip(values, -bound, bound).astype(kind)


def bell_draw_with(stream_key, extent, spread, bound, cuts, heavy, held_as=jnp.bfloat16):
    array = spread * jax.random.normal(stream_key, extent, jnp.float32)
    if cuts:
        array = array * levels(stream_key, extent, cuts, -0.22, 0.18)
    return jnp.clip(with_spikes(array, jax.random.fold_in(stream_key, 3), *heavy), -bound, bound).astype(held_as)


def setup_inputs(seed: int = 0) -> dict:
    seeds = jax.random.split(jax.random.key(seed), 16)
    tokens = bell_draw_with(seeds[0], (TOKENS, D), 1.0, 6.0, ((0, 32),), (0, 1, 32, 2.75))
    cotangent = noise(seeds[1], (TOKENS, D), 1.0, 6.0, ((0, 32),))
    gain_attn = jnp.clip(1.0 + 0.1 * jax.random.normal(seeds[2], (D,), jnp.float32), 0.5, 1.5)
    w_query = noise(seeds[3], (D, D), D ** -0.5, 0.1875)
    w_key = noise(seeds[4], (D, D), D ** -0.5, 0.1875)
    w_value = noise(seeds[5], (D, D), D ** -0.5, 0.1875)
    w_out = noise(seeds[6], (D, D), (D // 64) ** -0.5, 1.5)
    rel_bias = noise(seeds[7], (BUCKETS, HEADS), 1.0, 3.0, (), jnp.float32)
    gain_moe = jnp.clip(1.0 + 0.1 * jax.random.normal(seeds[8], (D,), jnp.float32), 0.5, 1.5)
    w_router = noise(seeds[9], (D, EXPERTS), (4 * D) ** -0.5, 0.09375)
    w_gate = noise(seeds[10], (EXPERTS, D, FF), D ** -0.5, 0.1875, ((0, 4),))
    w_up = noise(seeds[11], (EXPERTS, D, FF), D ** -0.5, 0.1875, ((0, 4),))
    w_down = noise(seeds[12], (EXPERTS, FF, D), (FF // (EXPERTS * EXPERTS)) ** -0.5, 0.4375, ((0, 4),))
    segments = jax.vmap(lambda own: jnp.searchsorted(jnp.cumsum(uneven_parts(own, 8, TOK_DEV, TOK_DEV // 2, 2)), jnp.arange(TOK_DEV), side="right"))(jax.random.split(seeds[13], SEQS)).reshape((SEQS, TOK_DEV)).astype(jnp.int32)
    routes_keys = jax.random.split(jax.random.fold_in(seeds[14], 1), TOKENS // TOK_DEV)
    routes_turns = jax.random.permutation(jax.random.fold_in(seeds[14], 3), TOKENS // TOK_DEV)
    routes = jax.vmap(lambda own, number: assign_block(jax.random.fold_in(seeds[14], 2), own, number, TOK_DEV, EXPERTS, 2, CAP, 2))(routes_keys, routes_turns).reshape((TOKENS, 2))
    return {"tokens": tokens, "cotangent": cotangent, "gain_attn": gain_attn, "w_query": w_query, "w_key": w_key, "w_value": w_value, "w_out": w_out, "rel_bias": rel_bias, "gain_moe": gain_moe, "w_router": w_router, "w_gate": w_gate, "w_up": w_up, "w_down": w_down, "segments": segments, "routes": routes}


@jax.custom_vjp
def low(v):
    return lax.optimization_barrier(v.astype(jnp.bfloat16)).astype(jnp.float32)

@jax.custom_vjp
def low_back(v):
    return v

def low_keep(v):
    return (low(v), None)

def low_pass(kept, grad):
    return (grad,)

def back_keep(v):
    return (v, None)

def back_low(kept, grad):
    return (low(grad),)
low.defvjp(low_keep, low_pass)
low_back.defvjp(back_keep, back_low)
EPS = 1e-06
HIGHEST = lax.Precision.HIGHEST

def bucket_of(relative, buckets):
    halfway = buckets // 2
    exact_span = halfway // 2
    distance = np.abs(relative)
    beyond = exact_span + (np.log(np.maximum(distance, 1) / exact_span) / np.log(128.0 / exact_span) * (halfway - exact_span)).astype(np.int64)
    beyond = np.minimum(beyond, halfway - 1)
    return ((relative > 0).astype(np.int64) * halfway + np.where(distance < exact_span, distance, beyond)).astype(np.int32)

def rms_apply(values, gain_row):
    return values * lax.rsqrt(lax.optimization_barrier(jnp.mean(values * values, axis=-1, keepdims=True)) + EPS) * gain_row

def slot_numbers(route_rows):
    flat_routes = route_rows.reshape(-1)
    marked = (flat_routes[:, None] == jnp.arange(EXPERTS, dtype=jnp.int32)[None, :]).astype(jnp.int32)
    before = jnp.cumsum(marked, axis=0) - marked
    return lax.optimization_barrier(jnp.sum(before * marked, axis=1)).reshape(route_rows.shape).astype(jnp.int32)

def reference(tokens, cotangent, gain_attn, w_query, w_key, w_value, w_out, rel_bias, gain_moe, w_router, w_gate, w_up, w_down, segments, routes):
    blocks = segments.shape[0]
    slot_index = jax.vmap(slot_numbers)(routes.reshape(blocks, TOK_DEV, 2)).reshape(-1, 2)
    owner_block = jnp.broadcast_to((jnp.arange(blocks * TOK_DEV, dtype=jnp.int32) // TOK_DEV)[:, None], routes.shape)
    bucket_table = jnp.asarray(bucket_of(np.arange(TOK_DEV)[None, :] - np.arange(TOK_DEV)[:, None], BUCKETS))
    score_scale = HEAD_DIM ** (-0.5)

    def head_blocks(matrix):
        return matrix.reshape(blocks, TOK_DEV, HEADS, HEAD_DIM)

    def forward(start_rows, gain_first, query_w, key_w, value_w, out_w, bias_table, gain_second, router_w, gate_all, up_all, down_all):
        normed = low(rms_apply(start_rows, gain_first))
        queries = low_back(low(jnp.dot(normed, query_w, precision=HIGHEST)))
        keys_all = low_back(low(jnp.dot(normed, key_w, precision=HIGHEST)))
        values_all = low_back(low(jnp.dot(normed, value_w, precision=HIGHEST)))
        positional = jnp.transpose(bias_table[bucket_table], (2, 0, 1))

        def attend(pieces):
            query_seq, key_seq, value_seq, document = pieces
            scores = jnp.einsum('qhd,khd->hqk', query_seq, key_seq, precision=HIGHEST) * score_scale + positional
            scores = low_back(scores)
            same_doc = (document[:, None] == document[None, :])[None]
            weights_soft = jax.nn.softmax(jnp.where(same_doc, scores, -1e+30), axis=-1)
            mixed_heads = jnp.einsum('hqk,khd->qhd', low(weights_soft), value_seq, precision=HIGHEST)
            return low_back(low(mixed_heads)).reshape(TOK_DEV, D)
        attended = lax.map(jax.checkpoint(attend), (head_blocks(queries), head_blocks(keys_all), head_blocks(values_all), segments)).reshape(-1, D)
        branch = low_back(jnp.dot(attended, out_w, precision=HIGHEST))
        middle = start_rows + branch
        normed_moe = low(rms_apply(middle, gain_second))
        logits = jnp.dot(normed_moe, router_w, precision=HIGHEST)
        chances = jax.nn.softmax(logits, axis=-1)
        gate_values = jnp.take_along_axis(chances, routes, axis=1)
        copies = low_back(jnp.broadcast_to(normed_moe[:, None, :], routes.shape + (D,)))
        buffer = jnp.zeros((EXPERTS, blocks, CAP, D), jnp.float32).at[routes, owner_block, slot_index].add(copies)

        def expert(pieces):
            dispatched, gate_w, up_w, down_w = pieces
            flat_rows = dispatched.reshape(-1, D)
            gate_pre = low_back(jnp.dot(flat_rows, gate_w, precision=HIGHEST))
            up_pre = low_back(jnp.dot(flat_rows, up_w, precision=HIGHEST))
            hidden = low(jax.nn.gelu(gate_pre, approximate=True) * up_pre)
            return low_back(low(jnp.dot(hidden, down_w, precision=HIGHEST))).reshape(dispatched.shape)
        returned = lax.map(jax.checkpoint(expert), (buffer, gate_all, up_all, down_all))
        picked = returned[routes, owner_block, slot_index]
        return middle + lax.optimization_barrier(jnp.sum(gate_values[:, :, None] * picked, axis=1))
    floats = tuple((item.astype(jnp.float32) for item in (tokens, gain_attn, w_query, w_key, w_value, w_out, rel_bias, gain_moe, w_router, w_gate, w_up, w_down)))
    result, pullback = jax.vjp(forward, *floats)
    gradients = pullback(cotangent.astype(jnp.float32))
    return (result.astype(jnp.bfloat16), gradients[0], gradients[2], gradients[3], gradients[4], gradients[5], gradients[1], gradients[7], gradients[6].reshape(-1), gradients[8], gradients[9], gradients[10], gradients[11])
```

```python
import functools

import jax
import jax.numpy as jnp
import numpy as np
from jax import lax
from jax.experimental import pallas as pl
from jax.experimental.pallas import tpu as pltpu
from jax.sharding import PartitionSpec as P

EPS = 1e-06
HIGHEST = lax.Precision.HIGHEST
LANES = 128
BAND = 4 * LANES
HEAD_GROUP = 4
TAIL = 16
FAR = -1e30
BF = jnp.bfloat16
F32 = jnp.float32
VMEM_LIMIT = 56 * 1024 * 1024


def bucket_of(relative, buckets):
    halfway = buckets // 2
    exact_span = halfway // 2
    distance = np.abs(relative)
    beyond = exact_span + (
        np.log(np.maximum(distance, 1) / exact_span)
        / np.log(128.0 / exact_span)
        * (halfway - exact_span)
    ).astype(np.int64)
    beyond = np.minimum(beyond, halfway - 1)
    return (
        (relative > 0).astype(np.int64) * halfway
        + np.where(distance < exact_span, distance, beyond)
    ).astype(np.int32)


def band_onehot(length, buckets):
    place = np.arange(BAND)
    relative = np.where(place <= 3 * LANES, LANES - place, BAND + LANES - place)
    table = (bucket_of(relative, buckets)[None, :] == np.arange(buckets)[:, None]).astype(np.float32)
    table[:, 3 * LANES] = 0.0
    far = np.arange(LANES, length)
    assert np.all(bucket_of(far, buckets) == bucket_of(far, buckets)[0])
    assert np.all(bucket_of(-far, buckets) == bucket_of(-far, buckets)[0])
    return table


FAR_AFTER = 3 * LANES + 1
FAR_BEFORE = 3 * LANES - 1


def dot(a, b):
    return lax.dot_general(a, b, (((1,), (0,)), ((), ())), preferred_element_type=F32)


def dot_nt(a, b):
    return lax.dot_general(a, b, (((1,), (1,)), ((), ())), preferred_element_type=F32)


def dot_tn(a, b):
    return lax.dot_general(a, b, (((0,), (0,)), ((), ())), preferred_element_type=F32)


def split3(value):
    hi = value.astype(BF)
    rest = value - hi.astype(F32)
    mid = rest.astype(BF)
    low = (rest - mid.astype(F32)).astype(BF)
    return hi, mid, low


def rms_scale(value):
    return lax.rsqrt(jnp.mean(value * value, axis=-1, keepdims=True) + EPS)


def params(**kw):
    return pltpu.CompilerParams(vmem_limit_bytes=VMEM_LIMIT, **kw)


COST_SCALE = 0.05


def cost_us(time):
    return pl.CostEstimate(flops=int(time * 1.15e9 * COST_SCALE), bytes_accessed=100000, transcendentals=0)


def call(kernel, args, in_specs, **kw):
    return pl.pallas_call(kernel, in_specs=list(in_specs), compiler_params=params(), **kw)(*args)


def whole_specs(args):
    return [const_spec(a.shape) for a in args]


def const_spec(shape):
    return pl.BlockSpec(shape, lambda *_: (0,) * len(shape))


def selector(code_row, rows):
    place = lax.broadcasted_iota(jnp.int32, (rows, code_row.shape[1]), 0)
    return jnp.where(place == code_row, 1.0, 0.0).astype(BF)


def selector_t(code_column, rows):
    place = lax.broadcasted_iota(jnp.int32, (code_column.shape[0], rows), 1)
    return jnp.where(place == code_column, 1.0, 0.0).astype(BF)


def cot_dispatch_kernel(cot_ref, code_ref, *outs):
    cap = outs[0].shape[0]
    cot = cot_ref[...]
    for m, out in enumerate(outs):
        out[...] = dot(selector(code_ref[m : m + 1, :], cap), cot).astype(BF)


def cot_dispatch(cot, code, experts, cap):
    rows, width = cot.shape
    return pl.pallas_call(
        cot_dispatch_kernel,
        out_shape=[jax.ShapeDtypeStruct((cap, width), BF)] * experts,
        compiler_params=params(),
        cost_estimate=cost_us(3.6),
        name="cot_dispatch",
    )(cot, code)


def band_of(row):
    return pltpu.roll(jnp.broadcast_to(row, (LANES, BAND)), 0, 1, stride=1, stride_axis=0)


def diagonal_sums(skewed):
    eight = skewed[0:8]
    for start in range(8, LANES, 8):
        eight = eight + pltpu.roll(skewed[start : start + 8], BAND - start, 1)
    total = eight[0:1]
    for row in range(1, 8):
        total = total + pltpu.roll(eight[row : row + 1], BAND - row, 1)
    return total


def bias_column(band, row, q_block, k_blocks):
    pieces = []
    for k_block in range(k_blocks):
        d = k_block - q_block
        if d > 1:
            pieces.append(jnp.broadcast_to(row[:, FAR_AFTER : FAR_AFTER + 1], (LANES, LANES)))
        elif d < -1:
            pieces.append(jnp.broadcast_to(row[:, FAR_BEFORE : FAR_BEFORE + 1], (LANES, LANES)))
        else:
            pieces.append(band[:, LANES * (1 - d) : LANES * (2 - d)])
    return jnp.concatenate(pieces, axis=0)


def only_rows(value, h, head_dim):
    mine = value[h * head_dim : (h + 1) * head_dim]
    none = jnp.zeros_like(mine)
    return jnp.concatenate([mine, none] if h % 2 == 0 else [none, mine], axis=0)


def attn_fwd_kernel(
    tok_ref, gain_a_ref, wq_ref, wk_ref, wv_ref, wo_ref, woff_ref, segc_ref, segr_ref, gain_m_ref, wr_ref, code_ref,
    qs_ref, k_ref, v_ref, att_ref, lse_ref, mid_ref, nm_ref, ch_ref, *rest,
    experts, head_dim,
):
    disp_refs, (n_scr, mask_scr) = rest[:-2], rest[-2:]
    step = pl.program_id(0)
    rows = tok_ref.shape[0]
    blocks = rows // LANES

    @pl.when(step == 0)
    def _():
        start = tok_ref[...].astype(F32)
        n_scr[...] = (start * rms_scale(start) * gain_a_ref[...]).astype(BF)
        mid_ref[...] = start
        mask_scr[...] = jnp.where(segc_ref[...] == segr_ref[...], 0.0, FAR)

    normed = n_scr[...]
    queries = dot(normed, wq_ref[...]).astype(BF)
    scaled = (queries.astype(F32) * head_dim ** (-0.5)).astype(BF)
    keys = dot(normed, wk_ref[...]).astype(BF)
    values = dot(normed, wv_ref[...]).astype(BF)
    qs_ref[...] = scaled
    k_ref[...] = keys
    v_ref[...] = values
    q_t = scaled.T
    v_t = values.T
    heads_t = []
    for h in range(HEAD_GROUP):
        row = woff_ref[0, h : h + 1, :]
        band = band_of(row)
        pair = slice(LANES * (h // 2), LANES * (h // 2 + 1))
        k_pair = keys[:, pair]
        q_only = only_rows(q_t, h, head_dim)
        v_h = v_t[h * head_dim : (h + 1) * head_dim]
        pieces = []
        for b in range(blocks):
            lanes = slice(b * LANES, (b + 1) * LANES)
            s = dot(k_pair, q_only[:, lanes]) + bias_column(band, row, b, blocks) + mask_scr[:, lanes]
            peak = jnp.max(s, axis=0, keepdims=True)
            p = jnp.exp(s - peak)
            total = jnp.sum(p, axis=0, keepdims=True)
            pieces.append(dot(v_h, p.astype(BF)) * (1.0 / total))
            lse_ref[0, h : h + 1, lanes] = peak + jnp.log(total)
        heads_t.append(jnp.concatenate(pieces, axis=1))
    att = jnp.concatenate(heads_t, axis=0).T.astype(BF)
    att_ref[...] = att
    mid_ref[...] += dot(att, wo_ref[...])

    @pl.when(step == pl.num_programs(0) - 1)
    def _():
        mid = mid_ref[...]
        nm = (mid * rms_scale(mid) * gain_m_ref[...]).astype(BF)
        nm_ref[...] = nm
        logits = dot_nt(wr_ref[...], nm)
        live = lax.broadcasted_iota(jnp.int32, logits.shape, 0) < experts
        logits = jnp.where(live, logits, FAR)
        raised = jnp.exp(logits - jnp.max(logits, axis=0, keepdims=True))
        chances = raised / jnp.sum(raised, axis=0, keepdims=True)
        ch_ref[...] = chances
        hi = chances.astype(BF)
        low = (chances - hi.astype(F32)).astype(BF)
        both = jnp.concatenate([hi, low], axis=0)
        cap = disp_refs[0].shape[0] - TAIL
        cap_lanes = -(-cap // LANES) * LANES
        lane_row = lax.broadcasted_iota(jnp.int32, (TAIL, cap_lanes), 0)
        for m, out in enumerate(disp_refs):
            chosen = selector(code_ref[m : m + 1, :], cap_lanes)
            out[0:cap, :] = dot(chosen[:cap], nm).astype(BF)
            gates = dot_nt(both, chosen)
            packed = jnp.where(lane_row == 0, gates[m : m + 1], jnp.where(lane_row == 1, gates[TAIL + m : TAIL + m + 1], 0.0))
            out[cap:, :] = jnp.zeros((TAIL, out.shape[1]), BF)
            out[cap:, 0:cap_lanes] = packed.astype(BF)


def attn_fwd(tokens, gain_attn, w_query, w_key, w_value, w_out, woff, seg, gain_moe, wr_t, code, experts, cap):
    rows, width = tokens.shape
    groups = woff.shape[0]
    cols = width // groups
    col_block = pl.BlockSpec((rows, cols), lambda g: (0, g))
    weight_block = pl.BlockSpec((width, cols), lambda g: (0, g))
    head_dim = cols // HEAD_GROUP
    wide = jax.ShapeDtypeStruct((rows, width), BF)
    return pl.pallas_call(
        functools.partial(attn_fwd_kernel, experts=experts, head_dim=head_dim),
        grid=(groups,),
        in_specs=[
            const_spec((rows, width)),
            const_spec((1, width)),
            weight_block,
            weight_block,
            weight_block,
            pl.BlockSpec((cols, width), lambda g: (g, 0)),
            pl.BlockSpec((1, HEAD_GROUP, BAND), lambda g: (g, 0, 0)),
            const_spec((rows, 1)),
            const_spec((1, rows)),
            const_spec((1, width)),
            const_spec((TAIL, width)),
            const_spec(code.shape),
        ],
        out_specs=[
            col_block,
            col_block,
            col_block,
            col_block,
            pl.BlockSpec((1, HEAD_GROUP, rows), lambda g: (g, 0, 0)),
            const_spec((rows, width)),
            const_spec((rows, width)),
            const_spec((TAIL, rows)),
        ]
        + [const_spec((cap + TAIL, width))] * experts,
        out_shape=[
            wide,
            wide,
            wide,
            wide,
            jax.ShapeDtypeStruct((groups, HEAD_GROUP, rows), F32),
            jax.ShapeDtypeStruct((rows, width), F32),
            wide,
            jax.ShapeDtypeStruct((TAIL, rows), F32),
        ]
        + [jax.ShapeDtypeStruct((cap + TAIL, width), BF)] * experts,
        scratch_shapes=[pltpu.VMEM((rows, width), BF), pltpu.VMEM((rows, rows), F32)],
        compiler_params=params(),
        cost_estimate=cost_us(31),
        name="attn_fwd",
    )(
        tokens, gain_attn[None], w_query, w_key, w_value, w_out, woff, seg.reshape(rows, 1), seg.reshape(1, rows),
        gain_moe[None], wr_t, code,
    )


def gelu_parts(gate):
    c0 = np.float32(np.sqrt(2.0 / np.pi))
    c1 = np.float32(0.044715)
    square = gate * gate
    t = jnp.tanh(c0 * gate * (1.0 + c1 * square))
    half = 0.5 * (1.0 + t)
    value = gate * half
    slope = half + 0.5 * gate * (1.0 - t * t) * (c0 * (1.0 + 3.0 * c1 * square))
    return value, slope


def column_of(packed, cap):
    total = jnp.sum(packed.astype(F32), axis=0, keepdims=True)
    row = lax.broadcasted_iota(jnp.int32, (cap, cap), 0)
    lane = lax.broadcasted_iota(jnp.int32, (cap, cap), 1)
    return jnp.sum(jnp.where(row == lane, total, 0.0), axis=1, keepdims=True)


FF_BLOCK = 256


def cot_hidden_kernel(*refs):
    c_refs, wd_ref, out_ref, c_scr = refs[:-3], refs[-3], refs[-2], refs[-1]
    cap = c_refs[0].shape[0]

    @pl.when(pl.program_id(0) == 0)
    def _():
        for m, c_ref in enumerate(c_refs):
            c_scr[m * cap : (m + 1) * cap, :] = c_ref[...]

    out_ref[...] = dot_nt(c_scr[...], wd_ref[0]).astype(BF)


def cot_hidden(cs, w_down):
    experts = len(cs)
    cap, width = cs[0].shape
    rows, ff = experts * cap, w_down.shape[1]
    return call(
        cot_hidden_kernel,
        (*cs, w_down),
        whole_specs(cs) + [pl.BlockSpec((1, FF_BLOCK, width), lambda f: (0, f, 0))],
        grid=(ff // FF_BLOCK,),
        out_specs=pl.BlockSpec((rows, FF_BLOCK), lambda f: (0, f)),
        out_shape=jax.ShapeDtypeStruct((rows, ff), BF),
        scratch_shapes=[pltpu.VMEM((rows, width), BF)],
        cost_estimate=cost_us(14.7),
        name="cot_hidden",
    )


def expert_first(place_ref, x_refs, c_refs, x_ref, xt_ref, gate_ref, gc_ref):
    cap = c_refs[0].shape[0]
    for m, (x_part, c_part) in enumerate(zip(x_refs, c_refs)):
        part = slice(m * cap, (m + 1) * cap)
        x_ref[part, :] = x_part[0:cap, :]
        gate = column_of(x_part[cap:, 0:cap], cap)
        gate_ref[part, :] = jnp.broadcast_to(gate, (cap, LANES))
        gc_ref[part, :] = (c_part[...].astype(F32) * gate).astype(BF)
    flipped = x_ref[...].T
    owners = place_ref.shape[0]
    rows = flipped.shape[0] // owners
    for b in range(owners):
        at = pl.multiple_of(place_ref[b] * rows, rows)
        xt_ref[pl.ds(at, rows), :] = flipped[b * rows : (b + 1) * rows]


ROW_BLOCK = 320


def expert_a_kernel(*refs, experts, second_first):
    step = pl.program_id(0)
    if experts:
        place_ref, x_parts, c_parts = refs[0], refs[1 : 1 + experts], refs[1 + experts : 1 + 2 * experts]
        gh_ref, wg_ref, wu_ref = refs[1 + 2 * experts : 4 + 2 * experts]
        x_ref, xt_ref, gate_ref, gc_ref = refs[4 + 2 * experts : 8 + 2 * experts]

        @pl.when(step == 0)
        def _():
            expert_first(place_ref, x_parts, c_parts, x_ref, xt_ref, gate_ref, gc_ref)

    else:
        x_ref, xt_ref, gate_ref, gh_ref, wg_ref, wu_ref = refs[:6]
    keep_ref, send_ref, sc_ref, hid_ref, hidt_ref, gg_ref, gu_ref = refs[-7:]

    @pl.when(step == 0)
    def _():
        sc_ref[...] = jnp.zeros_like(sc_ref)

    wg, wu = wg_ref[0], wu_ref[0]
    width = wg.shape[1]
    for start in range(0, x_ref.shape[0], ROW_BLOCK):
        part = slice(start, start + ROW_BLOCK)
        x = x_ref[part, :]
        gate_pre = dot(x, wg)
        up_pre = dot(x, wu)
        grad = gh_ref[part, :].astype(F32)
        act, slope = gelu_parts(gate_pre)
        hidden = act * up_pre
        hid_ref[part, :] = hidden.astype(BF)
        product = hidden * grad
        folded = product[:, 0:LANES]
        for i in range(1, width // LANES):
            folded = folded + product[:, i * LANES : (i + 1) * LANES]
        sc_ref[part, :] += folded
        grad = grad * gate_ref[part, 0:1]
        gg_ref[part, :] = (slope * up_pre * grad).astype(BF)
        gu_ref[part, :] = (act * grad).astype(BF)
    hidt_ref[...] = hid_ref[...].T
    xt = xt_ref[...]
    cut = xt.shape[0] // 4
    for i, grad_ref in enumerate((gg_ref, gu_ref)):
        term = dot(xt, grad_ref[...]).astype(BF)
        for q in range(4):
            upper, lower = (q % 2, q // 2) if second_first else (q // 2, q % 2)
            (send_ref if upper else keep_ref)[i, lower * cut : (lower + 1) * cut] = term[q * cut : (q + 1) * cut]


def expert_a(source, gh, w_gate, w_up, first, count, second_first, filled=()):
    opening = len(source[1]) if isinstance(source[1], (list, tuple)) else 0
    rows, ff = gh.shape
    width = w_gate.shape[1]
    span = count * FF_BLOCK
    col_weight = pl.BlockSpec((1, width, FF_BLOCK), lambda f: (0, 0, first + f))
    out_block = pl.BlockSpec((rows, FF_BLOCK), lambda f: (0, first + f))
    wide = jax.ShapeDtypeStruct((rows, ff), BF)
    tall = jax.ShapeDtypeStruct((ff, rows), BF)
    term = jax.ShapeDtypeStruct((2, width // 2, span), BF)
    term_block = pl.BlockSpec((2, width // 2, FF_BLOCK), lambda f: (0, 0, f))
    if opening:
        place, xs, cs = source
        args = (place, *xs, *cs)
        specs = [pl.BlockSpec(memory_space=pltpu.SMEM)] + whole_specs(xs) + whole_specs(cs)
        shared = [
            jax.ShapeDtypeStruct((rows, width), BF),
            jax.ShapeDtypeStruct((width, rows), BF),
            jax.ShapeDtypeStruct((rows, LANES), F32),
            jax.ShapeDtypeStruct((rows, width), BF),
        ]
    else:
        args = tuple(source)
        specs = whole_specs(source)
        shared = []
    args = (*args, gh, w_gate, w_up)
    used = len(args)
    first_filled = len(shared) + 3

    def run(*refs):
        expert_a_kernel(*refs[:used], *refs[used + len(filled) :], experts=opening, second_first=second_first)

    return pl.pallas_call(
        run,
        grid=(count,),
        in_specs=specs
        + [out_block, col_weight, col_weight]
        + [pl.BlockSpec(memory_space=pl.ANY)] * len(filled),
        out_specs=whole_specs(shared)
        + [term_block, term_block, const_spec((rows, LANES)), out_block]
        + [pl.BlockSpec((FF_BLOCK, rows), lambda f: (first + f, 0)), out_block, out_block],
        out_shape=shared + [term, term, jax.ShapeDtypeStruct((rows, LANES), F32), wide, tall, wide, wide],
        input_output_aliases={used + i: first_filled + i for i in range(len(filled))},
        compiler_params=params(),
        cost_estimate=cost_us(5.4 * count),
        name="expert_grads",
    )(*args, *filled)


def expert_b_kernel(gg_ref, gu_ref, *refs, cap):
    sc_refs, (wg_ref, wu_ref, out_ref, acc) = refs[:-4], refs[-4:]
    part_sum = dot_nt(gg_ref[...], wg_ref[0]) + dot_nt(gu_ref[...], wu_ref[0])
    step, block = pl.program_id(0), pl.program_id(1)

    @pl.when(step == 0)
    def _():
        acc[block] = part_sum

    @pl.when(step == pl.num_programs(0) - 1)
    def _():
        total = acc[block] + part_sum
        row = lax.broadcasted_iota(jnp.int32, (cap, cap), 0)
        lane = lax.broadcasted_iota(jnp.int32, (cap, cap), 1)
        place = lax.broadcasted_iota(jnp.int32, (TAIL, cap), 0)
        for at in range(total.shape[0] // cap):
            part = slice(at * cap, (at + 1) * cap)
            out_ref[at, 0:cap, :] = total[part].astype(BF)
            folded = sc_refs[0][part, :]
            for other in sc_refs[1:]:
                folded = folded + other[part, :]
            column = jnp.sum(folded, axis=1, keepdims=True)
            flat = jnp.sum(jnp.where(row == lane, column, 0.0), axis=0, keepdims=True)
            hi, mid, low = split3(flat)
            packed = jnp.where(
                place == 0, hi.astype(F32), jnp.where(place == 1, mid.astype(F32), jnp.where(place == 2, low.astype(F32), 0.0))
            )
            out_ref[at, cap : cap + TAIL, :] = jnp.zeros((TAIL, total.shape[1]), BF)
            out_ref[at, cap : cap + TAIL, 0:cap] = packed.astype(BF)


def expert_b(gg, gu, scs, w_gate, w_up, experts, upper):
    rows, ff = gg.shape
    width = w_gate.shape[1]
    cap = rows // experts
    blocks = rows // 2 // ROW_BLOCK
    first = blocks if upper else 0
    cut = ff // 2
    grads = pl.BlockSpec((ROW_BLOCK, cut), lambda k, m: (first + m, k))
    sums = pl.BlockSpec((ROW_BLOCK, LANES), lambda k, m: (first + m, 0))
    weight = pl.BlockSpec((1, width, cut), lambda k, m: (0, 0, k))
    return call(
        functools.partial(expert_b_kernel, cap=cap),
        (gg, gu, *scs, w_gate, w_up),
        [grads, grads] + [sums] * len(scs) + [weight, weight],
        grid=(2, blocks),
        out_specs=pl.BlockSpec((ROW_BLOCK // cap, cap + TAIL, width), lambda k, m: (m, 0, 0)),
        out_shape=jax.ShapeDtypeStruct((experts // 2, cap + TAIL, width), BF),
        scratch_shapes=[pltpu.VMEM((blocks, ROW_BLOCK, width), F32)],
        cost_estimate=cost_us(16),
        name="expert_input_grad",
    )


def down_kernel(place_a_ref, place_b_ref, hidt_ref, gc_ref, *outs):
    ff, half = outs[0].shape
    shard = ff // place_a_ref.shape[0]
    size = int(np.gcd(shard, 32))
    rows = hidt_ref.shape[0]
    step = pl.program_id(0)
    total = dot(hidt_ref[...], gc_ref[...]).astype(BF)
    for i in range(rows // size):
        row = step * rows + i * size
        owner = row // shard
        piece = total[i * size : (i + 1) * size]
        for out, place_ref, cols in ((outs[0], place_a_ref, piece[:, :half]), (outs[1], place_b_ref, piece[:, half:])):
            at = place_ref[owner] * shard + (row - owner * shard)
            out[pl.ds(pl.multiple_of(at, size), size), :] = cols


def down_grads(hid_t, grad_cots, place_a, place_b):
    rows, width = grad_cots.shape
    ff = hid_t.shape[0]
    table = pl.BlockSpec(memory_space=pltpu.SMEM)
    half = jax.ShapeDtypeStruct((ff, width // 2), BF)
    return call(
        down_kernel,
        (place_a, place_b, hid_t, grad_cots),
        [table, table, pl.BlockSpec((ff // 4, rows), lambda f: (f, 0)), const_spec((rows, width))],
        grid=(4,),
        out_specs=[const_spec(half.shape)] * 2,
        out_shape=[half] * 2,
        cost_estimate=cost_us(13),
        name="down_grads",
    )


def produced_kernel(me_ref, hid_ref, wd_ref, out_ref):
    del me_ref
    out_ref[0] = dot(hid_ref[...], wd_ref[0]).astype(BF)


def produced_rows(me, hid, w_down, experts):
    rows, ff = hid.shape
    width = w_down.shape[2]
    cap = rows // experts
    return pl.pallas_call(
        produced_kernel,
        grid_spec=pltpu.PrefetchScalarGridSpec(
            num_scalar_prefetch=1,
            grid=(experts,),
            in_specs=[
                pl.BlockSpec((cap, ff), lambda m, me_ref: (m, 0)),
                pl.BlockSpec(w_down.shape, lambda m, me_ref: (0, 0, 0)),
            ],
            out_specs=pl.BlockSpec((1, cap, width), lambda m, me_ref: (m ^ me_ref[0], 0, 0)),
        ),
        out_shape=jax.ShapeDtypeStruct((experts, cap, width), BF),
        compiler_params=params(),
        cost_estimate=cost_us(2000),
        name="produced_rows",
    )(me.reshape(1).astype(jnp.int32), hid, w_down)


def layer_out_kernel(mid_ref, ch_ref, code_ref, parts_ref, out_ref):
    cap = parts_ref.shape[1]
    total = mid_ref[...]
    for e in range(parts_ref.shape[0]):
        picked = dot(selector_t(code_ref[:, e : e + 1], cap), parts_ref[e])
        total = total + ch_ref[:, e : e + 1] * picked
    out_ref[...] = total.astype(BF)


def distinct(slots):
    arrays = []
    found = []
    for array, index in slots:
        which = next((i for i, other in enumerate(arrays) if other is array), None)
        if which is None:
            which = len(arrays)
            arrays.append(array)
        found.append((which, index))
    return arrays, found


def layer_output(middle, chances_t, code_t, returned):
    rows, width = middle.shape
    return call(
        layer_out_kernel,
        (middle, chances_t, code_t, returned),
        [pl.BlockSpec(memory_space=pltpu.VMEM)] * 4,
        out_shape=jax.ShapeDtypeStruct((rows, width), BF),
        cost_estimate=cost_us(2000),
        name="layer_output",
    )


def moe_bwd_kernel(
    place_ref, cot_ref, mid_ref, gain_ref, nm_ref, ch_ref, wr_ref, code_ref, codet_ref, att_ref, wo_ref, *refs, places
):
    gmid_ref, ga_ref, keep_ref, send_ref, gain_o_ref, router_o_ref, att_scr = refs[-7:]
    experts = len(places)
    cap = refs[0].shape[1] - TAIL
    rows = cot_ref.shape[0]
    grad = jnp.zeros(mid_ref.shape, F32)
    gate_rows = []
    for m, (which, index) in enumerate(places):
        grad = grad + dot(selector_t(codet_ref[:, m : m + 1], cap), refs[which][index, 0:cap, :])
        picked = dot(refs[which][index, cap : cap + TAIL, 0:cap], selector(code_ref[m : m + 1, :], cap))
        gate_rows.append(jnp.sum(picked, axis=0, keepdims=True))
    gate_rows.append(jnp.zeros((TAIL - experts, rows), F32))
    grad_chances = jnp.concatenate(gate_rows, axis=0)
    chances = ch_ref[...]
    grad_logits = chances * (grad_chances - jnp.sum(chances * grad_chances, axis=0, keepdims=True))
    pieces = jnp.concatenate(split3(grad_logits), axis=0)
    wr = wr_ref[...]
    grad = grad + dot_tn(pieces, jnp.concatenate([wr, wr, wr], axis=0))
    router = dot(pieces, nm_ref[...])
    router_o_ref[...] = router[0:TAIL] + router[TAIL : 2 * TAIL] + router[2 * TAIL : 3 * TAIL]
    mid = mid_ref[...]
    scale = rms_scale(mid)
    unit = mid * scale
    gain_o_ref[...] = jnp.sum(grad * unit, axis=0, keepdims=True)
    scaled = grad * gain_ref[...]
    grad_mid = cot_ref[...].astype(F32) + scale * (scaled - unit * jnp.mean(scaled * unit, axis=-1, keepdims=True))
    gmid_ref[...] = grad_mid
    branch = grad_mid.astype(BF)
    ga_ref[...] = dot_nt(branch, wo_ref[...]).astype(BF)
    sort_rows(place_ref, att_ref[...].astype(F32).T, att_scr)
    half = att_scr.shape[0] // 2
    term = dot(att_scr[...].astype(BF), branch).astype(BF)
    keep_ref[0] = term[:half]
    send_ref[0] = term[half:]


def sort_rows(place_ref, value, out_ref):
    owners = place_ref.shape[0]
    rows = value.shape[0] // owners
    for b in range(owners):
        out_ref[pl.ds(pl.multiple_of(place_ref[b] * rows, rows), rows), :] = value[b * rows : (b + 1) * rows]


def moe_bwd(place, cot, middle, gain_moe, normed_moe, chances, wr_t, code, code_t, attended, w_out, slots):
    rows, width = cot.shape
    arrays, found = distinct(slots)
    args = (cot, middle, gain_moe[None], normed_moe, chances, wr_t, code, code_t, attended, w_out, *arrays)
    half = jax.ShapeDtypeStruct((1, width // 2, width), BF)
    return call(
        functools.partial(moe_bwd_kernel, places=found),
        (place, *args),
        [pl.BlockSpec(memory_space=pltpu.SMEM)] + [pl.BlockSpec(memory_space=pltpu.VMEM)] * len(args),
        out_shape=[
            jax.ShapeDtypeStruct((rows, width), F32),
            jax.ShapeDtypeStruct((rows, width), BF),
            half,
            half,
            jax.ShapeDtypeStruct((1, width), F32),
            jax.ShapeDtypeStruct((TAIL, width), F32),
        ],
        scratch_shapes=[pltpu.VMEM((width, rows), F32)],
        cost_estimate=cost_us(11.5),
        name="moe_bwd",
    )


def attn_bwd_kernel(
    qs_ref, k_ref, v_ref, ga_ref, lse_ref, woff_ref, segc_ref, segr_ref,
    dq_ref, dk_ref, dv_ref, dwoff_ref, mask_scr, p_scr, ds_scr,
    *, head_dim,
):
    rows = qs_ref.shape[0]
    blocks = rows // LANES

    @pl.when(pl.program_id(0) == 0)
    def _():
        mask_scr[...] = jnp.where(segc_ref[...] == segr_ref[...], 0.0, FAR)

    scaled, keys, values, grads = qs_ref[...], k_ref[...], v_ref[...], ga_ref[...]
    q_t, g_t, k_t = scaled.T, grads.T, keys.T
    low_half = lax.broadcasted_iota(jnp.int32, (rows, LANES), 1) < head_dim
    dq_t, dk_parts, dv_parts = [], [], []
    lane = lax.broadcasted_iota(jnp.int32, (1, BAND), 1)
    for h in range(HEAD_GROUP):
        row = woff_ref[0, h : h + 1, :]
        band = band_of(row)
        pair = slice(LANES * (h // 2), LANES * (h // 2 + 1))
        k_pair, v_pair = keys[:, pair], values[:, pair]
        q_only, g_only = only_rows(q_t, h, head_dim), only_rows(g_t, h, head_dim)
        tiles = {}
        for b in range(blocks):
            lanes = slice(b * LANES, (b + 1) * LANES)
            s = dot(k_pair, q_only[:, lanes]) + bias_column(band, row, b, blocks) + mask_scr[:, lanes]
            p = jnp.exp(s - lse_ref[0, h : h + 1, lanes])
            dp = dot(v_pair, g_only[:, lanes])
            ds = p * (dp - jnp.sum(p * dp, axis=0, keepdims=True))
            p_scr[:, lanes] = p.astype(BF)
            ds_scr[:, lanes] = ds.astype(BF)
            for k_block in range(blocks):
                d = max(-2, min(2, k_block - b))
                tile = ds[k_block * LANES : (k_block + 1) * LANES]
                tiles[d] = tiles[d] + tile if d in tiles else tile
        skewed = jnp.concatenate([tiles[1], tiles[0], tiles[-1], jnp.zeros_like(tiles[0])], axis=1)
        offsets = diagonal_sums(skewed)
        offsets = offsets + jnp.where(lane == FAR_AFTER, jnp.sum(tiles[2]), 0.0)
        offsets = offsets + jnp.where(lane == FAR_BEFORE, jnp.sum(tiles[-2]), 0.0)
        dwoff_ref[0, h : h + 1, :] = offsets
        p_all, ds_all = p_scr[...], ds_scr[...]
        dv_parts.append(dot(p_all, grads[:, pair]))
        dk_parts.append(dot(ds_all, scaled[:, pair]))
        dq_t.append(dot(k_t[h * head_dim : (h + 1) * head_dim], ds_all))
    dq = jnp.concatenate(dq_t, axis=0).T * head_dim ** (-0.5)
    dq_ref[...] = dq.astype(BF)
    for i in range(HEAD_GROUP // 2):
        pair = slice(LANES * i, LANES * (i + 1))
        dk_ref[:, pair] = jnp.where(low_half, dk_parts[2 * i], dk_parts[2 * i + 1]).astype(BF)
        dv_ref[:, pair] = jnp.where(low_half, dv_parts[2 * i], dv_parts[2 * i + 1]).astype(BF)


def attn_bwd(scaled, keys, values, grad_att, lse, woff, seg):
    rows, width = scaled.shape
    groups = woff.shape[0]
    cols = width // groups
    col_block = pl.BlockSpec((rows, cols), lambda g: (0, g))
    wide = jax.ShapeDtypeStruct((rows, width), BF)
    return call(
        functools.partial(attn_bwd_kernel, head_dim=cols // HEAD_GROUP),
        (scaled, keys, values, grad_att, lse, woff, seg.reshape(rows, 1), seg.reshape(1, rows)),
        [
            col_block,
            col_block,
            col_block,
            col_block,
            pl.BlockSpec((1, HEAD_GROUP, rows), lambda g: (g, 0, 0)),
            pl.BlockSpec((1, HEAD_GROUP, BAND), lambda g: (g, 0, 0)),
            const_spec((rows, 1)),
            const_spec((1, rows)),
        ],
        grid=(groups,),
        out_specs=[col_block, col_block, col_block, pl.BlockSpec((1, HEAD_GROUP, BAND), lambda g: (g, 0, 0))],
        out_shape=[wide, wide, wide, jax.ShapeDtypeStruct((groups, HEAD_GROUP, BAND), F32)],
        scratch_shapes=[
            pltpu.VMEM((rows, rows), F32),
            pltpu.VMEM((rows, rows), BF),
            pltpu.VMEM((rows, rows), BF),
        ],
        cost_estimate=cost_us(2000),
        name="attn_bwd",
    )


def dense_bwd_kernel(
    pq_ref, pk_ref, pv_ref, tok_ref, gain_ref, gmid_ref, dq_ref, dk_ref, dv_ref, wq_ref, wk_ref, wv_ref,
    tg_ref, keep_ref, send_ref, gain_o_ref, sort_scr, nt_scr, acc,
):
    step = pl.program_id(0)

    @pl.when(step == 0)
    def _():
        start = tok_ref[...].astype(F32)
        normed_t = (start * rms_scale(start) * gain_ref[...]).T
        for i, place_ref in enumerate((pq_ref, pk_ref, pv_ref)):
            sort_rows(place_ref, normed_t, sort_scr)
            nt_scr[i] = sort_scr[...].astype(BF)
        acc[...] = jnp.zeros_like(acc)

    total = acc[...]
    half = keep_ref.shape[1]
    for i, (d_ref, w_ref) in enumerate(((dq_ref, wq_ref), (dk_ref, wk_ref), (dv_ref, wv_ref))):
        part = d_ref[...]
        term = dot(nt_scr[i], part).astype(BF)
        keep_ref[i] = term[:half]
        send_ref[i] = term[half:]
        total = total + dot_nt(part, w_ref[...])
    acc[...] = total

    @pl.when(step == pl.num_programs(0) - 1)
    def _():
        grad = acc[...]
        start = tok_ref[...].astype(F32)
        scale = rms_scale(start)
        unit = start * scale
        gain_o_ref[...] = jnp.sum(grad * unit, axis=0, keepdims=True)
        scaled = grad * gain_ref[...]
        tg_ref[...] = gmid_ref[...] + scale * (scaled - unit * jnp.mean(scaled * unit, axis=-1, keepdims=True))


def dense_bwd(places, tokens, gain_attn, grad_mid, dq, dk, dv, w_query, w_key, w_value):
    rows, width = tokens.shape
    cols = 256
    col_block = pl.BlockSpec((rows, cols), lambda g: (0, g))
    weight_block = pl.BlockSpec((width, cols), lambda g: (0, g))
    term = jax.ShapeDtypeStruct((3, width // 2, width), BF)
    term_block = pl.BlockSpec((3, width // 2, cols), lambda g: (0, 0, g))
    return call(
        dense_bwd_kernel,
        (*places, tokens, gain_attn[None], grad_mid, dq, dk, dv, w_query, w_key, w_value),
        [pl.BlockSpec(memory_space=pltpu.SMEM)] * 3
        + [const_spec((rows, width)), const_spec((1, width)), const_spec((rows, width))]
        + [col_block] * 3
        + [weight_block] * 3,
        grid=(width // cols,),
        out_specs=[const_spec((rows, width)), term_block, term_block, const_spec((1, width))],
        out_shape=[jax.ShapeDtypeStruct((rows, width), F32), term, term, jax.ShapeDtypeStruct((1, width), F32)],
        scratch_shapes=[
            pltpu.VMEM((width, rows), F32),
            pltpu.VMEM((3, width, rows), BF),
            pltpu.VMEM((rows, width), F32),
        ],
        cost_estimate=cost_us(15.5),
        name="dense_bwd",
    )


def bits_of(size):
    return size.bit_length() - 1


def swap(value, axis, size, mask):
    return lax.ppermute(value, axis, [(i, i ^ mask) for i in range(size)])


def exchange(parts, axis, size, name):
    with jax.named_scope(name):
        return [part if m == 0 else swap(part, axis, size, m) for m, part in enumerate(parts)]


def pick(value, index, axis):
    return lax.dynamic_index_in_dim(value, index, axis, keepdims=False)


class Order:
    def __init__(self, token):
        self.token = token

    def enter(self, tree):
        tree, self.token = lax.optimization_barrier((tree, self.token))
        return tree

    leave = enter


def places(me, bits, order):
    key = jnp.arange(1 << bits, dtype=jnp.int32) ^ me
    place = jnp.zeros_like(key)
    for bit in order:
        place = place * 2 + ((key >> bit) & 1)
    return place


class Halving:
    def __init__(self, order, keep, send, dim, route, name):
        self.order, self.keep, self.to_send, self.dim, self.route, self.name = order, keep, send, dim, list(route), name
        self.got = None

    def start(self):
        axis, size, bit = self.route[0]
        with jax.named_scope(f"{self.name}_{axis}{1 << bit}"):
            value = self.order.enter(self.keep if self.to_send is None else self.to_send)
            self.got = swap(value, axis, size, 1 << bit)


def fold_kernel(*refs, cuts):
    pairs, outs = refs[: 2 * len(cuts)], list(refs[2 * len(cuts) :])
    for i, (dim, last) in enumerate(cuts):
        keep, got = pairs[2 * i][...].astype(F32), pairs[2 * i + 1][...].astype(F32)
        total = keep + got
        if last:
            outs.pop(0)[...] = total
            continue
        rows = total.shape[dim] // 2
        for start in (0, rows):
            outs.pop(0)[...] = lax.slice_in_dim(total, start, start + rows, axis=dim).astype(BF)


def fold(*units, cost=3):
    order = units[0].order
    args, cuts, shapes = [], [], []
    for unit in units:
        unit.route.pop(0)
        got = order.leave(unit.got)
        args += [unit.keep, got]
        whole = unit.to_send is None
        last = whole or not unit.route
        cuts.append((unit.dim, last))
        if last:
            shapes.append(jax.ShapeDtypeStruct(got.shape, F32))
        else:
            shape = list(got.shape)
            shape[unit.dim] //= 2
            shapes += [jax.ShapeDtypeStruct(tuple(shape), BF)] * 2
    args = order.enter(args)
    outs = list(
        call(
            functools.partial(fold_kernel, cuts=cuts),
            args,
            [pl.BlockSpec(memory_space=pltpu.VMEM)] * len(args),
            out_shape=shapes,
            cost_estimate=cost_us(cost),
            name="fold",
        )
    )
    outs = order.leave(outs)
    for unit, (_, last) in zip(units, cuts):
        unit.keep = outs.pop(0)
        if not last:
            unit.to_send = outs.pop(0)
        if unit.route:
            unit.start()


def fold_first_kernel(*refs, groups):
    pairs, outs = refs[: -2 * len(groups)], refs[-2 * len(groups) :]
    for i, members in enumerate(groups):
        for at, (array, index) in enumerate(members):
            total = pairs[2 * array][index].astype(F32) + pairs[2 * array + 1][index].astype(F32)
            rows = total.shape[0] // 2
            outs[2 * i][at] = total[:rows].astype(BF)
            outs[2 * i + 1][at] = total[rows:].astype(BF)


def fold_first(pairs, groups):
    args = [v for pair in pairs for v in pair]
    _, rows, width = args[0].shape
    shapes = [jax.ShapeDtypeStruct((len(members), rows // 2, width), BF) for members in groups for _ in range(2)]
    return call(
        functools.partial(fold_first_kernel, groups=groups),
        args,
        [pl.BlockSpec(memory_space=pltpu.VMEM)] * len(args),
        out_shape=shapes,
        cost_estimate=cost_us(5),
        name="fold_first",
    )


class Return:
    def __init__(self, order, high, axis, size, name):
        self.order, self.axis, self.size, self.name = order, axis, size, name
        self.slots = [None] * size
        self.bit = bits_of(size) - 1
        self.start(high)

    def low(self, value):
        for i in range(value.shape[0]):
            self.slots[i] = (value, i)

    def moving(self):
        return [m for m in range(self.size) if (m >> self.bit) & 1]

    def start(self, value):
        with jax.named_scope(f"{self.name}{1 << self.bit}"):
            self.got = swap(self.order.enter(value), self.axis, self.size, 1 << self.bit)

    def fold(self):
        got = self.order.leave(self.got)
        for i, m in enumerate(self.moving()):
            self.slots[m] = (got, i)
        self.bit -= 1
        if self.bit >= 0:
            self.start(jnp.stack([self.slots[m][0][self.slots[m][1]] for m in self.moving()]))

    def finish(self):
        while self.bit >= 0:
            self.fold()
        return self.slots


def body(
    tokens,
    cotangent,
    gain_attn,
    w_query,
    w_key,
    w_value,
    w_out,
    rel_bias,
    gain_moe,
    w_router,
    w_gate,
    w_up,
    w_down,
    segments,
    routes,
    *,
    dp_size,
    ep_size,
):
    rows, width = tokens.shape
    buckets, heads = rel_bias.shape
    experts = w_router.shape[1]
    cap = 10 * rows // (4 * experts)
    ff = w_gate.shape[2]
    me = lax.axis_index("expert")

    onehot = jnp.asarray(band_onehot(rows, buckets))
    woff = jnp.dot(rel_bias.T, onehot, precision=HIGHEST).reshape(heads // HEAD_GROUP, HEAD_GROUP, BAND)
    order = jnp.arange(experts, dtype=jnp.int32) ^ me
    named = jnp.any(routes[None, :, :] == order[:, None, None], axis=-1)
    marks = named.astype(BF)
    before = jnp.asarray(np.triu(np.ones((rows, rows), np.float32), 1)).astype(BF)
    slots = jnp.dot(marks, before, preferred_element_type=F32).astype(jnp.int32)
    code = jnp.where(named, slots, -1)
    code_t = code.T
    by_index = routes[None, :, :] == jnp.arange(experts, dtype=jnp.int32)[:, None, None]
    by_index = jnp.any(by_index, axis=-1)
    slots_by_index = jnp.dot(by_index.astype(BF), before, preferred_element_type=F32).astype(jnp.int32)
    code_by_index_t = jnp.where(by_index, slots_by_index, -1).T
    in_order = (order[:, None] == jnp.arange(experts, dtype=jnp.int32)[None, :]).astype(BF)
    wr_t = jnp.dot(in_order, w_router.T, preferred_element_type=F32).astype(BF)
    wr_t = jnp.pad(wr_t, ((0, TAIL - experts), (0, 0)))

    dp_bits, ep_bits = bits_of(dp_size), bits_of(ep_size)
    dp_me = lax.axis_index("dp")
    dp_order = list(range(dp_bits))
    z_order = [1, 0] + dp_order[2:]
    place_x = places(dp_me, dp_bits, dp_order)
    place_z = places(dp_me, dp_bits, z_order)

    def dp_route(bits):
        return [("dp", dp_size, b) for b in bits]

    dp_part = [ep_bits + b for b in dp_order]
    ep_part = list(range(1, ep_bits))
    q_bits = [0] + ep_part + dp_part
    k_bits = [0] + dp_part + ep_part
    whole_me = dp_me * ep_size + me

    def route(bits):
        return [("expert", ep_size, b) if b < ep_bits else ("dp", dp_size, b - ep_bits) for b in bits]

    place_q, place_k = [places(whole_me, dp_bits + ep_bits, bits) for bits in (q_bits, k_bits)]

    cot_blocks = cot_dispatch(cotangent, code, experts, cap)
    order = Order((routes[0, :1] < 0).astype(F32))
    cots = exchange(cot_blocks, "expert", ep_size, "cot_rows")
    scaled, keys, values, attended, lse, middle, normed_moe, chances, *sent = attn_fwd(
        tokens, gain_attn, w_query, w_key, w_value, w_out, woff, segments, gain_moe, wr_t, code, experts, cap
    )
    sent, cots = order.enter((sent, cots))
    xs = exchange(sent, "expert", ep_size, "token_rows")
    grad_hidden = order.leave(cot_hidden(cots, w_down))

    blocks = ff // FF_BLOCK
    counts = [blocks // 3, blocks // 3 + 1]
    counts.append(blocks - sum(counts))
    starts = [sum(counts[:i]) for i in range(len(counts))]
    scs, units = [], []

    def expert_part(i, source, filled=()):
        *shared, keep, send, sc, hid, hid_t, gg, gu = order.leave(
            expert_a(order.enter(source), grad_hidden, w_gate, w_up, starts[i], counts[i], i == 0, filled)
        )
        scs.append(sc)
        units.append(Halving(order, keep, send, 1, dp_route(z_order if i == 0 else dp_order), f"gate_up{i}"))
        return shared, (hid, hid_t, gg, gu)

    (x_all, x_t, gate_all, grad_cots), filled = expert_part(0, (place_x, xs, cots))
    units[0].start()
    _, filled = expert_part(1, (x_all, x_t, gate_all), filled)
    units[1].start()
    _, (hid, hid_t, gg, gu) = expert_part(2, (x_all, x_t, gate_all), filled)
    fold(units[0])
    units[2].to_send = order.enter(units[2].to_send)
    back_high = order.leave(expert_b(order.enter(gg), gu, scs, w_gate, w_up, experts, True))
    backs = Return(order, back_high, "expert", ep_size, "grad_rows")
    back_low = order.leave(expert_b(order.enter(gg), gu, scs, w_gate, w_up, experts, False))
    backs.low(back_low)
    units[2].start()
    down_halves = order.leave(down_grads(order.enter(hid_t), grad_cots, place_z, place_x))
    down_units = [
        Halving(order, half[: ff // 2], half[ff // 2 :], 0, dp_route(bits), f"down{i}")
        for i, (half, bits) in enumerate(zip(down_halves, (z_order, dp_order)))
    ]
    fold(units[0], units[1])
    backs.fold()
    produced = order.leave(produced_rows(me, order.enter(hid), w_down, experts))
    backs.finish()
    down_units[0].start()
    grad_mid, grad_att, out_keep, out_send, gain_moe_term, router_term = order.leave(
        moe_bwd(place_q, cotangent, middle, gain_moe, normed_moe, chances, wr_t, code, code_t, attended, w_out, backs.slots)
    )
    fold(units[0])
    out_unit = Halving(order, out_keep, out_send, 1, route(q_bits)[:1], "out")
    out_unit.start()
    with jax.named_scope("produced_back"):
        returned = lax.all_to_all(order.enter(produced), "expert", 0, 0, tiled=True)
    dq, dk, dv, dwoff = order.leave(attn_bwd(scaled, keys, values, order.enter(grad_att), lse, woff, segments))
    out_got = order.leave(out_unit.got)
    fold(units[1], units[2])
    down_units[1].start()
    token_grad, qkv_keep, qkv_send, gain_attn_term = order.leave(
        dense_bwd((place_q, place_k, place_k), tokens, gain_attn, grad_mid, order.enter(dq), dk, dv, w_query, w_key, w_value)
    )
    qkv = Halving(order, qkv_keep, qkv_send, 1, route(q_bits)[:1], "qkv")
    qkv.start()
    fold(units[1], units[2], down_units[0], cost=2000)
    bias_term = jnp.dot(onehot, dwoff.reshape(heads, BAND).T, precision=HIGHEST)
    router_term = jnp.dot(router_term[:experts].T, in_order.astype(F32), precision=HIGHEST)
    devices = dp_size * ep_size
    share = width // devices
    small = jnp.concatenate(
        [
            router_term.reshape(devices, -1),
            gain_attn_term.reshape(devices, -1),
            gain_moe_term.reshape(devices, -1),
            bias_term.reshape(devices, -1),
        ],
        axis=1,
    )
    with jax.named_scope("small_sums"):
        small = lax.all_to_all(order.enter(small), ("dp", "expert"), 0, 0, tiled=True)
    got = order.leave(qkv.got)
    halves = order.leave(
        fold_first([order.enter((out_keep, out_got)), (qkv_keep, got)], [[(0, 0), (1, 0)], [(1, 1), (1, 2)]])
    )
    dense = [
        Halving(order, halves[2 * i], halves[2 * i + 1], 1, route(bits)[1:], name)
        for i, (bits, name) in enumerate(((q_bits, "out_q"), (k_bits, "k_v")))
    ]
    for unit in dense:
        unit.start()
    returned = order.leave(returned)
    chances_by_index = jnp.stack([pick(chances, me ^ e, 0) for e in range(experts)], axis=1)
    layer_out = order.leave(layer_output(middle, chances_by_index, code_by_index_t, order.enter(returned)))
    fold(units[2], down_units[1], cost=2000)
    fold(down_units[0], *dense)
    fold(down_units[1], *dense)
    rest = units + down_units + dense
    while any(unit.route for unit in rest):
        fold(*[unit for unit in rest if unit.route])
    small_sum = jnp.sum(order.leave(small), axis=0) + order.token

    terms = [unit.keep for unit in units]
    gate_grad = jnp.concatenate([term[0] for term in terms], axis=1)[None]
    up_grad = jnp.concatenate([term[1] for term in terms], axis=1)[None]
    down_grad = jnp.concatenate([unit.keep for unit in down_units], axis=1)[None]
    n_router = width * experts // devices
    n_gain = width // devices
    router_grad = small_sum[:n_router].reshape(share, experts)
    gain_attn_grad = small_sum[n_router : n_router + n_gain]
    gain_moe_grad = small_sum[n_router + n_gain : n_router + 2 * n_gain]
    bias_grad = small_sum[n_router + 2 * n_gain :]
    return (
        layer_out,
        token_grad,
        dense[0].keep[1],
        dense[1].keep[0],
        dense[1].keep[1],
        dense[0].keep[0],
        gain_attn_grad,
        gain_moe_grad,
        bias_grad,
        router_grad,
        gate_grad,
        up_grad,
        down_grad,
    )


def solution(mesh):
    in_specs = (
        P(("dp", "expert"), None),
        P(("dp", "expert"), None),
        P(),
        P(),
        P(),
        P(),
        P(),
        P(),
        P(),
        P(),
        P("expert", None, None),
        P("expert", None, None),
        P("expert", None, None),
        P(("dp", "expert"), None),
        P(("dp", "expert"), None),
    )
    out_specs = (
        P(("dp", "expert"), None),
        P(("dp", "expert"), None),
        P(("dp", "expert"), None),
        P(("dp", "expert"), None),
        P(("dp", "expert"), None),
        P(("dp", "expert"), None),
        P(("dp", "expert")),
        P(("dp", "expert")),
        P(("dp", "expert")),
        P(("dp", "expert"), None),
        P("expert", "dp", None),
        P("expert", "dp", None),
        P("expert", "dp", None),
    )
    run = functools.partial(body, dp_size=mesh.shape["dp"], ep_size=mesh.shape["expert"])
    return jax.shard_map(run, mesh=mesh, in_specs=in_specs, out_specs=out_specs, check_vma=False)
```

```python
import functools

import jax
import jax.numpy as jnp
import numpy as np
from jax import lax
from jax.experimental import pallas as pl
from jax.experimental.pallas import tpu as pltpu
from jax.sharding import PartitionSpec as P

EPS = 1e-06
HIGHEST = lax.Precision.HIGHEST
LANES = 128
BAND = 4 * LANES
HEAD_GROUP = 4
TAIL = 16
FAR = -1e30
BF = jnp.bfloat16
F32 = jnp.float32
VMEM_LIMIT = 56 * 1024 * 1024


def bucket_of(relative, buckets):
    halfway = buckets // 2
    exact_span = halfway // 2
    distance = np.abs(relative)
    beyond = exact_span + (
        np.log(np.maximum(distance, 1) / exact_span)
        / np.log(128.0 / exact_span)
        * (halfway - exact_span)
    ).astype(np.int64)
    beyond = np.minimum(beyond, halfway - 1)
    return (
        (relative > 0).astype(np.int64) * halfway
        + np.where(distance < exact_span, distance, beyond)
    ).astype(np.int32)


def band_onehot(length, buckets):
    place = np.arange(BAND)
    relative = np.where(place <= 3 * LANES, LANES - place, BAND + LANES - place)
    table = (bucket_of(relative, buckets)[None, :] == np.arange(buckets)[:, None]).astype(np.float32)
    table[:, 3 * LANES] = 0.0
    far = np.arange(LANES, length)
    assert np.all(bucket_of(far, buckets) == bucket_of(far, buckets)[0])
    assert np.all(bucket_of(-far, buckets) == bucket_of(-far, buckets)[0])
    return table


FAR_AFTER = 3 * LANES + 1
FAR_BEFORE = 3 * LANES - 1


def dot(a, b):
    return lax.dot_general(a, b, (((1,), (0,)), ((), ())), preferred_element_type=F32)


def dot_nt(a, b):
    return lax.dot_general(a, b, (((1,), (1,)), ((), ())), preferred_element_type=F32)


def dot_tn(a, b):
    return lax.dot_general(a, b, (((0,), (0,)), ((), ())), preferred_element_type=F32)


def split3(value):
    hi = value.astype(BF)
    rest = value - hi.astype(F32)
    mid = rest.astype(BF)
    low = (rest - mid.astype(F32)).astype(BF)
    return hi, mid, low


def rms_scale(value):
    return lax.rsqrt(jnp.mean(value * value, axis=-1, keepdims=True) + EPS)


def params(**kw):
    return pltpu.CompilerParams(vmem_limit_bytes=VMEM_LIMIT, **kw)


TIMES = {
    ("attn_second", 0): 25.0,
    ("fold", 2): 2.0,
    ("norm_bwd", 0): 7.0,
    ("fold", 6): 40.0,
}


TURNS = {}


def estimate(name):
    turn = TURNS.get(name, 0)
    TURNS[name] = turn + 1
    time = TIMES.get((name, turn), 1.0)
    return pl.CostEstimate(flops=int(time * 1.15e9), bytes_accessed=100000, transcendentals=0)


def call(kernel, args, in_specs, **kw):
    return pl.pallas_call(kernel, in_specs=list(in_specs), compiler_params=params(), **kw)(*args)


def whole_specs(args):
    return [const_spec(a.shape) for a in args]


def const_spec(shape):
    return pl.BlockSpec(shape, lambda *_: (0,) * len(shape))


def selector(code_row, rows):
    place = lax.broadcasted_iota(jnp.int32, (rows, code_row.shape[1]), 0)
    return jnp.where(place == code_row, 1.0, 0.0).astype(BF)


def selector_t(code_column, rows):
    place = lax.broadcasted_iota(jnp.int32, (code_column.shape[0], rows), 1)
    return jnp.where(place == code_column, 1.0, 0.0).astype(BF)


def band_of(row):
    return pltpu.roll(jnp.broadcast_to(row, (LANES, BAND)), 0, 1, stride=1, stride_axis=0)


def diagonal_sums(skewed):
    eight = skewed[0:8]
    for start in range(8, LANES, 8):
        eight = eight + pltpu.roll(skewed[start : start + 8], BAND - start, 1)
    total = eight[0:1]
    for row in range(1, 8):
        total = total + pltpu.roll(eight[row : row + 1], BAND - row, 1)
    return total


def bias_block(band, row, first, count, k_blocks):
    far = [jnp.broadcast_to(row[:, at : at + 1], (LANES, LANES)) for at in (FAR_BEFORE, FAR_AFTER)]
    columns = []
    for q_block in range(first, first + count):
        pieces = []
        for k_block in range(k_blocks):
            d = k_block - q_block
            pieces.append(far[1] if d > 1 else far[0] if d < -1 else band[:, LANES * (1 - d) : LANES * (2 - d)])
        columns.append(jnp.concatenate(pieces, axis=0))
    return jnp.concatenate(columns, axis=1)


def only_rows(value, h, head_dim):
    mine = value[h * head_dim : (h + 1) * head_dim]
    none = jnp.zeros_like(mine)
    return jnp.concatenate([mine, none] if h % 2 == 0 else [none, mine], axis=0)


def attend(scaled, keys, values, woff_ref, mask, first, head_dim):
    count = scaled.shape[0] // LANES
    q_t, v_t = scaled.T, values.T
    heads_t, totals = [], []
    for h in range(HEAD_GROUP):
        row = woff_ref[0, h : h + 1, :]
        bias = bias_block(band_of(row), row, first, count, keys.shape[0] // LANES)
        k_pair = keys[:, LANES * (h // 2) : LANES * (h // 2 + 1)]
        s = dot(k_pair, only_rows(q_t, h, head_dim)) + bias + mask
        peak = jnp.max(s, axis=0, keepdims=True)
        p = jnp.exp(s - peak)
        total = jnp.sum(p, axis=0, keepdims=True)
        heads_t.append(dot(v_t[h * head_dim : (h + 1) * head_dim], p.astype(BF)) * (1.0 / total))
        totals.append(peak + jnp.log(total))
    return jnp.concatenate(heads_t, axis=0).T.astype(BF), jnp.concatenate(totals, axis=0)


def route_rows(mid, gain_ref, wr_ref, experts, nm_ref, ch_ref, payload_ref):
    rows = mid.shape[0]
    nm = (mid * rms_scale(mid) * gain_ref[...]).astype(BF)
    nm_ref[...] = nm
    router = jnp.concatenate([wr_ref[...].astype(F32).T, jnp.zeros((TAIL - experts, nm.shape[1]), F32)], axis=0)
    logits = dot_nt(router.astype(BF), nm)
    live = lax.broadcasted_iota(jnp.int32, logits.shape, 0) < experts
    logits = jnp.where(live, logits, FAR)
    raised = jnp.exp(logits - jnp.max(logits, axis=0, keepdims=True))
    chances = raised / jnp.sum(raised, axis=0, keepdims=True)
    ch_ref[...] = chances
    hi = chances.astype(BF).astype(F32)
    both = jnp.concatenate([hi[: TAIL // 2], (chances - hi)[: TAIL // 2]], axis=0)
    payload_ref[0:rows, :] = nm
    payload_ref[rows:, :] = jnp.concatenate([both, jnp.zeros((TAIL, nm.shape[1] - rows), F32)], axis=1).astype(BF)


def segment_mask(seg_ref, first, count):
    seg = seg_ref[...].astype(F32)
    column = jnp.broadcast_to(seg, (8, seg.shape[1])).T[:, 0:1]
    return jnp.where(column == seg[:, first : first + count], 0.0, FAR)


def attn_first_kernel(
    tok_ref, gain_a_ref, wq_ref, wk_ref, wv_ref, wo_ref, bias_ref, onehot_ref, seg_ref, gain_m_ref, wr_ref,
    qs_ref, k_ref, v_ref, woff_ref, token_ref, att_ref, lse_ref, mid_ref, nm_ref, ch_ref, payload_ref,
    n_scr, mask_scr, woff_scr,
    *, experts, head_dim,
):
    step = pl.program_id(0)
    rows = att_ref.shape[0]

    @pl.when(step == 0)
    def _():
        start = tok_ref[...].astype(F32)
        n_scr[...] = (start * rms_scale(start) * gain_a_ref[...]).astype(BF)
        mid_ref[...] = start[:rows]
        mask_scr[...] = segment_mask(seg_ref, 0, rows)
        token_ref[...] = jnp.where(seg_ref[:, 0:LANES] < 0, 1.0, 0.0)
        table = onehot_ref[...]
        offsets = sum(dot_tn(part, table) for part in split3(bias_ref[...]))
        for g in range(woff_scr.shape[0]):
            woff_scr[g] = offsets[g * HEAD_GROUP : (g + 1) * HEAD_GROUP]

    woff_ref[0] = woff_scr[step]

    normed = n_scr[...]
    scaled = (dot(normed, wq_ref[...]).astype(BF).astype(F32) * head_dim ** (-0.5)).astype(BF)
    keys = dot(normed, wk_ref[...]).astype(BF)
    values = dot(normed, wv_ref[...]).astype(BF)
    qs_ref[...] = scaled
    k_ref[...] = keys
    v_ref[...] = values
    att, totals = attend(scaled[:rows], keys, values, woff_ref, mask_scr[...], 0, head_dim)
    att_ref[...] = att
    lse_ref[0] = totals
    mid_ref[...] += dot(att, wo_ref[...])

    @pl.when(step == pl.num_programs(0) - 1)
    def _():
        route_rows(mid_ref[...], gain_m_ref, wr_ref, experts, nm_ref, ch_ref, payload_ref)


def attn_second_kernel(
    tok_ref, qs_ref, k_ref, v_ref, wo_ref, woff_ref, seg_ref, gain_m_ref, wr_ref, *refs, experts, head_dim
):
    att_ref, lse_ref, mid_ref, nm_ref, ch_ref, payload_ref, mask_scr = refs[-7:]
    step = pl.program_id(0)
    rows = att_ref.shape[0]

    @pl.when(step == 0)
    def _():
        mid_ref[...] = tok_ref[...].astype(F32)
        mask_scr[...] = segment_mask(seg_ref, rows, rows)

    att, totals = attend(qs_ref[...], k_ref[...], v_ref[...], woff_ref, mask_scr[...], rows // LANES, head_dim)
    att_ref[...] = att
    lse_ref[0] = totals
    mid_ref[...] += dot(att, wo_ref[...])

    @pl.when(step == pl.num_programs(0) - 1)
    def _():
        route_rows(mid_ref[...], gain_m_ref, wr_ref, experts, nm_ref, ch_ref, payload_ref)


def attn_halves(rows, width, groups, half):
    cols, part = width // groups, rows // 2
    wide = jax.ShapeDtypeStruct((rows, width), BF)
    shapes = [
        wide,
        jax.ShapeDtypeStruct((groups, HEAD_GROUP, rows), F32),
        jax.ShapeDtypeStruct((rows, width), F32),
        wide,
        jax.ShapeDtypeStruct((TAIL, rows), F32),
        jax.ShapeDtypeStruct((part + TAIL, width), BF),
    ]
    specs = [
        pl.BlockSpec((part, cols), lambda g: (half, g)),
        pl.BlockSpec((1, HEAD_GROUP, part), lambda g: (g, 0, half)),
        pl.BlockSpec((part, width), lambda g: (half, 0)),
        pl.BlockSpec((part, width), lambda g: (half, 0)),
        pl.BlockSpec((TAIL, part), lambda g: (0, half)),
        const_spec((part + TAIL, width)),
    ]
    return shapes, specs


def attn_first(tokens, gain_attn, w_query, w_key, w_value, w_out, rel_bias, seg, gain_moe, w_router):
    rows, width = tokens.shape
    buckets, heads = rel_bias.shape
    experts = w_router.shape[1]
    groups = heads // HEAD_GROUP
    cols, part = width // groups, rows // 2
    weight_block = pl.BlockSpec((width, cols), lambda g: (0, g))
    shapes, specs = attn_halves(rows, width, groups, 0)
    wide = jax.ShapeDtypeStruct((rows, width), BF)
    return call(
        functools.partial(attn_first_kernel, experts=experts, head_dim=cols // HEAD_GROUP),
        (tokens, gain_attn[None], w_query, w_key, w_value, w_out, rel_bias, jnp.asarray(band_onehot(rows, buckets)).astype(BF),
         seg, gain_moe[None], w_router),
        [
            const_spec((rows, width)),
            const_spec((1, width)),
            weight_block,
            weight_block,
            weight_block,
            pl.BlockSpec((cols, width), lambda g: (g, 0)),
            const_spec(rel_bias.shape),
            const_spec((buckets, BAND)),
            const_spec(seg.shape),
            const_spec((1, width)),
            const_spec(w_router.shape),
        ],
        grid=(groups,),
        out_specs=[pl.BlockSpec((rows, cols), lambda g: (0, g))] * 3
        + [pl.BlockSpec((1, HEAD_GROUP, BAND), lambda g: (g, 0, 0)), const_spec((1, LANES))]
        + specs,
        out_shape=[wide] * 3
        + [jax.ShapeDtypeStruct((groups, HEAD_GROUP, BAND), F32), jax.ShapeDtypeStruct((1, LANES), F32)]
        + shapes,
        scratch_shapes=[
            pltpu.VMEM((rows, width), BF),
            pltpu.VMEM((rows, part), F32),
            pltpu.VMEM((groups, HEAD_GROUP, BAND), F32),
        ],
        cost_estimate=estimate("attn_first"),
        name="attn_first",
    )


def attn_second(tokens, scaled, keys, values, w_out, woff, seg, gain_moe, w_router, filled):
    rows, width = tokens.shape
    experts = w_router.shape[1]
    groups = woff.shape[0]
    cols, part = width // groups, rows // 2
    col_block = pl.BlockSpec((rows, cols), lambda g: (0, g))
    shapes, specs = attn_halves(rows, width, groups, 1)
    args = (tokens, scaled, keys, values, w_out, woff, seg, gain_moe[None], w_router)
    return call(
        functools.partial(attn_second_kernel, experts=experts, head_dim=cols // HEAD_GROUP),
        (*args, *filled),
        [
            pl.BlockSpec((part, width), lambda g: (1, 0)),
            pl.BlockSpec((part, cols), lambda g: (1, g)),
            col_block,
            col_block,
            pl.BlockSpec((cols, width), lambda g: (g, 0)),
            pl.BlockSpec((1, HEAD_GROUP, BAND), lambda g: (g, 0, 0)),
            const_spec(seg.shape),
            const_spec((1, width)),
            const_spec(w_router.shape),
        ]
        + [pl.BlockSpec(memory_space=pl.ANY)] * len(filled),
        grid=(groups,),
        out_specs=specs,
        out_shape=shapes,
        scratch_shapes=[pltpu.VMEM((rows, part), F32)],
        input_output_aliases={len(args) + i: i for i in range(len(filled))},
        cost_estimate=estimate("attn_second"),
        name="attn_second",
    )


def gelu_parts(gate):
    c0 = np.float32(np.sqrt(2.0 / np.pi))
    c1 = np.float32(0.044715)
    square = gate * gate
    t = jnp.tanh(c0 * gate * (1.0 + c1 * square))
    half = 0.5 * (1.0 + t)
    value = gate * half
    slope = half + 0.5 * gate * (1.0 - t * t) * (c0 * (1.0 + 3.0 * c1 * square))
    return value, slope


FF_BLOCK = 256


def cot_hidden_kernel(*refs, experts):
    code_ref, cot_refs, wd_ref = refs[0], refs[1 : 1 + experts], refs[1 + experts]
    out_ref, rows_ref = refs[2 + experts :]

    @pl.when(pl.program_id(0) == 0)
    def _():
        cap = rows_ref.shape[0] // experts
        for m, cot_ref in enumerate(cot_refs):
            rows_ref[m * cap : (m + 1) * cap, :] = dot(selector(code_ref[m : m + 1, :], cap), cot_ref[...]).astype(BF)

    out_ref[...] = dot_nt(rows_ref[...], wd_ref[0]).astype(BF)


def cot_hidden(code, cots, w_down, cap, count):
    experts = len(cots)
    width = cots[0].shape[1]
    rows = experts * cap
    return call(
        functools.partial(cot_hidden_kernel, experts=experts),
        (code, *cots, w_down),
        whole_specs((code, *cots)) + [pl.BlockSpec((1, FF_BLOCK, width), lambda f: (0, f, 0))],
        grid=(count,),
        out_specs=[pl.BlockSpec((rows, FF_BLOCK), lambda f: (0, f)), const_spec((rows, width))],
        out_shape=[jax.ShapeDtypeStruct((rows, count * FF_BLOCK), BF), jax.ShapeDtypeStruct((rows, width), BF)],
        cost_estimate=estimate("cot_hidden"),
        name="cot_hidden",
    )


def cot_hidden_more_kernel(rows_ref, wd_ref, out_ref):
    out_ref[...] = dot_nt(rows_ref[...], wd_ref[0]).astype(BF)


def cot_hidden_more(cot_rows, w_down, first):
    rows, width = cot_rows.shape
    count = w_down.shape[1] // FF_BLOCK - first
    return call(
        cot_hidden_more_kernel,
        (cot_rows, w_down),
        [const_spec((rows, width)), pl.BlockSpec((1, FF_BLOCK, width), lambda f: (0, first + f, 0))],
        grid=(count,),
        out_specs=pl.BlockSpec((rows, FF_BLOCK), lambda f: (0, f)),
        out_shape=jax.ShapeDtypeStruct((rows, count * FF_BLOCK), BF),
        cost_estimate=estimate("cot_hidden_more"),
        name="cot_hidden_more",
    )


ROW_BLOCK = 320


def expert_first(me_ref, place_ref, code_ref, payloads, cot_ref, x_ref, xt_ref, gate_ref, gc_ref):
    experts = len(payloads) // 2
    cap = x_ref.shape[0] // experts
    part = payloads[0].shape[0] - TAIL
    row = lax.broadcasted_iota(jnp.int32, (TAIL, part), 0)
    mine = jnp.logical_or(row == me_ref[0], row == me_ref[0] + TAIL // 2)
    for m in range(experts):
        chosen = selector(code_ref[m : m + 1, :], cap)
        place = slice(m * cap, (m + 1) * cap)
        total = jnp.zeros((cap, x_ref.shape[1]), F32)
        gate = jnp.zeros((cap, 1), F32)
        for i in range(2):
            payload = payloads[2 * m + i]
            part_chosen = chosen[:, i * part : (i + 1) * part]
            total = total + dot(part_chosen, payload[0:part, :])
            chances = jnp.sum(jnp.where(mine, payload[part:, 0:part].astype(F32), 0.0), axis=0, keepdims=True)
            gate = gate + jnp.sum(part_chosen.astype(F32) * chances, axis=1, keepdims=True)
        x_ref[place, :] = total.astype(BF)
        gate_ref[place, :] = jnp.broadcast_to(gate, (cap, LANES))
        gc_ref[place, :] = (cot_ref[place, :].astype(F32) * gate).astype(BF)
    flipped = x_ref[...].T
    owners = place_ref.shape[0]
    rows = flipped.shape[0] // owners
    for b in range(owners):
        at = pl.multiple_of(place_ref[b] * rows, rows)
        xt_ref[pl.ds(at, rows), :] = flipped[b * rows : (b + 1) * rows]


def expert_a_kernel(*refs, experts, late_first):
    step = pl.program_id(0)
    if experts:
        me_ref, place_ref, code_ref = refs[:3]
        payloads = refs[3 : 3 + 2 * experts]
        cot_ref, gh_ref, wg_ref, wu_ref, x_ref, xt_ref, gate_ref, gc_ref = refs[3 + 2 * experts : 11 + 2 * experts]

        @pl.when(step == 0)
        def _():
            expert_first(me_ref, place_ref, code_ref, payloads, cot_ref, x_ref, xt_ref, gate_ref, gc_ref)

    else:
        x_ref, xt_ref, gate_ref, gh_ref, wg_ref, wu_ref = refs[:6]
    keep_ref, send_ref, sc_ref, hid_ref, hidt_ref, gg_ref, gu_ref = refs[-7:]

    @pl.when(step == 0)
    def _():
        sc_ref[...] = jnp.zeros_like(sc_ref)

    wg, wu = wg_ref[0], wu_ref[0]
    width = wg.shape[1]
    for start in range(0, x_ref.shape[0], ROW_BLOCK):
        part = slice(start, start + ROW_BLOCK)
        x = x_ref[part, :]
        gate_pre = dot(x, wg)
        up_pre = dot(x, wu)
        grad = gh_ref[part, :].astype(F32)
        act, slope = gelu_parts(gate_pre)
        hidden = act * up_pre
        hid_ref[part, :] = hidden.astype(BF)
        product = hidden * grad
        folded = product[:, 0:LANES]
        for i in range(1, width // LANES):
            folded = folded + product[:, i * LANES : (i + 1) * LANES]
        sc_ref[part, :] += folded
        grad = grad * gate_ref[part, 0:1]
        gg_ref[part, :] = (slope * up_pre * grad).astype(BF)
        gu_ref[part, :] = (act * grad).astype(BF)
    hidt_ref[...] = hid_ref[...].T
    xt = xt_ref[...]
    half = xt.shape[0] // 2
    for i, grad_ref in enumerate((gg_ref, gu_ref)):
        term = dot(xt, grad_ref[...]).astype(BF)
        if not late_first:
            keep_ref[i] = term[:half]
            send_ref[i] = term[half:]
            continue
        rows = term.shape[0] // late_first
        for place in range(late_first):
            block = (place & 1) * (late_first // 2) + (place >> 1)
            out_ref, at = (keep_ref, place) if place < late_first // 2 else (send_ref, place - late_first // 2)
            out_ref[i, at * rows : (at + 1) * rows] = term[block * rows : (block + 1) * rows]


def expert_a(source, gh, gh_first, w_gate, w_up, first, count, late_first, filled=()):
    opening = 0 if filled else len(source[3]) // 2
    rows = gh.shape[0]
    width, ff = w_gate.shape[1:]
    span = count * FF_BLOCK
    col_weight = pl.BlockSpec((1, width, FF_BLOCK), lambda f: (0, 0, first + f))
    out_block = pl.BlockSpec((rows, FF_BLOCK), lambda f: (0, first + f))
    wide = jax.ShapeDtypeStruct((rows, ff), BF)
    tall = jax.ShapeDtypeStruct((ff, rows), BF)
    term = jax.ShapeDtypeStruct((2, width // 2, span), BF)
    term_block = pl.BlockSpec((2, width // 2, FF_BLOCK), lambda f: (0, 0, f))
    if opening:
        me, place, code, payloads, cot_rows = source
        args = (me, place, code, *payloads, cot_rows)
        specs = [pl.BlockSpec(memory_space=pltpu.SMEM)] * 2 + whole_specs((code, *payloads, cot_rows))
        shared = [
            jax.ShapeDtypeStruct((rows, width), BF),
            jax.ShapeDtypeStruct((width, rows), BF),
            jax.ShapeDtypeStruct((rows, LANES), F32),
            jax.ShapeDtypeStruct((rows, width), BF),
        ]
    else:
        args = tuple(source)
        specs = whole_specs(source)
        shared = []
    args = (*args, gh, w_gate, w_up)
    used = len(args)
    first_filled = len(shared) + 3

    def run(*refs):
        expert_a_kernel(*refs[:used], *refs[used + len(filled) :], experts=opening, late_first=late_first)

    return call(
        run,
        (*args, *filled),
        specs
        + [pl.BlockSpec((rows, FF_BLOCK), lambda f: (0, first - gh_first + f)), col_weight, col_weight]
        + [pl.BlockSpec(memory_space=pl.ANY)] * len(filled),
        grid=(count,),
        out_specs=whole_specs(shared)
        + [term_block, term_block, const_spec((rows, LANES)), out_block]
        + [pl.BlockSpec((FF_BLOCK, rows), lambda f: (first + f, 0)), out_block, out_block],
        out_shape=shared + [term, term, jax.ShapeDtypeStruct((rows, LANES), F32), wide, tall, wide, wide],
        input_output_aliases={used + i: first_filled + i for i in range(len(filled))},
        cost_estimate=estimate("expert_grads"),
        name="expert_grads",
    )


def expert_b_kernel(gg_ref, gu_ref, *refs, cap, experts):
    outs, acc = refs[-1 - experts : -1], refs[-1]
    sc_refs, (wg_ref, wu_ref) = refs[: -3 - experts], refs[-3 - experts : -1 - experts]
    part_sum = dot_nt(gg_ref[...], wg_ref[0]) + dot_nt(gu_ref[...], wu_ref[0])
    step, block = pl.program_id(0), pl.program_id(1)

    @pl.when(step == 0)
    def _():
        acc[block] = part_sum

    def finish(out_ref):
        total = acc[block] + part_sum
        row = lax.broadcasted_iota(jnp.int32, (cap, cap), 0)
        lane = lax.broadcasted_iota(jnp.int32, (cap, cap), 1)
        place = lax.broadcasted_iota(jnp.int32, (TAIL, cap), 0)
        out_ref[0:cap, :] = total.astype(BF)
        folded = sc_refs[0][...]
        for other in sc_refs[1:]:
            folded = folded + other[...]
        column = jnp.sum(folded, axis=1, keepdims=True)
        flat = jnp.sum(jnp.where(row == lane, column, 0.0), axis=0, keepdims=True)
        hi, mid, low = split3(flat)
        packed = jnp.where(
            place == 0, hi.astype(F32), jnp.where(place == 1, mid.astype(F32), jnp.where(place == 2, low.astype(F32), 0.0))
        )
        out_ref[cap : cap + TAIL, :] = jnp.zeros((TAIL, total.shape[1]), BF)
        out_ref[cap : cap + TAIL, 0:cap] = packed.astype(BF)

    for m, out_ref in enumerate(outs):

        @pl.when(jnp.logical_and(step == pl.num_programs(0) - 1, block == m))
        def _(out_ref=out_ref):
            finish(out_ref)


def expert_b(gg, gu, scs, w_gate, w_up, experts):
    rows, ff = gg.shape
    width = w_gate.shape[1]
    cap = rows // experts
    cut = ff // 2
    grads = pl.BlockSpec((cap, cut), lambda k, m: (m, k))
    sums = pl.BlockSpec((cap, LANES), lambda k, m: (m, 0))
    weight = pl.BlockSpec((1, width, cut), lambda k, m: (0, 0, k))
    return call(
        functools.partial(expert_b_kernel, cap=cap, experts=experts),
        (gg, gu, *scs, w_gate, w_up),
        [grads, grads] + [sums] * len(scs) + [weight, weight],
        grid=(2, experts),
        out_specs=[const_spec((cap + TAIL, width))] * experts,
        out_shape=[jax.ShapeDtypeStruct((cap + TAIL, width), BF)] * experts,
        scratch_shapes=[pltpu.VMEM((experts, cap, width), F32)],
        cost_estimate=estimate("expert_input_grad"),
        name="expert_input_grad",
    )


def down_kernel(place_a_ref, place_b_ref, hidt_ref, gc_ref, *outs):
    owners = place_a_ref.shape[0]
    shard = 2 * outs[0].shape[0] // owners
    size = int(np.gcd(shard, 32))
    rows = hidt_ref.shape[0]
    step = pl.program_id(0)
    total = dot(hidt_ref[...], gc_ref[...]).astype(BF)
    half = total.shape[1] // 2
    for i in range(rows // size):
        row = step * rows + i * size
        owner = row // shard
        piece = total[i * size : (i + 1) * size]
        for keep_ref, send_ref, place_ref, cols in (
            (outs[0], outs[1], place_a_ref, piece[:, :half]),
            (outs[2], outs[3], place_b_ref, piece[:, half:]),
        ):
            place = place_ref[owner]
            at = pl.multiple_of((place % (owners // 2)) * shard + (row - owner * shard), size)

            @pl.when(place < owners // 2)
            def _(keep_ref=keep_ref, at=at, cols=cols):
                keep_ref[pl.ds(at, size), :] = cols

            @pl.when(place >= owners // 2)
            def _(send_ref=send_ref, at=at, cols=cols):
                send_ref[pl.ds(at, size), :] = cols


def down_grads(hid_t, grad_cots, place_a, place_b):
    rows, width = grad_cots.shape
    ff = hid_t.shape[0]
    table = pl.BlockSpec(memory_space=pltpu.SMEM)
    part = jax.ShapeDtypeStruct((ff // 2, width // 2), BF)
    return call(
        down_kernel,
        (place_a, place_b, hid_t, grad_cots),
        [table, table, pl.BlockSpec((ff // 4, rows), lambda f: (f, 0)), const_spec((rows, width))],
        grid=(4,),
        out_specs=[const_spec(part.shape)] * 4,
        out_shape=[part] * 4,
        cost_estimate=estimate("down_grads"),
        name="down_grads",
    )


def produced_kernel(hid_ref, wd_ref, low_ref, high_ref):
    rows = dot(hid_ref[...], wd_ref[0]).astype(BF)
    lower = pl.program_id(0) < pl.num_programs(0) // 2

    @pl.when(lower)
    def _():
        low_ref[0] = rows

    @pl.when(jnp.logical_not(lower))
    def _():
        high_ref[0] = rows


def produced_rows(hid, w_down, experts):
    rows, ff = hid.shape
    width = w_down.shape[2]
    cap, half = rows // experts, experts // 2
    return call(
        produced_kernel,
        (hid, w_down),
        [pl.BlockSpec((cap, ff), lambda m: (m, 0)), const_spec(w_down.shape)],
        grid=(experts,),
        out_specs=[
            pl.BlockSpec((1, cap, width), lambda m: (jnp.minimum(m, half - 1), 0, 0)),
            pl.BlockSpec((1, cap, width), lambda m: (jnp.maximum(m - half, 0), 0, 0)),
        ],
        out_shape=[jax.ShapeDtypeStruct((half, cap, width), BF)] * 2,
        cost_estimate=estimate("produced_rows"),
        name="produced_rows",
    )


def distinct(slots):
    arrays, found = [], []
    for array, index in slots:
        which = next((i for i, other in enumerate(arrays) if other is array), None)
        if which is None:
            which = len(arrays)
            arrays.append(array)
        found.append((which, index))
    return arrays, found


def layer_out_kernel(mid_ref, ch_ref, code_ref, *refs, slots):
    parts, out_ref = refs[:-1], refs[-1]
    cap = parts[0].shape[1]
    total = mid_ref[...]
    chances = ch_ref[...].T
    for m, (which, index) in enumerate(slots):
        picked = dot(selector_t(code_ref[:, m : m + 1], cap), parts[which][index])
        total = total + chances[:, m : m + 1] * picked
    out_ref[...] = total.astype(BF)


def layer_output(middle, chances, code_t, slots):
    rows, width = middle.shape
    arrays, found = distinct(slots)
    args = (middle, chances, code_t, *arrays)
    return call(
        functools.partial(layer_out_kernel, slots=found),
        args,
        [pl.BlockSpec(memory_space=pltpu.VMEM)] * len(args),
        out_shape=jax.ShapeDtypeStruct((rows, width), BF),
        cost_estimate=estimate("layer_output"),
        name="layer_output",
    )


def moe_bwd_kernel(
    cot_ref, mid_ref, gain_ref, nm_ref, ch_ref, wr_ref, code_ref, codet_ref, wo_ref, att_ref, *refs
):
    backs, (gmid_ref, branch_ref, ga_ref, keep_ref, send_ref, gain_o_ref, router_o_ref) = refs[:-7], refs[-7:]
    experts, cap = len(backs), backs[0].shape[0] - TAIL
    rows = cot_ref.shape[0]
    grad = jnp.zeros(mid_ref.shape, F32)
    gate_rows = []
    for m, back in enumerate(backs):
        grad = grad + dot(selector_t(codet_ref[:, m : m + 1], cap), back[0:cap, :])
        picked = dot(back[cap : cap + TAIL, 0:cap], selector(code_ref[m : m + 1, :], cap))
        gate_rows.append(jnp.sum(picked, axis=0, keepdims=True))
    gate_rows.append(jnp.zeros((TAIL - experts, rows), F32))
    grad_chances = jnp.concatenate(gate_rows, axis=0)
    chances = ch_ref[...]
    grad_logits = chances * (grad_chances - jnp.sum(chances * grad_chances, axis=0, keepdims=True))
    pieces = jnp.concatenate(split3(grad_logits), axis=0)
    wr = wr_ref[...]
    grad = grad + dot_tn(pieces, jnp.concatenate([wr, wr, wr], axis=0))
    router = dot(pieces, nm_ref[...])
    router_o_ref[...] = router[0:TAIL] + router[TAIL : 2 * TAIL] + router[2 * TAIL : 3 * TAIL]
    mid = mid_ref[...]
    scale = rms_scale(mid)
    unit = mid * scale
    gain_o_ref[...] = jnp.sum(grad * unit, axis=0, keepdims=True)
    scaled = grad * gain_ref[...]
    grad_mid = cot_ref[...].astype(F32) + scale * (scaled - unit * jnp.mean(scaled * unit, axis=-1, keepdims=True))
    gmid_ref[...] = grad_mid
    branch = grad_mid.astype(BF)
    branch_ref[...] = branch
    ga_ref[...] = dot_nt(branch, wo_ref[...]).astype(BF)
    term = dot(att_ref[...], branch).astype(BF)
    half = term.shape[0] // 2
    keep_ref[0] = term[:half]
    send_ref[0] = term[half:]


def sort_rows(place_ref, value, out_ref):
    owners = place_ref.shape[0]
    rows = value.shape[0] // owners
    for b in range(owners):
        out_ref[pl.ds(pl.multiple_of(place_ref[b] * rows, rows), rows), :] = value[b * rows : (b + 1) * rows]


def moe_bwd(cot, middle, gain_moe, normed_moe, chances, wr_t, code, code_t, w_out, att_t, backs):
    rows, width = cot.shape
    args = (cot, middle, gain_moe[None], normed_moe, chances, wr_t, code, code_t, w_out, att_t, *backs)
    wide = jax.ShapeDtypeStruct((rows, width), BF)
    half = jax.ShapeDtypeStruct((1, width // 2, width), BF)
    return call(
        moe_bwd_kernel,
        args,
        [pl.BlockSpec(memory_space=pltpu.VMEM)] * len(args),
        out_shape=[
            jax.ShapeDtypeStruct((rows, width), F32),
            wide,
            wide,
            half,
            half,
            jax.ShapeDtypeStruct((1, width), F32),
            jax.ShapeDtypeStruct((TAIL, width), F32),
        ],
        cost_estimate=estimate("moe_bwd"),
        name="moe_bwd",
    )


def attn_bwd_kernel(
    qs_ref, k_ref, v_ref, ga_ref, lse_ref, woff_ref, seg_ref,
    dq_ref, dk_ref, dv_ref, dwoff_ref, mask_scr, p_scr, ds_scr,
    *, head_dim,
):
    rows = qs_ref.shape[0]
    blocks = rows // LANES

    @pl.when(pl.program_id(0) == 0)
    def _():
        mask_scr[...] = segment_mask(seg_ref, 0, rows)

    scaled, keys, values, grads = qs_ref[...], k_ref[...], v_ref[...], ga_ref[...]
    q_t, g_t, k_t = scaled.T, grads.T, keys.T
    low_half = lax.broadcasted_iota(jnp.int32, (rows, LANES), 1) < head_dim
    dq_t, dk_parts, dv_parts = [], [], []
    lane = lax.broadcasted_iota(jnp.int32, (1, BAND), 1)
    for h in range(HEAD_GROUP):
        row = woff_ref[0, h : h + 1, :]
        band = band_of(row)
        pair = slice(LANES * (h // 2), LANES * (h // 2 + 1))
        k_pair, v_pair = keys[:, pair], values[:, pair]
        q_only, g_only = only_rows(q_t, h, head_dim), only_rows(g_t, h, head_dim)
        tiles = {}
        for b in range(0, blocks, 2):
            lanes = slice(b * LANES, (b + 2) * LANES)
            s = dot(k_pair, q_only[:, lanes]) + bias_block(band, row, b, 2, blocks) + mask_scr[:, lanes]
            p = jnp.exp(s - lse_ref[0, h : h + 1, lanes])
            dp = dot(v_pair, g_only[:, lanes])
            ds = p * (dp - jnp.sum(p * dp, axis=0, keepdims=True))
            p_scr[:, lanes] = p.astype(BF)
            ds_scr[:, lanes] = ds.astype(BF)
            for q_block in range(2):
                for k_block in range(blocks):
                    d = max(-2, min(2, k_block - b - q_block))
                    tile = ds[k_block * LANES : (k_block + 1) * LANES, q_block * LANES : (q_block + 1) * LANES]
                    tiles[d] = tiles[d] + tile if d in tiles else tile
        skewed = jnp.concatenate([tiles[1], tiles[0], tiles[-1], jnp.zeros_like(tiles[0])], axis=1)
        offsets = diagonal_sums(skewed)
        offsets = offsets + jnp.where(lane == FAR_AFTER, jnp.sum(tiles[2]), 0.0)
        offsets = offsets + jnp.where(lane == FAR_BEFORE, jnp.sum(tiles[-2]), 0.0)
        dwoff_ref[0, h : h + 1, :] = offsets
        p_all, ds_all = p_scr[...], ds_scr[...]
        dv_parts.append(dot(p_all, grads[:, pair]))
        dk_parts.append(dot(ds_all, scaled[:, pair]))
        dq_t.append(dot(k_t[h * head_dim : (h + 1) * head_dim], ds_all))
    dq = jnp.concatenate(dq_t, axis=0).T * head_dim ** (-0.5)
    dq_ref[...] = dq.astype(BF)
    for i in range(HEAD_GROUP // 2):
        pair = slice(LANES * i, LANES * (i + 1))
        dk_ref[:, pair] = jnp.where(low_half, dk_parts[2 * i], dk_parts[2 * i + 1]).astype(BF)
        dv_ref[:, pair] = jnp.where(low_half, dv_parts[2 * i], dv_parts[2 * i + 1]).astype(BF)


def attn_bwd(scaled, keys, values, grad_att, lse, woff, seg):
    rows, width = scaled.shape
    groups = woff.shape[0]
    cols = width // groups
    col_block = pl.BlockSpec((rows, cols), lambda g: (0, g))
    wide = jax.ShapeDtypeStruct((rows, width), BF)
    return call(
        functools.partial(attn_bwd_kernel, head_dim=cols // HEAD_GROUP),
        (scaled, keys, values, grad_att, lse, woff, seg),
        [
            col_block,
            col_block,
            col_block,
            col_block,
            pl.BlockSpec((1, HEAD_GROUP, rows), lambda g: (g, 0, 0)),
            pl.BlockSpec((1, HEAD_GROUP, BAND), lambda g: (g, 0, 0)),
            const_spec(seg.shape),
        ],
        grid=(groups,),
        out_specs=[col_block, col_block, col_block, pl.BlockSpec((1, HEAD_GROUP, BAND), lambda g: (g, 0, 0))],
        out_shape=[wide, wide, wide, jax.ShapeDtypeStruct((groups, HEAD_GROUP, BAND), F32)],
        scratch_shapes=[
            pltpu.VMEM((rows, rows), F32),
            pltpu.VMEM((rows, rows), BF),
            pltpu.VMEM((rows, rows), BF),
        ],
        cost_estimate=estimate("attn_bwd"),
        name="attn_bwd",
    )


def sorted_rows_kernel(pq_ref, pk_ref, tok_ref, gain_ref, att_ref, att_o_ref, out_ref, sort_scr):
    start = tok_ref[...].astype(F32)
    normed_t = (start * rms_scale(start) * gain_ref[...]).T
    attended_t = att_ref[...].astype(F32).T
    sort_rows(pq_ref, attended_t, sort_scr)
    att_o_ref[...] = sort_scr[...].astype(BF)
    for i, place_ref in enumerate((pq_ref, pk_ref)):
        sort_rows(place_ref, normed_t, sort_scr)
        out_ref[i] = sort_scr[...].astype(BF)


def sorted_rows(place_q, place_k, tokens, gain_attn, attended):
    rows, width = tokens.shape
    return call(
        sorted_rows_kernel,
        (place_q, place_k, tokens, gain_attn[None], attended),
        [pl.BlockSpec(memory_space=pltpu.SMEM)] * 2 + [pl.BlockSpec(memory_space=pltpu.VMEM)] * 3,
        out_shape=[jax.ShapeDtypeStruct((width, rows), BF), jax.ShapeDtypeStruct((2, width, rows), BF)],
        scratch_shapes=[pltpu.VMEM((width, rows), F32)],
        cost_estimate=estimate("sorted_rows"),
        name="sorted_rows",
    )


def dense_terms_kernel(rows_ref, dq_ref, dk_ref, dv_ref, keep_ref, send_ref):
    half = keep_ref.shape[1]
    for i, d_ref in enumerate((dq_ref, dk_ref, dv_ref)):
        term = dot(rows_ref[min(i, 1)], d_ref[...]).astype(BF)
        keep_ref[i] = term[:half]
        send_ref[i] = term[half:]


def dense_terms(lhs, dq, dk, dv):
    _, width, rows = lhs.shape
    cols = 256
    col_block = pl.BlockSpec((rows, cols), lambda g: (0, g))
    return call(
        dense_terms_kernel,
        (lhs, dq, dk, dv),
        [const_spec(lhs.shape)] + [col_block] * 3,
        grid=(width // cols,),
        out_specs=[pl.BlockSpec((3, width // 2, cols), lambda g: (0, 0, g))] * 2,
        out_shape=[jax.ShapeDtypeStruct((3, width // 2, width), BF)] * 2,
        cost_estimate=estimate("dense_terms"),
        name="dense_terms",
    )


def norm_bwd_kernel(
    tok_ref, gain_ref, gmid_ref, dq_ref, dk_ref, dv_ref, wq_ref, wk_ref, wv_ref, tg_ref, gain_o_ref, acc
):
    step = pl.program_id(0)
    total = dot_nt(dq_ref[...], wq_ref[...]) + dot_nt(dk_ref[...], wk_ref[...]) + dot_nt(dv_ref[...], wv_ref[...])

    @pl.when(step == 0)
    def _():
        acc[...] = total

    @pl.when(step > 0)
    def _():
        acc[...] += total

    @pl.when(step == pl.num_programs(0) - 1)
    def _():
        grad = acc[...]
        start = tok_ref[...].astype(F32)
        scale = rms_scale(start)
        unit = start * scale
        gain_o_ref[...] = jnp.sum(grad * unit, axis=0, keepdims=True)
        scaled = grad * gain_ref[...]
        tg_ref[...] = gmid_ref[...] + scale * (scaled - unit * jnp.mean(scaled * unit, axis=-1, keepdims=True))


def norm_bwd(tokens, gain_attn, grad_mid, dq, dk, dv, w_query, w_key, w_value):
    rows, width = tokens.shape
    cols = 256
    col_block = pl.BlockSpec((rows, cols), lambda g: (0, g))
    weight_block = pl.BlockSpec((width, cols), lambda g: (0, g))
    return call(
        norm_bwd_kernel,
        (tokens, gain_attn[None], grad_mid, dq, dk, dv, w_query, w_key, w_value),
        [const_spec((rows, width)), const_spec((1, width)), const_spec((rows, width))] + [col_block] * 3 + [weight_block] * 3,
        grid=(width // cols,),
        out_specs=[const_spec((rows, width)), const_spec((1, width))],
        out_shape=[jax.ShapeDtypeStruct((rows, width), F32), jax.ShapeDtypeStruct((1, width), F32)],
        scratch_shapes=[pltpu.VMEM((rows, width), F32)],
        cost_estimate=estimate("norm_bwd"),
        name="norm_bwd",
    )


def bits_of(size):
    return size.bit_length() - 1


def swap(value, axis, size, mask):
    return lax.ppermute(value, axis, [(i, i ^ mask) for i in range(size)])


def pick(value, index, axis):
    return lax.dynamic_index_in_dim(value, index, axis, keepdims=False)


class Order:
    def __init__(self, token):
        self.token = token

    def enter(self, tree):
        tree, self.token = lax.optimization_barrier((tree, self.token))
        return tree

    leave = enter


def places(me, bits, order):
    key = jnp.arange(1 << bits, dtype=jnp.int32) ^ me
    place = jnp.zeros_like(key)
    for bit in order:
        place = place * 2 + ((key >> bit) & 1)
    return place


class Halving:
    def __init__(self, order, keep, send, dim, route, name):
        self.order, self.keep, self.to_send, self.dim, self.route, self.name = order, keep, send, dim, list(route), name
        self.got = None

    def start(self):
        axis, size, bit = self.route[0]
        with jax.named_scope(f"{self.name}_{axis}{1 << bit}"):
            value = self.order.enter(self.keep if self.to_send is None else self.to_send)
            self.got = swap(value, axis, size, 1 << bit)


def fold_kernel(*refs, cuts):
    pairs, outs = refs[: 2 * len(cuts)], list(refs[2 * len(cuts) :])
    for i, (dim, last) in enumerate(cuts):
        keep, got = pairs[2 * i][...].astype(F32), pairs[2 * i + 1][...].astype(F32)
        total = keep + got
        if last:
            outs.pop(0)[...] = total
            continue
        rows = total.shape[dim] // 2
        for start in (0, rows):
            outs.pop(0)[...] = lax.slice_in_dim(total, start, start + rows, axis=dim).astype(BF)


def fold(*units, hold=()):
    order = units[0].order
    args, cuts, shapes = [], [], []
    for unit in units:
        unit.route.pop(0)
        got = order.leave(unit.got)
        args += [unit.keep, got]
        whole = unit.to_send is None
        last = whole or not unit.route
        cuts.append((unit.dim, last))
        if last:
            shapes.append(jax.ShapeDtypeStruct(got.shape, F32))
        else:
            shape = list(got.shape)
            shape[unit.dim] //= 2
            shapes += [jax.ShapeDtypeStruct(tuple(shape), BF)] * 2
    args = order.enter(args)
    outs = list(
        call(
            functools.partial(fold_kernel, cuts=cuts),
            args,
            [pl.BlockSpec(memory_space=pltpu.VMEM)] * len(args),
            out_shape=shapes,
            cost_estimate=estimate("fold"),
            name="fold",
        )
    )
    outs = order.leave(outs)
    for unit, (_, last) in zip(units, cuts):
        unit.keep = outs.pop(0)
        if not last:
            unit.to_send = outs.pop(0)
        if unit.route and unit not in hold:
            unit.start()


def fold_first_kernel(*refs, groups):
    pairs, outs = refs[: -2 * len(groups)], refs[-2 * len(groups) :]
    for i, members in enumerate(groups):
        for at, (array, index) in enumerate(members):
            total = pairs[2 * array][index].astype(F32) + pairs[2 * array + 1][index].astype(F32)
            rows = total.shape[0] // 2
            outs[2 * i][at] = total[:rows].astype(BF)
            outs[2 * i + 1][at] = total[rows:].astype(BF)


def fold_first(pairs, groups):
    args = [v for pair in pairs for v in pair]
    _, rows, width = args[0].shape
    shapes = [jax.ShapeDtypeStruct((len(members), rows // 2, width), BF) for members in groups for _ in range(2)]
    return call(
        functools.partial(fold_first_kernel, groups=groups),
        args,
        [pl.BlockSpec(memory_space=pltpu.VMEM)] * len(args),
        out_shape=shapes,
        cost_estimate=estimate("fold_first"),
        name="fold_first",
    )


class Return:
    def __init__(self, order, low, high, axis, size, name):
        self.order, self.axis, self.size, self.name = order, axis, size, name
        half = low.shape[0]
        self.slots = [(low, i) for i in range(half)] + [(high, i) for i in range(half)]
        self.bit = bits_of(size) - 1
        self.start(high)

    def moving(self):
        return [m for m in range(self.size) if (m >> self.bit) & 1]

    def start(self, value):
        with jax.named_scope(f"{self.name}{1 << self.bit}"):
            self.got = swap(self.order.enter(value), self.axis, self.size, 1 << self.bit)

    def fold(self):
        got = self.order.leave(self.got)
        for i, m in enumerate(self.moving()):
            self.slots[m] = (got[i], 0) if isinstance(got, list) else (got, i)
        self.bit -= 1
        if self.bit >= 0:
            self.pieces = [self.slots[m][0][self.slots[m][1]][None] for m in self.moving()]
            self.got = []
            for i, piece in enumerate(self.pieces):
                with jax.named_scope(f"{self.name}{1 << self.bit}_{i}"):
                    self.got.append(swap(self.order.enter(piece), self.axis, self.size, 1 << self.bit))

    def finish(self):
        while self.bit >= 0:
            self.fold()


class Gather:
    def __init__(self, order, value, axis, size, name):
        self.order, self.axis, self.size, self.name = order, axis, size, name
        self.blocks = {0: value}
        self.send(0, size // 2)
        if size > 2:
            self.send(0, 1)

    def send(self, m, bit):
        with jax.named_scope(f"{self.name}{m}_{bit}"):
            self.blocks[m ^ bit] = swap(self.blocks[m], self.axis, self.size, bit)

    def relay(self):
        self.blocks[self.size // 2] = self.order.leave(self.blocks[self.size // 2])
        bit = self.size // 2
        while bit:
            for m in range(0, self.size, 2 * bit):
                if m ^ bit not in self.blocks:
                    self.send(m, bit)
            bit //= 2

    def finish(self):
        self.blocks = self.order.leave(self.blocks)
        return [self.blocks[m] for m in range(self.size)]


def body(
    tokens,
    cotangent,
    gain_attn,
    w_query,
    w_key,
    w_value,
    w_out,
    rel_bias,
    gain_moe,
    w_router,
    w_gate,
    w_up,
    w_down,
    segments,
    routes,
    *,
    dp_size,
    ep_size,
):
    TURNS.clear()
    rows, width = tokens.shape
    buckets, heads = rel_bias.shape
    experts = w_router.shape[1]
    cap = 10 * rows // (4 * experts)
    ff = w_gate.shape[2]
    me = lax.axis_index("expert")

    cots = Gather(None, cotangent, "expert", ep_size, "cot")
    scaled, keys, values, woff, token, *filled, payload = attn_first(
        tokens, gain_attn, w_query, w_key, w_value, w_out, rel_bias, segments, gain_moe, w_router
    )
    order = Order(token)
    cots.order = order
    numbers = jnp.arange(experts, dtype=jnp.int32)
    named = jnp.any(order.enter(routes)[None, :, :] == numbers[:, None, None], axis=-1)
    before = jnp.asarray(np.triu(np.ones((rows, rows), np.float32), 1)).astype(BF)
    slots = jnp.dot(named.astype(BF), before, preferred_element_type=F32).astype(jnp.int32)
    code = jnp.where(named, slots, -1)

    dp_bits, ep_bits = bits_of(dp_size), bits_of(ep_size)
    dp_me = lax.axis_index("dp")
    dp_order = list(range(dp_bits))
    late_x = dp_order[1:] + [0]
    place_x = places(dp_me, dp_bits, dp_order)
    place_late = places(dp_me, dp_bits, late_x)

    def dp_route(bits):
        return [("dp", dp_size, b) for b in bits]

    dp_part = [ep_bits + b for b in dp_order]
    ep_part = list(range(1, ep_bits))
    q_bits = [0] + ep_part + dp_part
    k_bits = [0] + dp_part + ep_part
    whole_me = dp_me * ep_size + me

    def route(bits):
        return [("expert", ep_size, b) if b < ep_bits else ("dp", dp_size, b - ep_bits) for b in bits]

    place_q, place_k = [places(whole_me, dp_bits + ep_bits, bits) for bits in (q_bits, k_bits)]

    codes = Gather(order, order.enter(code), "expert", ep_size, "code")
    cots.relay()
    codes.relay()
    first_half = Gather(order, order.enter(payload), "expert", ep_size, "rows_a")
    attended, lse, middle, normed_moe, chances, payload = order.leave(
        attn_second(tokens, order.enter(scaled), keys, values, w_out, woff, segments, gain_moe, w_router, filled)
    )
    second_half = Gather(order, order.enter(payload), "expert", ep_size, "rows_b")
    first_half.relay()
    cots, codes = cots.finish(), codes.finish()
    code_here = jnp.stack([pick(v, me, 0) for v in codes])
    blocks = ff // FF_BLOCK
    counts = [blocks // 2, blocks - blocks // 2]
    starts = [sum(counts[:i]) for i in range(len(counts))]
    gh_first, cot_rows = order.leave(cot_hidden(order.enter(code_here), cots, w_down, cap, starts[1]))
    second_half.relay()
    payloads = [v for pair in zip(first_half.finish(), second_half.finish()) for v in pair]
    me_ref = me.reshape(1).astype(jnp.int32)
    scs, units = [], []

    def expert_part(i, source, filled=()):
        *shared, keep, send, sc, hid, hid_t, gg, gu = order.leave(
            expert_a(
                order.enter(source), gh_second if i else gh_first, starts[i], w_gate, w_up,
                starts[i], counts[i], 0 if i else dp_size, filled,
            )
        )
        scs.append(sc)
        units.append(Halving(order, keep, send, 1, dp_route(dp_order if i else late_x), f"gate_up{i}"))
        return shared, (hid, hid_t, gg, gu)

    def by_xor(value):
        return jnp.stack([pick(value, me ^ m, 0) for m in range(experts)])

    def padded(value):
        return jnp.pad(value, ((0, TAIL - experts), (0, 0)))

    (x_all, x_t, gate_all, grad_cots), filled = expert_part(0, (me_ref, place_x, code_here, payloads, cot_rows))
    units[0].start()
    gh_second = order.leave(cot_hidden_more(order.enter(cot_rows), w_down, starts[1]))
    _, (hid, hid_t, gg, gu) = expert_part(1, (x_all, x_t, gate_all), filled)
    units[1].start()
    backs = list(order.leave(expert_b(order.enter(gg), gu, scs, w_gate, w_up, experts)))
    for m in reversed(range(1, experts)):
        with jax.named_scope(f"grad_rows{m}"):
            backs[m] = swap(order.enter(backs[m]), "expert", ep_size, m)
    fold(units[0])
    down_parts = order.leave(down_grads(order.enter(hid_t), grad_cots, place_x, place_late))
    down_units = [
        Halving(order, down_parts[2 * i], down_parts[2 * i + 1], 0, dp_route(bits), f"down{i}")
        for i, bits in enumerate((dp_order, late_x))
    ]
    code_xor, chances_xor, wr_xor = order.enter((by_xor(code), padded(by_xor(chances)), padded(by_xor(w_router.T))))
    att_t, normed_t = order.leave(sorted_rows(place_q, place_k, order.enter(tokens), gain_attn, attended))
    backs = order.leave(backs)
    down_units[0].start()
    down_units[1].start()
    grad_mid, branch, grad_att, out_keep, out_send, gain_moe_term, router_term = order.leave(
        moe_bwd(
            cotangent, order.enter(middle), gain_moe, normed_moe, chances_xor, wr_xor, code_xor, code_xor.T, w_out, att_t,
            backs,
        )
    )
    out_unit = Halving(order, out_keep, out_send, 1, route(q_bits)[:1], "out")
    out_unit.start()
    fold(units[1])
    dq, dk, dv, dwoff = order.leave(attn_bwd(scaled, keys, values, order.enter(grad_att), lse, woff, segments))
    out_got = order.leave(out_unit.got)
    fold(units[0])
    qkv_keep, qkv_send = order.leave(dense_terms(normed_t, order.enter(dq), dk, dv))
    fold(*down_units)
    core = Halving(order, qkv_keep, qkv_send, 1, route(q_bits)[:1], "qkv")
    core.start()
    token_grad, gain_attn_term = order.leave(
        norm_bwd(tokens, gain_attn, grad_mid, order.enter(dq), dk, dv, w_query, w_key, w_value)
    )
    onehot = jnp.asarray(band_onehot(rows, buckets))
    bias_term = jnp.dot(onehot, dwoff.reshape(heads, BAND).T, precision=HIGHEST)
    devices = dp_size * ep_size
    share = width // devices
    small = jnp.concatenate(
        [
            by_xor(router_term).T.reshape(devices, -1),
            gain_attn_term.reshape(devices, -1),
            gain_moe_term.reshape(devices, -1),
            bias_term.reshape(devices, -1),
        ],
        axis=1,
    )
    small = Halving(order, small, None, 0, route(q_bits), "small")
    small.start()
    core_got = order.leave(core.got)
    halves = order.leave(
        fold_first([order.enter((out_keep, out_got)), (qkv_keep, core_got)], [[(0, 0), (1, 0)], [(1, 1), (1, 2)]])
    )
    dense = [
        Halving(order, halves[2 * i], halves[2 * i + 1], 1, route(bits)[1:], name)
        for i, (bits, name) in enumerate(((q_bits, "out_q"), (k_bits, "k_v")))
    ]
    out_q, k_v = dense
    k_v.start()
    out_q.start()
    fold(small, *units)
    prod_low, prod_high = order.leave(produced_rows(order.enter(hid), w_down, experts))
    fold(small, down_units[1], k_v)
    returned = Return(order, prod_low, prod_high, "expert", ep_size, "produced_rows")
    fold(small, down_units[0], out_q)
    fold(small, units[1], k_v)
    fold(small, down_units[1], out_q)
    fold(k_v)
    returned.fold()
    fold(down_units[0], out_q)
    returned.finish()
    layer_out = order.leave(layer_output(middle, chances_xor, code_xor.T, returned.slots))
    rest = units + down_units + dense + [small]
    while any(unit.route for unit in rest):
        fold(*[unit for unit in rest if unit.route])
    small_sum = pick(small.keep, whole_me, 0) + order.token[0, :1]

    terms = [unit.keep for unit in units]
    gate_grad = jnp.concatenate([term[0] for term in terms], axis=1)[None]
    up_grad = jnp.concatenate([term[1] for term in terms], axis=1)[None]
    down_grad = jnp.concatenate([unit.keep for unit in down_units], axis=1)[None]
    n_router = width * experts // devices
    n_gain = width // devices
    router_grad = small_sum[:n_router].reshape(share, experts)
    gain_attn_grad = small_sum[n_router : n_router + n_gain]
    gain_moe_grad = small_sum[n_router + n_gain : n_router + 2 * n_gain]
    bias_grad = small_sum[n_router + 2 * n_gain :]
    return (
        layer_out,
        token_grad,
        dense[0].keep[1],
        dense[1].keep[0],
        dense[1].keep[1],
        dense[0].keep[0],
        gain_attn_grad,
        gain_moe_grad,
        bias_grad,
        router_grad,
        gate_grad,
        up_grad,
        down_grad,
    )


def solution(mesh):
    in_specs = (
        P(("dp", "expert"), None),
        P(("dp", "expert"), None),
        P(),
        P(),
        P(),
        P(),
        P(),
        P(),
        P(),
        P(),
        P("expert", None, None),
        P("expert", None, None),
        P("expert", None, None),
        P(("dp", "expert"), None),
        P(("dp", "expert"), None),
    )
    out_specs = (
        P(("dp", "expert"), None),
        P(("dp", "expert"), None),
        P(("dp", "expert"), None),
        P(("dp", "expert"), None),
        P(("dp", "expert"), None),
        P(("dp", "expert"), None),
        P(("dp", "expert")),
        P(("dp", "expert")),
        P(("dp", "expert")),
        P(("dp", "expert"), None),
        P("expert", "dp", None),
        P("expert", "dp", None),
        P("expert", "dp", None),
    )
    run = functools.partial(body, dp_size=mesh.shape["dp"], ep_size=mesh.shape["expert"])
    return jax.shard_map(run, mesh=mesh, in_specs=in_specs, out_specs=out_specs, check_vma=False)
```

```python
import functools

import jax
import jax.numpy as jnp
import numpy as np
from jax import lax
from jax.experimental import pallas as pl
from jax.experimental.pallas import tpu as pltpu
from jax.sharding import PartitionSpec as P

EPS = 1e-06
HIGHEST = lax.Precision.HIGHEST
LANES = 128
BAND = 4 * LANES
HEAD_GROUP = 4
TAIL = 16
FAR = -1e30
BF = jnp.bfloat16
F32 = jnp.float32
VMEM_LIMIT = 56 * 1024 * 1024


def bucket_of(relative, buckets):
    halfway = buckets // 2
    exact_span = halfway // 2
    distance = np.abs(relative)
    beyond = exact_span + (
        np.log(np.maximum(distance, 1) / exact_span)
        / np.log(128.0 / exact_span)
        * (halfway - exact_span)
    ).astype(np.int64)
    beyond = np.minimum(beyond, halfway - 1)
    return (
        (relative > 0).astype(np.int64) * halfway
        + np.where(distance < exact_span, distance, beyond)
    ).astype(np.int32)


def band_onehot(length, buckets):
    place = np.arange(BAND)
    relative = np.where(place <= 3 * LANES, LANES - place, BAND + LANES - place)
    table = (bucket_of(relative, buckets)[None, :] == np.arange(buckets)[:, None]).astype(np.float32)
    table[:, 3 * LANES] = 0.0
    far = np.arange(LANES, length)
    assert np.all(bucket_of(far, buckets) == bucket_of(far, buckets)[0])
    assert np.all(bucket_of(-far, buckets) == bucket_of(-far, buckets)[0])
    return table


FAR_AFTER = 3 * LANES + 1
FAR_BEFORE = 3 * LANES - 1


def dot(a, b):
    return lax.dot_general(a, b, (((1,), (0,)), ((), ())), preferred_element_type=F32)


def dot_nt(a, b):
    return lax.dot_general(a, b, (((1,), (1,)), ((), ())), preferred_element_type=F32)


def dot_tn(a, b):
    return lax.dot_general(a, b, (((0,), (0,)), ((), ())), preferred_element_type=F32)


def split3(value):
    hi = value.astype(BF)
    rest = value - hi.astype(F32)
    mid = rest.astype(BF)
    low = (rest - mid.astype(F32)).astype(BF)
    return hi, mid, low


def rms_scale(value):
    return lax.rsqrt(jnp.mean(value * value, axis=-1, keepdims=True) + EPS)


def params(**kw):
    return pltpu.CompilerParams(vmem_limit_bytes=VMEM_LIMIT, **kw)


TIMES = {
    ("down_grads", 0): 10.0,
    ("dense_terms", 0): 13.1,
    ("fold", 2): 2.0,
}


TURNS = {}


def estimate(name):
    turn = TURNS.get(name, 0)
    TURNS[name] = turn + 1
    time = TIMES.get((name, turn), 0.1)
    return pl.CostEstimate(flops=int(time * 1.15e9), bytes_accessed=100000, transcendentals=0)


def call(kernel, args, in_specs, **kw):
    return pl.pallas_call(kernel, in_specs=list(in_specs), compiler_params=params(), **kw)(*args)


def whole_specs(args):
    return [const_spec(a.shape) for a in args]


def const_spec(shape):
    return pl.BlockSpec(shape, lambda *_: (0,) * len(shape))


def selector(code_row, rows):
    place = lax.broadcasted_iota(jnp.int32, (rows, code_row.shape[1]), 0)
    return jnp.where(place == code_row, 1.0, 0.0).astype(BF)


def selector_t(code_column, rows):
    place = lax.broadcasted_iota(jnp.int32, (code_column.shape[0], rows), 1)
    return jnp.where(place == code_column, 1.0, 0.0).astype(BF)


def band_of(row):
    return pltpu.roll(jnp.broadcast_to(row, (LANES, BAND)), 0, 1, stride=1, stride_axis=0)


def diagonal_sums(skewed):
    eight = skewed[0:8]
    for start in range(8, LANES, 8):
        eight = eight + pltpu.roll(skewed[start : start + 8], BAND - start, 1)
    total = eight[0:1]
    for row in range(1, 8):
        total = total + pltpu.roll(eight[row : row + 1], BAND - row, 1)
    return total


def bias_block(band, row, first, count, k_blocks):
    far = [jnp.broadcast_to(row[:, at : at + 1], (LANES, LANES)) for at in (FAR_BEFORE, FAR_AFTER)]
    columns = []
    for q_block in range(first, first + count):
        pieces = []
        for k_block in range(k_blocks):
            d = k_block - q_block
            pieces.append(far[1] if d > 1 else far[0] if d < -1 else band[:, LANES * (1 - d) : LANES * (2 - d)])
        columns.append(jnp.concatenate(pieces, axis=0))
    return jnp.concatenate(columns, axis=1)


def only_rows(value, h, head_dim):
    mine = value[h * head_dim : (h + 1) * head_dim]
    none = jnp.zeros_like(mine)
    return jnp.concatenate([mine, none] if h % 2 == 0 else [none, mine], axis=0)


def attend(scaled, keys, values, woff_ref, mask, first, head_dim):
    count = scaled.shape[0] // LANES
    q_t, v_t = scaled.T, values.T
    heads_t, totals = [], []
    for h in range(HEAD_GROUP):
        row = woff_ref[0, h : h + 1, :]
        bias = bias_block(band_of(row), row, first, count, keys.shape[0] // LANES)
        k_pair = keys[:, LANES * (h // 2) : LANES * (h // 2 + 1)]
        s = dot(k_pair, only_rows(q_t, h, head_dim)) + bias + mask
        peak = jnp.max(s, axis=0, keepdims=True)
        p = jnp.exp(s - peak)
        total = jnp.sum(p, axis=0, keepdims=True)
        heads_t.append(dot(v_t[h * head_dim : (h + 1) * head_dim], p.astype(BF)) * (1.0 / total))
        totals.append(peak + jnp.log(total))
    return jnp.concatenate(heads_t, axis=0).T.astype(BF), jnp.concatenate(totals, axis=0)


def slot_codes(routes):
    chosen = routes.astype(F32).T
    tokens = chosen.shape[1]
    numbers = lax.broadcasted_iota(jnp.int32, (TAIL // 2, tokens), 0).astype(F32)
    named = jnp.logical_or(numbers == chosen[0:1], numbers == chosen[1:2])
    row = lax.broadcasted_iota(jnp.int32, (tokens, tokens), 0)
    lane = lax.broadcasted_iota(jnp.int32, (tokens, tokens), 1)
    before = jnp.where(row < lane, 1.0, 0.0).astype(BF)
    return jnp.where(named, dot(jnp.where(named, 1.0, 0.0).astype(BF), before), -1.0)


def packed_codes(codes):
    upper = jnp.floor((codes + 1.0) * (1.0 / 16.0))
    return jnp.concatenate([upper, codes + 1.0 - 16.0 * upper], axis=0)


def own_code(me, packed):
    row = lax.broadcasted_iota(jnp.int32, packed.shape, 0)
    weight = jnp.where(row == me, 16.0, jnp.where(row == me + TAIL // 2, 1.0, 0.0))
    return (jnp.sum(packed.astype(F32) * weight, axis=0, keepdims=True) - 1.0).astype(jnp.int32)


def route_rows(mid, gain_ref, wr_ref, experts, nm_ref, ch_ref, payload_ref, codes=None):
    rows = mid.shape[0]
    nm = (mid * rms_scale(mid) * gain_ref[...]).astype(BF)
    nm_ref[...] = nm
    router = jnp.concatenate([wr_ref[...].astype(F32).T, jnp.zeros((TAIL - experts, nm.shape[1]), F32)], axis=0)
    logits = dot_nt(router.astype(BF), nm)
    live = lax.broadcasted_iota(jnp.int32, logits.shape, 0) < experts
    logits = jnp.where(live, logits, FAR)
    raised = jnp.exp(logits - jnp.max(logits, axis=0, keepdims=True))
    chances = raised / jnp.sum(raised, axis=0, keepdims=True)
    ch_ref[...] = chances
    hi = chances.astype(BF).astype(F32)
    both = jnp.concatenate([hi[: TAIL // 2], (chances - hi)[: TAIL // 2]], axis=0)
    payload_ref[0:rows, :] = nm
    tail = [both] if codes is None else [both, packed_codes(codes)]
    used = sum(v.shape[1] for v in tail)
    tail.append(jnp.zeros((TAIL, nm.shape[1] - used), F32))
    payload_ref[rows:, :] = jnp.concatenate(tail, axis=1).astype(BF)


def segment_mask(seg_ref, first, count):
    seg = seg_ref[...].astype(F32)
    column = jnp.broadcast_to(seg, (8, seg.shape[1])).T[:, 0:1]
    return jnp.where(column == seg[:, first : first + count], 0.0, FAR)


def attn_first_kernel(
    tok_ref, gain_a_ref, wq_ref, wk_ref, wv_ref, wo_ref, bias_ref, onehot_ref, seg_ref, gain_m_ref, wr_ref, routes_ref,
    qs_ref, k_ref, v_ref, woff_ref, token_ref, code_ref, att_ref, lse_ref, mid_ref, nm_ref, ch_ref, payload_ref,
    n_scr, mask_scr, woff_scr, code_scr,
    *, experts, head_dim,
):
    step = pl.program_id(0)
    rows = att_ref.shape[0]

    @pl.when(step == 0)
    def _():
        start = tok_ref[...].astype(F32)
        n_scr[...] = (start * rms_scale(start) * gain_a_ref[...]).astype(BF)
        mid_ref[...] = start[:rows]
        mask_scr[...] = segment_mask(seg_ref, 0, rows)
        token_ref[...] = jnp.where(seg_ref[:, 0:LANES] < 0, 1.0, 0.0)
        codes = slot_codes(routes_ref[...])
        code_scr[...] = codes
        code_ref[...] = codes[:experts].astype(jnp.int32)
        table = onehot_ref[...]
        offsets = sum(dot_tn(part, table) for part in split3(bias_ref[...]))
        for g in range(woff_scr.shape[0]):
            woff_scr[g] = offsets[g * HEAD_GROUP : (g + 1) * HEAD_GROUP]

    woff_ref[0] = woff_scr[step]

    normed = n_scr[...]
    scaled = (dot(normed, wq_ref[...]).astype(BF).astype(F32) * head_dim ** (-0.5)).astype(BF)
    keys = dot(normed, wk_ref[...]).astype(BF)
    values = dot(normed, wv_ref[...]).astype(BF)
    qs_ref[...] = scaled
    k_ref[...] = keys
    v_ref[...] = values
    att, totals = attend(scaled[:rows], keys, values, woff_ref, mask_scr[...], 0, head_dim)
    att_ref[...] = att
    lse_ref[0] = totals
    mid_ref[...] += dot(att, wo_ref[...])

    @pl.when(step == pl.num_programs(0) - 1)
    def _():
        route_rows(mid_ref[...], gain_m_ref, wr_ref, experts, nm_ref, ch_ref, payload_ref, code_scr[...])


def attn_second_kernel(
    tok_ref, qs_ref, k_ref, v_ref, wo_ref, woff_ref, seg_ref, gain_m_ref, wr_ref, *refs, experts, head_dim
):
    att_ref, lse_ref, mid_ref, nm_ref, ch_ref, payload_ref, mask_scr = refs[-7:]
    step = pl.program_id(0)
    rows = att_ref.shape[0]

    @pl.when(step == 0)
    def _():
        mid_ref[...] = tok_ref[...].astype(F32)
        mask_scr[...] = segment_mask(seg_ref, rows, rows)

    att, totals = attend(qs_ref[...], k_ref[...], v_ref[...], woff_ref, mask_scr[...], rows // LANES, head_dim)
    att_ref[...] = att
    lse_ref[0] = totals
    mid_ref[...] += dot(att, wo_ref[...])

    @pl.when(step == pl.num_programs(0) - 1)
    def _():
        route_rows(mid_ref[...], gain_m_ref, wr_ref, experts, nm_ref, ch_ref, payload_ref)


def attn_halves(rows, width, groups, half):
    cols, part = width // groups, rows // 2
    wide = jax.ShapeDtypeStruct((rows, width), BF)
    shapes = [
        wide,
        jax.ShapeDtypeStruct((groups, HEAD_GROUP, rows), F32),
        jax.ShapeDtypeStruct((rows, width), F32),
        wide,
        jax.ShapeDtypeStruct((TAIL, rows), F32),
        jax.ShapeDtypeStruct((part + TAIL, width), BF),
    ]
    specs = [
        pl.BlockSpec((part, cols), lambda g: (half, g)),
        pl.BlockSpec((1, HEAD_GROUP, part), lambda g: (g, 0, half)),
        pl.BlockSpec((part, width), lambda g: (half, 0)),
        pl.BlockSpec((part, width), lambda g: (half, 0)),
        pl.BlockSpec((TAIL, part), lambda g: (0, half)),
        const_spec((part + TAIL, width)),
    ]
    return shapes, specs


def attn_first(tokens, gain_attn, w_query, w_key, w_value, w_out, rel_bias, seg, gain_moe, w_router, routes):
    rows, width = tokens.shape
    buckets, heads = rel_bias.shape
    experts = w_router.shape[1]
    groups = heads // HEAD_GROUP
    cols, part = width // groups, rows // 2
    weight_block = pl.BlockSpec((width, cols), lambda g: (0, g))
    shapes, specs = attn_halves(rows, width, groups, 0)
    wide = jax.ShapeDtypeStruct((rows, width), BF)
    return call(
        functools.partial(attn_first_kernel, experts=experts, head_dim=cols // HEAD_GROUP),
        (tokens, gain_attn[None], w_query, w_key, w_value, w_out, rel_bias, jnp.asarray(band_onehot(rows, buckets)).astype(BF),
         seg, gain_moe[None], w_router, routes),
        [
            const_spec((rows, width)),
            const_spec((1, width)),
            weight_block,
            weight_block,
            weight_block,
            pl.BlockSpec((cols, width), lambda g: (g, 0)),
            const_spec(rel_bias.shape),
            const_spec((buckets, BAND)),
            const_spec(seg.shape),
            const_spec((1, width)),
            const_spec(w_router.shape),
            const_spec(routes.shape),
        ],
        grid=(groups,),
        out_specs=[pl.BlockSpec((rows, cols), lambda g: (0, g))] * 3
        + [pl.BlockSpec((1, HEAD_GROUP, BAND), lambda g: (g, 0, 0)), const_spec((1, LANES)), const_spec((experts, rows))]
        + specs,
        out_shape=[wide] * 3
        + [jax.ShapeDtypeStruct((groups, HEAD_GROUP, BAND), F32), jax.ShapeDtypeStruct((1, LANES), F32)]
        + [jax.ShapeDtypeStruct((experts, rows), jnp.int32)]
        + shapes,
        scratch_shapes=[
            pltpu.VMEM((rows, width), BF),
            pltpu.VMEM((rows, part), F32),
            pltpu.VMEM((groups, HEAD_GROUP, BAND), F32),
            pltpu.VMEM((TAIL // 2, rows), F32),
        ],
        cost_estimate=estimate("attn_first"),
        name="attn_first",
    )


def attn_second(tokens, scaled, keys, values, w_out, woff, seg, gain_moe, w_router, filled):
    rows, width = tokens.shape
    experts = w_router.shape[1]
    groups = woff.shape[0]
    cols, part = width // groups, rows // 2
    col_block = pl.BlockSpec((rows, cols), lambda g: (0, g))
    shapes, specs = attn_halves(rows, width, groups, 1)
    args = (tokens, scaled, keys, values, w_out, woff, seg, gain_moe[None], w_router)
    return call(
        functools.partial(attn_second_kernel, experts=experts, head_dim=cols // HEAD_GROUP),
        (*args, *filled),
        [
            pl.BlockSpec((part, width), lambda g: (1, 0)),
            pl.BlockSpec((part, cols), lambda g: (1, g)),
            col_block,
            col_block,
            pl.BlockSpec((cols, width), lambda g: (g, 0)),
            pl.BlockSpec((1, HEAD_GROUP, BAND), lambda g: (g, 0, 0)),
            const_spec(seg.shape),
            const_spec((1, width)),
            const_spec(w_router.shape),
        ]
        + [pl.BlockSpec(memory_space=pl.ANY)] * len(filled),
        grid=(groups,),
        out_specs=specs,
        out_shape=shapes,
        scratch_shapes=[pltpu.VMEM((rows, part), F32)],
        input_output_aliases={len(args) + i: i for i in range(len(filled))},
        cost_estimate=estimate("attn_second"),
        name="attn_second",
    )


def gelu_parts(gate):
    c0 = np.float32(np.sqrt(2.0 / np.pi))
    c1 = np.float32(0.044715)
    square = gate * gate
    t = jnp.tanh(c0 * gate * (1.0 + c1 * square))
    half = 0.5 * (1.0 + t)
    value = gate * half
    slope = half + 0.5 * gate * (1.0 - t * t) * (c0 * (1.0 + 3.0 * c1 * square))
    return value, slope


FF_BLOCK = 256


def cot_hidden_kernel(me_ref, *refs, experts):
    tail_refs, cot_refs, wd_ref = refs[:experts], refs[experts : 2 * experts], refs[2 * experts]
    out_ref, rows_ref = refs[2 * experts + 1 :]

    @pl.when(pl.program_id(0) == 0)
    def _():
        cap = rows_ref.shape[0] // experts
        tokens = cot_refs[0].shape[0]
        for m, (tail_ref, cot_ref) in enumerate(zip(tail_refs, cot_refs)):
            code = own_code(me_ref[0], tail_ref[:, tokens // 2 : tokens // 2 + tokens])
            rows_ref[m * cap : (m + 1) * cap, :] = dot(selector(code, cap), cot_ref[...]).astype(BF)

    out_ref[...] = dot_nt(rows_ref[...], wd_ref[0]).astype(BF)


def cot_hidden(me, payloads, cots, w_down, cap, count):
    experts = len(cots)
    width = cots[0].shape[1]
    rows = experts * cap
    last = payloads[0].shape[0] // TAIL - 1
    return call(
        functools.partial(cot_hidden_kernel, experts=experts),
        (me, *payloads, *cots, w_down),
        [pl.BlockSpec(memory_space=pltpu.SMEM)]
        + [pl.BlockSpec((TAIL, width), lambda f: (last, 0))] * experts
        + whole_specs(cots)
        + [pl.BlockSpec((1, FF_BLOCK, width), lambda f: (0, f, 0))],
        grid=(count,),
        out_specs=[pl.BlockSpec((rows, FF_BLOCK), lambda f: (0, f)), const_spec((rows, width))],
        out_shape=[jax.ShapeDtypeStruct((rows, count * FF_BLOCK), BF), jax.ShapeDtypeStruct((rows, width), BF)],
        cost_estimate=estimate("cot_hidden"),
        name="cot_hidden",
    )


def cot_hidden_more_kernel(rows_ref, wd_ref, out_ref):
    out_ref[...] = dot_nt(rows_ref[...], wd_ref[0]).astype(BF)


def cot_hidden_more(cot_rows, w_down, first):
    rows, width = cot_rows.shape
    count = w_down.shape[1] // FF_BLOCK - first
    return call(
        cot_hidden_more_kernel,
        (cot_rows, w_down),
        [const_spec((rows, width)), pl.BlockSpec((1, FF_BLOCK, width), lambda f: (0, first + f, 0))],
        grid=(count,),
        out_specs=pl.BlockSpec((rows, FF_BLOCK), lambda f: (0, f)),
        out_shape=jax.ShapeDtypeStruct((rows, count * FF_BLOCK), BF),
        cost_estimate=estimate("cot_hidden_more"),
        name="cot_hidden_more",
    )


ROW_BLOCK = 320


def expert_first(me_ref, place_ref, payloads, cot_ref, x_ref, xt_ref, gate_ref, gc_ref):
    experts = len(payloads) // 2
    cap = x_ref.shape[0] // experts
    part = payloads[0].shape[0] - TAIL
    row = lax.broadcasted_iota(jnp.int32, (TAIL, part), 0)
    mine = jnp.logical_or(row == me_ref[0], row == me_ref[0] + TAIL // 2)
    for m in range(experts):
        code = own_code(me_ref[0], payloads[2 * m][part:, part : 3 * part])
        chosen = selector(code, cap)
        place = slice(m * cap, (m + 1) * cap)
        total = jnp.zeros((cap, x_ref.shape[1]), F32)
        gate = jnp.zeros((cap, 1), F32)
        for i in range(2):
            payload = payloads[2 * m + i]
            part_chosen = chosen[:, i * part : (i + 1) * part]
            total = total + dot(part_chosen, payload[0:part, :])
            chances = jnp.sum(jnp.where(mine, payload[part:, 0:part].astype(F32), 0.0), axis=0, keepdims=True)
            gate = gate + jnp.sum(part_chosen.astype(F32) * chances, axis=1, keepdims=True)
        x_ref[place, :] = total.astype(BF)
        gate_ref[place, :] = jnp.broadcast_to(gate, (cap, LANES))
        gc_ref[place, :] = (cot_ref[place, :].astype(F32) * gate).astype(BF)
    flipped = x_ref[...].T
    owners = place_ref.shape[0]
    rows = flipped.shape[0] // owners
    for b in range(owners):
        at = pl.multiple_of(place_ref[b] * rows, rows)
        xt_ref[pl.ds(at, rows), :] = flipped[b * rows : (b + 1) * rows]


def expert_a_kernel(*refs, experts):
    step = pl.program_id(0)
    if experts:
        me_ref, place_ref = refs[:2]
        payloads = refs[2 : 2 + 2 * experts]
        cot_ref, gh_ref, wg_ref, wu_ref, x_ref, xt_ref, gate_ref, gc_ref = refs[2 + 2 * experts : 10 + 2 * experts]

        @pl.when(step == 0)
        def _():
            expert_first(me_ref, place_ref, payloads, cot_ref, x_ref, xt_ref, gate_ref, gc_ref)

    else:
        x_ref, xt_ref, gate_ref, gh_ref, wg_ref, wu_ref = refs[:6]
    gate_keep_ref, gate_send_ref, up_keep_ref, up_send_ref, sc_ref, hid_ref, hidt_ref, gg_ref, gu_ref = refs[-9:]

    @pl.when(step == 0)
    def _():
        sc_ref[...] = jnp.zeros_like(sc_ref)

    wg, wu = wg_ref[0], wu_ref[0]
    width = wg.shape[1]
    for start in range(0, x_ref.shape[0], ROW_BLOCK):
        part = slice(start, start + ROW_BLOCK)
        x = x_ref[part, :]
        gate_pre = dot(x, wg)
        up_pre = dot(x, wu)
        grad = gh_ref[part, :].astype(F32)
        act, slope = gelu_parts(gate_pre)
        hidden = act * up_pre
        hid_ref[part, :] = hidden.astype(BF)
        product = hidden * grad
        folded = product[:, 0:LANES]
        for i in range(1, width // LANES):
            folded = folded + product[:, i * LANES : (i + 1) * LANES]
        sc_ref[part, :] += folded
        grad = grad * gate_ref[part, 0:1]
        gg_ref[part, :] = (slope * up_pre * grad).astype(BF)
        gu_ref[part, :] = (act * grad).astype(BF)
    hidt_ref[...] = hid_ref[...].T
    xt = xt_ref[...]
    cut = xt.shape[0] // 4
    for grad_ref, keep_ref, send_ref, second in ((gg_ref, gate_keep_ref, gate_send_ref, 1), (gu_ref, up_keep_ref, up_send_ref, 0)):
        term = dot(xt, grad_ref[...]).astype(BF)
        for q in range(4):
            upper, lower = (q % 2, q // 2) if second else (q // 2, q % 2)
            (send_ref if upper else keep_ref)[lower * cut : (lower + 1) * cut] = term[q * cut : (q + 1) * cut]


def expert_a(source, gh, gh_first, w_gate, w_up, first, count, filled=()):
    opening = 0 if filled else len(source[2]) // 2
    rows = gh.shape[0]
    width, ff = w_gate.shape[1:]
    span = count * FF_BLOCK
    col_weight = pl.BlockSpec((1, width, FF_BLOCK), lambda f: (0, 0, first + f))
    out_block = pl.BlockSpec((rows, FF_BLOCK), lambda f: (0, first + f))
    wide = jax.ShapeDtypeStruct((rows, ff), BF)
    tall = jax.ShapeDtypeStruct((ff, rows), BF)
    term = jax.ShapeDtypeStruct((width // 2, span), BF)
    term_block = pl.BlockSpec((width // 2, FF_BLOCK), lambda f: (0, f))
    if opening:
        me, place, payloads, cot_rows = source
        args = (me, place, *payloads, cot_rows)
        specs = [pl.BlockSpec(memory_space=pltpu.SMEM)] * 2 + whole_specs((*payloads, cot_rows))
        shared = [
            jax.ShapeDtypeStruct((rows, width), BF),
            jax.ShapeDtypeStruct((width, rows), BF),
            jax.ShapeDtypeStruct((rows, LANES), F32),
            jax.ShapeDtypeStruct((rows, width), BF),
        ]
    else:
        args = tuple(source)
        specs = whole_specs(source)
        shared = []
    args = (*args, gh, w_gate, w_up)
    used = len(args)
    first_filled = len(shared) + 5

    def run(*refs):
        expert_a_kernel(*refs[:used], *refs[used + len(filled) :], experts=opening)

    return call(
        run,
        (*args, *filled),
        specs
        + [pl.BlockSpec((rows, FF_BLOCK), lambda f: (0, first - gh_first + f)), col_weight, col_weight]
        + [pl.BlockSpec(memory_space=pl.ANY)] * len(filled),
        grid=(count,),
        out_specs=whole_specs(shared)
        + [term_block] * 4
        + [const_spec((rows, LANES)), out_block]
        + [pl.BlockSpec((FF_BLOCK, rows), lambda f: (first + f, 0)), out_block, out_block],
        out_shape=shared + [term] * 4 + [jax.ShapeDtypeStruct((rows, LANES), F32), wide, tall, wide, wide],
        input_output_aliases={used + i: first_filled + i for i in range(len(filled))},
        cost_estimate=estimate("expert_grads"),
        name="expert_grads",
    )


def expert_b_kernel(gg_ref, gu_ref, *refs, cap, experts):
    sc_refs, (wg_ref, wu_ref, *outs, acc) = refs[:-5], refs[-5:]
    part_sum = dot_nt(gg_ref[...], wg_ref[0]) + dot_nt(gu_ref[...], wu_ref[0])
    step, block = pl.program_id(0), pl.program_id(1)

    @pl.when(step == 0)
    def _():
        acc[block] = part_sum

    def finish(out_ref):
        total = acc[block] + part_sum
        row = lax.broadcasted_iota(jnp.int32, (cap, cap), 0)
        lane = lax.broadcasted_iota(jnp.int32, (cap, cap), 1)
        place = lax.broadcasted_iota(jnp.int32, (TAIL, cap), 0)
        out_ref[0:cap, :] = total.astype(BF)
        folded = sc_refs[0][...]
        for other in sc_refs[1:]:
            folded = folded + other[...]
        column = jnp.sum(folded, axis=1, keepdims=True)
        flat = jnp.sum(jnp.where(row == lane, column, 0.0), axis=0, keepdims=True)
        hi, mid, low = split3(flat)
        packed = jnp.where(
            place == 0, hi.astype(F32), jnp.where(place == 1, mid.astype(F32), jnp.where(place == 2, low.astype(F32), 0.0))
        )
        out_ref[cap : cap + TAIL, :] = jnp.zeros((TAIL, total.shape[1]), BF)
        out_ref[cap : cap + TAIL, 0:cap] = packed.astype(BF)

    last = step == pl.num_programs(0) - 1
    for m in range(experts):

        @pl.when(jnp.logical_and(last, block == m))
        def _(m=m):
            finish(outs[m // (experts // 2)].at[m % (experts // 2)])


def expert_b(gg, gu, scs, w_gate, w_up, experts):
    rows, ff = gg.shape
    width = w_gate.shape[1]
    cap = rows // experts
    cut = ff // 2
    grads = pl.BlockSpec((cap, cut), lambda k, m: (m, k))
    sums = pl.BlockSpec((cap, LANES), lambda k, m: (m, 0))
    weight = pl.BlockSpec((1, width, cut), lambda k, m: (0, 0, k))
    return call(
        functools.partial(expert_b_kernel, cap=cap, experts=experts),
        (gg, gu, *scs, w_gate, w_up),
        [grads, grads] + [sums] * len(scs) + [weight, weight],
        grid=(2, experts),
        out_specs=[const_spec((experts // 2, cap + TAIL, width))] * 2,
        out_shape=[jax.ShapeDtypeStruct((experts // 2, cap + TAIL, width), BF)] * 2,
        scratch_shapes=[pltpu.VMEM((experts, cap, width), F32)],
        cost_estimate=estimate("expert_input_grad"),
        name="expert_input_grad",
    )


def down_kernel(place_a_ref, place_b_ref, hidt_ref, gc_ref, *outs):
    owners = place_a_ref.shape[0]
    shard = 2 * outs[0].shape[0] // owners
    size = int(np.gcd(shard, 32))
    rows = hidt_ref.shape[0]
    step = pl.program_id(0)
    total = dot(hidt_ref[...], gc_ref[...]).astype(BF)
    half = total.shape[1] // 2
    for i in range(rows // size):
        row = step * rows + i * size
        owner = row // shard
        piece = total[i * size : (i + 1) * size]
        for keep_ref, send_ref, place_ref, cols in (
            (outs[0], outs[1], place_a_ref, piece[:, :half]),
            (outs[2], outs[3], place_b_ref, piece[:, half:]),
        ):
            place = place_ref[owner]
            at = pl.multiple_of((place % (owners // 2)) * shard + (row - owner * shard), size)

            @pl.when(place < owners // 2)
            def _(keep_ref=keep_ref, at=at, cols=cols):
                keep_ref[pl.ds(at, size), :] = cols

            @pl.when(place >= owners // 2)
            def _(send_ref=send_ref, at=at, cols=cols):
                send_ref[pl.ds(at, size), :] = cols


def down_grads(hid_t, grad_cots, place_a, place_b):
    rows, width = grad_cots.shape
    ff = hid_t.shape[0]
    table = pl.BlockSpec(memory_space=pltpu.SMEM)
    part = jax.ShapeDtypeStruct((ff // 2, width // 2), BF)
    return call(
        down_kernel,
        (place_a, place_b, hid_t, grad_cots),
        [table, table, pl.BlockSpec((ff // 4, rows), lambda f: (f, 0)), const_spec((rows, width))],
        grid=(4,),
        out_specs=[const_spec(part.shape)] * 4,
        out_shape=[part] * 4,
        cost_estimate=estimate("down_grads"),
        name="down_grads",
    )


def produced_kernel(hid_ref, wd_ref, low_ref, high_ref):
    rows = dot(hid_ref[...], wd_ref[0]).astype(BF)
    lower = pl.program_id(0) < pl.num_programs(0) // 2

    @pl.when(lower)
    def _():
        low_ref[0] = rows

    @pl.when(jnp.logical_not(lower))
    def _():
        high_ref[0] = rows


def produced_rows(hid, w_down, experts):
    rows, ff = hid.shape
    width = w_down.shape[2]
    cap, half = rows // experts, experts // 2
    return call(
        produced_kernel,
        (hid, w_down),
        [pl.BlockSpec((cap, ff), lambda m: (m, 0)), const_spec(w_down.shape)],
        grid=(experts,),
        out_specs=[
            pl.BlockSpec((1, cap, width), lambda m: (jnp.minimum(m, half - 1), 0, 0)),
            pl.BlockSpec((1, cap, width), lambda m: (jnp.maximum(m - half, 0), 0, 0)),
        ],
        out_shape=[jax.ShapeDtypeStruct((half, cap, width), BF)] * 2,
        cost_estimate=estimate("produced_rows"),
        name="produced_rows",
    )


def distinct(slots):
    arrays, found = [], []
    for array, index in slots:
        which = next((i for i, other in enumerate(arrays) if other is array), None)
        if which is None:
            which = len(arrays)
            arrays.append(array)
        found.append((which, index))
    return arrays, found


def layer_out_kernel(mid_ref, ch_ref, code_ref, *refs, slots):
    parts, out_ref = refs[:-1], refs[-1]
    cap = parts[0].shape[1]
    total = mid_ref[...]
    chances = ch_ref[...].T
    for m, (which, index) in enumerate(slots):
        picked = dot(selector_t(code_ref[:, m : m + 1], cap), parts[which][index])
        total = total + chances[:, m : m + 1] * picked
    out_ref[...] = total.astype(BF)


def layer_output(middle, chances, code_t, slots):
    rows, width = middle.shape
    arrays, found = distinct(slots)
    args = (middle, chances, code_t, *arrays)
    return call(
        functools.partial(layer_out_kernel, slots=found),
        args,
        [pl.BlockSpec(memory_space=pltpu.VMEM)] * len(args),
        out_shape=jax.ShapeDtypeStruct((rows, width), BF),
        cost_estimate=estimate("layer_output"),
        name="layer_output",
    )


def moe_bwd_kernel(
    cot_ref, mid_ref, gain_ref, nm_ref, ch_ref, wr_ref, code_ref, codet_ref, wo_ref, *refs, slots
):
    backs, (gmid_ref, branch_ref, ga_ref, gain_o_ref, router_o_ref) = refs[:-5], refs[-5:]
    experts, cap = len(slots), backs[0].shape[1] - TAIL
    rows = cot_ref.shape[0]
    grad = jnp.zeros(mid_ref.shape, F32)
    gate_rows = []
    for m, (which, index) in enumerate(slots):
        grad = grad + dot(selector_t(codet_ref[:, m : m + 1], cap), backs[which][index, 0:cap, :])
        picked = dot(backs[which][index, cap : cap + TAIL, 0:cap], selector(code_ref[m : m + 1, :], cap))
        gate_rows.append(jnp.sum(picked, axis=0, keepdims=True))
    gate_rows.append(jnp.zeros((TAIL - experts, rows), F32))
    grad_chances = jnp.concatenate(gate_rows, axis=0)
    chances = ch_ref[...]
    grad_logits = chances * (grad_chances - jnp.sum(chances * grad_chances, axis=0, keepdims=True))
    pieces = jnp.concatenate(split3(grad_logits), axis=0)
    wr = wr_ref[...]
    grad = grad + dot_tn(pieces, jnp.concatenate([wr, wr, wr], axis=0))
    router = dot(pieces, nm_ref[...])
    router_o_ref[...] = router[0:TAIL] + router[TAIL : 2 * TAIL] + router[2 * TAIL : 3 * TAIL]
    mid = mid_ref[...]
    scale = rms_scale(mid)
    unit = mid * scale
    gain_o_ref[...] = jnp.sum(grad * unit, axis=0, keepdims=True)
    scaled = grad * gain_ref[...]
    grad_mid = cot_ref[...].astype(F32) + scale * (scaled - unit * jnp.mean(scaled * unit, axis=-1, keepdims=True))
    gmid_ref[...] = grad_mid
    branch = grad_mid.astype(BF)
    branch_ref[...] = branch
    ga_ref[...] = dot_nt(branch, wo_ref[...]).astype(BF)


def sort_rows(place_ref, value, out_ref):
    owners = place_ref.shape[0]
    rows = value.shape[0] // owners
    for b in range(owners):
        out_ref[pl.ds(pl.multiple_of(place_ref[b] * rows, rows), rows), :] = value[b * rows : (b + 1) * rows]


def moe_bwd(cot, middle, gain_moe, normed_moe, chances, wr_t, code, code_t, w_out, slots):
    rows, width = cot.shape
    arrays, found = distinct(slots)
    args = (cot, middle, gain_moe[None], normed_moe, chances, wr_t, code, code_t, w_out, *arrays)
    wide = jax.ShapeDtypeStruct((rows, width), BF)
    return call(
        functools.partial(moe_bwd_kernel, slots=found),
        args,
        [pl.BlockSpec(memory_space=pltpu.VMEM)] * len(args),
        out_shape=[
            jax.ShapeDtypeStruct((rows, width), F32),
            wide,
            wide,
            jax.ShapeDtypeStruct((1, width), F32),
            jax.ShapeDtypeStruct((TAIL, width), F32),
        ],
        cost_estimate=estimate("moe_bwd"),
        name="moe_bwd",
    )


def attn_bwd_kernel(
    qs_ref, k_ref, v_ref, ga_ref, lse_ref, woff_ref, seg_ref,
    dq_ref, dk_ref, dv_ref, dwoff_ref, mask_scr, p_scr, ds_scr,
    *, head_dim,
):
    rows = qs_ref.shape[0]
    blocks = rows // LANES

    @pl.when(pl.program_id(0) == 0)
    def _():
        mask_scr[...] = segment_mask(seg_ref, 0, rows)

    scaled, keys, values, grads = qs_ref[...], k_ref[...], v_ref[...], ga_ref[...]
    q_t, g_t, k_t = scaled.T, grads.T, keys.T
    low_half = lax.broadcasted_iota(jnp.int32, (rows, LANES), 1) < head_dim
    dq_t, dk_parts, dv_parts = [], [], []
    lane = lax.broadcasted_iota(jnp.int32, (1, BAND), 1)
    for h in range(HEAD_GROUP):
        row = woff_ref[0, h : h + 1, :]
        band = band_of(row)
        pair = slice(LANES * (h // 2), LANES * (h // 2 + 1))
        k_pair, v_pair = keys[:, pair], values[:, pair]
        q_only, g_only = only_rows(q_t, h, head_dim), only_rows(g_t, h, head_dim)
        tiles = {}
        for b in range(0, blocks, 2):
            lanes = slice(b * LANES, (b + 2) * LANES)
            s = dot(k_pair, q_only[:, lanes]) + bias_block(band, row, b, 2, blocks) + mask_scr[:, lanes]
            p = jnp.exp(s - lse_ref[0, h : h + 1, lanes])
            dp = dot(v_pair, g_only[:, lanes])
            ds = p * (dp - jnp.sum(p * dp, axis=0, keepdims=True))
            p_scr[:, lanes] = p.astype(BF)
            ds_scr[:, lanes] = ds.astype(BF)
            for q_block in range(2):
                for k_block in range(blocks):
                    d = max(-2, min(2, k_block - b - q_block))
                    tile = ds[k_block * LANES : (k_block + 1) * LANES, q_block * LANES : (q_block + 1) * LANES]
                    tiles[d] = tiles[d] + tile if d in tiles else tile
        skewed = jnp.concatenate([tiles[1], tiles[0], tiles[-1], jnp.zeros_like(tiles[0])], axis=1)
        offsets = diagonal_sums(skewed)
        offsets = offsets + jnp.where(lane == FAR_AFTER, jnp.sum(tiles[2]), 0.0)
        offsets = offsets + jnp.where(lane == FAR_BEFORE, jnp.sum(tiles[-2]), 0.0)
        dwoff_ref[0, h : h + 1, :] = offsets
        p_all, ds_all = p_scr[...], ds_scr[...]
        dv_parts.append(dot(p_all, grads[:, pair]))
        dk_parts.append(dot(ds_all, scaled[:, pair]))
        dq_t.append(dot(k_t[h * head_dim : (h + 1) * head_dim], ds_all))
    dq = jnp.concatenate(dq_t, axis=0).T * head_dim ** (-0.5)
    dq_ref[...] = dq.astype(BF)
    for i in range(HEAD_GROUP // 2):
        pair = slice(LANES * i, LANES * (i + 1))
        dk_ref[:, pair] = jnp.where(low_half, dk_parts[2 * i], dk_parts[2 * i + 1]).astype(BF)
        dv_ref[:, pair] = jnp.where(low_half, dv_parts[2 * i], dv_parts[2 * i + 1]).astype(BF)


def attn_bwd(scaled, keys, values, grad_att, lse, woff, seg):
    rows, width = scaled.shape
    groups = woff.shape[0]
    cols = width // groups
    col_block = pl.BlockSpec((rows, cols), lambda g: (0, g))
    wide = jax.ShapeDtypeStruct((rows, width), BF)
    return call(
        functools.partial(attn_bwd_kernel, head_dim=cols // HEAD_GROUP),
        (scaled, keys, values, grad_att, lse, woff, seg),
        [
            col_block,
            col_block,
            col_block,
            col_block,
            pl.BlockSpec((1, HEAD_GROUP, rows), lambda g: (g, 0, 0)),
            pl.BlockSpec((1, HEAD_GROUP, BAND), lambda g: (g, 0, 0)),
            const_spec(seg.shape),
        ],
        grid=(groups,),
        out_specs=[col_block, col_block, col_block, pl.BlockSpec((1, HEAD_GROUP, BAND), lambda g: (g, 0, 0))],
        out_shape=[wide, wide, wide, jax.ShapeDtypeStruct((groups, HEAD_GROUP, BAND), F32)],
        scratch_shapes=[
            pltpu.VMEM((rows, rows), F32),
            pltpu.VMEM((rows, rows), BF),
            pltpu.VMEM((rows, rows), BF),
        ],
        cost_estimate=estimate("attn_bwd"),
        name="attn_bwd",
    )


def sorted_rows_kernel(pq_ref, pk_ref, tok_ref, gain_ref, att_ref, att_o_ref, out_ref, sort_scr):
    start = tok_ref[...].astype(F32)
    normed_t = (start * rms_scale(start) * gain_ref[...]).T
    attended_t = att_ref[...].astype(F32).T
    sort_rows(pq_ref, attended_t, sort_scr)
    att_o_ref[...] = sort_scr[...].astype(BF)
    for i, place_ref in enumerate((pq_ref, pk_ref)):
        sort_rows(place_ref, normed_t, sort_scr)
        out_ref[i] = sort_scr[...].astype(BF)


def sorted_rows(place_q, place_k, tokens, gain_attn, attended):
    rows, width = tokens.shape
    return call(
        sorted_rows_kernel,
        (place_q, place_k, tokens, gain_attn[None], attended),
        [pl.BlockSpec(memory_space=pltpu.SMEM)] * 2 + [pl.BlockSpec(memory_space=pltpu.VMEM)] * 3,
        out_shape=[jax.ShapeDtypeStruct((width, rows), BF), jax.ShapeDtypeStruct((2, width, rows), BF)],
        scratch_shapes=[pltpu.VMEM((width, rows), F32)],
        cost_estimate=estimate("sorted_rows"),
        name="sorted_rows",
    )


def dense_terms_kernel(att_ref, rows_ref, branch_ref, dq_ref, dk_ref, dv_ref, keep_ref, send_ref):
    half = keep_ref.shape[1]
    for i, d_ref in enumerate((branch_ref, dq_ref, dk_ref, dv_ref)):
        lhs = att_ref[...] if i == 0 else rows_ref[min(i - 1, 1)]
        term = dot(lhs, d_ref[...]).astype(BF)
        keep_ref[i] = term[:half]
        send_ref[i] = term[half:]


def dense_terms(att_t, lhs, branch, dq, dk, dv):
    _, width, rows = lhs.shape
    cols = 256
    col_block = pl.BlockSpec((rows, cols), lambda g: (0, g))
    return call(
        dense_terms_kernel,
        (att_t, lhs, branch, dq, dk, dv),
        [const_spec(att_t.shape), const_spec(lhs.shape)] + [col_block] * 4,
        grid=(width // cols,),
        out_specs=[pl.BlockSpec((4, width // 2, cols), lambda g: (0, 0, g))] * 2,
        out_shape=[jax.ShapeDtypeStruct((4, width // 2, width), BF)] * 2,
        cost_estimate=estimate("dense_terms"),
        name="dense_terms",
    )


def norm_bwd_kernel(
    tok_ref, gain_ref, gmid_ref, dq_ref, dk_ref, dv_ref, wq_ref, wk_ref, wv_ref, tg_ref, gain_o_ref, acc
):
    step = pl.program_id(0)
    total = dot_nt(dq_ref[...], wq_ref[...]) + dot_nt(dk_ref[...], wk_ref[...]) + dot_nt(dv_ref[...], wv_ref[...])

    @pl.when(step == 0)
    def _():
        acc[...] = total

    @pl.when(step > 0)
    def _():
        acc[...] += total

    @pl.when(step == pl.num_programs(0) - 1)
    def _():
        grad = acc[...]
        start = tok_ref[...].astype(F32)
        scale = rms_scale(start)
        unit = start * scale
        gain_o_ref[...] = jnp.sum(grad * unit, axis=0, keepdims=True)
        scaled = grad * gain_ref[...]
        tg_ref[...] = gmid_ref[...] + scale * (scaled - unit * jnp.mean(scaled * unit, axis=-1, keepdims=True))


def norm_bwd(tokens, gain_attn, grad_mid, dq, dk, dv, w_query, w_key, w_value):
    rows, width = tokens.shape
    cols = 256
    col_block = pl.BlockSpec((rows, cols), lambda g: (0, g))
    weight_block = pl.BlockSpec((width, cols), lambda g: (0, g))
    return call(
        norm_bwd_kernel,
        (tokens, gain_attn[None], grad_mid, dq, dk, dv, w_query, w_key, w_value),
        [const_spec((rows, width)), const_spec((1, width)), const_spec((rows, width))] + [col_block] * 3 + [weight_block] * 3,
        grid=(width // cols,),
        out_specs=[const_spec((rows, width)), const_spec((1, width))],
        out_shape=[jax.ShapeDtypeStruct((rows, width), F32), jax.ShapeDtypeStruct((1, width), F32)],
        scratch_shapes=[pltpu.VMEM((rows, width), F32)],
        cost_estimate=estimate("norm_bwd"),
        name="norm_bwd",
    )


def bits_of(size):
    return size.bit_length() - 1


def swap(value, axis, size, mask):
    return lax.ppermute(value, axis, [(i, i ^ mask) for i in range(size)])


def pick(value, index, axis):
    return lax.dynamic_index_in_dim(value, index, axis, keepdims=False)


class Order:
    def __init__(self, token):
        self.token = token

    def enter(self, tree):
        tree, self.token = lax.optimization_barrier((tree, self.token))
        return tree

    leave = enter


def places(me, bits, order):
    key = jnp.arange(1 << bits, dtype=jnp.int32) ^ me
    place = jnp.zeros_like(key)
    for bit in order:
        place = place * 2 + ((key >> bit) & 1)
    return place


class Halving:
    def __init__(self, order, keep, send, dim, route, name):
        self.order, self.keep, self.to_send, self.dim, self.route, self.name = order, keep, send, dim, list(route), name
        self.got = None

    def start(self):
        axis, size, bit = self.route[0]
        with jax.named_scope(f"{self.name}_{axis}{1 << bit}"):
            value = self.order.enter(self.keep if self.to_send is None else self.to_send)
            self.got = swap(value, axis, size, 1 << bit)


def arrive(*units):
    for unit in units:
        unit.got = unit.order.leave(unit.got)


def fold_kernel(*refs, cuts, inputs):
    pairs, outs = refs[:inputs], list(refs[inputs:])
    at = 0
    for dim, last, width in cuts:
        total = []
        for _ in range(width):
            total.append(pairs[at][...].astype(F32) + pairs[at + 1][...].astype(F32))
            at += 2
        if last:
            outs.pop(0)[...] = total[0]
            continue
        rows = total[0].shape[dim] // 2
        for start in (0, rows):
            out = outs.pop(0)
            cut = [lax.slice_in_dim(v, start, start + rows, axis=dim).astype(BF) for v in total]
            if width == 1:
                out[...] = cut[0]
            else:
                for i in range(width):
                    out[i] = cut[i]


def fold(*units, hold=()):
    groups = [unit if isinstance(unit, tuple) else (unit,) for unit in units]
    order = groups[0][0].order
    args, cuts, shapes = [], [], []
    for group in groups:
        for unit in group:
            unit.route.pop(0)
            got = order.leave(unit.got)
            args += [unit.keep, got]
        unit = group[0]
        last = unit.to_send is None or not unit.route
        cuts.append((unit.dim, last, len(group)))
        if last:
            shapes.append(jax.ShapeDtypeStruct(got.shape, F32))
        else:
            shape = list(got.shape)
            shape[unit.dim] //= 2
            if len(group) > 1:
                shape = [len(group)] + shape
            shapes += [jax.ShapeDtypeStruct(tuple(shape), BF)] * 2
    args = order.enter(args)
    outs = list(
        call(
            functools.partial(fold_kernel, cuts=cuts, inputs=len(args)),
            args,
            [pl.BlockSpec(memory_space=pltpu.VMEM)] * len(args),
            out_shape=shapes,
            cost_estimate=estimate("fold"),
            name="fold",
        )
    )
    outs = order.leave(outs)
    for group, (_, last, width) in zip(groups, cuts):
        unit = group[0]
        unit.keep = outs.pop(0)
        if not last:
            unit.to_send = outs.pop(0)
        if width > 1:
            unit.dim += 1
        if unit.route and unit not in hold:
            unit.start()


def fold_first_kernel(keep_ref, got_ref, small_keep_ref, small_got_ref, *outs):
    width = keep_ref.shape[2]
    small = (small_keep_ref[...] + small_got_ref[...]).astype(F32)
    for i in range(keep_ref.shape[0]):
        total = keep_ref[i].astype(F32) + got_ref[i].astype(F32)
        rows = total.shape[0] // 2
        for j in range(2):
            out = outs[i // 2 * 2 + j]
            out[i % 2, :, 0:width] = total[j * rows : (j + 1) * rows].astype(BF)
            if i < 2:
                extra = small[j * rows : (j + 1) * rows] if i == 0 else jnp.zeros((rows, LANES), F32)
                out[i, :, width:] = extra.astype(BF)


def fold_first(keep, got, small_keep, small_got):
    _, rows, width = keep.shape
    shapes = [jax.ShapeDtypeStruct((2, rows // 2, width + extra), BF) for extra in (LANES, LANES, 0, 0)]
    return call(
        fold_first_kernel,
        (keep, got, small_keep, small_got),
        [pl.BlockSpec(memory_space=pltpu.VMEM)] * 4,
        out_shape=shapes,
        cost_estimate=estimate("fold_first"),
        name="fold_first",
    )


class Return:
    def __init__(self, order, low, high, axis, size, name, pieces=False):
        self.order, self.axis, self.size, self.name = order, axis, size, name
        half = low.shape[0]
        self.slots = [(low, i) for i in range(half)] + [(high, i) for i in range(half)]
        self.bit = bits_of(size) - 1
        if pieces:
            self.start_pieces()
        else:
            with jax.named_scope(f"{self.name}{1 << self.bit}"):
                self.got = swap(self.order.enter(high), self.axis, self.size, 1 << self.bit)

    def moving(self):
        return [m for m in range(self.size) if (m >> self.bit) & 1]

    def start_pieces(self):
        self.got = []
        for m in self.moving():
            array, index = self.slots[m]
            with jax.named_scope(f"{self.name}{1 << self.bit}_{m}"):
                self.got.append(swap(self.order.enter(array[index][None]), self.axis, self.size, 1 << self.bit))

    def fold(self):
        got = self.order.leave(self.got)
        for i, m in enumerate(self.moving()):
            self.slots[m] = (got[i], 0) if isinstance(got, list) else (got, i)
        self.bit -= 1
        if self.bit >= 0:
            self.start_pieces()

    def finish(self):
        while self.bit >= 0:
            self.fold()


class Gather:
    def __init__(self, order, value, axis, size, name):
        self.order, self.axis, self.size, self.name = order, axis, size, name
        self.blocks = {0: value}
        self.send(0, size // 2)
        if size > 2:
            self.send(0, 1)

    def send(self, m, bit):
        with jax.named_scope(f"{self.name}{m}_{bit}"):
            self.blocks[m ^ bit] = swap(self.blocks[m], self.axis, self.size, bit)

    def relay(self):
        self.blocks[self.size // 2] = self.order.leave(self.blocks[self.size // 2])
        bit = self.size // 2
        while bit:
            for m in range(0, self.size, 2 * bit):
                if m ^ bit not in self.blocks:
                    self.send(m, bit)
            bit //= 2

    def finish(self):
        self.blocks = self.order.leave(self.blocks)
        return [self.blocks[m] for m in range(self.size)]


def body(
    tokens,
    cotangent,
    gain_attn,
    w_query,
    w_key,
    w_value,
    w_out,
    rel_bias,
    gain_moe,
    w_router,
    w_gate,
    w_up,
    w_down,
    segments,
    routes,
    *,
    dp_size,
    ep_size,
):
    TURNS.clear()
    rows, width = tokens.shape
    buckets, heads = rel_bias.shape
    experts = w_router.shape[1]
    cap = 10 * rows // (4 * experts)
    ff = w_gate.shape[2]
    me = lax.axis_index("expert")

    cots = Gather(None, cotangent, "expert", ep_size, "cot")
    scaled, keys, values, woff, token, code, *filled, payload = attn_first(
        tokens, gain_attn, w_query, w_key, w_value, w_out, rel_bias, segments, gain_moe, w_router, routes
    )
    order = Order(token)
    cots.order = order
    me_ref = me.reshape(1).astype(jnp.int32)

    dp_bits, ep_bits = bits_of(dp_size), bits_of(ep_size)
    dp_me = lax.axis_index("dp")
    dp_order = list(range(dp_bits))
    z_order = [1, 0] + dp_order[2:]
    place_x = places(dp_me, dp_bits, dp_order)
    place_z = places(dp_me, dp_bits, z_order)

    def dp_route(bits):
        return [("dp", dp_size, b) for b in bits]

    dp_part = [ep_bits + b for b in dp_order]
    ep_part = list(range(1, ep_bits))
    q_bits = [0] + ep_part + dp_part
    k_bits = [0] + dp_part[:2] + ep_part + dp_part[2:]
    whole_me = dp_me * ep_size + me

    def route(bits):
        return [("expert", ep_size, b) if b < ep_bits else ("dp", dp_size, b - ep_bits) for b in bits]

    place_q, place_k = [places(whole_me, dp_bits + ep_bits, bits) for bits in (q_bits, k_bits)]

    cots.relay()
    first_half = Gather(order, order.enter(payload), "expert", ep_size, "rows_a")
    attended, lse, middle, normed_moe, chances, payload = order.leave(
        attn_second(tokens, order.enter(scaled), keys, values, w_out, woff, segments, gain_moe, w_router, filled)
    )
    second_half = Gather(order, order.enter(payload), "expert", ep_size, "rows_b")
    first_half.relay()
    cots, heads_rows = cots.finish(), first_half.finish()
    blocks = ff // FF_BLOCK
    counts = [blocks - blocks // 2, blocks // 2]
    starts = [sum(counts[:i]) for i in range(len(counts))]
    gh_first, cot_rows = order.leave(cot_hidden(order.enter(me_ref), heads_rows, cots, w_down, cap, starts[1]))
    second_half.relay()
    payloads = [v for pair in zip(heads_rows, second_half.finish()) for v in pair]
    scs, units = [], []

    def expert_part(i, source, filled=()):
        *shared, gate_keep, gate_send, up_keep, up_send, sc, hid, hid_t, gg, gu = order.leave(
            expert_a(
                order.enter(source), gh_second if i else gh_first, starts[i], w_gate, w_up, starts[i], counts[i], filled
            )
        )
        scs.append(sc)
        gate = Halving(order, gate_keep, gate_send, 0, dp_route(z_order), f"gate{i}")
        units.append((gate, Halving(order, up_keep, up_send, 0, dp_route(dp_order), f"up{i}")))
        return shared, (hid, hid_t, gg, gu)

    def by_xor(value):
        return jnp.stack([pick(value, me ^ m, 0) for m in range(experts)])

    def padded(value):
        return jnp.pad(value, ((0, TAIL - experts), (0, 0)))

    (x_all, x_t, gate_all, grad_cots), filled = expert_part(0, (me_ref, place_x, payloads, cot_rows))
    for unit in units[0]:
        unit.start()
    gh_second = order.leave(cot_hidden_more(order.enter(cot_rows), w_down, starts[1]))
    _, (hid, hid_t, gg, gu) = expert_part(1, (x_all, x_t, gate_all), filled)
    fold(*units[0])
    for unit in units[1]:
        unit.start()
    back_low, back_high = order.leave(expert_b(order.enter(gg), gu, scs, w_gate, w_up, experts))
    backs = Return(order, back_low, back_high, "expert", ep_size, "grad_rows")
    first, second = units[0][0], units[1][0]
    fold(units[0])
    down_parts = order.leave(down_grads(order.enter(hid_t), grad_cots, place_z, place_x))
    down_units = tuple(
        Halving(order, down_parts[2 * i], down_parts[2 * i + 1], 0, dp_route(bits), f"down{i}")
        for i, bits in enumerate((z_order, dp_order))
    )
    down = down_units[0]
    fold(*units[1])
    code_xor, chances_xor, wr_xor = order.enter((by_xor(code), padded(by_xor(chances)), padded(by_xor(w_router.T))))
    backs.fold()
    att_t, normed_t = order.leave(sorted_rows(place_q, place_k, order.enter(tokens), gain_attn, attended))
    backs.finish()
    for unit in down_units:
        unit.start()
    grad_mid, branch, grad_att, gain_moe_term, router_term = order.leave(
        moe_bwd(
            cotangent, order.enter(middle), gain_moe, normed_moe, chances_xor, wr_xor, code_xor, code_xor.T, w_out,
            backs.slots,
        )
    )
    dq, dk, dv, dwoff = order.leave(attn_bwd(scaled, keys, values, order.enter(grad_att), lse, woff, segments))
    arrive(first, *units[1])
    dense_keep, dense_send = order.leave(dense_terms(att_t, normed_t, branch, order.enter(dq), dk, dv))
    arrive(*units[1], *down_units)
    core = Halving(order, dense_keep, dense_send, 1, route(q_bits)[:1], "dense")
    core.start()
    fold(*down_units, first, units[1], hold=units[1])
    token_grad, gain_attn_term = order.leave(
        norm_bwd(tokens, gain_attn, grad_mid, order.enter(dq), dk, dv, w_query, w_key, w_value)
    )
    onehot = jnp.asarray(band_onehot(rows, buckets))
    bias_term = jnp.dot(onehot, dwoff.reshape(heads, BAND).T, precision=HIGHEST)
    devices = dp_size * ep_size
    share = width // devices
    small = jnp.concatenate(
        [
            by_xor(router_term).T.reshape(devices, -1),
            gain_attn_term.reshape(devices, -1),
            gain_moe_term.reshape(devices, -1),
            bias_term.reshape(devices, -1),
        ],
        axis=1,
    )
    count = small.shape[1]
    lines = -(-count // LANES)
    at_place = (place_q[None, :] == jnp.arange(devices, dtype=jnp.int32)[:, None]).astype(F32)
    small = jnp.dot(at_place, jnp.pad(small, ((0, 0), (0, lines * LANES - count))), precision=HIGHEST)
    small = small.reshape(devices, lines, LANES).astype(BF)
    small = jnp.pad(small, ((0, 0), (0, share - lines), (0, 0))).reshape(2, width // 2, LANES)
    small_keep, small_send = order.enter((small[0], small[1]))
    with jax.named_scope("small_expert1"):
        small_got = swap(small_send, "expert", ep_size, 1)
    core_got = order.leave(core.got)
    halves = order.leave(fold_first(order.enter(dense_keep), core_got, small_keep, order.leave(small_got)))
    dense = [
        Halving(order, halves[2 * i], halves[2 * i + 1], 1, route(bits)[1:], name)
        for i, (bits, name) in enumerate(((q_bits, "out_q"), (k_bits, "k_v")))
    ]
    out_q, k_v = dense
    arrive(*down_units)
    k_v.start()
    out_q.start()
    second.start()
    prod_low, prod_high = order.leave(produced_rows(order.enter(hid), w_down, experts))
    returned = Return(order, prod_low, prod_high, "expert", ep_size, "produced_rows")
    fold(k_v, out_q, down_units)
    fold(k_v, out_q, second)
    returned.fold()
    returned.finish()
    layer_out = order.leave(layer_output(middle, chances_xor, code_xor.T, returned.slots))
    fold(k_v, out_q, down)
    rest = [first, second, down, *dense]
    while any(unit.route for unit in rest):
        fold(*[unit for unit in rest if unit.route])
    small_sum = out_q.keep[0, 0:lines, width:].reshape(-1)[:count] + order.token[0, :1]

    terms = [first.keep, second.keep]
    gate_grad = jnp.concatenate([term[0] for term in terms], axis=1)[None]
    up_grad = jnp.concatenate([term[1] for term in terms], axis=1)[None]
    down_grad = jnp.concatenate([down.keep[0], down.keep[1]], axis=1)[None]
    n_router = width * experts // devices
    n_gain = width // devices
    router_grad = small_sum[:n_router].reshape(share, experts)
    gain_attn_grad = small_sum[n_router : n_router + n_gain]
    gain_moe_grad = small_sum[n_router + n_gain : n_router + 2 * n_gain]
    bias_grad = small_sum[n_router + 2 * n_gain :]
    return (
        layer_out,
        token_grad,
        out_q.keep[1, :, :width],
        k_v.keep[0],
        k_v.keep[1],
        out_q.keep[0, :, :width],
        gain_attn_grad,
        gain_moe_grad,
        bias_grad,
        router_grad,
        gate_grad,
        up_grad,
        down_grad,
    )


def solution(mesh):
    in_specs = (
        P(("dp", "expert"), None),
        P(("dp", "expert"), None),
        P(),
        P(),
        P(),
        P(),
        P(),
        P(),
        P(),
        P(),
        P("expert", None, None),
        P("expert", None, None),
        P("expert", None, None),
        P(("dp", "expert"), None),
        P(("dp", "expert"), None),
    )
    out_specs = (
        P(("dp", "expert"), None),
        P(("dp", "expert"), None),
        P(("dp", "expert"), None),
        P(("dp", "expert"), None),
        P(("dp", "expert"), None),
        P(("dp", "expert"), None),
        P(("dp", "expert")),
        P(("dp", "expert")),
        P(("dp", "expert")),
        P(("dp", "expert"), None),
        P("expert", "dp", None),
        P("expert", "dp", None),
        P("expert", "dp", None),
    )
    run = functools.partial(body, dp_size=mesh.shape["dp"], ep_size=mesh.shape["expert"])
    return jax.shard_map(run, mesh=mesh, in_specs=in_specs, out_specs=out_specs, check_vma=False)
```

```python
import functools

import jax
import jax.numpy as jnp
import numpy as np
from jax import lax
from jax.experimental import pallas as pl
from jax.experimental.pallas import tpu as pltpu
from jax.sharding import PartitionSpec as P

EPS = 1e-06
HIGHEST = lax.Precision.HIGHEST
LANES = 128
BAND = 4 * LANES
HEAD_GROUP = 4
TAIL = 16
FAR = -1e30
BF = jnp.bfloat16
F32 = jnp.float32
VMEM_LIMIT = 56 * 1024 * 1024


def bucket_of(relative, buckets):
    halfway = buckets // 2
    exact_span = halfway // 2
    distance = np.abs(relative)
    beyond = exact_span + (
        np.log(np.maximum(distance, 1) / exact_span)
        / np.log(128.0 / exact_span)
        * (halfway - exact_span)
    ).astype(np.int64)
    beyond = np.minimum(beyond, halfway - 1)
    return (
        (relative > 0).astype(np.int64) * halfway
        + np.where(distance < exact_span, distance, beyond)
    ).astype(np.int32)


def band_onehot(length, buckets):
    place = np.arange(BAND)
    relative = np.where(place <= 3 * LANES, LANES - place, BAND + LANES - place)
    table = (bucket_of(relative, buckets)[None, :] == np.arange(buckets)[:, None]).astype(np.float32)
    table[:, 3 * LANES] = 0.0
    far = np.arange(LANES, length)
    assert np.all(bucket_of(far, buckets) == bucket_of(far, buckets)[0])
    assert np.all(bucket_of(-far, buckets) == bucket_of(-far, buckets)[0])
    return table


FAR_AFTER = 3 * LANES + 1
FAR_BEFORE = 3 * LANES - 1


def dot(a, b):
    return lax.dot_general(a, b, (((1,), (0,)), ((), ())), preferred_element_type=F32)


def dot_nt(a, b):
    return lax.dot_general(a, b, (((1,), (1,)), ((), ())), preferred_element_type=F32)


def dot_tn(a, b):
    return lax.dot_general(a, b, (((0,), (0,)), ((), ())), preferred_element_type=F32)


def split3(value):
    hi = value.astype(BF)
    rest = value - hi.astype(F32)
    mid = rest.astype(BF)
    low = (rest - mid.astype(F32)).astype(BF)
    return hi, mid, low


def rms_scale(value):
    return lax.rsqrt(jnp.mean(value * value, axis=-1, keepdims=True) + EPS)


def params(**kw):
    return pltpu.CompilerParams(vmem_limit_bytes=VMEM_LIMIT, **kw)


TIMES = {
    ("down_grads", 0): 10.0,
    ("dense_terms", 0): 13.1,
    ("fold", 2): 2.0,
}


TURNS = {}


def estimate(name):
    turn = TURNS.get(name, 0)
    TURNS[name] = turn + 1
    time = TIMES.get((name, turn), 0.1)
    return pl.CostEstimate(flops=int(time * 1.15e9), bytes_accessed=100000, transcendentals=0)


def call(kernel, args, in_specs, **kw):
    return pl.pallas_call(kernel, in_specs=list(in_specs), compiler_params=params(), **kw)(*args)


def whole_specs(args):
    return [const_spec(a.shape) for a in args]


def const_spec(shape):
    return pl.BlockSpec(shape, lambda *_: (0,) * len(shape))


def selector(code_row, rows):
    place = lax.broadcasted_iota(jnp.int32, (rows, code_row.shape[1]), 0)
    return jnp.where(place == code_row, 1.0, 0.0).astype(BF)


def selector_t(code_column, rows):
    place = lax.broadcasted_iota(jnp.int32, (code_column.shape[0], rows), 1)
    return jnp.where(place == code_column, 1.0, 0.0).astype(BF)


def band_of(row):
    return pltpu.roll(jnp.broadcast_to(row, (LANES, BAND)), 0, 1, stride=1, stride_axis=0)


def diagonal_sums(skewed):
    eight = skewed[0:8]
    for start in range(8, LANES, 8):
        eight = eight + pltpu.roll(skewed[start : start + 8], BAND - start, 1)
    total = eight[0:1]
    for row in range(1, 8):
        total = total + pltpu.roll(eight[row : row + 1], BAND - row, 1)
    return total


def bias_block(band, row, first, count, k_blocks):
    far = [jnp.broadcast_to(row[:, at : at + 1], (LANES, LANES)) for at in (FAR_BEFORE, FAR_AFTER)]
    columns = []
    for q_block in range(first, first + count):
        pieces = []
        for k_block in range(k_blocks):
            d = k_block - q_block
            pieces.append(far[1] if d > 1 else far[0] if d < -1 else band[:, LANES * (1 - d) : LANES * (2 - d)])
        columns.append(jnp.concatenate(pieces, axis=0))
    return jnp.concatenate(columns, axis=1)


def only_rows(value, h, head_dim):
    mine = value[h * head_dim : (h + 1) * head_dim]
    none = jnp.zeros_like(mine)
    return jnp.concatenate([mine, none] if h % 2 == 0 else [none, mine], axis=0)


def attend(scaled, keys, values, woff_ref, mask, first, head_dim):
    count = scaled.shape[0] // LANES
    q_t, v_t = scaled.T, values.T
    heads_t, totals = [], []
    for h in range(HEAD_GROUP):
        row = woff_ref[0, h : h + 1, :]
        bias = bias_block(band_of(row), row, first, count, keys.shape[0] // LANES)
        k_pair = keys[:, LANES * (h // 2) : LANES * (h // 2 + 1)]
        s = dot(k_pair, only_rows(q_t, h, head_dim)) + bias + mask
        peak = jnp.max(s, axis=0, keepdims=True)
        p = jnp.exp(s - peak)
        total = jnp.sum(p, axis=0, keepdims=True)
        heads_t.append(dot(v_t[h * head_dim : (h + 1) * head_dim], p.astype(BF)) * (1.0 / total))
        totals.append(peak + jnp.log(total))
    return jnp.concatenate(heads_t, axis=0).T.astype(BF), jnp.concatenate(totals, axis=0)


def slot_codes(routes):
    chosen = routes.astype(F32)
    tokens = chosen.shape[1]
    numbers = lax.broadcasted_iota(jnp.int32, (TAIL // 2, tokens), 0).astype(F32)
    named = jnp.logical_or(numbers == chosen[0:1], numbers == chosen[1:2])
    row = lax.broadcasted_iota(jnp.int32, (tokens, tokens), 0)
    lane = lax.broadcasted_iota(jnp.int32, (tokens, tokens), 1)
    before = jnp.where(row < lane, 1.0, 0.0).astype(BF)
    return jnp.where(named, dot(jnp.where(named, 1.0, 0.0).astype(BF), before), -1.0)


def packed_codes(codes):
    upper = jnp.floor((codes + 1.0) * (1.0 / 16.0))
    return jnp.concatenate([upper, codes + 1.0 - 16.0 * upper], axis=0)


def own_code(me, packed):
    row = lax.broadcasted_iota(jnp.int32, packed.shape, 0)
    weight = jnp.where(row == me, 16.0, jnp.where(row == me + TAIL // 2, 1.0, 0.0))
    return (jnp.sum(packed.astype(F32) * weight, axis=0, keepdims=True) - 1.0).astype(jnp.int32)


def route_rows(mid, gain_ref, wr_ref, experts, nm_ref, ch_ref, payload_ref, codes=None):
    rows = mid.shape[0]
    nm = (mid * rms_scale(mid) * gain_ref[...]).astype(BF)
    nm_ref[...] = nm
    router = jnp.concatenate([wr_ref[...], jnp.zeros((TAIL - experts, nm.shape[1]), BF)], axis=0)
    logits = dot_nt(router, nm)
    live = lax.broadcasted_iota(jnp.int32, logits.shape, 0) < experts
    logits = jnp.where(live, logits, FAR)
    raised = jnp.exp(logits - jnp.max(logits, axis=0, keepdims=True))
    chances = raised / jnp.sum(raised, axis=0, keepdims=True)
    ch_ref[...] = chances
    hi = chances.astype(BF).astype(F32)
    both = jnp.concatenate([hi[: TAIL // 2], (chances - hi)[: TAIL // 2]], axis=0)
    payload_ref[0:rows, :] = nm
    tail = [both] if codes is None else [both, packed_codes(codes)]
    used = sum(v.shape[1] for v in tail)
    tail.append(jnp.zeros((TAIL, nm.shape[1] - used), F32))
    payload_ref[rows:, :] = jnp.concatenate(tail, axis=1).astype(BF)


def segment_mask(seg_ref, first, count):
    seg = seg_ref[...].astype(F32)
    column = jnp.broadcast_to(seg, (8, seg.shape[1])).T[:, 0:1]
    return jnp.where(column == seg[:, first : first + count], 0.0, FAR)


def attn_first_kernel(
    tok_ref, gain_a_ref, wq_ref, wk_ref, wv_ref, wo_ref, bias_ref, onehot_ref, seg_ref, gain_m_ref, wr_ref, routes_ref,
    qs_ref, k_ref, v_ref, woff_ref, token_ref, code_ref, att_ref, lse_ref, mid_ref, nm_ref, ch_ref, payload_ref,
    n_scr, mask_scr, woff_scr, code_scr,
    *, experts, head_dim,
):
    step = pl.program_id(0)
    rows = att_ref.shape[0]

    @pl.when(step == 0)
    def _():
        start = tok_ref[...].astype(F32)
        n_scr[...] = (start * rms_scale(start) * gain_a_ref[...]).astype(BF)
        mid_ref[...] = start[:rows]
        mask_scr[...] = segment_mask(seg_ref, 0, rows)
        token_ref[...] = jnp.where(seg_ref[:, 0:LANES] < 0, 1.0, 0.0)
        codes = slot_codes(routes_ref[...])
        code_scr[...] = codes
        code_ref[...] = codes[:experts].astype(jnp.int32)
        table = onehot_ref[...]
        offsets = sum(dot(part, table) for part in split3(bias_ref[...]))
        for g in range(woff_scr.shape[0]):
            woff_scr[g] = offsets[g * HEAD_GROUP : (g + 1) * HEAD_GROUP]

    woff_ref[0] = woff_scr[step]

    normed = n_scr[...]
    scaled = (dot(normed, wq_ref[...]).astype(BF).astype(F32) * head_dim ** (-0.5)).astype(BF)
    keys = dot(normed, wk_ref[...]).astype(BF)
    values = dot(normed, wv_ref[...]).astype(BF)
    qs_ref[...] = scaled
    k_ref[...] = keys
    v_ref[...] = values
    att, totals = attend(scaled[:rows], keys, values, woff_ref, mask_scr[...], 0, head_dim)
    att_ref[...] = att
    lse_ref[0] = totals
    mid_ref[...] += dot(att, wo_ref[...])

    @pl.when(step == pl.num_programs(0) - 1)
    def _():
        route_rows(mid_ref[...], gain_m_ref, wr_ref, experts, nm_ref, ch_ref, payload_ref, code_scr[...])


def attn_second_kernel(
    tok_ref, qs_ref, k_ref, v_ref, wo_ref, woff_ref, seg_ref, gain_m_ref, wr_ref, *refs, experts, head_dim
):
    att_ref, lse_ref, mid_ref, nm_ref, ch_ref, payload_ref, mask_scr = refs[-7:]
    step = pl.program_id(0)
    rows = att_ref.shape[0]

    @pl.when(step == 0)
    def _():
        mid_ref[...] = tok_ref[...].astype(F32)
        mask_scr[...] = segment_mask(seg_ref, rows, rows)

    att, totals = attend(qs_ref[...], k_ref[...], v_ref[...], woff_ref, mask_scr[...], rows // LANES, head_dim)
    att_ref[...] = att
    lse_ref[0] = totals
    mid_ref[...] += dot(att, wo_ref[...])

    @pl.when(step == pl.num_programs(0) - 1)
    def _():
        route_rows(mid_ref[...], gain_m_ref, wr_ref, experts, nm_ref, ch_ref, payload_ref)


def attn_halves(rows, width, groups, half):
    cols, part = width // groups, rows // 2
    wide = jax.ShapeDtypeStruct((rows, width), BF)
    shapes = [
        wide,
        jax.ShapeDtypeStruct((groups, HEAD_GROUP, rows), F32),
        jax.ShapeDtypeStruct((rows, width), F32),
        wide,
        jax.ShapeDtypeStruct((TAIL, rows), F32),
        jax.ShapeDtypeStruct((part + TAIL, width), BF),
    ]
    specs = [
        pl.BlockSpec((part, cols), lambda g: (half, g)),
        pl.BlockSpec((1, HEAD_GROUP, part), lambda g: (g, 0, half)),
        pl.BlockSpec((part, width), lambda g: (half, 0)),
        pl.BlockSpec((part, width), lambda g: (half, 0)),
        pl.BlockSpec((TAIL, part), lambda g: (0, half)),
        const_spec((part + TAIL, width)),
    ]
    return shapes, specs


def attn_first(tokens, gain_attn, w_query, w_key, w_value, w_out, rel_bias, seg, gain_moe, w_router, routes):
    rows, width = tokens.shape
    heads, buckets = rel_bias.shape
    experts = w_router.shape[0]
    groups = heads // HEAD_GROUP
    cols, part = width // groups, rows // 2
    weight_block = pl.BlockSpec((width, cols), lambda g: (0, g))
    shapes, specs = attn_halves(rows, width, groups, 0)
    wide = jax.ShapeDtypeStruct((rows, width), BF)
    return call(
        functools.partial(attn_first_kernel, experts=experts, head_dim=cols // HEAD_GROUP),
        (tokens, gain_attn[None], w_query, w_key, w_value, w_out, rel_bias, jnp.asarray(band_onehot(rows, buckets)).astype(BF),
         seg, gain_moe[None], w_router, routes),
        [
            const_spec((rows, width)),
            const_spec((1, width)),
            weight_block,
            weight_block,
            weight_block,
            pl.BlockSpec((cols, width), lambda g: (g, 0)),
            const_spec(rel_bias.shape),
            const_spec((buckets, BAND)),
            const_spec(seg.shape),
            const_spec((1, width)),
            const_spec(w_router.shape),
            const_spec(routes.shape),
        ],
        grid=(groups,),
        out_specs=[pl.BlockSpec((rows, cols), lambda g: (0, g))] * 3
        + [pl.BlockSpec((1, HEAD_GROUP, BAND), lambda g: (g, 0, 0)), const_spec((1, LANES)), const_spec((experts, rows))]
        + specs,
        out_shape=[wide] * 3
        + [jax.ShapeDtypeStruct((groups, HEAD_GROUP, BAND), F32), jax.ShapeDtypeStruct((1, LANES), F32)]
        + [jax.ShapeDtypeStruct((experts, rows), jnp.int32)]
        + shapes,
        scratch_shapes=[
            pltpu.VMEM((rows, width), BF),
            pltpu.VMEM((rows, part), F32),
            pltpu.VMEM((groups, HEAD_GROUP, BAND), F32),
            pltpu.VMEM((TAIL // 2, rows), F32),
        ],
        cost_estimate=estimate("attn_first"),
        name="attn_first",
    )


def attn_second(tokens, scaled, keys, values, w_out, woff, seg, gain_moe, w_router, filled):
    rows, width = tokens.shape
    experts = w_router.shape[0]
    groups = woff.shape[0]
    cols, part = width // groups, rows // 2
    col_block = pl.BlockSpec((rows, cols), lambda g: (0, g))
    shapes, specs = attn_halves(rows, width, groups, 1)
    args = (tokens, scaled, keys, values, w_out, woff, seg, gain_moe[None], w_router)
    return call(
        functools.partial(attn_second_kernel, experts=experts, head_dim=cols // HEAD_GROUP),
        (*args, *filled),
        [
            pl.BlockSpec((part, width), lambda g: (1, 0)),
            pl.BlockSpec((part, cols), lambda g: (1, g)),
            col_block,
            col_block,
            pl.BlockSpec((cols, width), lambda g: (g, 0)),
            pl.BlockSpec((1, HEAD_GROUP, BAND), lambda g: (g, 0, 0)),
            const_spec(seg.shape),
            const_spec((1, width)),
            const_spec(w_router.shape),
        ]
        + [pl.BlockSpec(memory_space=pl.ANY)] * len(filled),
        grid=(groups,),
        out_specs=specs,
        out_shape=shapes,
        scratch_shapes=[pltpu.VMEM((rows, part), F32)],
        input_output_aliases={len(args) + i: i for i in range(len(filled))},
        cost_estimate=estimate("attn_second"),
        name="attn_second",
    )


def gelu_parts(gate):
    c0 = np.float32(np.sqrt(2.0 / np.pi))
    c1 = np.float32(0.044715)
    square = gate * gate
    t = jnp.tanh(c0 * gate * (1.0 + c1 * square))
    half = 0.5 * (1.0 + t)
    value = gate * half
    slope = half + 0.5 * gate * (1.0 - t * t) * (c0 * (1.0 + 3.0 * c1 * square))
    return value, slope


FF_BLOCK = 256


def cot_hidden_kernel(me_ref, *refs, experts):
    tail_refs, cot_refs, wd_ref = refs[:experts], refs[experts : 2 * experts], refs[2 * experts]
    out_ref, rows_ref = refs[2 * experts + 1 :]

    @pl.when(pl.program_id(0) == 0)
    def _():
        cap = rows_ref.shape[0] // experts
        tokens = cot_refs[0].shape[0]
        for m, (tail_ref, cot_ref) in enumerate(zip(tail_refs, cot_refs)):
            code = own_code(me_ref[0], tail_ref[:, tokens // 2 : tokens // 2 + tokens])
            rows_ref[m * cap : (m + 1) * cap, :] = dot(selector(code, cap), cot_ref[...]).astype(BF)

    out_ref[...] = dot_nt(rows_ref[...], wd_ref[0]).astype(BF)


def cot_hidden(me, payloads, cots, w_down, cap, count):
    experts = len(cots)
    width = cots[0].shape[1]
    rows = experts * cap
    last = payloads[0].shape[0] // TAIL - 1
    return call(
        functools.partial(cot_hidden_kernel, experts=experts),
        (me, *payloads, *cots, w_down),
        [pl.BlockSpec(memory_space=pltpu.SMEM)]
        + [pl.BlockSpec((TAIL, width), lambda f: (last, 0))] * experts
        + whole_specs(cots)
        + [pl.BlockSpec((1, FF_BLOCK, width), lambda f: (0, f, 0))],
        grid=(count,),
        out_specs=[pl.BlockSpec((rows, FF_BLOCK), lambda f: (0, f)), const_spec((rows, width))],
        out_shape=[jax.ShapeDtypeStruct((rows, count * FF_BLOCK), BF), jax.ShapeDtypeStruct((rows, width), BF)],
        cost_estimate=estimate("cot_hidden"),
        name="cot_hidden",
    )


def cot_hidden_more_kernel(rows_ref, wd_ref, out_ref):
    out_ref[...] = dot_nt(rows_ref[...], wd_ref[0]).astype(BF)


def cot_hidden_more(cot_rows, w_down, first):
    rows, width = cot_rows.shape
    count = w_down.shape[1] // FF_BLOCK - first
    return call(
        cot_hidden_more_kernel,
        (cot_rows, w_down),
        [const_spec((rows, width)), pl.BlockSpec((1, FF_BLOCK, width), lambda f: (0, first + f, 0))],
        grid=(count,),
        out_specs=pl.BlockSpec((rows, FF_BLOCK), lambda f: (0, f)),
        out_shape=jax.ShapeDtypeStruct((rows, count * FF_BLOCK), BF),
        cost_estimate=estimate("cot_hidden_more"),
        name="cot_hidden_more",
    )


ROW_BLOCK = 320


def expert_first(me_ref, place_ref, payloads, cot_ref, x_ref, xt_ref, gate_ref, gc_ref):
    experts = len(payloads) // 2
    cap = x_ref.shape[0] // experts
    part = payloads[0].shape[0] - TAIL
    row = lax.broadcasted_iota(jnp.int32, (TAIL, part), 0)
    mine = jnp.logical_or(row == me_ref[0], row == me_ref[0] + TAIL // 2)
    for m in range(experts):
        code = own_code(me_ref[0], payloads[2 * m][part:, part : 3 * part])
        chosen = selector(code, cap)
        place = slice(m * cap, (m + 1) * cap)
        total = jnp.zeros((cap, x_ref.shape[1]), F32)
        gate = jnp.zeros((cap, 1), F32)
        for i in range(2):
            payload = payloads[2 * m + i]
            part_chosen = chosen[:, i * part : (i + 1) * part]
            total = total + dot(part_chosen, payload[0:part, :])
            chances = jnp.sum(jnp.where(mine, payload[part:, 0:part].astype(F32), 0.0), axis=0, keepdims=True)
            gate = gate + jnp.sum(part_chosen.astype(F32) * chances, axis=1, keepdims=True)
        x_ref[place, :] = total.astype(BF)
        gate_ref[place, :] = jnp.broadcast_to(gate, (cap, LANES))
        gc_ref[place, :] = (cot_ref[place, :].astype(F32) * gate).astype(BF)
    flipped = x_ref[...].T
    owners = place_ref.shape[0]
    rows = flipped.shape[0] // owners
    for b in range(owners):
        at = pl.multiple_of(place_ref[b] * rows, rows)
        xt_ref[pl.ds(at, rows), :] = flipped[b * rows : (b + 1) * rows]


def expert_a_kernel(*refs, experts):
    step = pl.program_id(0)
    if experts:
        me_ref, place_ref = refs[:2]
        payloads = refs[2 : 2 + 2 * experts]
        cot_ref, gh_ref, wg_ref, wu_ref, x_ref, xt_ref, gate_ref, gc_ref = refs[2 + 2 * experts : 10 + 2 * experts]

        @pl.when(step == 0)
        def _():
            expert_first(me_ref, place_ref, payloads, cot_ref, x_ref, xt_ref, gate_ref, gc_ref)

    else:
        x_ref, xt_ref, gate_ref, gh_ref, wg_ref, wu_ref = refs[:6]
    gate_keep_ref, gate_send_ref, up_keep_ref, up_send_ref, sc_ref, hid_ref, hidt_ref, gg_ref, gu_ref = refs[-9:]

    @pl.when(step == 0)
    def _():
        sc_ref[...] = jnp.zeros_like(sc_ref)

    wg, wu = wg_ref[0], wu_ref[0]
    width = wg.shape[1]
    for start in range(0, x_ref.shape[0], ROW_BLOCK):
        part = slice(start, start + ROW_BLOCK)
        x = x_ref[part, :]
        gate_pre = dot(x, wg)
        up_pre = dot(x, wu)
        grad = gh_ref[part, :].astype(F32)
        act, slope = gelu_parts(gate_pre)
        hidden = act * up_pre
        hid_ref[part, :] = hidden.astype(BF)
        product = hidden * grad
        folded = product[:, 0:LANES]
        for i in range(1, width // LANES):
            folded = folded + product[:, i * LANES : (i + 1) * LANES]
        sc_ref[part, :] += folded
        grad = grad * gate_ref[part, 0:1]
        gg_ref[part, :] = (slope * up_pre * grad).astype(BF)
        gu_ref[part, :] = (act * grad).astype(BF)
    hidt_ref[...] = hid_ref[...].T
    xt = xt_ref[...]
    cut = xt.shape[0] // 4
    for grad_ref, keep_ref, send_ref, second in ((gg_ref, gate_keep_ref, gate_send_ref, 1), (gu_ref, up_keep_ref, up_send_ref, 0)):
        term = dot(xt, grad_ref[...]).astype(BF)
        for q in range(4):
            upper, lower = (q % 2, q // 2) if second else (q // 2, q % 2)
            (send_ref if upper else keep_ref)[lower * cut : (lower + 1) * cut] = term[q * cut : (q + 1) * cut]


def expert_a(source, gh, gh_first, w_gate, w_up, first, count, filled=()):
    opening = 0 if filled else len(source[2]) // 2
    rows = gh.shape[0]
    width, ff = w_gate.shape[1:]
    span = count * FF_BLOCK
    col_weight = pl.BlockSpec((1, width, FF_BLOCK), lambda f: (0, 0, first + f))
    out_block = pl.BlockSpec((rows, FF_BLOCK), lambda f: (0, first + f))
    wide = jax.ShapeDtypeStruct((rows, ff), BF)
    tall = jax.ShapeDtypeStruct((ff, rows), BF)
    term = jax.ShapeDtypeStruct((width // 2, span), BF)
    term_block = pl.BlockSpec((width // 2, FF_BLOCK), lambda f: (0, f))
    if opening:
        me, place, payloads, cot_rows = source
        args = (me, place, *payloads, cot_rows)
        specs = [pl.BlockSpec(memory_space=pltpu.SMEM)] * 2 + whole_specs((*payloads, cot_rows))
        shared = [
            jax.ShapeDtypeStruct((rows, width), BF),
            jax.ShapeDtypeStruct((width, rows), BF),
            jax.ShapeDtypeStruct((rows, LANES), F32),
            jax.ShapeDtypeStruct((rows, width), BF),
        ]
    else:
        args = tuple(source)
        specs = whole_specs(source)
        shared = []
    args = (*args, gh, w_gate, w_up)
    used = len(args)
    first_filled = len(shared) + 5

    def run(*refs):
        expert_a_kernel(*refs[:used], *refs[used + len(filled) :], experts=opening)

    return call(
        run,
        (*args, *filled),
        specs
        + [pl.BlockSpec((rows, FF_BLOCK), lambda f: (0, first - gh_first + f)), col_weight, col_weight]
        + [pl.BlockSpec(memory_space=pl.ANY)] * len(filled),
        grid=(count,),
        out_specs=whole_specs(shared)
        + [term_block] * 4
        + [const_spec((rows, LANES)), out_block]
        + [pl.BlockSpec((FF_BLOCK, rows), lambda f: (first + f, 0)), out_block, out_block],
        out_shape=shared + [term] * 4 + [jax.ShapeDtypeStruct((rows, LANES), F32), wide, tall, wide, wide],
        input_output_aliases={used + i: first_filled + i for i in range(len(filled))},
        cost_estimate=estimate("expert_grads"),
        name="expert_grads",
    )


def expert_b_kernel(gg_ref, gu_ref, *refs, cap, experts):
    sc_refs, (wg_ref, wu_ref, *outs, acc) = refs[:-5], refs[-5:]
    part_sum = dot_nt(gg_ref[...], wg_ref[0]) + dot_nt(gu_ref[...], wu_ref[0])
    step, block = pl.program_id(0), pl.program_id(1)

    @pl.when(step == 0)
    def _():
        acc[block] = part_sum

    def finish(out_ref):
        total = acc[block] + part_sum
        row = lax.broadcasted_iota(jnp.int32, (cap, cap), 0)
        lane = lax.broadcasted_iota(jnp.int32, (cap, cap), 1)
        place = lax.broadcasted_iota(jnp.int32, (TAIL, cap), 0)
        out_ref[0:cap, :] = total.astype(BF)
        folded = sc_refs[0][...]
        for other in sc_refs[1:]:
            folded = folded + other[...]
        column = jnp.sum(folded, axis=1, keepdims=True)
        flat = jnp.sum(jnp.where(row == lane, column, 0.0), axis=0, keepdims=True)
        hi, mid, low = split3(flat)
        packed = jnp.where(
            place == 0, hi.astype(F32), jnp.where(place == 1, mid.astype(F32), jnp.where(place == 2, low.astype(F32), 0.0))
        )
        out_ref[cap : cap + TAIL, :] = jnp.zeros((TAIL, total.shape[1]), BF)
        out_ref[cap : cap + TAIL, 0:cap] = packed.astype(BF)

    last = step == pl.num_programs(0) - 1
    for m in range(experts):

        @pl.when(jnp.logical_and(last, block == m))
        def _(m=m):
            finish(outs[m // (experts // 2)].at[m % (experts // 2)])


def expert_b(gg, gu, scs, w_gate, w_up, experts):
    rows, ff = gg.shape
    width = w_gate.shape[1]
    cap = rows // experts
    cut = ff // 2
    grads = pl.BlockSpec((cap, cut), lambda k, m: (m, k))
    sums = pl.BlockSpec((cap, LANES), lambda k, m: (m, 0))
    weight = pl.BlockSpec((1, width, cut), lambda k, m: (0, 0, k))
    return call(
        functools.partial(expert_b_kernel, cap=cap, experts=experts),
        (gg, gu, *scs, w_gate, w_up),
        [grads, grads] + [sums] * len(scs) + [weight, weight],
        grid=(2, experts),
        out_specs=[const_spec((experts // 2, cap + TAIL, width))] * 2,
        out_shape=[jax.ShapeDtypeStruct((experts // 2, cap + TAIL, width), BF)] * 2,
        scratch_shapes=[pltpu.VMEM((experts, cap, width), F32)],
        cost_estimate=estimate("expert_input_grad"),
        name="expert_input_grad",
    )


def down_kernel(place_a_ref, place_b_ref, hidt_ref, gc_ref, *outs):
    owners = place_a_ref.shape[0]
    shard = 2 * outs[0].shape[0] // owners
    size = int(np.gcd(shard, 32))
    rows = hidt_ref.shape[0]
    step = pl.program_id(0)
    total = dot(hidt_ref[...], gc_ref[...]).astype(BF)
    half = total.shape[1] // 2
    for i in range(rows // size):
        row = step * rows + i * size
        owner = row // shard
        piece = total[i * size : (i + 1) * size]
        for keep_ref, send_ref, place_ref, cols in (
            (outs[0], outs[1], place_a_ref, piece[:, :half]),
            (outs[2], outs[3], place_b_ref, piece[:, half:]),
        ):
            place = place_ref[owner]
            at = pl.multiple_of((place % (owners // 2)) * shard + (row - owner * shard), size)

            @pl.when(place < owners // 2)
            def _(keep_ref=keep_ref, at=at, cols=cols):
                keep_ref[pl.ds(at, size), :] = cols

            @pl.when(place >= owners // 2)
            def _(send_ref=send_ref, at=at, cols=cols):
                send_ref[pl.ds(at, size), :] = cols


def down_grads(hid_t, grad_cots, place_a, place_b):
    rows, width = grad_cots.shape
    ff = hid_t.shape[0]
    table = pl.BlockSpec(memory_space=pltpu.SMEM)
    part = jax.ShapeDtypeStruct((ff // 2, width // 2), BF)
    return call(
        down_kernel,
        (place_a, place_b, hid_t, grad_cots),
        [table, table, pl.BlockSpec((ff // 4, rows), lambda f: (f, 0)), const_spec((rows, width))],
        grid=(4,),
        out_specs=[const_spec(part.shape)] * 4,
        out_shape=[part] * 4,
        cost_estimate=estimate("down_grads"),
        name="down_grads",
    )


def produced_kernel(hid_ref, wd_ref, low_ref, high_ref):
    rows = dot(hid_ref[...], wd_ref[0]).astype(BF)
    lower = pl.program_id(0) < pl.num_programs(0) // 2

    @pl.when(lower)
    def _():
        low_ref[0] = rows

    @pl.when(jnp.logical_not(lower))
    def _():
        high_ref[0] = rows


def produced_rows(hid, w_down, experts):
    rows, ff = hid.shape
    width = w_down.shape[2]
    cap, half = rows // experts, experts // 2
    return call(
        produced_kernel,
        (hid, w_down),
        [pl.BlockSpec((cap, ff), lambda m: (m, 0)), const_spec(w_down.shape)],
        grid=(experts,),
        out_specs=[
            pl.BlockSpec((1, cap, width), lambda m: (jnp.minimum(m, half - 1), 0, 0)),
            pl.BlockSpec((1, cap, width), lambda m: (jnp.maximum(m - half, 0), 0, 0)),
        ],
        out_shape=[jax.ShapeDtypeStruct((half, cap, width), BF)] * 2,
        cost_estimate=estimate("produced_rows"),
        name="produced_rows",
    )


def distinct(slots):
    arrays, found = [], []
    for array, index in slots:
        which = next((i for i, other in enumerate(arrays) if other is array), None)
        if which is None:
            which = len(arrays)
            arrays.append(array)
        found.append((which, index))
    return arrays, found


def layer_out_kernel(mid_ref, ch_ref, code_ref, *refs, slots):
    parts, out_ref = refs[:-1], refs[-1]
    cap = parts[0].shape[1]
    total = mid_ref[...]
    chances = ch_ref[...].T
    for m, (which, index) in enumerate(slots):
        picked = dot(selector_t(code_ref[:, m : m + 1], cap), parts[which][index])
        total = total + chances[:, m : m + 1] * picked
    out_ref[...] = total.astype(BF)


def layer_output(middle, chances, code_t, slots):
    rows, width = middle.shape
    arrays, found = distinct(slots)
    args = (middle, chances, code_t, *arrays)
    return call(
        functools.partial(layer_out_kernel, slots=found),
        args,
        [pl.BlockSpec(memory_space=pltpu.VMEM)] * len(args),
        out_shape=jax.ShapeDtypeStruct((rows, width), BF),
        cost_estimate=estimate("layer_output"),
        name="layer_output",
    )


def moe_bwd_kernel(
    cot_ref, mid_ref, gain_ref, nm_ref, ch_ref, wr_ref, code_ref, codet_ref, wo_ref, *refs, slots
):
    backs, (gmid_ref, branch_ref, ga_ref, gain_o_ref, router_o_ref) = refs[:-5], refs[-5:]
    experts, cap = len(slots), backs[0].shape[1] - TAIL
    rows = cot_ref.shape[0]
    grad = jnp.zeros(mid_ref.shape, F32)
    gate_rows = []
    for m, (which, index) in enumerate(slots):
        grad = grad + dot(selector_t(codet_ref[:, m : m + 1], cap), backs[which][index, 0:cap, :])
        picked = dot(backs[which][index, cap : cap + TAIL, 0:cap], selector(code_ref[m : m + 1, :], cap))
        gate_rows.append(jnp.sum(picked, axis=0, keepdims=True))
    gate_rows.append(jnp.zeros((TAIL - experts, rows), F32))
    grad_chances = jnp.concatenate(gate_rows, axis=0)
    chances = ch_ref[...]
    grad_logits = chances * (grad_chances - jnp.sum(chances * grad_chances, axis=0, keepdims=True))
    pieces = jnp.concatenate(split3(grad_logits), axis=0)
    wr = wr_ref[...]
    grad = grad + dot_tn(pieces, jnp.concatenate([wr, wr, wr], axis=0))
    router = dot(pieces, nm_ref[...])
    router_o_ref[...] = router[0:TAIL] + router[TAIL : 2 * TAIL] + router[2 * TAIL : 3 * TAIL]
    mid = mid_ref[...]
    scale = rms_scale(mid)
    unit = mid * scale
    gain_o_ref[...] = jnp.sum(grad * unit, axis=0, keepdims=True)
    scaled = grad * gain_ref[...]
    grad_mid = cot_ref[...].astype(F32) + scale * (scaled - unit * jnp.mean(scaled * unit, axis=-1, keepdims=True))
    gmid_ref[...] = grad_mid
    branch = grad_mid.astype(BF)
    branch_ref[...] = branch
    ga_ref[...] = dot_nt(branch, wo_ref[...]).astype(BF)


def sort_rows(place_ref, value, out_ref):
    owners = place_ref.shape[0]
    rows = value.shape[0] // owners
    for b in range(owners):
        out_ref[pl.ds(pl.multiple_of(place_ref[b] * rows, rows), rows), :] = value[b * rows : (b + 1) * rows]


def moe_bwd(cot, middle, gain_moe, normed_moe, chances, wr_t, code, code_t, w_out, slots):
    rows, width = cot.shape
    arrays, found = distinct(slots)
    args = (cot, middle, gain_moe[None], normed_moe, chances, wr_t, code, code_t, w_out, *arrays)
    wide = jax.ShapeDtypeStruct((rows, width), BF)
    return call(
        functools.partial(moe_bwd_kernel, slots=found),
        args,
        [pl.BlockSpec(memory_space=pltpu.VMEM)] * len(args),
        out_shape=[
            jax.ShapeDtypeStruct((rows, width), F32),
            wide,
            wide,
            jax.ShapeDtypeStruct((1, width), F32),
            jax.ShapeDtypeStruct((TAIL, width), F32),
        ],
        cost_estimate=estimate("moe_bwd"),
        name="moe_bwd",
    )


def attn_bwd_kernel(
    qs_ref, k_ref, v_ref, ga_ref, lse_ref, woff_ref, seg_ref,
    dq_ref, dk_ref, dv_ref, dwoff_ref, mask_scr, p_scr, ds_scr,
    *, head_dim,
):
    rows = qs_ref.shape[0]
    blocks = rows // LANES

    @pl.when(pl.program_id(0) == 0)
    def _():
        mask_scr[...] = segment_mask(seg_ref, 0, rows)

    scaled, keys, values, grads = qs_ref[...], k_ref[...], v_ref[...], ga_ref[...]
    q_t, g_t, k_t = scaled.T, grads.T, keys.T
    low_half = lax.broadcasted_iota(jnp.int32, (rows, LANES), 1) < head_dim
    dq_t, dk_parts, dv_parts = [], [], []
    lane = lax.broadcasted_iota(jnp.int32, (1, BAND), 1)
    for h in range(HEAD_GROUP):
        row = woff_ref[0, h : h + 1, :]
        band = band_of(row)
        pair = slice(LANES * (h // 2), LANES * (h // 2 + 1))
        k_pair, v_pair = keys[:, pair], values[:, pair]
        q_only, g_only = only_rows(q_t, h, head_dim), only_rows(g_t, h, head_dim)
        tiles = {}
        for b in range(0, blocks, 2):
            lanes = slice(b * LANES, (b + 2) * LANES)
            s = dot(k_pair, q_only[:, lanes]) + bias_block(band, row, b, 2, blocks) + mask_scr[:, lanes]
            p = jnp.exp(s - lse_ref[0, h : h + 1, lanes])
            dp = dot(v_pair, g_only[:, lanes])
            ds = p * (dp - jnp.sum(p * dp, axis=0, keepdims=True))
            p_scr[:, lanes] = p.astype(BF)
            ds_scr[:, lanes] = ds.astype(BF)
            for q_block in range(2):
                for k_block in range(blocks):
                    d = max(-2, min(2, k_block - b - q_block))
                    tile = ds[k_block * LANES : (k_block + 1) * LANES, q_block * LANES : (q_block + 1) * LANES]
                    tiles[d] = tiles[d] + tile if d in tiles else tile
        skewed = jnp.concatenate([tiles[1], tiles[0], tiles[-1], jnp.zeros_like(tiles[0])], axis=1)
        offsets = diagonal_sums(skewed)
        offsets = offsets + jnp.where(lane == FAR_AFTER, jnp.sum(tiles[2]), 0.0)
        offsets = offsets + jnp.where(lane == FAR_BEFORE, jnp.sum(tiles[-2]), 0.0)
        dwoff_ref[0, h : h + 1, :] = offsets
        p_all, ds_all = p_scr[...], ds_scr[...]
        dv_parts.append(dot(p_all, grads[:, pair]))
        dk_parts.append(dot(ds_all, scaled[:, pair]))
        dq_t.append(dot(k_t[h * head_dim : (h + 1) * head_dim], ds_all))
    dq = jnp.concatenate(dq_t, axis=0).T * head_dim ** (-0.5)
    dq_ref[...] = dq.astype(BF)
    for i in range(HEAD_GROUP // 2):
        pair = slice(LANES * i, LANES * (i + 1))
        dk_ref[:, pair] = jnp.where(low_half, dk_parts[2 * i], dk_parts[2 * i + 1]).astype(BF)
        dv_ref[:, pair] = jnp.where(low_half, dv_parts[2 * i], dv_parts[2 * i + 1]).astype(BF)


def attn_bwd(scaled, keys, values, grad_att, lse, woff, seg):
    rows, width = scaled.shape
    groups = woff.shape[0]
    cols = width // groups
    col_block = pl.BlockSpec((rows, cols), lambda g: (0, g))
    wide = jax.ShapeDtypeStruct((rows, width), BF)
    return call(
        functools.partial(attn_bwd_kernel, head_dim=cols // HEAD_GROUP),
        (scaled, keys, values, grad_att, lse, woff, seg),
        [
            col_block,
            col_block,
            col_block,
            col_block,
            pl.BlockSpec((1, HEAD_GROUP, rows), lambda g: (g, 0, 0)),
            pl.BlockSpec((1, HEAD_GROUP, BAND), lambda g: (g, 0, 0)),
            const_spec(seg.shape),
        ],
        grid=(groups,),
        out_specs=[col_block, col_block, col_block, pl.BlockSpec((1, HEAD_GROUP, BAND), lambda g: (g, 0, 0))],
        out_shape=[wide, wide, wide, jax.ShapeDtypeStruct((groups, HEAD_GROUP, BAND), F32)],
        scratch_shapes=[
            pltpu.VMEM((rows, rows), F32),
            pltpu.VMEM((rows, rows), BF),
            pltpu.VMEM((rows, rows), BF),
        ],
        cost_estimate=estimate("attn_bwd"),
        name="attn_bwd",
    )


def sorted_rows_kernel(pq_ref, pk_ref, tok_ref, gain_ref, att_ref, att_o_ref, out_ref, sort_scr):
    start = tok_ref[...].astype(F32)
    normed_t = (start * rms_scale(start) * gain_ref[...]).T
    attended_t = att_ref[...].astype(F32).T
    sort_rows(pq_ref, attended_t, sort_scr)
    att_o_ref[...] = sort_scr[...].astype(BF)
    for i, place_ref in enumerate((pq_ref, pk_ref)):
        sort_rows(place_ref, normed_t, sort_scr)
        out_ref[i] = sort_scr[...].astype(BF)


def sorted_rows(place_q, place_k, tokens, gain_attn, attended):
    rows, width = tokens.shape
    return call(
        sorted_rows_kernel,
        (place_q, place_k, tokens, gain_attn[None], attended),
        [pl.BlockSpec(memory_space=pltpu.SMEM)] * 2 + [pl.BlockSpec(memory_space=pltpu.VMEM)] * 3,
        out_shape=[jax.ShapeDtypeStruct((width, rows), BF), jax.ShapeDtypeStruct((2, width, rows), BF)],
        scratch_shapes=[pltpu.VMEM((width, rows), F32)],
        cost_estimate=estimate("sorted_rows"),
        name="sorted_rows",
    )


def dense_terms_kernel(att_ref, rows_ref, branch_ref, dq_ref, dk_ref, dv_ref, keep_ref, send_ref):
    half = keep_ref.shape[1]
    for i, d_ref in enumerate((branch_ref, dq_ref, dk_ref, dv_ref)):
        lhs = att_ref[...] if i == 0 else rows_ref[min(i - 1, 1)]
        term = dot(lhs, d_ref[...]).astype(BF)
        keep_ref[i] = term[:half]
        send_ref[i] = term[half:]


def dense_terms(att_t, lhs, branch, dq, dk, dv):
    _, width, rows = lhs.shape
    cols = 256
    col_block = pl.BlockSpec((rows, cols), lambda g: (0, g))
    return call(
        dense_terms_kernel,
        (att_t, lhs, branch, dq, dk, dv),
        [const_spec(att_t.shape), const_spec(lhs.shape)] + [col_block] * 4,
        grid=(width // cols,),
        out_specs=[pl.BlockSpec((4, width // 2, cols), lambda g: (0, 0, g))] * 2,
        out_shape=[jax.ShapeDtypeStruct((4, width // 2, width), BF)] * 2,
        cost_estimate=estimate("dense_terms"),
        name="dense_terms",
    )


def norm_bwd_kernel(
    place_ref, tok_ref, gain_ref, gmid_ref, small_ref, dq_ref, dk_ref, dv_ref, wq_ref, wk_ref, wv_ref,
    tg_ref, keep_ref, send_ref, acc, sort_scr, *, gain_row,
):
    step = pl.program_id(0)
    total = dot_nt(dq_ref[...], wq_ref[...]) + dot_nt(dk_ref[...], wk_ref[...]) + dot_nt(dv_ref[...], wv_ref[...])

    @pl.when(step == 0)
    def _():
        acc[...] = total

    @pl.when(step > 0)
    def _():
        acc[...] += total

    @pl.when(step == pl.num_programs(0) - 1)
    def _():
        grad = acc[...]
        start = tok_ref[...].astype(F32)
        scale = rms_scale(start)
        unit = start * scale
        gain_grad = jnp.sum(grad * unit, axis=0, keepdims=True)
        scaled = grad * gain_ref[...]
        tg_ref[...] = gmid_ref[...] + scale * (scaled - unit * jnp.mean(scaled * unit, axis=-1, keepdims=True))
        small = small_ref[...]
        row = lax.broadcasted_iota(jnp.int32, small.shape, 0)
        small = jnp.where(row == gain_row, gain_grad, small)
        small = jnp.concatenate([small, jnp.zeros((LANES - small.shape[0], small.shape[1]), F32)], axis=0)
        sort_rows(place_ref, small.T, sort_scr)
        half = sort_scr.shape[0] // 2
        keep_ref[...] = sort_scr[0:half].astype(BF)
        send_ref[...] = sort_scr[half:].astype(BF)


def norm_bwd(place, tokens, gain_attn, grad_mid, small, gain_row, dq, dk, dv, w_query, w_key, w_value):
    rows, width = tokens.shape
    cols = 256
    col_block = pl.BlockSpec((rows, cols), lambda g: (0, g))
    weight_block = pl.BlockSpec((width, cols), lambda g: (0, g))
    half = jax.ShapeDtypeStruct((width // 2, LANES), BF)
    return call(
        functools.partial(norm_bwd_kernel, gain_row=gain_row),
        (place, tokens, gain_attn[None], grad_mid, small, dq, dk, dv, w_query, w_key, w_value),
        [pl.BlockSpec(memory_space=pltpu.SMEM)]
        + [const_spec((rows, width)), const_spec((1, width)), const_spec((rows, width)), const_spec(small.shape)]
        + [col_block] * 3
        + [weight_block] * 3,
        grid=(width // cols,),
        out_specs=[const_spec((rows, width)), const_spec(half.shape), const_spec(half.shape)],
        out_shape=[jax.ShapeDtypeStruct((rows, width), F32), half, half],
        scratch_shapes=[pltpu.VMEM((rows, width), F32), pltpu.VMEM((width, LANES), F32)],
        cost_estimate=estimate("norm_bwd"),
        name="norm_bwd",
    )


def last_sums_kernel(token_ref, *refs, experts, counts):
    pairs, outs = refs[:4], refs[4:]
    first = pairs[0][...].astype(F32) + pairs[1][...].astype(F32)
    second = pairs[2][...].astype(F32) + pairs[3][...].astype(F32)
    width = second.shape[2]
    outs[0][...] = first[0, :, 0:width]
    outs[1][...] = first[1, :, 0:width]
    outs[2][...] = second[0]
    outs[3][...] = second[1]
    small = first[0, :, width:] + token_ref[...]
    outs[4][...] = small[:, 0:experts]
    flat = small.T
    for i, count in enumerate(counts):
        outs[5 + i][...] = flat[TAIL // 2 + i : TAIL // 2 + i + 1, 0:count]


def last_sums(token, pairs, experts, counts):
    rows, width = pairs[2].shape[1:]
    args = (token, *pairs)
    return call(
        functools.partial(last_sums_kernel, experts=experts, counts=counts),
        args,
        [pl.BlockSpec(memory_space=pltpu.VMEM)] * len(args),
        out_shape=[jax.ShapeDtypeStruct((rows, width), F32)] * 4
        + [jax.ShapeDtypeStruct((rows, experts), F32)]
        + [jax.ShapeDtypeStruct((1, count), F32) for count in counts],
        cost_estimate=estimate("last_sums"),
        name="last_sums",
    )


def bits_of(size):
    return size.bit_length() - 1


def swap(value, axis, size, mask):
    return lax.ppermute(value, axis, [(i, i ^ mask) for i in range(size)])


def pick(value, index, axis):
    return lax.dynamic_index_in_dim(value, index, axis, keepdims=False)


class Order:
    def __init__(self, token):
        self.token = token

    def enter(self, tree):
        tree, self.token = lax.optimization_barrier((tree, self.token))
        return tree

    leave = enter


def places(me, bits, order):
    key = jnp.arange(1 << bits, dtype=jnp.int32) ^ me
    place = jnp.zeros_like(key)
    for bit in order:
        place = place * 2 + ((key >> bit) & 1)
    return place


class Halving:
    def __init__(self, order, keep, send, dim, route, name):
        self.order, self.keep, self.to_send, self.dim, self.route, self.name = order, keep, send, dim, list(route), name
        self.got = None

    def start(self):
        axis, size, bit = self.route[0]
        with jax.named_scope(f"{self.name}_{axis}{1 << bit}"):
            value = self.order.enter(self.keep if self.to_send is None else self.to_send)
            self.got = swap(value, axis, size, 1 << bit)


def arrive(*units):
    for unit in units:
        unit.got = unit.order.leave(unit.got)


def fold_kernel(*refs, cuts, inputs):
    pairs, outs = refs[:inputs], list(refs[inputs:])
    at = 0
    for dim, last, width in cuts:
        total = []
        for _ in range(width):
            total.append(pairs[at][...].astype(F32) + pairs[at + 1][...].astype(F32))
            at += 2
        if last:
            outs.pop(0)[...] = total[0]
            continue
        rows = total[0].shape[dim] // 2
        for start in (0, rows):
            out = outs.pop(0)
            cut = [lax.slice_in_dim(v, start, start + rows, axis=dim).astype(BF) for v in total]
            if width == 1:
                out[...] = cut[0]
            else:
                for i in range(width):
                    out[i] = cut[i]


def fold(*units, hold=()):
    groups = [unit if isinstance(unit, tuple) else (unit,) for unit in units]
    order = groups[0][0].order
    args, cuts, shapes = [], [], []
    for group in groups:
        for unit in group:
            unit.route.pop(0)
            got = order.leave(unit.got)
            args += [unit.keep, got]
        unit = group[0]
        last = unit.to_send is None or not unit.route
        cuts.append((unit.dim, last, len(group)))
        if last:
            shapes.append(jax.ShapeDtypeStruct(got.shape, F32))
        else:
            shape = list(got.shape)
            shape[unit.dim] //= 2
            if len(group) > 1:
                shape = [len(group)] + shape
            shapes += [jax.ShapeDtypeStruct(tuple(shape), BF)] * 2
    args = order.enter(args)
    outs = list(
        call(
            functools.partial(fold_kernel, cuts=cuts, inputs=len(args)),
            args,
            [pl.BlockSpec(memory_space=pltpu.VMEM)] * len(args),
            out_shape=shapes,
            cost_estimate=estimate("fold"),
            name="fold",
        )
    )
    outs = order.leave(outs)
    for group, (_, last, width) in zip(groups, cuts):
        unit = group[0]
        unit.keep = outs.pop(0)
        if not last:
            unit.to_send = outs.pop(0)
        if width > 1:
            unit.dim += 1
        if unit.route and unit not in hold:
            unit.start()


def fold_first_kernel(keep_ref, got_ref, small_keep_ref, small_got_ref, *outs):
    width = keep_ref.shape[2]
    small = (small_keep_ref[...] + small_got_ref[...]).astype(F32)
    for i in range(keep_ref.shape[0]):
        total = keep_ref[i].astype(F32) + got_ref[i].astype(F32)
        rows = total.shape[0] // 2
        for j in range(2):
            out = outs[i // 2 * 2 + j]
            out[i % 2, :, 0:width] = total[j * rows : (j + 1) * rows].astype(BF)
            if i < 2:
                extra = small[j * rows : (j + 1) * rows] if i == 0 else jnp.zeros((rows, LANES), F32)
                out[i, :, width:] = extra.astype(BF)


def fold_first(keep, got, small_keep, small_got):
    _, rows, width = keep.shape
    shapes = [jax.ShapeDtypeStruct((2, rows // 2, width + extra), BF) for extra in (LANES, LANES, 0, 0)]
    return call(
        fold_first_kernel,
        (keep, got, small_keep, small_got),
        [pl.BlockSpec(memory_space=pltpu.VMEM)] * 4,
        out_shape=shapes,
        cost_estimate=estimate("fold_first"),
        name="fold_first",
    )


class Return:
    def __init__(self, order, low, high, axis, size, name, pieces=False):
        self.order, self.axis, self.size, self.name = order, axis, size, name
        half = low.shape[0]
        self.slots = [(low, i) for i in range(half)] + [(high, i) for i in range(half)]
        self.bit = bits_of(size) - 1
        if pieces:
            self.start_pieces()
        else:
            with jax.named_scope(f"{self.name}{1 << self.bit}"):
                self.got = swap(self.order.enter(high), self.axis, self.size, 1 << self.bit)

    def moving(self):
        return [m for m in range(self.size) if (m >> self.bit) & 1]

    def start_pieces(self):
        self.got = []
        for m in self.moving():
            array, index = self.slots[m]
            with jax.named_scope(f"{self.name}{1 << self.bit}_{m}"):
                self.got.append(swap(self.order.enter(array[index][None]), self.axis, self.size, 1 << self.bit))

    def fold(self):
        got = self.order.leave(self.got)
        for i, m in enumerate(self.moving()):
            self.slots[m] = (got[i], 0) if isinstance(got, list) else (got, i)
        self.bit -= 1
        if self.bit >= 0:
            self.start_pieces()

    def finish(self):
        while self.bit >= 0:
            self.fold()


class Gather:
    def __init__(self, order, value, axis, size, name):
        self.order, self.axis, self.size, self.name = order, axis, size, name
        self.blocks = {0: value}
        self.send(0, size // 2)
        if size > 2:
            self.send(0, 1)

    def send(self, m, bit):
        with jax.named_scope(f"{self.name}{m}_{bit}"):
            self.blocks[m ^ bit] = swap(self.blocks[m], self.axis, self.size, bit)

    def relay(self):
        self.blocks[self.size // 2] = self.order.leave(self.blocks[self.size // 2])
        bit = self.size // 2
        while bit:
            for m in range(0, self.size, 2 * bit):
                if m ^ bit not in self.blocks:
                    self.send(m, bit)
            bit //= 2

    def finish(self):
        self.blocks = self.order.leave(self.blocks)
        return [self.blocks[m] for m in range(self.size)]


def body(
    tokens,
    cotangent,
    gain_attn,
    w_query,
    w_key,
    w_value,
    w_out,
    rel_bias,
    gain_moe,
    w_router,
    w_gate,
    w_up,
    w_down,
    segments,
    routes,
    *,
    dp_size,
    ep_size,
):
    TURNS.clear()
    rows, width = tokens.shape
    buckets, heads = rel_bias.shape
    experts = w_router.shape[1]
    cap = 10 * rows // (4 * experts)
    ff = w_gate.shape[2]
    me = lax.axis_index("expert")

    cots = Gather(None, cotangent, "expert", ep_size, "cot")
    scaled, keys, values, woff, token, code, *filled, payload = attn_first(
        tokens, gain_attn, w_query, w_key, w_value, w_out, rel_bias.T, segments, gain_moe, w_router.T, routes.T
    )
    order = Order(token)
    cots.order = order
    me_ref = me.reshape(1).astype(jnp.int32)

    dp_bits, ep_bits = bits_of(dp_size), bits_of(ep_size)
    dp_me = lax.axis_index("dp")
    dp_order = list(range(dp_bits))
    z_order = [1, 0] + dp_order[2:]
    place_x = places(dp_me, dp_bits, dp_order)
    place_z = places(dp_me, dp_bits, z_order)

    def dp_route(bits):
        return [("dp", dp_size, b) for b in bits]

    dp_part = [ep_bits + b for b in dp_order]
    ep_part = list(range(1, ep_bits))
    q_bits = [0] + ep_part + dp_part
    k_bits = [0] + dp_part[:2] + ep_part + dp_part[2:]
    whole_me = dp_me * ep_size + me

    def route(bits):
        return [("expert", ep_size, b) if b < ep_bits else ("dp", dp_size, b - ep_bits) for b in bits]

    place_q, place_k = [places(whole_me, dp_bits + ep_bits, bits) for bits in (q_bits, k_bits)]

    cots.relay()
    first_half = Gather(order, order.enter(payload), "expert", ep_size, "rows_a")
    attended, lse, middle, normed_moe, chances, payload = order.leave(
        attn_second(tokens, order.enter(scaled), keys, values, w_out, woff, segments, gain_moe, w_router.T, filled)
    )
    second_half = Gather(order, order.enter(payload), "expert", ep_size, "rows_b")
    first_half.relay()
    cots, heads_rows = cots.finish(), first_half.finish()
    blocks = ff // FF_BLOCK
    counts = [blocks - blocks // 2, blocks // 2]
    starts = [sum(counts[:i]) for i in range(len(counts))]
    gh_first, cot_rows = order.leave(cot_hidden(order.enter(me_ref), heads_rows, cots, w_down, cap, starts[1]))
    second_half.relay()
    payloads = [v for pair in zip(heads_rows, second_half.finish()) for v in pair]
    scs, units = [], []

    def expert_part(i, source, filled=()):
        *shared, gate_keep, gate_send, up_keep, up_send, sc, hid, hid_t, gg, gu = order.leave(
            expert_a(
                order.enter(source), gh_second if i else gh_first, starts[i], w_gate, w_up, starts[i], counts[i], filled
            )
        )
        scs.append(sc)
        gate = Halving(order, gate_keep, gate_send, 0, dp_route(z_order), f"gate{i}")
        units.append((gate, Halving(order, up_keep, up_send, 0, dp_route(dp_order), f"up{i}")))
        return shared, (hid, hid_t, gg, gu)

    def by_xor(value):
        return jnp.stack([pick(value, me ^ m, 0) for m in range(experts)])

    def padded(value):
        return jnp.pad(value, ((0, TAIL - experts), (0, 0)))

    (x_all, x_t, gate_all, grad_cots), filled = expert_part(0, (me_ref, place_x, payloads, cot_rows))
    for unit in units[0]:
        unit.start()
    gh_second = order.leave(cot_hidden_more(order.enter(cot_rows), w_down, starts[1]))
    _, (hid, hid_t, gg, gu) = expert_part(1, (x_all, x_t, gate_all), filled)
    fold(*units[0])
    for unit in units[1]:
        unit.start()
    back_low, back_high = order.leave(expert_b(order.enter(gg), gu, scs, w_gate, w_up, experts))
    backs = Return(order, back_low, back_high, "expert", ep_size, "grad_rows")
    first, second = units[0][0], units[1][0]
    fold(units[0], hold=units[0])
    down_parts = order.leave(down_grads(order.enter(hid_t), grad_cots, place_z, place_x))
    down_units = tuple(
        Halving(order, down_parts[2 * i], down_parts[2 * i + 1], 0, dp_route(bits), f"down{i}")
        for i, bits in enumerate((z_order, dp_order))
    )
    down = down_units[0]
    fold(*units[1])
    code_xor, chances_xor, wr_xor = order.enter((by_xor(code), padded(by_xor(chances)), padded(by_xor(w_router.T))))
    backs.fold()
    att_t, normed_t = order.leave(sorted_rows(place_q, place_k, order.enter(tokens), gain_attn, attended))
    backs.finish()
    for unit in down_units:
        unit.start()
    grad_mid, branch, grad_att, gain_moe_term, router_term = order.leave(
        moe_bwd(
            cotangent, order.enter(middle), gain_moe, normed_moe, chances_xor, wr_xor, code_xor, code_xor.T, w_out,
            backs.slots,
        )
    )
    dq, dk, dv, dwoff = order.leave(attn_bwd(scaled, keys, values, order.enter(grad_att), lse, woff, segments))
    arrive(*units[1])
    dense_keep, dense_send = order.leave(dense_terms(att_t, normed_t, branch, order.enter(dq), dk, dv))
    arrive(*down_units)
    core = Halving(order, dense_keep, dense_send, 1, route(q_bits)[:1], "dense")
    core.start()
    first.start()
    fold(*down_units, units[1], hold=units[1])
    devices = dp_size * ep_size
    share = width // devices
    onehot = jnp.asarray(band_onehot(rows, buckets))
    bias_term = jnp.dot(onehot, dwoff.reshape(heads, BAND).T, precision=HIGHEST).reshape(devices, -1)
    bias_share = bias_term.shape[1]
    bias_row = jnp.pad(bias_term, ((0, 0), (0, share - bias_share))).reshape(1, width)
    small = jnp.concatenate(
        [
            jnp.pad(by_xor(router_term), ((0, TAIL // 2 - experts), (0, 0))),
            jnp.zeros((1, width), F32),
            gain_moe_term,
            bias_row,
            jnp.zeros((TAIL // 2 - 3, width), F32),
        ],
        axis=0,
    )
    token_grad, small_keep, small_send = order.leave(
        norm_bwd(
            place_q, tokens, gain_attn, grad_mid, order.enter(small), TAIL // 2, dq, dk, dv, w_query, w_key, w_value
        )
    )
    with jax.named_scope("small_expert1"):
        small_got = swap(order.enter(small_send), "expert", ep_size, 1)
    core_got = order.leave(core.got)
    halves = order.leave(fold_first(order.enter(dense_keep), core_got, small_keep, order.leave(small_got)))
    dense = [
        Halving(order, halves[2 * i], halves[2 * i + 1], 1, route(bits)[1:], name)
        for i, (bits, name) in enumerate(((q_bits, "out_q"), (k_bits, "k_v")))
    ]
    out_q, k_v = dense
    arrive(*down_units, first)
    k_v.start()
    out_q.start()
    second.start()
    prod_low, prod_high = order.leave(produced_rows(order.enter(hid), w_down, experts))
    returned = Return(order, prod_low, prod_high, "expert", ep_size, "produced_rows")
    fold(k_v, out_q, down_units, first, second)
    fold(k_v, out_q)
    while first.route or second.route:
        fold(*[unit for unit in (first, second) if unit.route])
    terms = [first.keep, second.keep]
    gate_grad = order.leave(jnp.concatenate([term[0] for term in terms], axis=1)[None])
    up_grad = order.leave(jnp.concatenate([term[1] for term in terms], axis=1)[None])
    returned.fold()
    returned.finish()
    layer_out = order.leave(layer_output(middle, chances_xor, code_xor.T, returned.slots))
    fold(k_v, out_q, down)
    rest = [first, second, down, *dense]
    while any(unit.route[1:] for unit in rest) or down.route:
        fold(*[unit for unit in rest if unit.route])
    down_grad = order.leave(jnp.concatenate([down.keep[0], down.keep[1]], axis=1)[None])
    pairs = order.leave([out_q.keep, out_q.got, k_v.keep, k_v.got])
    out_grad, query_grad, key_grad, value_grad, router_grad, *gains = last_sums(
        order.token, pairs, experts, (share, share, bias_share)
    )
    gain_attn_grad, gain_moe_grad, bias_grad = [value.reshape(-1) for value in gains]
    return (
        layer_out,
        token_grad,
        query_grad,
        key_grad,
        value_grad,
        out_grad,
        gain_attn_grad,
        gain_moe_grad,
        bias_grad,
        router_grad,
        gate_grad,
        up_grad,
        down_grad,
    )


def solution(mesh):
    in_specs = (
        P(("dp", "expert"), None),
        P(("dp", "expert"), None),
        P(),
        P(),
        P(),
        P(),
        P(),
        P(),
        P(),
        P(),
        P("expert", None, None),
        P("expert", None, None),
        P("expert", None, None),
        P(("dp", "expert"), None),
        P(("dp", "expert"), None),
    )
    out_specs = (
        P(("dp", "expert"), None),
        P(("dp", "expert"), None),
        P(("dp", "expert"), None),
        P(("dp", "expert"), None),
        P(("dp", "expert"), None),
        P(("dp", "expert"), None),
        P(("dp", "expert")),
        P(("dp", "expert")),
        P(("dp", "expert")),
        P(("dp", "expert"), None),
        P("expert", "dp", None),
        P("expert", "dp", None),
        P("expert", "dp", None),
    )
    run = functools.partial(body, dp_size=mesh.shape["dp"], ep_size=mesh.shape["expert"])
    return jax.shard_map(run, mesh=mesh, in_specs=in_specs, out_specs=out_specs, check_vma=False)
```

```python
import functools

import jax
import jax.numpy as jnp
import numpy as np
from jax import lax
from jax.experimental import pallas as pl
from jax.experimental.pallas import tpu as pltpu
from jax.sharding import PartitionSpec as P

EPS = 1e-06
HIGHEST = lax.Precision.HIGHEST
LANES = 128
BAND = 4 * LANES
HEAD_GROUP = 4
TAIL = 16
FAR = -1e30
BF = jnp.bfloat16
F32 = jnp.float32
VMEM_LIMIT = 56 * 1024 * 1024


def bucket_of(relative, buckets):
    halfway = buckets // 2
    exact_span = halfway // 2
    distance = np.abs(relative)
    beyond = exact_span + (
        np.log(np.maximum(distance, 1) / exact_span)
        / np.log(128.0 / exact_span)
        * (halfway - exact_span)
    ).astype(np.int64)
    beyond = np.minimum(beyond, halfway - 1)
    return (
        (relative > 0).astype(np.int64) * halfway
        + np.where(distance < exact_span, distance, beyond)
    ).astype(np.int32)


def band_onehot(length, buckets):
    place = np.arange(BAND)
    relative = np.where(place <= 3 * LANES, LANES - place, BAND + LANES - place)
    table = (bucket_of(relative, buckets)[None, :] == np.arange(buckets)[:, None]).astype(np.float32)
    table[:, 3 * LANES] = 0.0
    far = np.arange(LANES, length)
    assert np.all(bucket_of(far, buckets) == bucket_of(far, buckets)[0])
    assert np.all(bucket_of(-far, buckets) == bucket_of(-far, buckets)[0])
    return table


FAR_AFTER = 3 * LANES + 1
FAR_BEFORE = 3 * LANES - 1


def dot(a, b):
    return lax.dot_general(a, b, (((1,), (0,)), ((), ())), preferred_element_type=F32)


def dot_nt(a, b):
    return lax.dot_general(a, b, (((1,), (1,)), ((), ())), preferred_element_type=F32)


def dot_tn(a, b):
    return lax.dot_general(a, b, (((0,), (0,)), ((), ())), preferred_element_type=F32)


def split3(value):
    hi = value.astype(BF)
    rest = value - hi.astype(F32)
    mid = rest.astype(BF)
    low = (rest - mid.astype(F32)).astype(BF)
    return hi, mid, low


def rms_scale(value):
    return lax.rsqrt(jnp.mean(value * value, axis=-1, keepdims=True) + EPS)


def params(**kw):
    return pltpu.CompilerParams(vmem_limit_bytes=VMEM_LIMIT, **kw)


TIMES = {
    ("down_grads", 0): 10.0,
    ("dense_terms", 0): 13.1,
    ("fold", 1): 2.0,
}


TURNS = {}


def estimate(name):
    turn = TURNS.get(name, 0)
    TURNS[name] = turn + 1
    time = TIMES.get((name, turn), 0.1)
    return pl.CostEstimate(flops=int(time * 1.15e9), bytes_accessed=100000, transcendentals=0)


def call(kernel, args, in_specs, **kw):
    return pl.pallas_call(kernel, in_specs=list(in_specs), compiler_params=params(), **kw)(*args)


def whole_specs(args):
    return [const_spec(a.shape) for a in args]


def const_spec(shape):
    return pl.BlockSpec(shape, lambda *_: (0,) * len(shape))


def selector(code_row, rows):
    place = lax.broadcasted_iota(jnp.int32, (rows, code_row.shape[1]), 0)
    return jnp.where(place == code_row, 1.0, 0.0).astype(BF)


def selector_t(code_column, rows):
    place = lax.broadcasted_iota(jnp.int32, (code_column.shape[0], rows), 1)
    return jnp.where(place == code_column, 1.0, 0.0).astype(BF)


def band_of(row):
    return pltpu.roll(jnp.broadcast_to(row, (LANES, BAND)), 0, 1, stride=1, stride_axis=0)


def diagonal_sums(skewed):
    eight = skewed[0:8]
    for start in range(8, LANES, 8):
        eight = eight + pltpu.roll(skewed[start : start + 8], BAND - start, 1)
    total = eight[0:1]
    for row in range(1, 8):
        total = total + pltpu.roll(eight[row : row + 1], BAND - row, 1)
    return total


def bias_block(band, row, first, count, k_blocks):
    far = [jnp.broadcast_to(row[:, at : at + 1], (LANES, LANES)) for at in (FAR_BEFORE, FAR_AFTER)]
    columns = []
    for q_block in range(first, first + count):
        pieces = []
        for k_block in range(k_blocks):
            d = k_block - q_block
            pieces.append(far[1] if d > 1 else far[0] if d < -1 else band[:, LANES * (1 - d) : LANES * (2 - d)])
        columns.append(jnp.concatenate(pieces, axis=0))
    return jnp.concatenate(columns, axis=1)


def only_rows(value, h, head_dim):
    mine = value[h * head_dim : (h + 1) * head_dim]
    none = jnp.zeros_like(mine)
    return jnp.concatenate([mine, none] if h % 2 == 0 else [none, mine], axis=0)


def attend(scaled, keys, values, woff_ref, mask, first, head_dim):
    count = scaled.shape[0] // LANES
    q_t, v_t = scaled.T, values.T
    heads_t, totals = [], []
    for h in range(HEAD_GROUP):
        row = woff_ref[0, h : h + 1, :]
        bias = bias_block(band_of(row), row, first, count, keys.shape[0] // LANES)
        k_pair = keys[:, LANES * (h // 2) : LANES * (h // 2 + 1)]
        s = dot(k_pair, only_rows(q_t, h, head_dim)) + bias + mask
        peak = jnp.max(s, axis=0, keepdims=True)
        p = jnp.exp(s - peak)
        total = jnp.sum(p, axis=0, keepdims=True)
        heads_t.append(dot(v_t[h * head_dim : (h + 1) * head_dim], p.astype(BF)) * (1.0 / total))
        totals.append(peak + jnp.log(total))
    return jnp.concatenate(heads_t, axis=0).T.astype(BF), jnp.concatenate(totals, axis=0)


def slot_codes(routes):
    chosen = routes.astype(F32)
    tokens = chosen.shape[1]
    numbers = lax.broadcasted_iota(jnp.int32, (TAIL // 2, tokens), 0).astype(F32)
    named = jnp.logical_or(numbers == chosen[0:1], numbers == chosen[1:2])
    row = lax.broadcasted_iota(jnp.int32, (tokens, tokens), 0)
    lane = lax.broadcasted_iota(jnp.int32, (tokens, tokens), 1)
    before = jnp.where(row < lane, 1.0, 0.0).astype(BF)
    return jnp.where(named, dot(jnp.where(named, 1.0, 0.0).astype(BF), before), -1.0)


def packed_codes(codes):
    upper = jnp.floor((codes + 1.0) * (1.0 / 16.0))
    return jnp.concatenate([upper, codes + 1.0 - 16.0 * upper], axis=0)


def own_code(me, packed):
    row = lax.broadcasted_iota(jnp.int32, packed.shape, 0)
    weight = jnp.where(row == me, 16.0, jnp.where(row == me + TAIL // 2, 1.0, 0.0))
    return (jnp.sum(packed.astype(F32) * weight, axis=0, keepdims=True) - 1.0).astype(jnp.int32)


def route_rows(mid, gain_ref, wr_ref, experts, nm_ref, ch_ref, payload_ref, codes=None):
    rows = mid.shape[0]
    nm = (mid * rms_scale(mid) * gain_ref[...]).astype(BF)
    nm_ref[...] = nm
    router = jnp.concatenate([wr_ref[...], jnp.zeros((TAIL - experts, nm.shape[1]), BF)], axis=0)
    logits = dot_nt(router, nm)
    live = lax.broadcasted_iota(jnp.int32, logits.shape, 0) < experts
    logits = jnp.where(live, logits, FAR)
    raised = jnp.exp(logits - jnp.max(logits, axis=0, keepdims=True))
    chances = raised / jnp.sum(raised, axis=0, keepdims=True)
    ch_ref[...] = chances
    hi = chances.astype(BF).astype(F32)
    both = jnp.concatenate([hi[: TAIL // 2], (chances - hi)[: TAIL // 2]], axis=0)
    payload_ref[0:rows, :] = nm
    tail = [both] if codes is None else [both, packed_codes(codes)]
    used = sum(v.shape[1] for v in tail)
    tail.append(jnp.zeros((TAIL, nm.shape[1] - used), F32))
    payload_ref[rows:, :] = jnp.concatenate(tail, axis=1).astype(BF)


def segment_mask(seg_ref, first, count):
    seg = seg_ref[...].astype(F32)
    column = jnp.broadcast_to(seg, (8, seg.shape[1])).T[:, 0:1]
    return jnp.where(column == seg[:, first : first + count], 0.0, FAR)


def attn_first_kernel(
    tok_ref, gain_a_ref, wq_ref, wk_ref, wv_ref, wo_ref, bias_ref, onehot_ref, seg_ref, gain_m_ref, wr_ref, routes_ref,
    qs_ref, k_ref, v_ref, woff_ref, token_ref, code_ref, att_ref, lse_ref, mid_ref, nm_ref, ch_ref, payload_ref,
    n_scr, mask_scr, woff_scr, code_scr,
    *, experts, head_dim,
):
    step = pl.program_id(0)
    rows = att_ref.shape[0]

    @pl.when(step == 0)
    def _():
        start = tok_ref[...].astype(F32)
        n_scr[...] = (start * rms_scale(start) * gain_a_ref[...]).astype(BF)
        mid_ref[...] = start[:rows]
        mask_scr[...] = segment_mask(seg_ref, 0, rows)
        token_ref[...] = jnp.where(seg_ref[:, 0:LANES] < 0, 1.0, 0.0)
        codes = slot_codes(routes_ref[...])
        code_scr[...] = codes
        code_ref[...] = codes[:experts].astype(jnp.int32)
        table = onehot_ref[...]
        offsets = sum(dot(part, table) for part in split3(bias_ref[...]))
        for g in range(woff_scr.shape[0]):
            woff_scr[g] = offsets[g * HEAD_GROUP : (g + 1) * HEAD_GROUP]

    woff_ref[0] = woff_scr[step]

    normed = n_scr[...]
    scaled = (dot(normed, wq_ref[...]).astype(BF).astype(F32) * head_dim ** (-0.5)).astype(BF)
    keys = dot(normed, wk_ref[...]).astype(BF)
    values = dot(normed, wv_ref[...]).astype(BF)
    qs_ref[...] = scaled
    k_ref[...] = keys
    v_ref[...] = values
    att, totals = attend(scaled[:rows], keys, values, woff_ref, mask_scr[...], 0, head_dim)
    att_ref[...] = att
    lse_ref[0] = totals
    mid_ref[...] += dot(att, wo_ref[...])

    @pl.when(step == pl.num_programs(0) - 1)
    def _():
        route_rows(mid_ref[...], gain_m_ref, wr_ref, experts, nm_ref, ch_ref, payload_ref, code_scr[...])


def attn_second_kernel(
    tok_ref, qs_ref, k_ref, v_ref, wo_ref, woff_ref, seg_ref, gain_m_ref, wr_ref, *refs, experts, head_dim
):
    att_ref, lse_ref, mid_ref, nm_ref, ch_ref, payload_ref, mask_scr = refs[-7:]
    step = pl.program_id(0)
    rows = att_ref.shape[0]

    @pl.when(step == 0)
    def _():
        mid_ref[...] = tok_ref[...].astype(F32)
        mask_scr[...] = segment_mask(seg_ref, rows, rows)

    att, totals = attend(qs_ref[...], k_ref[...], v_ref[...], woff_ref, mask_scr[...], rows // LANES, head_dim)
    att_ref[...] = att
    lse_ref[0] = totals
    mid_ref[...] += dot(att, wo_ref[...])

    @pl.when(step == pl.num_programs(0) - 1)
    def _():
        route_rows(mid_ref[...], gain_m_ref, wr_ref, experts, nm_ref, ch_ref, payload_ref)


def attn_halves(rows, width, groups, half):
    cols, part = width // groups, rows // 2
    wide = jax.ShapeDtypeStruct((rows, width), BF)
    shapes = [
        wide,
        jax.ShapeDtypeStruct((groups, HEAD_GROUP, rows), F32),
        jax.ShapeDtypeStruct((rows, width), F32),
        wide,
        jax.ShapeDtypeStruct((TAIL, rows), F32),
        jax.ShapeDtypeStruct((part + TAIL, width), BF),
    ]
    specs = [
        pl.BlockSpec((part, cols), lambda g: (half, g)),
        pl.BlockSpec((1, HEAD_GROUP, part), lambda g: (g, 0, half)),
        pl.BlockSpec((part, width), lambda g: (half, 0)),
        pl.BlockSpec((part, width), lambda g: (half, 0)),
        pl.BlockSpec((TAIL, part), lambda g: (0, half)),
        const_spec((part + TAIL, width)),
    ]
    return shapes, specs


def attn_first(tokens, gain_attn, w_query, w_key, w_value, w_out, rel_bias, seg, gain_moe, w_router, routes):
    rows, width = tokens.shape
    heads, buckets = rel_bias.shape
    experts = w_router.shape[0]
    groups = heads // HEAD_GROUP
    cols, part = width // groups, rows // 2
    weight_block = pl.BlockSpec((width, cols), lambda g: (0, g))
    shapes, specs = attn_halves(rows, width, groups, 0)
    wide = jax.ShapeDtypeStruct((rows, width), BF)
    return call(
        functools.partial(attn_first_kernel, experts=experts, head_dim=cols // HEAD_GROUP),
        (tokens, gain_attn[None], w_query, w_key, w_value, w_out, rel_bias, jnp.asarray(band_onehot(rows, buckets)).astype(BF),
         seg, gain_moe[None], w_router, routes),
        [
            const_spec((rows, width)),
            const_spec((1, width)),
            weight_block,
            weight_block,
            weight_block,
            pl.BlockSpec((cols, width), lambda g: (g, 0)),
            const_spec(rel_bias.shape),
            const_spec((buckets, BAND)),
            const_spec(seg.shape),
            const_spec((1, width)),
            const_spec(w_router.shape),
            const_spec(routes.shape),
        ],
        grid=(groups,),
        out_specs=[pl.BlockSpec((rows, cols), lambda g: (0, g))] * 3
        + [pl.BlockSpec((1, HEAD_GROUP, BAND), lambda g: (g, 0, 0)), const_spec((1, LANES)), const_spec((experts, rows))]
        + specs,
        out_shape=[wide] * 3
        + [jax.ShapeDtypeStruct((groups, HEAD_GROUP, BAND), F32), jax.ShapeDtypeStruct((1, LANES), F32)]
        + [jax.ShapeDtypeStruct((experts, rows), jnp.int32)]
        + shapes,
        scratch_shapes=[
            pltpu.VMEM((rows, width), BF),
            pltpu.VMEM((rows, part), F32),
            pltpu.VMEM((groups, HEAD_GROUP, BAND), F32),
            pltpu.VMEM((TAIL // 2, rows), F32),
        ],
        cost_estimate=estimate("attn_first"),
        name="attn_first",
    )


def attn_second(tokens, scaled, keys, values, w_out, woff, seg, gain_moe, w_router, filled):
    rows, width = tokens.shape
    experts = w_router.shape[0]
    groups = woff.shape[0]
    cols, part = width // groups, rows // 2
    col_block = pl.BlockSpec((rows, cols), lambda g: (0, g))
    shapes, specs = attn_halves(rows, width, groups, 1)
    args = (tokens, scaled, keys, values, w_out, woff, seg, gain_moe[None], w_router)
    return call(
        functools.partial(attn_second_kernel, experts=experts, head_dim=cols // HEAD_GROUP),
        (*args, *filled),
        [
            pl.BlockSpec((part, width), lambda g: (1, 0)),
            pl.BlockSpec((part, cols), lambda g: (1, g)),
            col_block,
            col_block,
            pl.BlockSpec((cols, width), lambda g: (g, 0)),
            pl.BlockSpec((1, HEAD_GROUP, BAND), lambda g: (g, 0, 0)),
            const_spec(seg.shape),
            const_spec((1, width)),
            const_spec(w_router.shape),
        ]
        + [pl.BlockSpec(memory_space=pl.ANY)] * len(filled),
        grid=(groups,),
        out_specs=specs,
        out_shape=shapes,
        scratch_shapes=[pltpu.VMEM((rows, part), F32)],
        input_output_aliases={len(args) + i: i for i in range(len(filled))},
        cost_estimate=estimate("attn_second"),
        name="attn_second",
    )


def gelu_parts(gate):
    c0 = np.float32(np.sqrt(2.0 / np.pi))
    c1 = np.float32(0.044715)
    square = gate * gate
    t = jnp.tanh(c0 * gate * (1.0 + c1 * square))
    half = 0.5 * (1.0 + t)
    value = gate * half
    slope = half + 0.5 * gate * (1.0 - t * t) * (c0 * (1.0 + 3.0 * c1 * square))
    return value, slope


FF_BLOCK = 256


def cot_hidden_kernel(me_ref, *refs, experts):
    tail_refs, cot_refs, wd_ref = refs[:experts], refs[experts : 2 * experts], refs[2 * experts]
    out_ref, rows_ref = refs[2 * experts + 1 :]

    @pl.when(pl.program_id(0) == 0)
    def _():
        cap = rows_ref.shape[0] // experts
        tokens = cot_refs[0].shape[0]
        for m, (tail_ref, cot_ref) in enumerate(zip(tail_refs, cot_refs)):
            code = own_code(me_ref[0], tail_ref[:, tokens // 2 : tokens // 2 + tokens])
            rows_ref[m * cap : (m + 1) * cap, :] = dot(selector(code, cap), cot_ref[...]).astype(BF)

    out_ref[...] = dot_nt(rows_ref[...], wd_ref[0]).astype(BF)


def cot_hidden(me, payloads, cots, w_down, cap, count):
    experts = len(cots)
    width = cots[0].shape[1]
    rows = experts * cap
    last = payloads[0].shape[0] // TAIL - 1
    return call(
        functools.partial(cot_hidden_kernel, experts=experts),
        (me, *payloads, *cots, w_down),
        [pl.BlockSpec(memory_space=pltpu.SMEM)]
        + [pl.BlockSpec((TAIL, width), lambda f: (last, 0))] * experts
        + whole_specs(cots)
        + [pl.BlockSpec((1, FF_BLOCK, width), lambda f: (0, f, 0))],
        grid=(count,),
        out_specs=[pl.BlockSpec((rows, FF_BLOCK), lambda f: (0, f)), const_spec((rows, width))],
        out_shape=[jax.ShapeDtypeStruct((rows, count * FF_BLOCK), BF), jax.ShapeDtypeStruct((rows, width), BF)],
        cost_estimate=estimate("cot_hidden"),
        name="cot_hidden",
    )


def cot_hidden_more_kernel(rows_ref, wd_ref, out_ref):
    out_ref[...] = dot_nt(rows_ref[...], wd_ref[0]).astype(BF)


def cot_hidden_more(cot_rows, w_down, first):
    rows, width = cot_rows.shape
    count = w_down.shape[1] // FF_BLOCK - first
    return call(
        cot_hidden_more_kernel,
        (cot_rows, w_down),
        [const_spec((rows, width)), pl.BlockSpec((1, FF_BLOCK, width), lambda f: (0, first + f, 0))],
        grid=(count,),
        out_specs=pl.BlockSpec((rows, FF_BLOCK), lambda f: (0, f)),
        out_shape=jax.ShapeDtypeStruct((rows, count * FF_BLOCK), BF),
        cost_estimate=estimate("cot_hidden_more"),
        name="cot_hidden_more",
    )


ROW_BLOCK = 320


def expert_first(me_ref, place_ref, payloads, cot_ref, x_ref, xt_ref, gate_ref, gc_ref):
    experts = len(payloads) // 2
    cap = x_ref.shape[0] // experts
    part = payloads[0].shape[0] - TAIL
    row = lax.broadcasted_iota(jnp.int32, (TAIL, part), 0)
    mine = jnp.logical_or(row == me_ref[0], row == me_ref[0] + TAIL // 2)
    for m in range(experts):
        code = own_code(me_ref[0], payloads[2 * m][part:, part : 3 * part])
        chosen = selector(code, cap)
        place = slice(m * cap, (m + 1) * cap)
        total = jnp.zeros((cap, x_ref.shape[1]), F32)
        gate = jnp.zeros((cap, 1), F32)
        for i in range(2):
            payload = payloads[2 * m + i]
            part_chosen = chosen[:, i * part : (i + 1) * part]
            total = total + dot(part_chosen, payload[0:part, :])
            chances = jnp.sum(jnp.where(mine, payload[part:, 0:part].astype(F32), 0.0), axis=0, keepdims=True)
            gate = gate + jnp.sum(part_chosen.astype(F32) * chances, axis=1, keepdims=True)
        x_ref[place, :] = total.astype(BF)
        gate_ref[place, :] = jnp.broadcast_to(gate, (cap, LANES))
        gc_ref[place, :] = (cot_ref[place, :].astype(F32) * gate).astype(BF)
    flipped = x_ref[...].T
    owners = place_ref.shape[0]
    rows = flipped.shape[0] // owners
    for b in range(owners):
        at = pl.multiple_of(place_ref[b] * rows, rows)
        xt_ref[pl.ds(at, rows), :] = flipped[b * rows : (b + 1) * rows]


def expert_a_kernel(*refs, experts):
    step = pl.program_id(0)
    if experts:
        me_ref, place_ref = refs[:2]
        payloads = refs[2 : 2 + 2 * experts]
        cot_ref, gh_ref, wg_ref, wu_ref, x_ref, xt_ref, gate_ref, gc_ref = refs[2 + 2 * experts : 10 + 2 * experts]

        @pl.when(step == 0)
        def _():
            expert_first(me_ref, place_ref, payloads, cot_ref, x_ref, xt_ref, gate_ref, gc_ref)

    else:
        x_ref, xt_ref, gate_ref, gh_ref, wg_ref, wu_ref = refs[:6]
    gate_keep_ref, gate_send_ref, up_keep_ref, up_send_ref, sc_ref, hid_ref, hidt_ref, gg_ref, gu_ref = refs[-9:]

    @pl.when(step == 0)
    def _():
        sc_ref[...] = jnp.zeros_like(sc_ref)

    wg, wu = wg_ref[0], wu_ref[0]
    width = wg.shape[1]
    for start in range(0, x_ref.shape[0], ROW_BLOCK):
        part = slice(start, start + ROW_BLOCK)
        x = x_ref[part, :]
        gate_pre = dot(x, wg)
        up_pre = dot(x, wu)
        grad = gh_ref[part, :].astype(F32)
        act, slope = gelu_parts(gate_pre)
        hidden = act * up_pre
        hid_ref[part, :] = hidden.astype(BF)
        product = hidden * grad
        folded = product[:, 0:LANES]
        for i in range(1, width // LANES):
            folded = folded + product[:, i * LANES : (i + 1) * LANES]
        sc_ref[part, :] += folded
        grad = grad * gate_ref[part, 0:1]
        gg_ref[part, :] = (slope * up_pre * grad).astype(BF)
        gu_ref[part, :] = (act * grad).astype(BF)
    hidt_ref[...] = hid_ref[...].T
    xt = xt_ref[...]
    cut = xt.shape[0] // 4
    for grad_ref, keep_ref, send_ref, second in ((gg_ref, gate_keep_ref, gate_send_ref, 1), (gu_ref, up_keep_ref, up_send_ref, 0)):
        term = dot(xt, grad_ref[...]).astype(BF)
        for q in range(4):
            upper, lower = (q % 2, q // 2) if second else (q // 2, q % 2)
            (send_ref if upper else keep_ref)[lower * cut : (lower + 1) * cut] = term[q * cut : (q + 1) * cut]


def expert_a(source, gh, gh_first, w_gate, w_up, first, count, filled=()):
    opening = 0 if filled else len(source[2]) // 2
    rows = gh.shape[0]
    width, ff = w_gate.shape[1:]
    span = count * FF_BLOCK
    col_weight = pl.BlockSpec((1, width, FF_BLOCK), lambda f: (0, 0, first + f))
    out_block = pl.BlockSpec((rows, FF_BLOCK), lambda f: (0, first + f))
    wide = jax.ShapeDtypeStruct((rows, ff), BF)
    tall = jax.ShapeDtypeStruct((ff, rows), BF)
    term = jax.ShapeDtypeStruct((width // 2, span), BF)
    term_block = pl.BlockSpec((width // 2, FF_BLOCK), lambda f: (0, f))
    if opening:
        me, place, payloads, cot_rows = source
        args = (me, place, *payloads, cot_rows)
        specs = [pl.BlockSpec(memory_space=pltpu.SMEM)] * 2 + whole_specs((*payloads, cot_rows))
        shared = [
            jax.ShapeDtypeStruct((rows, width), BF),
            jax.ShapeDtypeStruct((width, rows), BF),
            jax.ShapeDtypeStruct((rows, LANES), F32),
            jax.ShapeDtypeStruct((rows, width), BF),
        ]
    else:
        args = tuple(source)
        specs = whole_specs(source)
        shared = []
    args = (*args, gh, w_gate, w_up)
    used = len(args)
    first_filled = len(shared) + 5

    def run(*refs):
        expert_a_kernel(*refs[:used], *refs[used + len(filled) :], experts=opening)

    return call(
        run,
        (*args, *filled),
        specs
        + [pl.BlockSpec((rows, FF_BLOCK), lambda f: (0, first - gh_first + f)), col_weight, col_weight]
        + [pl.BlockSpec(memory_space=pl.ANY)] * len(filled),
        grid=(count,),
        out_specs=whole_specs(shared)
        + [term_block] * 4
        + [const_spec((rows, LANES)), out_block]
        + [pl.BlockSpec((FF_BLOCK, rows), lambda f: (first + f, 0)), out_block, out_block],
        out_shape=shared + [term] * 4 + [jax.ShapeDtypeStruct((rows, LANES), F32), wide, tall, wide, wide],
        input_output_aliases={used + i: first_filled + i for i in range(len(filled))},
        cost_estimate=estimate("expert_grads"),
        name="expert_grads",
    )


def expert_b_kernel(gg_ref, gu_ref, *refs, cap, experts):
    sc_refs, (wg_ref, wu_ref, *outs, acc) = refs[:-5], refs[-5:]
    part_sum = dot_nt(gg_ref[...], wg_ref[0]) + dot_nt(gu_ref[...], wu_ref[0])
    step, block = pl.program_id(0), pl.program_id(1)

    @pl.when(step == 0)
    def _():
        acc[block] = part_sum

    def finish(out_ref):
        total = acc[block] + part_sum
        row = lax.broadcasted_iota(jnp.int32, (cap, cap), 0)
        lane = lax.broadcasted_iota(jnp.int32, (cap, cap), 1)
        place = lax.broadcasted_iota(jnp.int32, (TAIL, cap), 0)
        out_ref[0:cap, :] = total.astype(BF)
        folded = sc_refs[0][...]
        for other in sc_refs[1:]:
            folded = folded + other[...]
        column = jnp.sum(folded, axis=1, keepdims=True)
        flat = jnp.sum(jnp.where(row == lane, column, 0.0), axis=0, keepdims=True)
        hi, mid, low = split3(flat)
        packed = jnp.where(
            place == 0, hi.astype(F32), jnp.where(place == 1, mid.astype(F32), jnp.where(place == 2, low.astype(F32), 0.0))
        )
        out_ref[cap : cap + TAIL, :] = jnp.zeros((TAIL, total.shape[1]), BF)
        out_ref[cap : cap + TAIL, 0:cap] = packed.astype(BF)

    last = step == pl.num_programs(0) - 1
    for m in range(experts):

        @pl.when(jnp.logical_and(last, block == m))
        def _(m=m):
            finish(outs[m // (experts // 2)].at[m % (experts // 2)])


def expert_b(gg, gu, scs, w_gate, w_up, experts):
    rows, ff = gg.shape
    width = w_gate.shape[1]
    cap = rows // experts
    cut = ff // 2
    grads = pl.BlockSpec((cap, cut), lambda k, m: (m, k))
    sums = pl.BlockSpec((cap, LANES), lambda k, m: (m, 0))
    weight = pl.BlockSpec((1, width, cut), lambda k, m: (0, 0, k))
    return call(
        functools.partial(expert_b_kernel, cap=cap, experts=experts),
        (gg, gu, *scs, w_gate, w_up),
        [grads, grads] + [sums] * len(scs) + [weight, weight],
        grid=(2, experts),
        out_specs=[const_spec((experts // 2, cap + TAIL, width))] * 2,
        out_shape=[jax.ShapeDtypeStruct((experts // 2, cap + TAIL, width), BF)] * 2,
        scratch_shapes=[pltpu.VMEM((experts, cap, width), F32)],
        cost_estimate=estimate("expert_input_grad"),
        name="expert_input_grad",
    )


def down_kernel(place_a_ref, place_b_ref, hidt_ref, gc_ref, *outs):
    owners = place_a_ref.shape[0]
    shard = 2 * outs[0].shape[0] // owners
    size = int(np.gcd(shard, 32))
    rows = hidt_ref.shape[0]
    step = pl.program_id(0)
    total = dot(hidt_ref[...], gc_ref[...]).astype(BF)
    half = total.shape[1] // 2
    for i in range(rows // size):
        row = step * rows + i * size
        owner = row // shard
        piece = total[i * size : (i + 1) * size]
        for keep_ref, send_ref, place_ref, cols in (
            (outs[0], outs[1], place_a_ref, piece[:, :half]),
            (outs[2], outs[3], place_b_ref, piece[:, half:]),
        ):
            place = place_ref[owner]
            at = pl.multiple_of((place % (owners // 2)) * shard + (row - owner * shard), size)

            @pl.when(place < owners // 2)
            def _(keep_ref=keep_ref, at=at, cols=cols):
                keep_ref[pl.ds(at, size), :] = cols

            @pl.when(place >= owners // 2)
            def _(send_ref=send_ref, at=at, cols=cols):
                send_ref[pl.ds(at, size), :] = cols


def down_grads(hid_t, grad_cots, place_a, place_b):
    rows, width = grad_cots.shape
    ff = hid_t.shape[0]
    table = pl.BlockSpec(memory_space=pltpu.SMEM)
    part = jax.ShapeDtypeStruct((ff // 2, width // 2), BF)
    return call(
        down_kernel,
        (place_a, place_b, hid_t, grad_cots),
        [table, table, pl.BlockSpec((ff // 4, rows), lambda f: (f, 0)), const_spec((rows, width))],
        grid=(4,),
        out_specs=[const_spec(part.shape)] * 4,
        out_shape=[part] * 4,
        cost_estimate=estimate("down_grads"),
        name="down_grads",
    )


def produced_kernel(hid_ref, wd_ref, low_ref, high_ref):
    rows = dot(hid_ref[...], wd_ref[0]).astype(BF)
    lower = pl.program_id(0) < pl.num_programs(0) // 2

    @pl.when(lower)
    def _():
        low_ref[0] = rows

    @pl.when(jnp.logical_not(lower))
    def _():
        high_ref[0] = rows


def produced_rows(hid, w_down, experts):
    rows, ff = hid.shape
    width = w_down.shape[2]
    cap, half = rows // experts, experts // 2
    return call(
        produced_kernel,
        (hid, w_down),
        [pl.BlockSpec((cap, ff), lambda m: (m, 0)), const_spec(w_down.shape)],
        grid=(experts,),
        out_specs=[
            pl.BlockSpec((1, cap, width), lambda m: (jnp.minimum(m, half - 1), 0, 0)),
            pl.BlockSpec((1, cap, width), lambda m: (jnp.maximum(m - half, 0), 0, 0)),
        ],
        out_shape=[jax.ShapeDtypeStruct((half, cap, width), BF)] * 2,
        cost_estimate=estimate("produced_rows"),
        name="produced_rows",
    )


def distinct(slots):
    arrays, found = [], []
    for array, index in slots:
        which = next((i for i, other in enumerate(arrays) if other is array), None)
        if which is None:
            which = len(arrays)
            arrays.append(array)
        found.append((which, index))
    return arrays, found


def layer_out_kernel(mid_ref, ch_ref, code_ref, *refs, slots):
    parts, out_ref = refs[:-1], refs[-1]
    cap = parts[0].shape[1]
    total = mid_ref[...]
    chances = ch_ref[...].T
    for m, (which, index) in enumerate(slots):
        picked = dot(selector_t(code_ref[:, m : m + 1], cap), parts[which][index])
        total = total + chances[:, m : m + 1] * picked
    out_ref[...] = total.astype(BF)


def layer_output(middle, chances, code_t, slots):
    rows, width = middle.shape
    arrays, found = distinct(slots)
    args = (middle, chances, code_t, *arrays)
    return call(
        functools.partial(layer_out_kernel, slots=found),
        args,
        [pl.BlockSpec(memory_space=pltpu.VMEM)] * len(args),
        out_shape=jax.ShapeDtypeStruct((rows, width), BF),
        cost_estimate=estimate("layer_output"),
        name="layer_output",
    )


def moe_bwd_kernel(
    cot_ref, mid_ref, gain_ref, nm_ref, ch_ref, wr_ref, code_ref, codet_ref, wo_ref, *refs, slots
):
    backs, (gmid_ref, branch_ref, ga_ref, gain_o_ref, router_o_ref) = refs[:-5], refs[-5:]
    experts, cap = len(slots), backs[0].shape[1] - TAIL
    rows = cot_ref.shape[0]
    grad = jnp.zeros(mid_ref.shape, F32)
    gate_rows = []
    for m, (which, index) in enumerate(slots):
        grad = grad + dot(selector_t(codet_ref[:, m : m + 1], cap), backs[which][index, 0:cap, :])
        picked = dot(backs[which][index, cap : cap + TAIL, 0:cap], selector(code_ref[m : m + 1, :], cap))
        gate_rows.append(jnp.sum(picked, axis=0, keepdims=True))
    gate_rows.append(jnp.zeros((TAIL - experts, rows), F32))
    grad_chances = jnp.concatenate(gate_rows, axis=0)
    chances = ch_ref[...]
    grad_logits = chances * (grad_chances - jnp.sum(chances * grad_chances, axis=0, keepdims=True))
    pieces = jnp.concatenate(split3(grad_logits), axis=0)
    wr = wr_ref[...]
    grad = grad + dot_tn(pieces, jnp.concatenate([wr, wr, wr], axis=0))
    router = dot(pieces, nm_ref[...])
    router_o_ref[...] = router[0:TAIL] + router[TAIL : 2 * TAIL] + router[2 * TAIL : 3 * TAIL]
    mid = mid_ref[...]
    scale = rms_scale(mid)
    unit = mid * scale
    gain_o_ref[...] = jnp.sum(grad * unit, axis=0, keepdims=True)
    scaled = grad * gain_ref[...]
    grad_mid = cot_ref[...].astype(F32) + scale * (scaled - unit * jnp.mean(scaled * unit, axis=-1, keepdims=True))
    gmid_ref[...] = grad_mid
    branch = grad_mid.astype(BF)
    branch_ref[...] = branch
    ga_ref[...] = dot_nt(branch, wo_ref[...]).astype(BF)


def sort_rows(place_ref, value, out_ref):
    owners = place_ref.shape[0]
    rows = value.shape[0] // owners
    for b in range(owners):
        out_ref[pl.ds(pl.multiple_of(place_ref[b] * rows, rows), rows), :] = value[b * rows : (b + 1) * rows]


def moe_bwd(cot, middle, gain_moe, normed_moe, chances, wr_t, code, code_t, w_out, slots):
    rows, width = cot.shape
    arrays, found = distinct(slots)
    args = (cot, middle, gain_moe[None], normed_moe, chances, wr_t, code, code_t, w_out, *arrays)
    wide = jax.ShapeDtypeStruct((rows, width), BF)
    return call(
        functools.partial(moe_bwd_kernel, slots=found),
        args,
        [pl.BlockSpec(memory_space=pltpu.VMEM)] * len(args),
        out_shape=[
            jax.ShapeDtypeStruct((rows, width), F32),
            wide,
            wide,
            jax.ShapeDtypeStruct((1, width), F32),
            jax.ShapeDtypeStruct((TAIL, width), F32),
        ],
        cost_estimate=estimate("moe_bwd"),
        name="moe_bwd",
    )


def attn_bwd_kernel(
    qs_ref, k_ref, v_ref, ga_ref, lse_ref, woff_ref, seg_ref,
    dq_ref, dk_ref, dv_ref, dwoff_ref, mask_scr, p_scr, ds_scr,
    *, head_dim,
):
    rows = qs_ref.shape[0]
    blocks = rows // LANES

    @pl.when(pl.program_id(0) == 0)
    def _():
        mask_scr[...] = segment_mask(seg_ref, 0, rows)

    scaled, keys, values, grads = qs_ref[...], k_ref[...], v_ref[...], ga_ref[...]
    q_t, g_t, k_t = scaled.T, grads.T, keys.T
    low_half = lax.broadcasted_iota(jnp.int32, (rows, LANES), 1) < head_dim
    dq_t, dk_parts, dv_parts = [], [], []
    lane = lax.broadcasted_iota(jnp.int32, (1, BAND), 1)
    for h in range(HEAD_GROUP):
        row = woff_ref[0, h : h + 1, :]
        band = band_of(row)
        pair = slice(LANES * (h // 2), LANES * (h // 2 + 1))
        k_pair, v_pair = keys[:, pair], values[:, pair]
        q_only, g_only = only_rows(q_t, h, head_dim), only_rows(g_t, h, head_dim)
        tiles = {}
        for b in range(0, blocks, 2):
            lanes = slice(b * LANES, (b + 2) * LANES)
            s = dot(k_pair, q_only[:, lanes]) + bias_block(band, row, b, 2, blocks) + mask_scr[:, lanes]
            p = jnp.exp(s - lse_ref[0, h : h + 1, lanes])
            dp = dot(v_pair, g_only[:, lanes])
            ds = p * (dp - jnp.sum(p * dp, axis=0, keepdims=True))
            p_scr[:, lanes] = p.astype(BF)
            ds_scr[:, lanes] = ds.astype(BF)
            for q_block in range(2):
                for k_block in range(blocks):
                    d = max(-2, min(2, k_block - b - q_block))
                    tile = ds[k_block * LANES : (k_block + 1) * LANES, q_block * LANES : (q_block + 1) * LANES]
                    tiles[d] = tiles[d] + tile if d in tiles else tile
        skewed = jnp.concatenate([tiles[1], tiles[0], tiles[-1], jnp.zeros_like(tiles[0])], axis=1)
        offsets = diagonal_sums(skewed)
        offsets = offsets + jnp.where(lane == FAR_AFTER, jnp.sum(tiles[2]), 0.0)
        offsets = offsets + jnp.where(lane == FAR_BEFORE, jnp.sum(tiles[-2]), 0.0)
        dwoff_ref[0, h : h + 1, :] = offsets
        p_all, ds_all = p_scr[...], ds_scr[...]
        dv_parts.append(dot(p_all, grads[:, pair]))
        dk_parts.append(dot(ds_all, scaled[:, pair]))
        dq_t.append(dot(k_t[h * head_dim : (h + 1) * head_dim], ds_all))
    dq = jnp.concatenate(dq_t, axis=0).T * head_dim ** (-0.5)
    dq_ref[...] = dq.astype(BF)
    for i in range(HEAD_GROUP // 2):
        pair = slice(LANES * i, LANES * (i + 1))
        dk_ref[:, pair] = jnp.where(low_half, dk_parts[2 * i], dk_parts[2 * i + 1]).astype(BF)
        dv_ref[:, pair] = jnp.where(low_half, dv_parts[2 * i], dv_parts[2 * i + 1]).astype(BF)


def attn_bwd(scaled, keys, values, grad_att, lse, woff, seg):
    rows, width = scaled.shape
    groups = woff.shape[0]
    cols = width // groups
    col_block = pl.BlockSpec((rows, cols), lambda g: (0, g))
    wide = jax.ShapeDtypeStruct((rows, width), BF)
    return call(
        functools.partial(attn_bwd_kernel, head_dim=cols // HEAD_GROUP),
        (scaled, keys, values, grad_att, lse, woff, seg),
        [
            col_block,
            col_block,
            col_block,
            col_block,
            pl.BlockSpec((1, HEAD_GROUP, rows), lambda g: (g, 0, 0)),
            pl.BlockSpec((1, HEAD_GROUP, BAND), lambda g: (g, 0, 0)),
            const_spec(seg.shape),
        ],
        grid=(groups,),
        out_specs=[col_block, col_block, col_block, pl.BlockSpec((1, HEAD_GROUP, BAND), lambda g: (g, 0, 0))],
        out_shape=[wide, wide, wide, jax.ShapeDtypeStruct((groups, HEAD_GROUP, BAND), F32)],
        scratch_shapes=[
            pltpu.VMEM((rows, rows), F32),
            pltpu.VMEM((rows, rows), BF),
            pltpu.VMEM((rows, rows), BF),
        ],
        cost_estimate=estimate("attn_bwd"),
        name="attn_bwd",
    )


def sorted_rows_kernel(pq_ref, pk_ref, tok_ref, gain_ref, att_ref, att_o_ref, out_ref, sort_scr):
    start = tok_ref[...].astype(F32)
    normed_t = (start * rms_scale(start) * gain_ref[...]).T
    attended_t = att_ref[...].astype(F32).T
    sort_rows(pq_ref, attended_t, sort_scr)
    att_o_ref[...] = sort_scr[...].astype(BF)
    for i, place_ref in enumerate((pq_ref, pk_ref)):
        sort_rows(place_ref, normed_t, sort_scr)
        out_ref[i] = sort_scr[...].astype(BF)


def sorted_rows(place_q, place_k, tokens, gain_attn, attended):
    rows, width = tokens.shape
    return call(
        sorted_rows_kernel,
        (place_q, place_k, tokens, gain_attn[None], attended),
        [pl.BlockSpec(memory_space=pltpu.SMEM)] * 2 + [pl.BlockSpec(memory_space=pltpu.VMEM)] * 3,
        out_shape=[jax.ShapeDtypeStruct((width, rows), BF), jax.ShapeDtypeStruct((2, width, rows), BF)],
        scratch_shapes=[pltpu.VMEM((width, rows), F32)],
        cost_estimate=estimate("sorted_rows"),
        name="sorted_rows",
    )


def dense_terms_kernel(att_ref, rows_ref, branch_ref, dq_ref, dk_ref, dv_ref, keep_ref, send_ref):
    half = keep_ref.shape[1]
    for i, d_ref in enumerate((branch_ref, dq_ref, dk_ref, dv_ref)):
        lhs = att_ref[...] if i == 0 else rows_ref[min(i - 1, 1)]
        term = dot(lhs, d_ref[...]).astype(BF)
        keep_ref[i] = term[:half]
        send_ref[i] = term[half:]


def dense_terms(att_t, lhs, branch, dq, dk, dv):
    _, width, rows = lhs.shape
    cols = 256
    col_block = pl.BlockSpec((rows, cols), lambda g: (0, g))
    return call(
        dense_terms_kernel,
        (att_t, lhs, branch, dq, dk, dv),
        [const_spec(att_t.shape), const_spec(lhs.shape)] + [col_block] * 4,
        grid=(width // cols,),
        out_specs=[pl.BlockSpec((4, width // 2, cols), lambda g: (0, 0, g))] * 2,
        out_shape=[jax.ShapeDtypeStruct((4, width // 2, width), BF)] * 2,
        cost_estimate=estimate("dense_terms"),
        name="dense_terms",
    )


def norm_bwd_kernel(
    place_ref, tok_ref, gain_ref, gmid_ref, small_ref, dq_ref, dk_ref, dv_ref, wq_ref, wk_ref, wv_ref,
    tg_ref, keep_ref, send_ref, acc, sort_scr, *, gain_row,
):
    step = pl.program_id(0)
    total = dot_nt(dq_ref[...], wq_ref[...]) + dot_nt(dk_ref[...], wk_ref[...]) + dot_nt(dv_ref[...], wv_ref[...])

    @pl.when(step == 0)
    def _():
        acc[...] = total

    @pl.when(step > 0)
    def _():
        acc[...] += total

    @pl.when(step == pl.num_programs(0) - 1)
    def _():
        grad = acc[...]
        start = tok_ref[...].astype(F32)
        scale = rms_scale(start)
        unit = start * scale
        gain_grad = jnp.sum(grad * unit, axis=0, keepdims=True)
        scaled = grad * gain_ref[...]
        tg_ref[...] = gmid_ref[...] + scale * (scaled - unit * jnp.mean(scaled * unit, axis=-1, keepdims=True))
        small = small_ref[...]
        row = lax.broadcasted_iota(jnp.int32, small.shape, 0)
        small = jnp.where(row == gain_row, gain_grad, small)
        small = jnp.concatenate([small, jnp.zeros((LANES - small.shape[0], small.shape[1]), F32)], axis=0)
        sort_rows(place_ref, small.T, sort_scr)
        half = sort_scr.shape[0] // 2
        keep_ref[...] = sort_scr[0:half].astype(BF)
        send_ref[...] = sort_scr[half:].astype(BF)


def norm_bwd(place, tokens, gain_attn, grad_mid, small, gain_row, dq, dk, dv, w_query, w_key, w_value):
    rows, width = tokens.shape
    cols = 256
    col_block = pl.BlockSpec((rows, cols), lambda g: (0, g))
    weight_block = pl.BlockSpec((width, cols), lambda g: (0, g))
    half = jax.ShapeDtypeStruct((width // 2, LANES), BF)
    return call(
        functools.partial(norm_bwd_kernel, gain_row=gain_row),
        (place, tokens, gain_attn[None], grad_mid, small, dq, dk, dv, w_query, w_key, w_value),
        [pl.BlockSpec(memory_space=pltpu.SMEM)]
        + [const_spec((rows, width)), const_spec((1, width)), const_spec((rows, width)), const_spec(small.shape)]
        + [col_block] * 3
        + [weight_block] * 3,
        grid=(width // cols,),
        out_specs=[const_spec((rows, width)), const_spec(half.shape), const_spec(half.shape)],
        out_shape=[jax.ShapeDtypeStruct((rows, width), F32), half, half],
        scratch_shapes=[pltpu.VMEM((rows, width), F32), pltpu.VMEM((width, LANES), F32)],
        cost_estimate=estimate("norm_bwd"),
        name="norm_bwd",
    )


def last_sums_kernel(token_ref, keep_ref, got_ref, *outs, experts, counts):
    total = keep_ref[...].astype(F32) + got_ref[...].astype(F32)
    width = outs[0].shape[1]
    for i in range(2):
        outs[i][...] = total[i, :, 0:width]
        outs[2 + i][...] = total[i, :, width + LANES :]
    small = total[0, :, width : width + LANES] + token_ref[...]
    outs[4][...] = small[:, 0:experts]
    flat = small.T
    for i, count in enumerate(counts):
        outs[5 + i][...] = flat[TAIL // 2 + i : TAIL // 2 + i + 1, 0:count]


def last_sums(token, keep, got, width, experts, counts):
    rows = keep.shape[1]
    return call(
        functools.partial(last_sums_kernel, experts=experts, counts=counts),
        (token, keep, got),
        [pl.BlockSpec(memory_space=pltpu.VMEM)] * 3,
        out_shape=[jax.ShapeDtypeStruct((rows, width), F32)] * 4
        + [jax.ShapeDtypeStruct((rows, experts), F32)]
        + [jax.ShapeDtypeStruct((1, count), F32) for count in counts],
        cost_estimate=estimate("last_sums"),
        name="last_sums",
    )


def bits_of(size):
    return size.bit_length() - 1


def swap(value, axis, size, mask):
    return lax.ppermute(value, axis, [(i, i ^ mask) for i in range(size)])


def pick(value, index, axis):
    return lax.dynamic_index_in_dim(value, index, axis, keepdims=False)


class Order:
    def __init__(self, token):
        self.token = token

    def enter(self, tree):
        tree, self.token = lax.optimization_barrier((tree, self.token))
        return tree

    leave = enter


def places(me, bits, order):
    key = jnp.arange(1 << bits, dtype=jnp.int32) ^ me
    place = jnp.zeros_like(key)
    for bit in order:
        place = place * 2 + ((key >> bit) & 1)
    return place


class Halving:
    def __init__(self, order, keep, send, dim, route, name):
        self.order, self.keep, self.to_send, self.dim, self.route, self.name = order, keep, send, dim, list(route), name
        self.got = None

    def start(self):
        axis, size, bit = self.route[0]
        with jax.named_scope(f"{self.name}_{axis}{1 << bit}"):
            value = self.order.enter(self.keep if self.to_send is None else self.to_send)
            self.got = swap(value, axis, size, 1 << bit)


def arrive(*units):
    for unit in units:
        unit.got = unit.order.leave(unit.got)


def fold_kernel(*refs, cuts, inputs):
    pairs, outs = refs[:inputs], list(refs[inputs:])
    at = 0
    for dim, last, width in cuts:
        total = []
        for _ in range(width):
            total.append(pairs[at][...].astype(F32) + pairs[at + 1][...].astype(F32))
            at += 2
        if last:
            outs.pop(0)[...] = total[0]
            continue
        rows = total[0].shape[dim] // 2
        for start in (0, rows):
            out = outs.pop(0)
            cut = [lax.slice_in_dim(v, start, start + rows, axis=dim).astype(BF) for v in total]
            if len(out.shape) == len(cut[0].shape):
                at_lane = 0
                for part in cut:
                    out[..., at_lane : at_lane + part.shape[-1]] = part
                    at_lane += part.shape[-1]
            else:
                for i in range(width):
                    out[i] = cut[i]


def fold(*units, hold=()):
    groups = [unit if isinstance(unit, tuple) else (unit,) for unit in units]
    order = groups[0][0].order
    args, cuts, shapes = [], [], []
    for group in groups:
        for unit in group:
            unit.route.pop(0)
            got = order.leave(unit.got)
            args += [unit.keep, got]
        unit = group[0]
        last = unit.to_send is None or not unit.route
        cuts.append((unit.dim, last, len(group)))
        if last:
            shapes.append(jax.ShapeDtypeStruct(got.shape, F32))
        else:
            shape = list(got.shape)
            shape[unit.dim] //= 2
            stacked = len(group) > 1 and len(shape) == 2
            if stacked:
                shape = [len(group)] + shape
            else:
                shape[-1] = sum(member.keep.shape[-1] for member in group)
            shapes += [jax.ShapeDtypeStruct(tuple(shape), BF)] * 2
    args = order.enter(args)
    outs = list(
        call(
            functools.partial(fold_kernel, cuts=cuts, inputs=len(args)),
            args,
            [pl.BlockSpec(memory_space=pltpu.VMEM)] * len(args),
            out_shape=shapes,
            cost_estimate=estimate("fold"),
            name="fold",
        )
    )
    outs = order.leave(outs)
    for group, (_, last, width) in zip(groups, cuts):
        unit = group[0]
        unit.keep = outs.pop(0)
        if not last:
            unit.to_send = outs.pop(0)
        if width > 1 and unit.keep.ndim > group[1].keep.ndim:
            unit.dim += 1
        if unit.route and unit not in hold:
            unit.start()


def fold_first_kernel(keep_ref, got_ref, small_keep_ref, small_got_ref, *outs):
    width = keep_ref.shape[2]
    small = (small_keep_ref[...] + small_got_ref[...]).astype(F32)
    for i in range(keep_ref.shape[0]):
        total = keep_ref[i].astype(F32) + got_ref[i].astype(F32)
        rows = total.shape[0] // 2
        for j in range(2):
            out = outs[i // 2 * 2 + j]
            out[i % 2, :, 0:width] = total[j * rows : (j + 1) * rows].astype(BF)
            if i < 2:
                extra = small[j * rows : (j + 1) * rows] if i == 0 else jnp.zeros((rows, LANES), F32)
                out[i, :, width:] = extra.astype(BF)


def fold_first(keep, got, small_keep, small_got):
    _, rows, width = keep.shape
    shapes = [jax.ShapeDtypeStruct((2, rows // 2, width + extra), BF) for extra in (LANES, LANES, 0, 0)]
    return call(
        fold_first_kernel,
        (keep, got, small_keep, small_got),
        [pl.BlockSpec(memory_space=pltpu.VMEM)] * 4,
        out_shape=shapes,
        cost_estimate=estimate("fold_first"),
        name="fold_first",
    )


class Return:
    def __init__(self, order, low, high, axis, size, name, pieces=False):
        self.order, self.axis, self.size, self.name = order, axis, size, name
        half = low.shape[0]
        self.slots = [(low, i) for i in range(half)] + [(high, i) for i in range(half)]
        self.bit = bits_of(size) - 1
        if pieces:
            self.start_pieces()
        else:
            with jax.named_scope(f"{self.name}{1 << self.bit}"):
                self.got = swap(self.order.enter(high), self.axis, self.size, 1 << self.bit)

    def moving(self):
        return [m for m in range(self.size) if (m >> self.bit) & 1]

    def start_pieces(self):
        self.got = []
        for m in self.moving():
            array, index = self.slots[m]
            with jax.named_scope(f"{self.name}{1 << self.bit}_{m}"):
                self.got.append(swap(self.order.enter(array[index][None]), self.axis, self.size, 1 << self.bit))

    def fold(self):
        got = self.order.leave(self.got)
        for i, m in enumerate(self.moving()):
            self.slots[m] = (got[i], 0) if isinstance(got, list) else (got, i)
        self.bit -= 1
        if self.bit >= 0:
            self.start_pieces()

    def finish(self):
        while self.bit >= 0:
            self.fold()


class Gather:
    def __init__(self, order, value, axis, size, name):
        self.order, self.axis, self.size, self.name = order, axis, size, name
        self.blocks = {0: value}
        self.send(0, size // 2)
        if size > 2:
            self.send(0, 1)

    def send(self, m, bit):
        with jax.named_scope(f"{self.name}{m}_{bit}"):
            self.blocks[m ^ bit] = swap(self.blocks[m], self.axis, self.size, bit)

    def relay(self):
        self.blocks[self.size // 2] = self.order.leave(self.blocks[self.size // 2])
        bit = self.size // 2
        while bit:
            for m in range(0, self.size, 2 * bit):
                if m ^ bit not in self.blocks:
                    self.send(m, bit)
            bit //= 2

    def finish(self):
        self.blocks = self.order.leave(self.blocks)
        return [self.blocks[m] for m in range(self.size)]


def body(
    tokens,
    cotangent,
    gain_attn,
    w_query,
    w_key,
    w_value,
    w_out,
    rel_bias,
    gain_moe,
    w_router,
    w_gate,
    w_up,
    w_down,
    segments,
    routes,
    *,
    dp_size,
    ep_size,
):
    TURNS.clear()
    rows, width = tokens.shape
    buckets, heads = rel_bias.shape
    experts = w_router.shape[1]
    cap = 10 * rows // (4 * experts)
    ff = w_gate.shape[2]
    me = lax.axis_index("expert")

    cots = Gather(None, cotangent, "expert", ep_size, "cot")
    scaled, keys, values, woff, token, code, *filled, payload = attn_first(
        tokens, gain_attn, w_query, w_key, w_value, w_out, rel_bias.T, segments, gain_moe, w_router.T, routes.T
    )
    order = Order(token)
    cots.order = order
    me_ref = me.reshape(1).astype(jnp.int32)

    dp_bits, ep_bits = bits_of(dp_size), bits_of(ep_size)
    dp_me = lax.axis_index("dp")
    dp_order = list(range(dp_bits))
    z_order = [1, 0] + dp_order[2:]
    place_x = places(dp_me, dp_bits, dp_order)
    place_z = places(dp_me, dp_bits, z_order)

    def dp_route(bits):
        return [("dp", dp_size, b) for b in bits]

    dp_part = [ep_bits + b for b in dp_order]
    ep_part = list(range(1, ep_bits))
    q_bits = [0] + ep_part + dp_part
    k_bits = [0] + dp_part[:2] + ep_part + dp_part[2:]
    whole_me = dp_me * ep_size + me

    def route(bits):
        return [("expert", ep_size, b) if b < ep_bits else ("dp", dp_size, b - ep_bits) for b in bits]

    place_q, place_k = [places(whole_me, dp_bits + ep_bits, bits) for bits in (q_bits, k_bits)]

    cots.relay()
    first_half = Gather(order, order.enter(payload), "expert", ep_size, "rows_a")
    attended, lse, middle, normed_moe, chances, payload = order.leave(
        attn_second(tokens, order.enter(scaled), keys, values, w_out, woff, segments, gain_moe, w_router.T, filled)
    )
    second_half = Gather(order, order.enter(payload), "expert", ep_size, "rows_b")
    first_half.relay()
    cots, heads_rows = cots.finish(), first_half.finish()
    blocks = ff // FF_BLOCK
    counts = [blocks - blocks // 2, blocks // 2]
    starts = [sum(counts[:i]) for i in range(len(counts))]
    gh_first, cot_rows = order.leave(cot_hidden(order.enter(me_ref), heads_rows, cots, w_down, cap, starts[1]))
    second_half.relay()
    payloads = [v for pair in zip(heads_rows, second_half.finish()) for v in pair]
    scs, units = [], []

    def expert_part(i, source, filled=()):
        *shared, gate_keep, gate_send, up_keep, up_send, sc, hid, hid_t, gg, gu = order.leave(
            expert_a(
                order.enter(source), gh_second if i else gh_first, starts[i], w_gate, w_up, starts[i], counts[i], filled
            )
        )
        scs.append(sc)
        gate = Halving(order, gate_keep, gate_send, 0, dp_route(z_order), f"gate{i}")
        units.append((gate, Halving(order, up_keep, up_send, 0, dp_route(dp_order), f"up{i}")))
        return shared, (hid, hid_t, gg, gu)

    def by_xor(value):
        return jnp.stack([pick(value, me ^ m, 0) for m in range(experts)])

    def padded(value):
        return jnp.pad(value, ((0, TAIL - experts), (0, 0)))

    (x_all, x_t, gate_all, grad_cots), filled = expert_part(0, (me_ref, place_x, payloads, cot_rows))
    for unit in units[0]:
        unit.start()
    gh_second = order.leave(cot_hidden_more(order.enter(cot_rows), w_down, starts[1]))
    _, (hid, hid_t, gg, gu) = expert_part(1, (x_all, x_t, gate_all), filled)
    for unit in units[1]:
        unit.start()
    back_low, back_high = order.leave(expert_b(order.enter(gg), gu, scs, w_gate, w_up, experts))
    backs = Return(order, back_low, back_high, "expert", ep_size, "grad_rows")
    first, second = units[0][0], units[1][0]
    fold(*units[0])
    down_parts = order.leave(down_grads(order.enter(hid_t), grad_cots, place_z, place_x))
    down_units = tuple(
        Halving(order, down_parts[2 * i], down_parts[2 * i + 1], 0, dp_route(bits), f"down{i}")
        for i, bits in enumerate((z_order, dp_order))
    )
    down = down_units[0]
    fold(*units[1], units[0], hold=units[0])
    code_xor, chances_xor, wr_xor = order.enter((by_xor(code), padded(by_xor(chances)), padded(by_xor(w_router.T))))
    backs.fold()
    att_t, normed_t = order.leave(sorted_rows(place_q, place_k, tokens, gain_attn, order.enter(attended)))
    backs.finish()
    for unit in down_units:
        unit.start()
    grad_mid, branch, grad_att, gain_moe_term, router_term = order.leave(
        moe_bwd(
            cotangent, middle, gain_moe, normed_moe, chances_xor, wr_xor, code_xor, code_xor.T, w_out,
            backs.slots,
        )
    )
    dq, dk, dv, dwoff = order.leave(attn_bwd(scaled, keys, values, order.enter(grad_att), lse, woff, segments))
    arrive(*units[1])
    dense_keep, dense_send = order.leave(dense_terms(att_t, normed_t, branch, order.enter(dq), dk, dv))
    arrive(*down_units)
    core = Halving(order, dense_keep, dense_send, 1, route(q_bits)[:1], "dense")
    core.start()
    first.start()
    fold(*down_units, units[1], hold=units[1])
    devices = dp_size * ep_size
    share = width // devices
    onehot = jnp.asarray(band_onehot(rows, buckets))
    bias_term = jnp.dot(onehot, dwoff.reshape(heads, BAND).T, precision=HIGHEST).reshape(devices, -1)
    bias_share = bias_term.shape[1]
    bias_row = jnp.pad(bias_term, ((0, 0), (0, share - bias_share))).reshape(1, width)
    small = jnp.concatenate(
        [
            jnp.pad(by_xor(router_term), ((0, TAIL // 2 - experts), (0, 0))),
            jnp.zeros((1, width), F32),
            gain_moe_term,
            bias_row,
            jnp.zeros((TAIL // 2 - 3, width), F32),
        ],
        axis=0,
    )
    token_grad, small_keep, small_send = order.leave(
        norm_bwd(
            place_q, tokens, gain_attn, grad_mid, order.enter(small), TAIL // 2, dq, dk, dv, w_query, w_key, w_value
        )
    )
    with jax.named_scope("small_expert1"):
        small_got = swap(order.enter(small_send), "expert", ep_size, 1)
    core_got = order.leave(core.got)
    halves = order.leave(fold_first(order.enter(dense_keep), core_got, small_keep, order.leave(small_got)))
    dense = [
        Halving(order, halves[2 * i], halves[2 * i + 1], 1, route(bits)[1:], name)
        for i, (bits, name) in enumerate(((q_bits, "out_q"), (k_bits, "k_v")))
    ]
    out_q, k_v = dense
    arrive(down, first)
    k_v.start()
    out_q.start()
    second.start()
    prod_low, prod_high = order.leave(produced_rows(order.enter(hid), w_down, experts))
    returned = Return(order, prod_low, prod_high, "expert", ep_size, "produced_rows")
    fold(k_v, out_q, down_units, first, second)
    fold(k_v, out_q)
    while first.route or second.route:
        fold(*[unit for unit in (first, second) if unit.route])
    terms = [first.keep, second.keep]
    gate_grad = order.leave(jnp.concatenate([term[0] for term in terms], axis=1)[None])
    up_grad = order.leave(jnp.concatenate([term[1] for term in terms], axis=1)[None])
    returned.fold()
    returned.finish()
    layer_out = order.leave(layer_output(middle, chances_xor, code_xor.T, returned.slots))
    while len(out_q.route) > 2:
        fold(*[unit for unit in (out_q, k_v, down) if unit.route])
    fold(*[(out_q, k_v)] + ([down] if down.route else []))
    down_grad = order.leave(jnp.concatenate([down.keep[0], down.keep[1]], axis=1)[None])
    pairs = order.leave([out_q.keep, out_q.got])
    out_grad, query_grad, key_grad, value_grad, router_grad, *gains = last_sums(
        order.token, *pairs, width, experts, (share, share, bias_share)
    )
    gain_attn_grad, gain_moe_grad, bias_grad = [value.reshape(-1) for value in gains]
    return (
        layer_out,
        token_grad,
        query_grad,
        key_grad,
        value_grad,
        out_grad,
        gain_attn_grad,
        gain_moe_grad,
        bias_grad,
        router_grad,
        gate_grad,
        up_grad,
        down_grad,
    )


def solution(mesh):
    in_specs = (
        P(("dp", "expert"), None),
        P(("dp", "expert"), None),
        P(),
        P(),
        P(),
        P(),
        P(),
        P(),
        P(),
        P(),
        P("expert", None, None),
        P("expert", None, None),
        P("expert", None, None),
        P(("dp", "expert"), None),
        P(("dp", "expert"), None),
    )
    out_specs = (
        P(("dp", "expert"), None),
        P(("dp", "expert"), None),
        P(("dp", "expert"), None),
        P(("dp", "expert"), None),
        P(("dp", "expert"), None),
        P(("dp", "expert"), None),
        P(("dp", "expert")),
        P(("dp", "expert")),
        P(("dp", "expert")),
        P(("dp", "expert"), None),
        P("expert", "dp", None),
        P("expert", "dp", None),
        P("expert", "dp", None),
    )
    run = functools.partial(body, dp_size=mesh.shape["dp"], ep_size=mesh.shape["expert"])
    return jax.shard_map(run, mesh=mesh, in_specs=in_specs, out_specs=out_specs, check_vma=False)
```

```python
import functools

import jax
import jax.numpy as jnp
import numpy as np
from jax import lax
from jax.experimental import pallas as pl
from jax.experimental.pallas import tpu as pltpu
from jax.sharding import PartitionSpec as P

EPS = 1e-06
HIGHEST = lax.Precision.HIGHEST
LANES = 128
BAND = 4 * LANES
HEAD_GROUP = 4
TAIL = 16
FAR = -1e30
BF = jnp.bfloat16
F32 = jnp.float32
VMEM_LIMIT = 56 * 1024 * 1024


def bucket_of(relative, buckets):
    halfway = buckets // 2
    exact_span = halfway // 2
    distance = np.abs(relative)
    beyond = exact_span + (
        np.log(np.maximum(distance, 1) / exact_span)
        / np.log(128.0 / exact_span)
        * (halfway - exact_span)
    ).astype(np.int64)
    beyond = np.minimum(beyond, halfway - 1)
    return (
        (relative > 0).astype(np.int64) * halfway
        + np.where(distance < exact_span, distance, beyond)
    ).astype(np.int32)


def band_onehot(length, buckets):
    place = np.arange(BAND)
    relative = np.where(place <= 3 * LANES, LANES - place, BAND + LANES - place)
    table = (bucket_of(relative, buckets)[None, :] == np.arange(buckets)[:, None]).astype(np.float32)
    table[:, 3 * LANES] = 0.0
    far = np.arange(LANES, length)
    assert np.all(bucket_of(far, buckets) == bucket_of(far, buckets)[0])
    assert np.all(bucket_of(-far, buckets) == bucket_of(-far, buckets)[0])
    return table


FAR_AFTER = 3 * LANES + 1
FAR_BEFORE = 3 * LANES - 1


def dot(a, b):
    return lax.dot_general(a, b, (((1,), (0,)), ((), ())), preferred_element_type=F32)


def dot_nt(a, b):
    return lax.dot_general(a, b, (((1,), (1,)), ((), ())), preferred_element_type=F32)


def dot_tn(a, b):
    return lax.dot_general(a, b, (((0,), (0,)), ((), ())), preferred_element_type=F32)


def split3(value):
    hi = value.astype(BF)
    rest = value - hi.astype(F32)
    mid = rest.astype(BF)
    low = (rest - mid.astype(F32)).astype(BF)
    return hi, mid, low


def rms_scale(value):
    return lax.rsqrt(jnp.mean(value * value, axis=-1, keepdims=True) + EPS)


def params(**kw):
    return pltpu.CompilerParams(vmem_limit_bytes=VMEM_LIMIT, **kw)


TIMES = {
    ("down_grads", 0): 10.0,
    ("dense_terms", 0): 13.1,
    ("fold", 1): 2.0,
}


TURNS = {}


def estimate(name):
    turn = TURNS.get(name, 0)
    TURNS[name] = turn + 1
    time = TIMES.get((name, turn), 0.1)
    return pl.CostEstimate(flops=int(time * 1.15e9), bytes_accessed=100000, transcendentals=0)


def call(kernel, args, in_specs, **kw):
    return pl.pallas_call(kernel, in_specs=list(in_specs), compiler_params=params(), **kw)(*args)


def whole_specs(args):
    return [const_spec(a.shape) for a in args]


def const_spec(shape):
    return pl.BlockSpec(shape, lambda *_: (0,) * len(shape))


def selector(code_row, rows):
    place = lax.broadcasted_iota(jnp.int32, (rows, code_row.shape[1]), 0)
    return jnp.where(place == code_row, 1.0, 0.0).astype(BF)


def selector_t(code_column, rows):
    place = lax.broadcasted_iota(jnp.int32, (code_column.shape[0], rows), 1)
    return jnp.where(place == code_column, 1.0, 0.0).astype(BF)


def band_of(row):
    return pltpu.roll(jnp.broadcast_to(row, (LANES, BAND)), 0, 1, stride=1, stride_axis=0)


def diagonal_sums(skewed):
    eight = skewed[0:8]
    for start in range(8, LANES, 8):
        eight = eight + pltpu.roll(skewed[start : start + 8], BAND - start, 1)
    total = eight[0:1]
    for row in range(1, 8):
        total = total + pltpu.roll(eight[row : row + 1], BAND - row, 1)
    return total


def bias_block(band, row, first, count, k_blocks):
    far = [jnp.broadcast_to(row[:, at : at + 1], (LANES, LANES)) for at in (FAR_BEFORE, FAR_AFTER)]
    columns = []
    for q_block in range(first, first + count):
        pieces = []
        for k_block in range(k_blocks):
            d = k_block - q_block
            pieces.append(far[1] if d > 1 else far[0] if d < -1 else band[:, LANES * (1 - d) : LANES * (2 - d)])
        columns.append(jnp.concatenate(pieces, axis=0))
    return jnp.concatenate(columns, axis=1)


def only_rows(value, h, head_dim):
    mine = value[h * head_dim : (h + 1) * head_dim]
    none = jnp.zeros_like(mine)
    return jnp.concatenate([mine, none] if h % 2 == 0 else [none, mine], axis=0)


def attend(scaled, keys, values, woff_ref, mask, first, head_dim):
    count = scaled.shape[0] // LANES
    q_t, v_t = scaled.T, values.T
    heads_t, totals = [], []
    for h in range(HEAD_GROUP):
        row = woff_ref[0, h : h + 1, :]
        bias = bias_block(band_of(row), row, first, count, keys.shape[0] // LANES)
        k_pair = keys[:, LANES * (h // 2) : LANES * (h // 2 + 1)]
        s = dot(k_pair, only_rows(q_t, h, head_dim)) + bias + mask
        peak = jnp.max(s, axis=0, keepdims=True)
        p = jnp.exp(s - peak)
        total = jnp.sum(p, axis=0, keepdims=True)
        heads_t.append(dot(v_t[h * head_dim : (h + 1) * head_dim], p.astype(BF)) * (1.0 / total))
        totals.append(peak + jnp.log(total))
    return jnp.concatenate(heads_t, axis=0).T.astype(BF), jnp.concatenate(totals, axis=0)


def slot_codes(routes):
    chosen = routes.astype(F32)
    tokens = chosen.shape[1]
    numbers = lax.broadcasted_iota(jnp.int32, (TAIL // 2, tokens), 0).astype(F32)
    named = jnp.logical_or(numbers == chosen[0:1], numbers == chosen[1:2])
    row = lax.broadcasted_iota(jnp.int32, (tokens, tokens), 0)
    lane = lax.broadcasted_iota(jnp.int32, (tokens, tokens), 1)
    before = jnp.where(row < lane, 1.0, 0.0).astype(BF)
    return jnp.where(named, dot(jnp.where(named, 1.0, 0.0).astype(BF), before), -1.0)


def packed_codes(codes):
    upper = jnp.floor((codes + 1.0) * (1.0 / 16.0))
    return jnp.concatenate([upper, codes + 1.0 - 16.0 * upper], axis=0)


def own_code(me, packed):
    row = lax.broadcasted_iota(jnp.int32, packed.shape, 0)
    weight = jnp.where(row == me, 16.0, jnp.where(row == me + TAIL // 2, 1.0, 0.0))
    return (jnp.sum(packed.astype(F32) * weight, axis=0, keepdims=True) - 1.0).astype(jnp.int32)


def route_rows(mid, gain_ref, wr_ref, experts, nm_ref, ch_ref, payload_ref, codes=None):
    rows = mid.shape[0]
    nm = (mid * rms_scale(mid) * gain_ref[...]).astype(BF)
    nm_ref[...] = nm
    router = jnp.concatenate([wr_ref[...], jnp.zeros((TAIL - experts, nm.shape[1]), BF)], axis=0)
    logits = dot_nt(router, nm)
    live = lax.broadcasted_iota(jnp.int32, logits.shape, 0) < experts
    logits = jnp.where(live, logits, FAR)
    raised = jnp.exp(logits - jnp.max(logits, axis=0, keepdims=True))
    chances = raised / jnp.sum(raised, axis=0, keepdims=True)
    ch_ref[...] = chances
    hi = chances.astype(BF).astype(F32)
    both = jnp.concatenate([hi[: TAIL // 2], (chances - hi)[: TAIL // 2]], axis=0)
    payload_ref[0:rows, :] = nm
    tail = [both] if codes is None else [both, packed_codes(codes)]
    used = sum(v.shape[1] for v in tail)
    tail.append(jnp.zeros((TAIL, nm.shape[1] - used), F32))
    payload_ref[rows:, :] = jnp.concatenate(tail, axis=1).astype(BF)


def segment_mask(seg_ref, first, count):
    seg = seg_ref[...].astype(F32)
    column = jnp.broadcast_to(seg, (8, seg.shape[1])).T[:, 0:1]
    return jnp.where(column == seg[:, first : first + count], 0.0, FAR)


def attn_first_kernel(
    tok_ref, gain_a_ref, wq_ref, wk_ref, wv_ref, wo_ref, bias_ref, onehot_ref, seg_ref, gain_m_ref, wr_ref, routes_ref,
    qs_ref, k_ref, v_ref, woff_ref, token_ref, code_ref, att_ref, lse_ref, mid_ref, nm_ref, ch_ref, payload_ref,
    n_scr, mask_scr, woff_scr, code_scr,
    *, experts, head_dim,
):
    step = pl.program_id(0)
    rows = att_ref.shape[0]

    @pl.when(step == 0)
    def _():
        start = tok_ref[...].astype(F32)
        n_scr[...] = (start * rms_scale(start) * gain_a_ref[...]).astype(BF)
        mid_ref[...] = start[:rows]
        mask_scr[...] = segment_mask(seg_ref, 0, rows)
        token_ref[...] = jnp.where(seg_ref[:, 0:LANES] < 0, 1.0, 0.0)
        codes = slot_codes(routes_ref[...])
        code_scr[...] = codes
        code_ref[...] = codes[:experts].astype(jnp.int32)
        table = onehot_ref[...]
        offsets = sum(dot(part, table) for part in split3(bias_ref[...]))
        for g in range(woff_scr.shape[0]):
            woff_scr[g] = offsets[g * HEAD_GROUP : (g + 1) * HEAD_GROUP]

    woff_ref[0] = woff_scr[step]

    normed = n_scr[...]
    scaled = (dot(normed, wq_ref[...]).astype(BF).astype(F32) * head_dim ** (-0.5)).astype(BF)
    keys = dot(normed, wk_ref[...]).astype(BF)
    values = dot(normed, wv_ref[...]).astype(BF)
    qs_ref[...] = scaled
    k_ref[...] = keys
    v_ref[...] = values
    att, totals = attend(scaled[:rows], keys, values, woff_ref, mask_scr[...], 0, head_dim)
    att_ref[...] = att
    lse_ref[0] = totals
    mid_ref[...] += dot(att, wo_ref[...])

    @pl.when(step == pl.num_programs(0) - 1)
    def _():
        route_rows(mid_ref[...], gain_m_ref, wr_ref, experts, nm_ref, ch_ref, payload_ref, code_scr[...])


def attn_second_kernel(
    tok_ref, qs_ref, k_ref, v_ref, wo_ref, woff_ref, seg_ref, gain_m_ref, wr_ref, *refs, experts, head_dim
):
    att_ref, lse_ref, mid_ref, nm_ref, ch_ref, payload_ref, mask_scr = refs[-7:]
    step = pl.program_id(0)
    rows = att_ref.shape[0]

    @pl.when(step == 0)
    def _():
        mid_ref[...] = tok_ref[...].astype(F32)
        mask_scr[...] = segment_mask(seg_ref, rows, rows)

    att, totals = attend(qs_ref[...], k_ref[...], v_ref[...], woff_ref, mask_scr[...], rows // LANES, head_dim)
    att_ref[...] = att
    lse_ref[0] = totals
    mid_ref[...] += dot(att, wo_ref[...])

    @pl.when(step == pl.num_programs(0) - 1)
    def _():
        route_rows(mid_ref[...], gain_m_ref, wr_ref, experts, nm_ref, ch_ref, payload_ref)


def attn_halves(rows, width, groups, half):
    cols, part = width // groups, rows // 2
    wide = jax.ShapeDtypeStruct((rows, width), BF)
    shapes = [
        wide,
        jax.ShapeDtypeStruct((groups, HEAD_GROUP, rows), F32),
        jax.ShapeDtypeStruct((rows, width), F32),
        wide,
        jax.ShapeDtypeStruct((TAIL, rows), F32),
        jax.ShapeDtypeStruct((part + TAIL, width), BF),
    ]
    specs = [
        pl.BlockSpec((part, cols), lambda g: (half, g)),
        pl.BlockSpec((1, HEAD_GROUP, part), lambda g: (g, 0, half)),
        pl.BlockSpec((part, width), lambda g: (half, 0)),
        pl.BlockSpec((part, width), lambda g: (half, 0)),
        pl.BlockSpec((TAIL, part), lambda g: (0, half)),
        const_spec((part + TAIL, width)),
    ]
    return shapes, specs


def attn_first(tokens, gain_attn, w_query, w_key, w_value, w_out, rel_bias, seg, gain_moe, w_router, routes):
    rows, width = tokens.shape
    heads, buckets = rel_bias.shape
    experts = w_router.shape[0]
    groups = heads // HEAD_GROUP
    cols, part = width // groups, rows // 2
    weight_block = pl.BlockSpec((width, cols), lambda g: (0, g))
    shapes, specs = attn_halves(rows, width, groups, 0)
    wide = jax.ShapeDtypeStruct((rows, width), BF)
    return call(
        functools.partial(attn_first_kernel, experts=experts, head_dim=cols // HEAD_GROUP),
        (tokens, gain_attn[None], w_query, w_key, w_value, w_out, rel_bias, jnp.asarray(band_onehot(rows, buckets)).astype(BF),
         seg, gain_moe[None], w_router, routes),
        [
            const_spec((rows, width)),
            const_spec((1, width)),
            weight_block,
            weight_block,
            weight_block,
            pl.BlockSpec((cols, width), lambda g: (g, 0)),
            const_spec(rel_bias.shape),
            const_spec((buckets, BAND)),
            const_spec(seg.shape),
            const_spec((1, width)),
            const_spec(w_router.shape),
            const_spec(routes.shape),
        ],
        grid=(groups,),
        out_specs=[pl.BlockSpec((rows, cols), lambda g: (0, g))] * 3
        + [pl.BlockSpec((1, HEAD_GROUP, BAND), lambda g: (g, 0, 0)), const_spec((1, LANES)), const_spec((experts, rows))]
        + specs,
        out_shape=[wide] * 3
        + [jax.ShapeDtypeStruct((groups, HEAD_GROUP, BAND), F32), jax.ShapeDtypeStruct((1, LANES), F32)]
        + [jax.ShapeDtypeStruct((experts, rows), jnp.int32)]
        + shapes,
        scratch_shapes=[
            pltpu.VMEM((rows, width), BF),
            pltpu.VMEM((rows, part), F32),
            pltpu.VMEM((groups, HEAD_GROUP, BAND), F32),
            pltpu.VMEM((TAIL // 2, rows), F32),
        ],
        cost_estimate=estimate("attn_first"),
        name="attn_first",
    )


def attn_second(tokens, scaled, keys, values, w_out, woff, seg, gain_moe, w_router, filled):
    rows, width = tokens.shape
    experts = w_router.shape[0]
    groups = woff.shape[0]
    cols, part = width // groups, rows // 2
    col_block = pl.BlockSpec((rows, cols), lambda g: (0, g))
    shapes, specs = attn_halves(rows, width, groups, 1)
    args = (tokens, scaled, keys, values, w_out, woff, seg, gain_moe[None], w_router)
    return call(
        functools.partial(attn_second_kernel, experts=experts, head_dim=cols // HEAD_GROUP),
        (*args, *filled),
        [
            pl.BlockSpec((part, width), lambda g: (1, 0)),
            pl.BlockSpec((part, cols), lambda g: (1, g)),
            col_block,
            col_block,
            pl.BlockSpec((cols, width), lambda g: (g, 0)),
            pl.BlockSpec((1, HEAD_GROUP, BAND), lambda g: (g, 0, 0)),
            const_spec(seg.shape),
            const_spec((1, width)),
            const_spec(w_router.shape),
        ]
        + [pl.BlockSpec(memory_space=pl.ANY)] * len(filled),
        grid=(groups,),
        out_specs=specs,
        out_shape=shapes,
        scratch_shapes=[pltpu.VMEM((rows, part), F32)],
        input_output_aliases={len(args) + i: i for i in range(len(filled))},
        cost_estimate=estimate("attn_second"),
        name="attn_second",
    )


def gelu_parts(gate):
    c0 = np.float32(np.sqrt(2.0 / np.pi))
    c1 = np.float32(0.044715)
    square = gate * gate
    t = jnp.tanh(c0 * gate * (1.0 + c1 * square))
    half = 0.5 * (1.0 + t)
    value = gate * half
    slope = half + 0.5 * gate * (1.0 - t * t) * (c0 * (1.0 + 3.0 * c1 * square))
    return value, slope


FF_BLOCK = 256


def cot_hidden_kernel(me_ref, *refs, experts):
    tail_refs, cot_refs, wd_ref = refs[:experts], refs[experts : 2 * experts], refs[2 * experts]
    out_ref, rows_ref = refs[2 * experts + 1 :]

    @pl.when(pl.program_id(0) == 0)
    def _():
        cap = rows_ref.shape[0] // experts
        tokens = cot_refs[0].shape[0]
        for m, (tail_ref, cot_ref) in enumerate(zip(tail_refs, cot_refs)):
            code = own_code(me_ref[0], tail_ref[:, tokens // 2 : tokens // 2 + tokens])
            rows_ref[m * cap : (m + 1) * cap, :] = dot(selector(code, cap), cot_ref[...]).astype(BF)

    out_ref[...] = dot_nt(rows_ref[...], wd_ref[0]).astype(BF)


def cot_hidden(me, payloads, cots, w_down, cap, count):
    experts = len(cots)
    width = cots[0].shape[1]
    rows = experts * cap
    last = payloads[0].shape[0] // TAIL - 1
    return call(
        functools.partial(cot_hidden_kernel, experts=experts),
        (me, *payloads, *cots, w_down),
        [pl.BlockSpec(memory_space=pltpu.SMEM)]
        + [pl.BlockSpec((TAIL, width), lambda f: (last, 0))] * experts
        + whole_specs(cots)
        + [pl.BlockSpec((1, FF_BLOCK, width), lambda f: (0, f, 0))],
        grid=(count,),
        out_specs=[pl.BlockSpec((rows, FF_BLOCK), lambda f: (0, f)), const_spec((rows, width))],
        out_shape=[jax.ShapeDtypeStruct((rows, count * FF_BLOCK), BF), jax.ShapeDtypeStruct((rows, width), BF)],
        cost_estimate=estimate("cot_hidden"),
        name="cot_hidden",
    )


def cot_hidden_more_kernel(rows_ref, wd_ref, out_ref):
    out_ref[...] = dot_nt(rows_ref[...], wd_ref[0]).astype(BF)


def cot_hidden_more(cot_rows, w_down, first):
    rows, width = cot_rows.shape
    count = w_down.shape[1] // FF_BLOCK - first
    return call(
        cot_hidden_more_kernel,
        (cot_rows, w_down),
        [const_spec((rows, width)), pl.BlockSpec((1, FF_BLOCK, width), lambda f: (0, first + f, 0))],
        grid=(count,),
        out_specs=pl.BlockSpec((rows, FF_BLOCK), lambda f: (0, f)),
        out_shape=jax.ShapeDtypeStruct((rows, count * FF_BLOCK), BF),
        cost_estimate=estimate("cot_hidden_more"),
        name="cot_hidden_more",
    )


ROW_BLOCK = 320


def expert_first(me_ref, place_ref, payloads, cot_ref, x_ref, xt_ref, gate_ref, gc_ref):
    experts = len(payloads) // 2
    cap = x_ref.shape[0] // experts
    part = payloads[0].shape[0] - TAIL
    row = lax.broadcasted_iota(jnp.int32, (TAIL, part), 0)
    mine = jnp.logical_or(row == me_ref[0], row == me_ref[0] + TAIL // 2)
    for m in range(experts):
        code = own_code(me_ref[0], payloads[2 * m][part:, part : 3 * part])
        chosen = selector(code, cap)
        place = slice(m * cap, (m + 1) * cap)
        total = jnp.zeros((cap, x_ref.shape[1]), F32)
        gate = jnp.zeros((cap, 1), F32)
        for i in range(2):
            payload = payloads[2 * m + i]
            part_chosen = chosen[:, i * part : (i + 1) * part]
            total = total + dot(part_chosen, payload[0:part, :])
            chances = jnp.sum(jnp.where(mine, payload[part:, 0:part].astype(F32), 0.0), axis=0, keepdims=True)
            gate = gate + jnp.sum(part_chosen.astype(F32) * chances, axis=1, keepdims=True)
        x_ref[place, :] = total.astype(BF)
        gate_ref[place, :] = jnp.broadcast_to(gate, (cap, LANES))
        gc_ref[place, :] = (cot_ref[place, :].astype(F32) * gate).astype(BF)
    flipped = x_ref[...].T
    owners = place_ref.shape[0]
    rows = flipped.shape[0] // owners
    for b in range(owners):
        at = pl.multiple_of(place_ref[b] * rows, rows)
        xt_ref[pl.ds(at, rows), :] = flipped[b * rows : (b + 1) * rows]


def expert_a_kernel(*refs, experts):
    step = pl.program_id(0)
    if experts:
        me_ref, place_ref = refs[:2]
        payloads = refs[2 : 2 + 2 * experts]
        cot_ref, gh_ref, wg_ref, wu_ref, x_ref, xt_ref, gate_ref, gc_ref = refs[2 + 2 * experts : 10 + 2 * experts]

        @pl.when(step == 0)
        def _():
            expert_first(me_ref, place_ref, payloads, cot_ref, x_ref, xt_ref, gate_ref, gc_ref)

    else:
        x_ref, xt_ref, gate_ref, gh_ref, wg_ref, wu_ref = refs[:6]
    gate_keep_ref, gate_send_ref, up_keep_ref, up_send_ref, sc_ref, hid_ref, hidt_ref, gg_ref, gu_ref = refs[-9:]

    @pl.when(step == 0)
    def _():
        sc_ref[...] = jnp.zeros_like(sc_ref)

    wg, wu = wg_ref[0], wu_ref[0]
    width = wg.shape[1]
    for start in range(0, x_ref.shape[0], ROW_BLOCK):
        part = slice(start, start + ROW_BLOCK)
        x = x_ref[part, :]
        gate_pre = dot(x, wg)
        up_pre = dot(x, wu)
        grad = gh_ref[part, :].astype(F32)
        act, slope = gelu_parts(gate_pre)
        hidden = act * up_pre
        hid_ref[part, :] = hidden.astype(BF)
        product = hidden * grad
        folded = product[:, 0:LANES]
        for i in range(1, width // LANES):
            folded = folded + product[:, i * LANES : (i + 1) * LANES]
        sc_ref[part, :] += folded
        grad = grad * gate_ref[part, 0:1]
        gg_ref[part, :] = (slope * up_pre * grad).astype(BF)
        gu_ref[part, :] = (act * grad).astype(BF)
    hidt_ref[...] = hid_ref[...].T
    xt = xt_ref[...]
    cut = xt.shape[0] // 4
    for grad_ref, keep_ref, send_ref, second in ((gg_ref, gate_keep_ref, gate_send_ref, 1), (gu_ref, up_keep_ref, up_send_ref, 0)):
        term = dot(xt, grad_ref[...]).astype(BF)
        for q in range(4):
            upper, lower = (q % 2, q // 2) if second else (q // 2, q % 2)
            (send_ref if upper else keep_ref)[lower * cut : (lower + 1) * cut] = term[q * cut : (q + 1) * cut]


def expert_a(source, gh, gh_first, w_gate, w_up, first, count, filled=()):
    opening = 0 if filled else len(source[2]) // 2
    rows = gh.shape[0]
    width, ff = w_gate.shape[1:]
    span = count * FF_BLOCK
    col_weight = pl.BlockSpec((1, width, FF_BLOCK), lambda f: (0, 0, first + f))
    out_block = pl.BlockSpec((rows, FF_BLOCK), lambda f: (0, first + f))
    wide = jax.ShapeDtypeStruct((rows, ff), BF)
    tall = jax.ShapeDtypeStruct((ff, rows), BF)
    term = jax.ShapeDtypeStruct((width // 2, span), BF)
    term_block = pl.BlockSpec((width // 2, FF_BLOCK), lambda f: (0, f))
    if opening:
        me, place, payloads, cot_rows = source
        args = (me, place, *payloads, cot_rows)
        specs = [pl.BlockSpec(memory_space=pltpu.SMEM)] * 2 + whole_specs((*payloads, cot_rows))
        shared = [
            jax.ShapeDtypeStruct((rows, width), BF),
            jax.ShapeDtypeStruct((width, rows), BF),
            jax.ShapeDtypeStruct((rows, LANES), F32),
            jax.ShapeDtypeStruct((rows, width), BF),
        ]
    else:
        args = tuple(source)
        specs = whole_specs(source)
        shared = []
    args = (*args, gh, w_gate, w_up)
    used = len(args)
    first_filled = len(shared) + 5

    def run(*refs):
        expert_a_kernel(*refs[:used], *refs[used + len(filled) :], experts=opening)

    return call(
        run,
        (*args, *filled),
        specs
        + [pl.BlockSpec((rows, FF_BLOCK), lambda f: (0, first - gh_first + f)), col_weight, col_weight]
        + [pl.BlockSpec(memory_space=pl.ANY)] * len(filled),
        grid=(count,),
        out_specs=whole_specs(shared)
        + [term_block] * 4
        + [const_spec((rows, LANES)), out_block]
        + [pl.BlockSpec((FF_BLOCK, rows), lambda f: (first + f, 0)), out_block, out_block],
        out_shape=shared + [term] * 4 + [jax.ShapeDtypeStruct((rows, LANES), F32), wide, tall, wide, wide],
        input_output_aliases={used + i: first_filled + i for i in range(len(filled))},
        cost_estimate=estimate("expert_grads"),
        name="expert_grads",
    )


def expert_b_kernel(gg_ref, gu_ref, *refs, cap, experts):
    count = experts // 2 + 4
    sc_refs, (wg_ref, wu_ref, *outs, acc) = refs[:-count], refs[-count:]
    part_sum = dot_nt(gg_ref[...], wg_ref[0]) + dot_nt(gu_ref[...], wu_ref[0])
    step, block = pl.program_id(0), pl.program_id(1)

    @pl.when(step == 0)
    def _():
        acc[block] = part_sum

    def finish(out_ref, at):
        total = acc[block] + part_sum
        row = lax.broadcasted_iota(jnp.int32, (cap, cap), 0)
        lane = lax.broadcasted_iota(jnp.int32, (cap, cap), 1)
        place = lax.broadcasted_iota(jnp.int32, (TAIL, cap), 0)
        out_ref[at, 0:cap, :] = total.astype(BF)
        folded = sc_refs[0][...]
        for other in sc_refs[1:]:
            folded = folded + other[...]
        column = jnp.sum(folded, axis=1, keepdims=True)
        flat = jnp.sum(jnp.where(row == lane, column, 0.0), axis=0, keepdims=True)
        hi, mid, low = split3(flat)
        packed = jnp.where(
            place == 0, hi.astype(F32), jnp.where(place == 1, mid.astype(F32), jnp.where(place == 2, low.astype(F32), 0.0))
        )
        out_ref[at, cap : cap + TAIL, :] = jnp.zeros((TAIL, total.shape[1]), BF)
        out_ref[at, cap : cap + TAIL, 0:cap] = packed.astype(BF)

    last = step == pl.num_programs(0) - 1
    half = experts // 2
    for m in range(experts):

        @pl.when(jnp.logical_and(last, block == m))
        def _(m=m):
            finish(outs[m] if m < half else outs[half], 0 if m < half else m - half)


def expert_b(gg, gu, scs, w_gate, w_up, experts):
    rows, ff = gg.shape
    width = w_gate.shape[1]
    cap = rows // experts
    cut = ff // 2
    grads = pl.BlockSpec((cap, cut), lambda k, m: (m, k))
    sums = pl.BlockSpec((cap, LANES), lambda k, m: (m, 0))
    weight = pl.BlockSpec((1, width, cut), lambda k, m: (0, 0, k))
    return call(
        functools.partial(expert_b_kernel, cap=cap, experts=experts),
        (gg, gu, *scs, w_gate, w_up),
        [grads, grads] + [sums] * len(scs) + [weight, weight],
        grid=(2, experts),
        out_specs=[const_spec((1, cap + TAIL, width))] * (experts // 2) + [const_spec((experts // 2, cap + TAIL, width))],
        out_shape=[jax.ShapeDtypeStruct((1, cap + TAIL, width), BF)] * (experts // 2)
        + [jax.ShapeDtypeStruct((experts // 2, cap + TAIL, width), BF)],
        scratch_shapes=[pltpu.VMEM((experts, cap, width), F32)],
        cost_estimate=estimate("expert_input_grad"),
        name="expert_input_grad",
    )


def down_kernel(place_a_ref, place_b_ref, hidt_ref, gc_ref, *outs):
    owners = place_a_ref.shape[0]
    shard = 2 * outs[0].shape[0] // owners
    size = int(np.gcd(shard, 32))
    rows = hidt_ref.shape[0]
    step = pl.program_id(0)
    total = dot(hidt_ref[...], gc_ref[...]).astype(BF)
    half = total.shape[1] // 2
    for i in range(rows // size):
        row = step * rows + i * size
        owner = row // shard
        piece = total[i * size : (i + 1) * size]
        for keep_ref, send_ref, place_ref, cols in (
            (outs[0], outs[1], place_a_ref, piece[:, :half]),
            (outs[2], outs[3], place_b_ref, piece[:, half:]),
        ):
            place = place_ref[owner]
            at = pl.multiple_of((place % (owners // 2)) * shard + (row - owner * shard), size)

            @pl.when(place < owners // 2)
            def _(keep_ref=keep_ref, at=at, cols=cols):
                keep_ref[pl.ds(at, size), :] = cols

            @pl.when(place >= owners // 2)
            def _(send_ref=send_ref, at=at, cols=cols):
                send_ref[pl.ds(at, size), :] = cols


def down_grads(hid_t, grad_cots, place_a, place_b):
    rows, width = grad_cots.shape
    ff = hid_t.shape[0]
    table = pl.BlockSpec(memory_space=pltpu.SMEM)
    part = jax.ShapeDtypeStruct((ff // 2, width // 2), BF)
    return call(
        down_kernel,
        (place_a, place_b, hid_t, grad_cots),
        [table, table, pl.BlockSpec((ff // 4, rows), lambda f: (f, 0)), const_spec((rows, width))],
        grid=(4,),
        out_specs=[const_spec(part.shape)] * 4,
        out_shape=[part] * 4,
        cost_estimate=estimate("down_grads"),
        name="down_grads",
    )


def produced_kernel(hid_ref, wd_ref, low_ref, high_ref):
    rows = dot(hid_ref[...], wd_ref[0]).astype(BF)
    lower = pl.program_id(0) < pl.num_programs(0) // 2

    @pl.when(lower)
    def _():
        low_ref[0] = rows

    @pl.when(jnp.logical_not(lower))
    def _():
        high_ref[0] = rows


def produced_rows(hid, w_down, experts):
    rows, ff = hid.shape
    width = w_down.shape[2]
    cap, half = rows // experts, experts // 2
    return call(
        produced_kernel,
        (hid, w_down),
        [pl.BlockSpec((cap, ff), lambda m: (m, 0)), const_spec(w_down.shape)],
        grid=(experts,),
        out_specs=[
            pl.BlockSpec((1, cap, width), lambda m: (jnp.minimum(m, half - 1), 0, 0)),
            pl.BlockSpec((1, cap, width), lambda m: (jnp.maximum(m - half, 0), 0, 0)),
        ],
        out_shape=[jax.ShapeDtypeStruct((half, cap, width), BF)] * 2,
        cost_estimate=estimate("produced_rows"),
        name="produced_rows",
    )


def distinct(slots):
    arrays, found = [], []
    for array, index in slots:
        which = next((i for i, other in enumerate(arrays) if other is array), None)
        if which is None:
            which = len(arrays)
            arrays.append(array)
        found.append((which, index))
    return arrays, found


def layer_out_kernel(mid_ref, ch_ref, code_ref, *refs, slots):
    parts, out_ref = refs[:-1], refs[-1]
    cap = parts[0].shape[1]
    total = mid_ref[...]
    chances = ch_ref[...].T
    for m, (which, index) in enumerate(slots):
        picked = dot(selector_t(code_ref[:, m : m + 1], cap), parts[which][index])
        total = total + chances[:, m : m + 1] * picked
    out_ref[...] = total.astype(BF)


def layer_output(middle, chances, code_t, slots):
    rows, width = middle.shape
    arrays, found = distinct(slots)
    args = (middle, chances, code_t, *arrays)
    return call(
        functools.partial(layer_out_kernel, slots=found),
        args,
        [pl.BlockSpec(memory_space=pltpu.VMEM)] * len(args),
        out_shape=jax.ShapeDtypeStruct((rows, width), BF),
        cost_estimate=estimate("layer_output"),
        name="layer_output",
    )


def moe_bwd_kernel(
    cot_ref, mid_ref, gain_ref, nm_ref, ch_ref, wr_ref, code_ref, codet_ref, wo_ref, *refs, slots
):
    backs, (gmid_ref, branch_ref, ga_ref, gain_o_ref, router_o_ref) = refs[:-5], refs[-5:]
    experts, cap = len(slots), backs[0].shape[1] - TAIL
    rows = cot_ref.shape[0]
    grad = jnp.zeros(mid_ref.shape, F32)
    gate_rows = []
    for m, (which, index) in enumerate(slots):
        grad = grad + dot(selector_t(codet_ref[:, m : m + 1], cap), backs[which][index, 0:cap, :])
        picked = dot(backs[which][index, cap : cap + TAIL, 0:cap], selector(code_ref[m : m + 1, :], cap))
        gate_rows.append(jnp.sum(picked, axis=0, keepdims=True))
    gate_rows.append(jnp.zeros((TAIL - experts, rows), F32))
    grad_chances = jnp.concatenate(gate_rows, axis=0)
    chances = ch_ref[...]
    grad_logits = chances * (grad_chances - jnp.sum(chances * grad_chances, axis=0, keepdims=True))
    pieces = jnp.concatenate(split3(grad_logits), axis=0)
    wr = wr_ref[...]
    grad = grad + dot_tn(pieces, jnp.concatenate([wr, wr, wr], axis=0))
    router = dot(pieces, nm_ref[...])
    router_o_ref[...] = router[0:TAIL] + router[TAIL : 2 * TAIL] + router[2 * TAIL : 3 * TAIL]
    mid = mid_ref[...]
    scale = rms_scale(mid)
    unit = mid * scale
    gain_o_ref[...] = jnp.sum(grad * unit, axis=0, keepdims=True)
    scaled = grad * gain_ref[...]
    grad_mid = cot_ref[...].astype(F32) + scale * (scaled - unit * jnp.mean(scaled * unit, axis=-1, keepdims=True))
    gmid_ref[...] = grad_mid
    branch = grad_mid.astype(BF)
    branch_ref[...] = branch
    ga_ref[...] = dot_nt(branch, wo_ref[...]).astype(BF)


def sort_rows(place_ref, value, out_ref):
    owners = place_ref.shape[0]
    rows = value.shape[0] // owners
    for b in range(owners):
        out_ref[pl.ds(pl.multiple_of(place_ref[b] * rows, rows), rows), :] = value[b * rows : (b + 1) * rows]


def moe_bwd(cot, middle, gain_moe, normed_moe, chances, wr_t, code, code_t, w_out, slots):
    rows, width = cot.shape
    arrays, found = distinct(slots)
    args = (cot, middle, gain_moe[None], normed_moe, chances, wr_t, code, code_t, w_out, *arrays)
    wide = jax.ShapeDtypeStruct((rows, width), BF)
    return call(
        functools.partial(moe_bwd_kernel, slots=found),
        args,
        [pl.BlockSpec(memory_space=pltpu.VMEM)] * len(args),
        out_shape=[
            jax.ShapeDtypeStruct((rows, width), F32),
            wide,
            wide,
            jax.ShapeDtypeStruct((1, width), F32),
            jax.ShapeDtypeStruct((TAIL, width), F32),
        ],
        cost_estimate=estimate("moe_bwd"),
        name="moe_bwd",
    )


def attn_bwd_kernel(
    qs_ref, k_ref, v_ref, ga_ref, lse_ref, woff_ref, seg_ref,
    dq_ref, dk_ref, dv_ref, dwoff_ref, mask_scr, p_scr, ds_scr,
    *, head_dim,
):
    rows = qs_ref.shape[0]
    blocks = rows // LANES

    @pl.when(pl.program_id(0) == 0)
    def _():
        mask_scr[...] = segment_mask(seg_ref, 0, rows)

    scaled, keys, values, grads = qs_ref[...], k_ref[...], v_ref[...], ga_ref[...]
    q_t, g_t, k_t = scaled.T, grads.T, keys.T
    low_half = lax.broadcasted_iota(jnp.int32, (rows, LANES), 1) < head_dim
    dq_t, dk_parts, dv_parts = [], [], []
    lane = lax.broadcasted_iota(jnp.int32, (1, BAND), 1)
    for h in range(HEAD_GROUP):
        row = woff_ref[0, h : h + 1, :]
        band = band_of(row)
        pair = slice(LANES * (h // 2), LANES * (h // 2 + 1))
        k_pair, v_pair = keys[:, pair], values[:, pair]
        q_only, g_only = only_rows(q_t, h, head_dim), only_rows(g_t, h, head_dim)
        tiles = {}
        for b in range(0, blocks, 2):
            lanes = slice(b * LANES, (b + 2) * LANES)
            s = dot(k_pair, q_only[:, lanes]) + bias_block(band, row, b, 2, blocks) + mask_scr[:, lanes]
            p = jnp.exp(s - lse_ref[0, h : h + 1, lanes])
            dp = dot(v_pair, g_only[:, lanes])
            ds = p * (dp - jnp.sum(p * dp, axis=0, keepdims=True))
            p_scr[:, lanes] = p.astype(BF)
            ds_scr[:, lanes] = ds.astype(BF)
            for q_block in range(2):
                for k_block in range(blocks):
                    d = max(-2, min(2, k_block - b - q_block))
                    tile = ds[k_block * LANES : (k_block + 1) * LANES, q_block * LANES : (q_block + 1) * LANES]
                    tiles[d] = tiles[d] + tile if d in tiles else tile
        skewed = jnp.concatenate([tiles[1], tiles[0], tiles[-1], jnp.zeros_like(tiles[0])], axis=1)
        offsets = diagonal_sums(skewed)
        offsets = offsets + jnp.where(lane == FAR_AFTER, jnp.sum(tiles[2]), 0.0)
        offsets = offsets + jnp.where(lane == FAR_BEFORE, jnp.sum(tiles[-2]), 0.0)
        dwoff_ref[0, h : h + 1, :] = offsets
        p_all, ds_all = p_scr[...], ds_scr[...]
        dv_parts.append(dot(p_all, grads[:, pair]))
        dk_parts.append(dot(ds_all, scaled[:, pair]))
        dq_t.append(dot(k_t[h * head_dim : (h + 1) * head_dim], ds_all))
    dq = jnp.concatenate(dq_t, axis=0).T * head_dim ** (-0.5)
    dq_ref[...] = dq.astype(BF)
    for i in range(HEAD_GROUP // 2):
        pair = slice(LANES * i, LANES * (i + 1))
        dk_ref[:, pair] = jnp.where(low_half, dk_parts[2 * i], dk_parts[2 * i + 1]).astype(BF)
        dv_ref[:, pair] = jnp.where(low_half, dv_parts[2 * i], dv_parts[2 * i + 1]).astype(BF)


def attn_bwd(scaled, keys, values, grad_att, lse, woff, seg):
    rows, width = scaled.shape
    groups = woff.shape[0]
    cols = width // groups
    col_block = pl.BlockSpec((rows, cols), lambda g: (0, g))
    wide = jax.ShapeDtypeStruct((rows, width), BF)
    return call(
        functools.partial(attn_bwd_kernel, head_dim=cols // HEAD_GROUP),
        (scaled, keys, values, grad_att, lse, woff, seg),
        [
            col_block,
            col_block,
            col_block,
            col_block,
            pl.BlockSpec((1, HEAD_GROUP, rows), lambda g: (g, 0, 0)),
            pl.BlockSpec((1, HEAD_GROUP, BAND), lambda g: (g, 0, 0)),
            const_spec(seg.shape),
        ],
        grid=(groups,),
        out_specs=[col_block, col_block, col_block, pl.BlockSpec((1, HEAD_GROUP, BAND), lambda g: (g, 0, 0))],
        out_shape=[wide, wide, wide, jax.ShapeDtypeStruct((groups, HEAD_GROUP, BAND), F32)],
        scratch_shapes=[
            pltpu.VMEM((rows, rows), F32),
            pltpu.VMEM((rows, rows), BF),
            pltpu.VMEM((rows, rows), BF),
        ],
        cost_estimate=estimate("attn_bwd"),
        name="attn_bwd",
    )


def sorted_rows_kernel(pq_ref, pk_ref, tok_ref, gain_ref, att_ref, att_o_ref, out_ref, sort_scr):
    start = tok_ref[...].astype(F32)
    normed_t = (start * rms_scale(start) * gain_ref[...]).T
    attended_t = att_ref[...].astype(F32).T
    sort_rows(pq_ref, attended_t, sort_scr)
    att_o_ref[...] = sort_scr[...].astype(BF)
    for i, place_ref in enumerate((pq_ref, pk_ref)):
        sort_rows(place_ref, normed_t, sort_scr)
        out_ref[i] = sort_scr[...].astype(BF)


def sorted_rows(place_q, place_k, tokens, gain_attn, attended):
    rows, width = tokens.shape
    return call(
        sorted_rows_kernel,
        (place_q, place_k, tokens, gain_attn[None], attended),
        [pl.BlockSpec(memory_space=pltpu.SMEM)] * 2 + [pl.BlockSpec(memory_space=pltpu.VMEM)] * 3,
        out_shape=[jax.ShapeDtypeStruct((width, rows), BF), jax.ShapeDtypeStruct((2, width, rows), BF)],
        scratch_shapes=[pltpu.VMEM((width, rows), F32)],
        cost_estimate=estimate("sorted_rows"),
        name="sorted_rows",
    )


def dense_terms_kernel(att_ref, rows_ref, branch_ref, dq_ref, dk_ref, dv_ref, keep_ref, send_ref):
    half = keep_ref.shape[1]
    for i, d_ref in enumerate((branch_ref, dq_ref, dk_ref, dv_ref)):
        lhs = att_ref[...] if i == 0 else rows_ref[min(i - 1, 1)]
        term = dot(lhs, d_ref[...]).astype(BF)
        keep_ref[i] = term[:half]
        send_ref[i] = term[half:]


def dense_terms(att_t, lhs, branch, dq, dk, dv):
    _, width, rows = lhs.shape
    cols = 256
    col_block = pl.BlockSpec((rows, cols), lambda g: (0, g))
    return call(
        dense_terms_kernel,
        (att_t, lhs, branch, dq, dk, dv),
        [const_spec(att_t.shape), const_spec(lhs.shape)] + [col_block] * 4,
        grid=(width // cols,),
        out_specs=[pl.BlockSpec((4, width // 2, cols), lambda g: (0, 0, g))] * 2,
        out_shape=[jax.ShapeDtypeStruct((4, width // 2, width), BF)] * 2,
        cost_estimate=estimate("dense_terms"),
        name="dense_terms",
    )


def norm_bwd_kernel(
    place_ref, tok_ref, gain_ref, gmid_ref, small_ref, dq_ref, dk_ref, dv_ref, wq_ref, wk_ref, wv_ref,
    tg_ref, keep_ref, send_ref, acc, sort_scr, *, gain_row,
):
    step = pl.program_id(0)
    total = dot_nt(dq_ref[...], wq_ref[...]) + dot_nt(dk_ref[...], wk_ref[...]) + dot_nt(dv_ref[...], wv_ref[...])

    @pl.when(step == 0)
    def _():
        acc[...] = total

    @pl.when(step > 0)
    def _():
        acc[...] += total

    @pl.when(step == pl.num_programs(0) - 1)
    def _():
        grad = acc[...]
        start = tok_ref[...].astype(F32)
        scale = rms_scale(start)
        unit = start * scale
        gain_grad = jnp.sum(grad * unit, axis=0, keepdims=True)
        scaled = grad * gain_ref[...]
        tg_ref[...] = gmid_ref[...] + scale * (scaled - unit * jnp.mean(scaled * unit, axis=-1, keepdims=True))
        small = small_ref[...]
        row = lax.broadcasted_iota(jnp.int32, small.shape, 0)
        small = jnp.where(row == gain_row, gain_grad, small)
        small = jnp.concatenate([small, jnp.zeros((LANES - small.shape[0], small.shape[1]), F32)], axis=0)
        sort_rows(place_ref, small.T, sort_scr)
        half = sort_scr.shape[0] // 2
        keep_ref[...] = sort_scr[0:half].astype(BF)
        send_ref[...] = sort_scr[half:].astype(BF)


def norm_bwd(place, tokens, gain_attn, grad_mid, small, gain_row, dq, dk, dv, w_query, w_key, w_value):
    rows, width = tokens.shape
    cols = 256
    col_block = pl.BlockSpec((rows, cols), lambda g: (0, g))
    weight_block = pl.BlockSpec((width, cols), lambda g: (0, g))
    half = jax.ShapeDtypeStruct((width // 2, LANES), BF)
    return call(
        functools.partial(norm_bwd_kernel, gain_row=gain_row),
        (place, tokens, gain_attn[None], grad_mid, small, dq, dk, dv, w_query, w_key, w_value),
        [pl.BlockSpec(memory_space=pltpu.SMEM)]
        + [const_spec((rows, width)), const_spec((1, width)), const_spec((rows, width)), const_spec(small.shape)]
        + [col_block] * 3
        + [weight_block] * 3,
        grid=(width // cols,),
        out_specs=[const_spec((rows, width)), const_spec(half.shape), const_spec(half.shape)],
        out_shape=[jax.ShapeDtypeStruct((rows, width), F32), half, half],
        scratch_shapes=[pltpu.VMEM((rows, width), F32), pltpu.VMEM((width, LANES), F32)],
        cost_estimate=estimate("norm_bwd"),
        name="norm_bwd",
    )


def last_sums_kernel(token_ref, keep_ref, got_ref, *outs, experts, counts):
    total = keep_ref[...].astype(F32) + got_ref[...].astype(F32)
    width = outs[0].shape[1]
    for i in range(2):
        outs[i][...] = total[i, :, 0:width]
        outs[2 + i][...] = total[i, :, width + LANES :]
    small = total[0, :, width : width + LANES] + token_ref[...]
    outs[4][...] = small[:, 0:experts]
    flat = small.T
    for i, count in enumerate(counts):
        outs[5 + i][...] = flat[TAIL // 2 + i : TAIL // 2 + i + 1, 0:count]


def last_sums(token, keep, got, width, experts, counts):
    rows = keep.shape[1]
    return call(
        functools.partial(last_sums_kernel, experts=experts, counts=counts),
        (token, keep, got),
        [pl.BlockSpec(memory_space=pltpu.VMEM)] * 3,
        out_shape=[jax.ShapeDtypeStruct((rows, width), F32)] * 4
        + [jax.ShapeDtypeStruct((rows, experts), F32)]
        + [jax.ShapeDtypeStruct((1, count), F32) for count in counts],
        cost_estimate=estimate("last_sums"),
        name="last_sums",
    )


def bits_of(size):
    return size.bit_length() - 1


def swap(value, axis, size, mask):
    return lax.ppermute(value, axis, [(i, i ^ mask) for i in range(size)])


def pick(value, index, axis):
    return lax.dynamic_index_in_dim(value, index, axis, keepdims=False)


class Order:
    def __init__(self, token):
        self.token = token

    def enter(self, tree):
        tree, self.token = lax.optimization_barrier((tree, self.token))
        return tree

    leave = enter


def places(me, bits, order):
    key = jnp.arange(1 << bits, dtype=jnp.int32) ^ me
    place = jnp.zeros_like(key)
    for bit in order:
        place = place * 2 + ((key >> bit) & 1)
    return place


class Halving:
    def __init__(self, order, keep, send, dim, route, name):
        self.order, self.keep, self.to_send, self.dim, self.route, self.name = order, keep, send, dim, list(route), name
        self.got = None

    def start(self):
        axis, size, bit = self.route[0]
        with jax.named_scope(f"{self.name}_{axis}{1 << bit}"):
            value = self.order.enter(self.keep if self.to_send is None else self.to_send)
            self.got = swap(value, axis, size, 1 << bit)


def arrive(*units):
    for unit in units:
        unit.got = unit.order.leave(unit.got)


def fold_kernel(*refs, cuts, inputs):
    pairs, outs = refs[:inputs], list(refs[inputs:])
    at = 0
    for dim, last, width in cuts:
        total = []
        for _ in range(width):
            total.append(pairs[at][...].astype(F32) + pairs[at + 1][...].astype(F32))
            at += 2
        if last:
            outs.pop(0)[...] = total[0]
            continue
        rows = total[0].shape[dim] // 2
        for start in (0, rows):
            out = outs.pop(0)
            cut = [lax.slice_in_dim(v, start, start + rows, axis=dim).astype(BF) for v in total]
            if len(out.shape) == len(cut[0].shape):
                at_lane = 0
                for part in cut:
                    out[..., at_lane : at_lane + part.shape[-1]] = part
                    at_lane += part.shape[-1]
            else:
                for i in range(width):
                    out[i] = cut[i]


def fold(*units, hold=()):
    groups = [unit if isinstance(unit, tuple) else (unit,) for unit in units]
    order = groups[0][0].order
    args, cuts, shapes = [], [], []
    for group in groups:
        for unit in group:
            unit.route.pop(0)
            got = order.leave(unit.got)
            args += [unit.keep, got]
        unit = group[0]
        last = unit.to_send is None or not unit.route
        cuts.append((unit.dim, last, len(group)))
        if last:
            shapes.append(jax.ShapeDtypeStruct(got.shape, F32))
        else:
            shape = list(got.shape)
            shape[unit.dim] //= 2
            stacked = len(group) > 1 and len(shape) == 2
            if stacked:
                shape = [len(group)] + shape
            else:
                shape[-1] = sum(member.keep.shape[-1] for member in group)
            shapes += [jax.ShapeDtypeStruct(tuple(shape), BF)] * 2
    args = order.enter(args)
    outs = list(
        call(
            functools.partial(fold_kernel, cuts=cuts, inputs=len(args)),
            args,
            [pl.BlockSpec(memory_space=pltpu.VMEM)] * len(args),
            out_shape=shapes,
            cost_estimate=estimate("fold"),
            name="fold",
        )
    )
    outs = order.leave(outs)
    for group, (_, last, width) in zip(groups, cuts):
        unit = group[0]
        unit.keep = outs.pop(0)
        if not last:
            unit.to_send = outs.pop(0)
        if width > 1 and unit.keep.ndim > group[1].keep.ndim:
            unit.dim += 1
        if unit.route and unit not in hold:
            unit.start()


def fold_first_kernel(keep_ref, got_ref, small_keep_ref, small_got_ref, *outs):
    width = keep_ref.shape[2]
    small = (small_keep_ref[...] + small_got_ref[...]).astype(F32)
    for i in range(keep_ref.shape[0]):
        total = keep_ref[i].astype(F32) + got_ref[i].astype(F32)
        rows = total.shape[0] // 2
        for j in range(2):
            out = outs[i // 2 * 2 + j]
            out[i % 2, :, 0:width] = total[j * rows : (j + 1) * rows].astype(BF)
            if i < 2:
                extra = small[j * rows : (j + 1) * rows] if i == 0 else jnp.zeros((rows, LANES), F32)
                out[i, :, width:] = extra.astype(BF)


def fold_first(keep, got, small_keep, small_got):
    _, rows, width = keep.shape
    shapes = [jax.ShapeDtypeStruct((2, rows // 2, width + extra), BF) for extra in (LANES, LANES, 0, 0)]
    return call(
        fold_first_kernel,
        (keep, got, small_keep, small_got),
        [pl.BlockSpec(memory_space=pltpu.VMEM)] * 4,
        out_shape=shapes,
        cost_estimate=estimate("fold_first"),
        name="fold_first",
    )


class Return:
    def __init__(self, order, low, high, axis, size, name, pieces=False):
        self.order, self.axis, self.size, self.name = order, axis, size, name
        half = high.shape[0]
        low = [(value, 0) for value in low] if isinstance(low, list) else [(low, i) for i in range(half)]
        self.slots = low + [(high, i) for i in range(half)]
        self.bit = bits_of(size) - 1
        if pieces:
            self.start_pieces()
        else:
            with jax.named_scope(f"{self.name}{1 << self.bit}"):
                self.got = swap(self.order.enter(high), self.axis, self.size, 1 << self.bit)

    def moving(self):
        return [m for m in range(self.size) if (m >> self.bit) & 1]

    def start_pieces(self):
        self.got = []
        for m in self.moving():
            array, index = self.slots[m]
            with jax.named_scope(f"{self.name}{1 << self.bit}_{m}"):
                piece = array if array.shape[0] == 1 else array[index][None]
                self.got.append(swap(self.order.enter(piece), self.axis, self.size, 1 << self.bit))

    def fold(self):
        got = self.order.leave(self.got)
        for i, m in enumerate(self.moving()):
            self.slots[m] = (got[i], 0) if isinstance(got, list) else (got, i)
        self.bit -= 1
        if self.bit >= 0:
            self.start_pieces()

    def finish(self):
        while self.bit >= 0:
            self.fold()


class Gather:
    def __init__(self, order, value, axis, size, name):
        self.order, self.axis, self.size, self.name = order, axis, size, name
        self.blocks = {0: value}
        self.send(0, size // 2)
        if size > 2:
            self.send(0, 1)

    def send(self, m, bit):
        with jax.named_scope(f"{self.name}{m}_{bit}"):
            self.blocks[m ^ bit] = swap(self.blocks[m], self.axis, self.size, bit)

    def settle(self):
        self.blocks[1] = self.order.leave(self.blocks[1])

    def relay(self):
        self.blocks[self.size // 2] = self.order.leave(self.blocks[self.size // 2])
        bit = self.size // 2
        while bit:
            for m in range(0, self.size, 2 * bit):
                if m ^ bit not in self.blocks:
                    self.send(m, bit)
            bit //= 2

    def finish(self):
        self.blocks = self.order.leave(self.blocks)
        return [self.blocks[m] for m in range(self.size)]


def body(
    tokens,
    cotangent,
    gain_attn,
    w_query,
    w_key,
    w_value,
    w_out,
    rel_bias,
    gain_moe,
    w_router,
    w_gate,
    w_up,
    w_down,
    segments,
    routes,
    *,
    dp_size,
    ep_size,
):
    TURNS.clear()
    rows, width = tokens.shape
    buckets, heads = rel_bias.shape
    experts = w_router.shape[1]
    cap = 10 * rows // (4 * experts)
    ff = w_gate.shape[2]
    me = lax.axis_index("expert")

    cots = Gather(None, cotangent, "expert", ep_size, "cot")
    scaled, keys, values, woff, token, code, *filled, payload = attn_first(
        tokens, gain_attn, w_query, w_key, w_value, w_out, rel_bias.T, segments, gain_moe, w_router.T, routes.T
    )
    order = Order(token)
    cots.order = order
    me_ref = me.reshape(1).astype(jnp.int32)

    dp_bits, ep_bits = bits_of(dp_size), bits_of(ep_size)
    dp_me = lax.axis_index("dp")
    dp_order = list(range(dp_bits))
    z_order = [1, 0] + dp_order[2:]
    place_x = places(dp_me, dp_bits, dp_order)
    place_z = places(dp_me, dp_bits, z_order)

    def dp_route(bits):
        return [("dp", dp_size, b) for b in bits]

    dp_part = [ep_bits + b for b in dp_order]
    ep_part = list(range(1, ep_bits))
    q_bits = [0] + ep_part + dp_part
    k_bits = [0] + dp_part[:2] + ep_part + dp_part[2:]
    whole_me = dp_me * ep_size + me

    def route(bits):
        return [("expert", ep_size, b) if b < ep_bits else ("dp", dp_size, b - ep_bits) for b in bits]

    place_q, place_k = [places(whole_me, dp_bits + ep_bits, bits) for bits in (q_bits, k_bits)]

    first_half = Gather(order, order.enter(payload), "expert", ep_size, "rows_a")
    attended, lse, middle, normed_moe, chances, payload = order.leave(
        attn_second(tokens, order.enter(scaled), keys, values, w_out, woff, segments, gain_moe, w_router.T, filled)
    )
    cots.settle()
    first_half.settle()
    second_half = Gather(order, order.enter(payload), "expert", ep_size, "rows_b")
    first_half.relay()
    cots.relay()
    cots, heads_rows = cots.finish(), first_half.finish()
    blocks = ff // FF_BLOCK
    counts = [blocks - blocks // 2, blocks // 2]
    starts = [sum(counts[:i]) for i in range(len(counts))]
    gh_first, cot_rows = order.leave(cot_hidden(order.enter(me_ref), heads_rows, cots, w_down, cap, starts[1]))
    second_half.relay()
    payloads = [v for pair in zip(heads_rows, second_half.finish()) for v in pair]
    scs, units = [], []

    def expert_part(i, source, filled=()):
        *shared, gate_keep, gate_send, up_keep, up_send, sc, hid, hid_t, gg, gu = order.leave(
            expert_a(
                order.enter(source), gh_second if i else gh_first, starts[i], w_gate, w_up, starts[i], counts[i], filled
            )
        )
        scs.append(sc)
        gate = Halving(order, gate_keep, gate_send, 0, dp_route(z_order), f"gate{i}")
        units.append((gate, Halving(order, up_keep, up_send, 0, dp_route(dp_order), f"up{i}")))
        return shared, (hid, hid_t, gg, gu)

    def by_xor(value):
        return jnp.stack([pick(value, me ^ m, 0) for m in range(experts)])

    def padded(value):
        return jnp.pad(value, ((0, TAIL - experts), (0, 0)))

    (x_all, x_t, gate_all, grad_cots), filled = expert_part(0, (me_ref, place_x, payloads, cot_rows))
    for unit in units[0]:
        unit.start()
    gh_second = order.leave(cot_hidden_more(order.enter(cot_rows), w_down, starts[1]))
    _, (hid, hid_t, gg, gu) = expert_part(1, (x_all, x_t, gate_all), filled)
    for unit in units[1]:
        unit.start()
    *back_low, back_high = order.leave(expert_b(order.enter(gg), gu, scs, w_gate, w_up, experts))
    backs = Return(order, back_low, back_high, "expert", ep_size, "grad_rows")
    first, second = units[0][0], units[1][0]
    fold(*units[0])
    down_parts = order.leave(down_grads(order.enter(hid_t), grad_cots, place_z, place_x))
    down_units = tuple(
        Halving(order, down_parts[2 * i], down_parts[2 * i + 1], 0, dp_route(bits), f"down{i}")
        for i, bits in enumerate((z_order, dp_order))
    )
    down = down_units[0]
    fold(*units[1], units[0], hold=units[0])
    code_xor, chances_xor, wr_xor = order.enter((by_xor(code), padded(by_xor(chances)), padded(by_xor(w_router.T))))
    backs.fold()
    att_t, normed_t = order.leave(sorted_rows(place_q, place_k, tokens, gain_attn, order.enter(attended)))
    backs.finish()
    for unit in down_units:
        unit.start()
    grad_mid, branch, grad_att, gain_moe_term, router_term = order.leave(
        moe_bwd(
            cotangent, middle, gain_moe, normed_moe, chances_xor, wr_xor, code_xor, code_xor.T, w_out,
            backs.slots,
        )
    )
    dq, dk, dv, dwoff = order.leave(attn_bwd(scaled, keys, values, order.enter(grad_att), lse, woff, segments))
    arrive(*units[1])
    dense_keep, dense_send = order.leave(dense_terms(att_t, normed_t, branch, order.enter(dq), dk, dv))
    arrive(*down_units)
    core = Halving(order, dense_keep, dense_send, 1, route(q_bits)[:1], "dense")
    core.start()
    first.start()
    fold(*down_units, units[1], hold=units[1])
    devices = dp_size * ep_size
    share = width // devices
    onehot = jnp.asarray(band_onehot(rows, buckets))
    bias_term = jnp.dot(onehot, dwoff.reshape(heads, BAND).T, precision=HIGHEST).reshape(devices, -1)
    bias_share = bias_term.shape[1]
    bias_row = jnp.pad(bias_term, ((0, 0), (0, share - bias_share))).reshape(1, width)
    small = jnp.concatenate(
        [
            jnp.pad(by_xor(router_term), ((0, TAIL // 2 - experts), (0, 0))),
            jnp.zeros((1, width), F32),
            gain_moe_term,
            bias_row,
            jnp.zeros((TAIL // 2 - 3, width), F32),
        ],
        axis=0,
    )
    token_grad, small_keep, small_send = order.leave(
        norm_bwd(
            place_q, tokens, gain_attn, grad_mid, order.enter(small), TAIL // 2, dq, dk, dv, w_query, w_key, w_value
        )
    )
    with jax.named_scope("small_expert1"):
        small_got = swap(order.enter(small_send), "expert", ep_size, 1)
    core_got = order.leave(core.got)
    halves = order.leave(fold_first(order.enter(dense_keep), core_got, small_keep, order.leave(small_got)))
    dense = [
        Halving(order, halves[2 * i], halves[2 * i + 1], 1, route(bits)[1:], name)
        for i, (bits, name) in enumerate(((q_bits, "out_q"), (k_bits, "k_v")))
    ]
    out_q, k_v = dense
    arrive(down, first)
    k_v.start()
    out_q.start()
    second.start()
    prod_low, prod_high = order.leave(produced_rows(order.enter(hid), w_down, experts))
    returned = Return(order, prod_low, prod_high, "expert", ep_size, "produced_rows")
    fold(k_v, out_q, down_units, first, second)
    fold(k_v, out_q)
    while first.route or second.route:
        fold(*[unit for unit in (first, second) if unit.route])
    terms = [first.keep, second.keep]
    gate_grad = order.leave(jnp.concatenate([term[0] for term in terms], axis=1)[None])
    up_grad = order.leave(jnp.concatenate([term[1] for term in terms], axis=1)[None])
    returned.fold()
    returned.finish()
    layer_out = order.leave(layer_output(middle, chances_xor, code_xor.T, returned.slots))
    while len(out_q.route) > 2:
        fold(*[unit for unit in (out_q, k_v, down) if unit.route])
    fold(*[(out_q, k_v)] + ([down] if down.route else []))
    down_grad = order.leave(jnp.concatenate([down.keep[0], down.keep[1]], axis=1)[None])
    pairs = order.leave([out_q.keep, out_q.got])
    out_grad, query_grad, key_grad, value_grad, router_grad, *gains = last_sums(
        order.token, *pairs, width, experts, (share, share, bias_share)
    )
    gain_attn_grad, gain_moe_grad, bias_grad = [value.reshape(-1) for value in gains]
    return (
        layer_out,
        token_grad,
        query_grad,
        key_grad,
        value_grad,
        out_grad,
        gain_attn_grad,
        gain_moe_grad,
        bias_grad,
        router_grad,
        gate_grad,
        up_grad,
        down_grad,
    )


def solution(mesh):
    in_specs = (
        P(("dp", "expert"), None),
        P(("dp", "expert"), None),
        P(),
        P(),
        P(),
        P(),
        P(),
        P(),
        P(),
        P(),
        P("expert", None, None),
        P("expert", None, None),
        P("expert", None, None),
        P(("dp", "expert"), None),
        P(("dp", "expert"), None),
    )
    out_specs = (
        P(("dp", "expert"), None),
        P(("dp", "expert"), None),
        P(("dp", "expert"), None),
        P(("dp", "expert"), None),
        P(("dp", "expert"), None),
        P(("dp", "expert"), None),
        P(("dp", "expert")),
        P(("dp", "expert")),
        P(("dp", "expert")),
        P(("dp", "expert"), None),
        P("expert", "dp", None),
        P("expert", "dp", None),
        P("expert", "dp", None),
    )
    run = functools.partial(body, dp_size=mesh.shape["dp"], ep_size=mesh.shape["expert"])
    return jax.shard_map(run, mesh=mesh, in_specs=in_specs, out_specs=out_specs, check_vma=False)
```

```python
import functools

import jax
import jax.numpy as jnp
import numpy as np
from jax import lax
from jax.experimental import pallas as pl
from jax.experimental.pallas import tpu as pltpu
from jax.sharding import PartitionSpec as P

EPS = 1e-06
HIGHEST = lax.Precision.HIGHEST
LANES = 128
BAND = 4 * LANES
HEAD_GROUP = 4
TAIL = 16
FAR = -1e30
BF = jnp.bfloat16
F32 = jnp.float32
VMEM_LIMIT = 56 * 1024 * 1024


def bucket_of(relative, buckets):
    halfway = buckets // 2
    exact_span = halfway // 2
    distance = np.abs(relative)
    beyond = exact_span + (
        np.log(np.maximum(distance, 1) / exact_span)
        / np.log(128.0 / exact_span)
        * (halfway - exact_span)
    ).astype(np.int64)
    beyond = np.minimum(beyond, halfway - 1)
    return (
        (relative > 0).astype(np.int64) * halfway
        + np.where(distance < exact_span, distance, beyond)
    ).astype(np.int32)


def band_onehot(length, buckets):
    place = np.arange(BAND)
    relative = np.where(place <= 3 * LANES, LANES - place, BAND + LANES - place)
    table = (bucket_of(relative, buckets)[None, :] == np.arange(buckets)[:, None]).astype(np.float32)
    table[:, 3 * LANES] = 0.0
    far = np.arange(LANES, length)
    assert np.all(bucket_of(far, buckets) == bucket_of(far, buckets)[0])
    assert np.all(bucket_of(-far, buckets) == bucket_of(-far, buckets)[0])
    return table


FAR_AFTER = 3 * LANES + 1
FAR_BEFORE = 3 * LANES - 1


def dot(a, b):
    return lax.dot_general(a, b, (((1,), (0,)), ((), ())), preferred_element_type=F32)


def dot_nt(a, b):
    return lax.dot_general(a, b, (((1,), (1,)), ((), ())), preferred_element_type=F32)


def dot_tn(a, b):
    return lax.dot_general(a, b, (((0,), (0,)), ((), ())), preferred_element_type=F32)


def split3(value):
    hi = value.astype(BF)
    rest = value - hi.astype(F32)
    mid = rest.astype(BF)
    low = (rest - mid.astype(F32)).astype(BF)
    return hi, mid, low


def rms_scale(value):
    return lax.rsqrt(jnp.mean(value * value, axis=-1, keepdims=True) + EPS)


def params(**kw):
    return pltpu.CompilerParams(vmem_limit_bytes=VMEM_LIMIT, **kw)


TIMES = {
    ("down_grads", 0): 10.0,
    ("dense_terms", 0): 13.1,
    ("fold", 1): 2.0,
}


TURNS = {}


def estimate(name):
    turn = TURNS.get(name, 0)
    TURNS[name] = turn + 1
    time = TIMES.get((name, turn), 0.1)
    return pl.CostEstimate(flops=int(time * 1.15e9), bytes_accessed=100000, transcendentals=0)


def call(kernel, args, in_specs, **kw):
    return pl.pallas_call(kernel, in_specs=list(in_specs), compiler_params=params(), **kw)(*args)


def whole_specs(args):
    return [const_spec(a.shape) for a in args]


def const_spec(shape):
    return pl.BlockSpec(shape, lambda *_: (0,) * len(shape))


def selector(code_row, rows):
    place = lax.broadcasted_iota(jnp.int32, (rows, code_row.shape[1]), 0)
    return jnp.where(place == code_row, 1.0, 0.0).astype(BF)


def selector_t(code_column, rows):
    place = lax.broadcasted_iota(jnp.int32, (code_column.shape[0], rows), 1)
    return jnp.where(place == code_column, 1.0, 0.0).astype(BF)


def band_of(row):
    return pltpu.roll(jnp.broadcast_to(row, (LANES, BAND)), 0, 1, stride=1, stride_axis=0)


def diagonal_sums(skewed):
    eight = skewed[0:8]
    for start in range(8, LANES, 8):
        eight = eight + pltpu.roll(skewed[start : start + 8], BAND - start, 1)
    total = eight[0:1]
    for row in range(1, 8):
        total = total + pltpu.roll(eight[row : row + 1], BAND - row, 1)
    return total


def bias_block(band, row, first, count, k_blocks):
    far = [jnp.broadcast_to(row[:, at : at + 1], (LANES, LANES)) for at in (FAR_BEFORE, FAR_AFTER)]
    columns = []
    for q_block in range(first, first + count):
        pieces = []
        for k_block in range(k_blocks):
            d = k_block - q_block
            pieces.append(far[1] if d > 1 else far[0] if d < -1 else band[:, LANES * (1 - d) : LANES * (2 - d)])
        columns.append(jnp.concatenate(pieces, axis=0))
    return jnp.concatenate(columns, axis=1)


def only_rows(value, h, head_dim):
    mine = value[h * head_dim : (h + 1) * head_dim]
    none = jnp.zeros_like(mine)
    return jnp.concatenate([mine, none] if h % 2 == 0 else [none, mine], axis=0)


def attend(scaled, keys, values, woff_ref, mask, first, head_dim):
    count = scaled.shape[0] // LANES
    q_t, v_t = scaled.T, values.T
    heads_t, totals = [], []
    for h in range(HEAD_GROUP):
        row = woff_ref[0, h : h + 1, :]
        bias = bias_block(band_of(row), row, first, count, keys.shape[0] // LANES)
        k_pair = keys[:, LANES * (h // 2) : LANES * (h // 2 + 1)]
        s = dot(k_pair, only_rows(q_t, h, head_dim)) + bias + mask
        peak = jnp.max(s, axis=0, keepdims=True)
        p = jnp.exp(s - peak)
        total = jnp.sum(p, axis=0, keepdims=True)
        heads_t.append(dot(v_t[h * head_dim : (h + 1) * head_dim], p.astype(BF)) * (1.0 / total))
        totals.append(peak + jnp.log(total))
    return jnp.concatenate(heads_t, axis=0).T.astype(BF), jnp.concatenate(totals, axis=0)


def slot_codes(routes):
    chosen = routes.astype(F32)
    tokens = chosen.shape[1]
    numbers = lax.broadcasted_iota(jnp.int32, (TAIL // 2, tokens), 0).astype(F32)
    named = jnp.logical_or(numbers == chosen[0:1], numbers == chosen[1:2])
    row = lax.broadcasted_iota(jnp.int32, (tokens, tokens), 0)
    lane = lax.broadcasted_iota(jnp.int32, (tokens, tokens), 1)
    before = jnp.where(row < lane, 1.0, 0.0).astype(BF)
    return jnp.where(named, dot(jnp.where(named, 1.0, 0.0).astype(BF), before), -1.0)


def packed_codes(codes):
    upper = jnp.floor((codes + 1.0) * (1.0 / 16.0))
    return jnp.concatenate([upper, codes + 1.0 - 16.0 * upper], axis=0)


def own_code(me, packed):
    row = lax.broadcasted_iota(jnp.int32, packed.shape, 0)
    weight = jnp.where(row == me, 16.0, jnp.where(row == me + TAIL // 2, 1.0, 0.0))
    return (jnp.sum(packed.astype(F32) * weight, axis=0, keepdims=True) - 1.0).astype(jnp.int32)


def route_rows(mid, gain_ref, wr_ref, experts, nm_ref, ch_ref, payload_ref, codes=None):
    rows = mid.shape[0]
    nm = (mid * rms_scale(mid) * gain_ref[...]).astype(BF)
    nm_ref[...] = nm
    router = jnp.concatenate([wr_ref[...].astype(F32), jnp.zeros((TAIL - experts, nm.shape[1]), F32)], axis=0)
    logits = dot_nt(router.astype(BF), nm)
    live = lax.broadcasted_iota(jnp.int32, logits.shape, 0) < experts
    logits = jnp.where(live, logits, FAR)
    raised = jnp.exp(logits - jnp.max(logits, axis=0, keepdims=True))
    chances = raised / jnp.sum(raised, axis=0, keepdims=True)
    ch_ref[...] = chances
    hi = chances.astype(BF).astype(F32)
    both = jnp.concatenate([hi[: TAIL // 2], (chances - hi)[: TAIL // 2]], axis=0)
    payload_ref[0:rows, :] = nm
    tail = [both] if codes is None else [both, packed_codes(codes)]
    used = sum(v.shape[1] for v in tail)
    tail.append(jnp.zeros((TAIL, nm.shape[1] - used), F32))
    payload_ref[rows:, :] = jnp.concatenate(tail, axis=1).astype(BF)


def segment_mask(seg_ref, first, count):
    seg = seg_ref[...].astype(F32)
    column = jnp.broadcast_to(seg, (8, seg.shape[1])).T[:, 0:1]
    return jnp.where(column == seg[:, first : first + count], 0.0, FAR)


def attn_first_kernel(
    tok_ref, gain_a_ref, wq_ref, wk_ref, wv_ref, wo_ref, bias_ref, onehot_ref, seg_ref, gain_m_ref, wr_ref, routes_ref,
    qs_ref, k_ref, v_ref, woff_ref, token_ref, code_ref, att_ref, lse_ref, mid_ref, nm_ref, ch_ref, payload_ref,
    n_scr, mask_scr, woff_scr, code_scr,
    *, experts, head_dim,
):
    step = pl.program_id(0)
    rows = att_ref.shape[0]

    @pl.when(step == 0)
    def _():
        start = tok_ref[...].astype(F32)
        n_scr[...] = (start * rms_scale(start) * gain_a_ref[...]).astype(BF)
        mid_ref[...] = start[:rows]
        mask_scr[...] = segment_mask(seg_ref, 0, rows)
        token_ref[...] = jnp.where(seg_ref[:, 0:LANES] < 0, 1.0, 0.0)
        codes = slot_codes(routes_ref[...])
        code_scr[...] = codes
        code_ref[...] = codes[:experts].astype(jnp.int32)
        table = onehot_ref[...]
        offsets = sum(dot(part, table) for part in split3(bias_ref[...]))
        for g in range(woff_scr.shape[0]):
            woff_scr[g] = offsets[g * HEAD_GROUP : (g + 1) * HEAD_GROUP]

    woff_ref[0] = woff_scr[step]

    normed = n_scr[...]
    scaled = (dot(normed, wq_ref[...]).astype(BF).astype(F32) * head_dim ** (-0.5)).astype(BF)
    keys = dot(normed, wk_ref[...]).astype(BF)
    values = dot(normed, wv_ref[...]).astype(BF)
    qs_ref[...] = scaled
    k_ref[...] = keys
    v_ref[...] = values
    att, totals = attend(scaled[:rows], keys, values, woff_ref, mask_scr[...], 0, head_dim)
    att_ref[...] = att
    lse_ref[0] = totals
    mid_ref[...] += dot(att, wo_ref[...])

    @pl.when(step == pl.num_programs(0) - 1)
    def _():
        route_rows(mid_ref[...], gain_m_ref, wr_ref, experts, nm_ref, ch_ref, payload_ref, code_scr[...])


def attn_second_kernel(
    tok_ref, qs_ref, k_ref, v_ref, wo_ref, woff_ref, seg_ref, gain_m_ref, wr_ref, *refs, experts, head_dim
):
    att_ref, lse_ref, mid_ref, nm_ref, ch_ref, payload_ref, mask_scr = refs[-7:]
    step = pl.program_id(0)
    rows = att_ref.shape[0]

    @pl.when(step == 0)
    def _():
        mid_ref[...] = tok_ref[...].astype(F32)
        mask_scr[...] = segment_mask(seg_ref, rows, rows)

    att, totals = attend(qs_ref[...], k_ref[...], v_ref[...], woff_ref, mask_scr[...], rows // LANES, head_dim)
    att_ref[...] = att
    lse_ref[0] = totals
    mid_ref[...] += dot(att, wo_ref[...])

    @pl.when(step == pl.num_programs(0) - 1)
    def _():
        route_rows(mid_ref[...], gain_m_ref, wr_ref, experts, nm_ref, ch_ref, payload_ref)


def attn_halves(rows, width, groups, half):
    cols, part = width // groups, rows // 2
    wide = jax.ShapeDtypeStruct((rows, width), BF)
    shapes = [
        wide,
        jax.ShapeDtypeStruct((groups, HEAD_GROUP, rows), F32),
        jax.ShapeDtypeStruct((rows, width), F32),
        wide,
        jax.ShapeDtypeStruct((TAIL, rows), F32),
        jax.ShapeDtypeStruct((part + TAIL, width), BF),
    ]
    specs = [
        pl.BlockSpec((part, cols), lambda g: (half, g)),
        pl.BlockSpec((1, HEAD_GROUP, part), lambda g: (g, 0, half)),
        pl.BlockSpec((part, width), lambda g: (half, 0)),
        pl.BlockSpec((part, width), lambda g: (half, 0)),
        pl.BlockSpec((TAIL, part), lambda g: (0, half)),
        const_spec((part + TAIL, width)),
    ]
    return shapes, specs


def attn_first(tokens, gain_attn, w_query, w_key, w_value, w_out, rel_bias, seg, gain_moe, w_router, routes):
    rows, width = tokens.shape
    heads, buckets = rel_bias.shape
    experts = w_router.shape[0]
    groups = heads // HEAD_GROUP
    cols, part = width // groups, rows // 2
    weight_block = pl.BlockSpec((width, cols), lambda g: (0, g))
    shapes, specs = attn_halves(rows, width, groups, 0)
    wide = jax.ShapeDtypeStruct((rows, width), BF)
    return call(
        functools.partial(attn_first_kernel, experts=experts, head_dim=cols // HEAD_GROUP),
        (tokens, gain_attn[None], w_query, w_key, w_value, w_out, rel_bias, jnp.asarray(band_onehot(rows, buckets)).astype(BF),
         seg, gain_moe[None], w_router, routes),
        [
            const_spec((rows, width)),
            const_spec((1, width)),
            weight_block,
            weight_block,
            weight_block,
            pl.BlockSpec((cols, width), lambda g: (g, 0)),
            const_spec(rel_bias.shape),
            const_spec((buckets, BAND)),
            const_spec(seg.shape),
            const_spec((1, width)),
            const_spec(w_router.shape),
            const_spec(routes.shape),
        ],
        grid=(groups,),
        out_specs=[pl.BlockSpec((rows, cols), lambda g: (0, g))] * 3
        + [pl.BlockSpec((1, HEAD_GROUP, BAND), lambda g: (g, 0, 0)), const_spec((1, LANES)), const_spec((experts, rows))]
        + specs,
        out_shape=[wide] * 3
        + [jax.ShapeDtypeStruct((groups, HEAD_GROUP, BAND), F32), jax.ShapeDtypeStruct((1, LANES), F32)]
        + [jax.ShapeDtypeStruct((experts, rows), jnp.int32)]
        + shapes,
        scratch_shapes=[
            pltpu.VMEM((rows, width), BF),
            pltpu.VMEM((rows, part), F32),
            pltpu.VMEM((groups, HEAD_GROUP, BAND), F32),
            pltpu.VMEM((TAIL // 2, rows), F32),
        ],
        cost_estimate=estimate("attn_first"),
        name="attn_first",
    )


def attn_second(tokens, scaled, keys, values, w_out, woff, seg, gain_moe, w_router, filled):
    rows, width = tokens.shape
    experts = w_router.shape[0]
    groups = woff.shape[0]
    cols, part = width // groups, rows // 2
    col_block = pl.BlockSpec((rows, cols), lambda g: (0, g))
    shapes, specs = attn_halves(rows, width, groups, 1)
    args = (tokens, scaled, keys, values, w_out, woff, seg, gain_moe[None], w_router)
    return call(
        functools.partial(attn_second_kernel, experts=experts, head_dim=cols // HEAD_GROUP),
        (*args, *filled),
        [
            pl.BlockSpec((part, width), lambda g: (1, 0)),
            pl.BlockSpec((part, cols), lambda g: (1, g)),
            col_block,
            col_block,
            pl.BlockSpec((cols, width), lambda g: (g, 0)),
            pl.BlockSpec((1, HEAD_GROUP, BAND), lambda g: (g, 0, 0)),
            const_spec(seg.shape),
            const_spec((1, width)),
            const_spec(w_router.shape),
        ]
        + [pl.BlockSpec(memory_space=pl.ANY)] * len(filled),
        grid=(groups,),
        out_specs=specs,
        out_shape=shapes,
        scratch_shapes=[pltpu.VMEM((rows, part), F32)],
        input_output_aliases={len(args) + i: i for i in range(len(filled))},
        cost_estimate=estimate("attn_second"),
        name="attn_second",
    )


def gelu_parts(gate):
    c0 = np.float32(np.sqrt(2.0 / np.pi))
    c1 = np.float32(0.044715)
    square = gate * gate
    t = jnp.tanh(c0 * gate * (1.0 + c1 * square))
    half = 0.5 * (1.0 + t)
    value = gate * half
    slope = half + 0.5 * gate * (1.0 - t * t) * (c0 * (1.0 + 3.0 * c1 * square))
    return value, slope


FF_BLOCK = 256


def cot_hidden_kernel(me_ref, *refs, experts):
    tail_refs, cot_refs, wd_ref = refs[:experts], refs[experts : 2 * experts], refs[2 * experts]
    out_ref, rows_ref = refs[2 * experts + 1 :]

    @pl.when(pl.program_id(0) == 0)
    def _():
        cap = rows_ref.shape[0] // experts
        tokens = cot_refs[0].shape[0]
        for m, (tail_ref, cot_ref) in enumerate(zip(tail_refs, cot_refs)):
            code = own_code(me_ref[0], tail_ref[:, tokens // 2 : tokens // 2 + tokens])
            rows_ref[m * cap : (m + 1) * cap, :] = dot(selector(code, cap), cot_ref[...]).astype(BF)

    out_ref[...] = dot_nt(rows_ref[...], wd_ref[0]).astype(BF)


def cot_hidden(me, payloads, cots, w_down, cap, count):
    experts = len(cots)
    width = cots[0].shape[1]
    rows = experts * cap
    last = payloads[0].shape[0] // TAIL - 1
    return call(
        functools.partial(cot_hidden_kernel, experts=experts),
        (me, *payloads, *cots, w_down),
        [pl.BlockSpec(memory_space=pltpu.SMEM)]
        + [pl.BlockSpec((TAIL, width), lambda f: (last, 0))] * experts
        + whole_specs(cots)
        + [pl.BlockSpec((1, FF_BLOCK, width), lambda f: (0, f, 0))],
        grid=(count,),
        out_specs=[pl.BlockSpec((rows, FF_BLOCK), lambda f: (0, f)), const_spec((rows, width))],
        out_shape=[jax.ShapeDtypeStruct((rows, count * FF_BLOCK), BF), jax.ShapeDtypeStruct((rows, width), BF)],
        cost_estimate=estimate("cot_hidden"),
        name="cot_hidden",
    )


def cot_hidden_more_kernel(rows_ref, wd_ref, out_ref):
    out_ref[...] = dot_nt(rows_ref[...], wd_ref[0]).astype(BF)


def cot_hidden_more(cot_rows, w_down, first):
    rows, width = cot_rows.shape
    count = w_down.shape[1] // FF_BLOCK - first
    return call(
        cot_hidden_more_kernel,
        (cot_rows, w_down),
        [const_spec((rows, width)), pl.BlockSpec((1, FF_BLOCK, width), lambda f: (0, first + f, 0))],
        grid=(count,),
        out_specs=pl.BlockSpec((rows, FF_BLOCK), lambda f: (0, f)),
        out_shape=jax.ShapeDtypeStruct((rows, count * FF_BLOCK), BF),
        cost_estimate=estimate("cot_hidden_more"),
        name="cot_hidden_more",
    )


ROW_BLOCK = 320


def expert_first(me_ref, place_ref, payloads, cot_ref, x_ref, xt_ref, gate_ref, gc_ref):
    experts = len(payloads) // 2
    cap = x_ref.shape[0] // experts
    part = payloads[0].shape[0] - TAIL
    row = lax.broadcasted_iota(jnp.int32, (TAIL, part), 0)
    mine = jnp.logical_or(row == me_ref[0], row == me_ref[0] + TAIL // 2)
    for m in range(experts):
        code = own_code(me_ref[0], payloads[2 * m][part:, part : 3 * part])
        chosen = selector(code, cap)
        place = slice(m * cap, (m + 1) * cap)
        total = jnp.zeros((cap, x_ref.shape[1]), F32)
        gate = jnp.zeros((cap, 1), F32)
        for i in range(2):
            payload = payloads[2 * m + i]
            part_chosen = chosen[:, i * part : (i + 1) * part]
            total = total + dot(part_chosen, payload[0:part, :])
            chances = jnp.sum(jnp.where(mine, payload[part:, 0:part].astype(F32), 0.0), axis=0, keepdims=True)
            gate = gate + jnp.sum(part_chosen.astype(F32) * chances, axis=1, keepdims=True)
        x_ref[place, :] = total.astype(BF)
        gate_ref[place, :] = jnp.broadcast_to(gate, (cap, LANES))
        gc_ref[place, :] = (cot_ref[place, :].astype(F32) * gate).astype(BF)
    flipped = x_ref[...].T
    owners = place_ref.shape[0]
    rows = flipped.shape[0] // owners
    for b in range(owners):
        at = pl.multiple_of(place_ref[b] * rows, rows)
        xt_ref[pl.ds(at, rows), :] = flipped[b * rows : (b + 1) * rows]


def expert_a_kernel(*refs, experts):
    step = pl.program_id(0)
    if experts:
        me_ref, place_ref = refs[:2]
        payloads = refs[2 : 2 + 2 * experts]
        cot_ref, gh_ref, wg_ref, wu_ref, x_ref, xt_ref, gate_ref, gc_ref = refs[2 + 2 * experts : 10 + 2 * experts]

        @pl.when(step == 0)
        def _():
            expert_first(me_ref, place_ref, payloads, cot_ref, x_ref, xt_ref, gate_ref, gc_ref)

    else:
        x_ref, xt_ref, gate_ref, gh_ref, wg_ref, wu_ref = refs[:6]
    gate_keep_ref, gate_send_ref, up_keep_ref, up_send_ref, sc_ref, hid_ref, hidt_ref, gg_ref, gu_ref = refs[-9:]

    @pl.when(step == 0)
    def _():
        sc_ref[...] = jnp.zeros_like(sc_ref)

    wg, wu = wg_ref[0], wu_ref[0]
    width = wg.shape[1]
    for start in range(0, x_ref.shape[0], ROW_BLOCK):
        part = slice(start, start + ROW_BLOCK)
        x = x_ref[part, :]
        gate_pre = dot(x, wg)
        up_pre = dot(x, wu)
        grad = gh_ref[part, :].astype(F32)
        act, slope = gelu_parts(gate_pre)
        hidden = act * up_pre
        hid_ref[part, :] = hidden.astype(BF)
        product = hidden * grad
        folded = product[:, 0:LANES]
        for i in range(1, width // LANES):
            folded = folded + product[:, i * LANES : (i + 1) * LANES]
        sc_ref[part, :] += folded
        grad = grad * gate_ref[part, 0:1]
        gg_ref[part, :] = (slope * up_pre * grad).astype(BF)
        gu_ref[part, :] = (act * grad).astype(BF)
    hidt_ref[...] = hid_ref[...].T
    xt = xt_ref[...]
    cut = xt.shape[0] // 4
    for grad_ref, keep_ref, send_ref, second in ((gg_ref, gate_keep_ref, gate_send_ref, 1), (gu_ref, up_keep_ref, up_send_ref, 0)):
        term = dot(xt, grad_ref[...]).astype(BF)
        for q in range(4):
            upper, lower = (q % 2, q // 2) if second else (q // 2, q % 2)
            (send_ref if upper else keep_ref)[lower * cut : (lower + 1) * cut] = term[q * cut : (q + 1) * cut]


def expert_a(source, gh, gh_first, w_gate, w_up, first, count, filled=()):
    opening = 0 if filled else len(source[2]) // 2
    rows = gh.shape[0]
    width, ff = w_gate.shape[1:]
    span = count * FF_BLOCK
    col_weight = pl.BlockSpec((1, width, FF_BLOCK), lambda f: (0, 0, first + f))
    out_block = pl.BlockSpec((rows, FF_BLOCK), lambda f: (0, first + f))
    wide = jax.ShapeDtypeStruct((rows, ff), BF)
    tall = jax.ShapeDtypeStruct((ff, rows), BF)
    term = jax.ShapeDtypeStruct((width // 2, span), BF)
    term_block = pl.BlockSpec((width // 2, FF_BLOCK), lambda f: (0, f))
    if opening:
        me, place, payloads, cot_rows = source
        args = (me, place, *payloads, cot_rows)
        specs = [pl.BlockSpec(memory_space=pltpu.SMEM)] * 2 + whole_specs((*payloads, cot_rows))
        shared = [
            jax.ShapeDtypeStruct((rows, width), BF),
            jax.ShapeDtypeStruct((width, rows), BF),
            jax.ShapeDtypeStruct((rows, LANES), F32),
            jax.ShapeDtypeStruct((rows, width), BF),
        ]
    else:
        args = tuple(source)
        specs = whole_specs(source)
        shared = []
    args = (*args, gh, w_gate, w_up)
    used = len(args)
    first_filled = len(shared) + 5

    def run(*refs):
        expert_a_kernel(*refs[:used], *refs[used + len(filled) :], experts=opening)

    return call(
        run,
        (*args, *filled),
        specs
        + [pl.BlockSpec((rows, FF_BLOCK), lambda f: (0, first - gh_first + f)), col_weight, col_weight]
        + [pl.BlockSpec(memory_space=pl.ANY)] * len(filled),
        grid=(count,),
        out_specs=whole_specs(shared)
        + [term_block] * 4
        + [const_spec((rows, LANES)), out_block]
        + [pl.BlockSpec((FF_BLOCK, rows), lambda f: (first + f, 0)), out_block, out_block],
        out_shape=shared + [term] * 4 + [jax.ShapeDtypeStruct((rows, LANES), F32), wide, tall, wide, wide],
        input_output_aliases={used + i: first_filled + i for i in range(len(filled))},
        cost_estimate=estimate("expert_grads"),
        name="expert_grads",
    )


def expert_b_kernel(gg_ref, gu_ref, *refs, cap, experts):
    count = experts // 2 + 4
    sc_refs, (wg_ref, wu_ref, *outs, acc) = refs[:-count], refs[-count:]
    part_sum = dot_nt(gg_ref[...], wg_ref[0]) + dot_nt(gu_ref[...], wu_ref[0])
    step, block = pl.program_id(0), pl.program_id(1)

    @pl.when(step == 0)
    def _():
        acc[block] = part_sum

    def finish(out_ref, at):
        total = acc[block] + part_sum
        row = lax.broadcasted_iota(jnp.int32, (cap, cap), 0)
        lane = lax.broadcasted_iota(jnp.int32, (cap, cap), 1)
        place = lax.broadcasted_iota(jnp.int32, (TAIL, cap), 0)
        out_ref[at, 0:cap, :] = total.astype(BF)
        folded = sc_refs[0][...]
        for other in sc_refs[1:]:
            folded = folded + other[...]
        column = jnp.sum(folded, axis=1, keepdims=True)
        flat = jnp.sum(jnp.where(row == lane, column, 0.0), axis=0, keepdims=True)
        hi, mid, low = split3(flat)
        packed = jnp.where(
            place == 0, hi.astype(F32), jnp.where(place == 1, mid.astype(F32), jnp.where(place == 2, low.astype(F32), 0.0))
        )
        out_ref[at, cap : cap + TAIL, :] = jnp.zeros((TAIL, total.shape[1]), BF)
        out_ref[at, cap : cap + TAIL, 0:cap] = packed.astype(BF)

    last = step == pl.num_programs(0) - 1
    half = experts // 2
    for m in range(experts):

        @pl.when(jnp.logical_and(last, block == m))
        def _(m=m):
            finish(outs[m] if m < half else outs[half], 0 if m < half else m - half)


def expert_b(gg, gu, scs, w_gate, w_up, experts):
    rows, ff = gg.shape
    width = w_gate.shape[1]
    cap = rows // experts
    cut = ff // 2
    grads = pl.BlockSpec((cap, cut), lambda k, m: (m, k))
    sums = pl.BlockSpec((cap, LANES), lambda k, m: (m, 0))
    weight = pl.BlockSpec((1, width, cut), lambda k, m: (0, 0, k))
    return call(
        functools.partial(expert_b_kernel, cap=cap, experts=experts),
        (gg, gu, *scs, w_gate, w_up),
        [grads, grads] + [sums] * len(scs) + [weight, weight],
        grid=(2, experts),
        out_specs=[const_spec((1, cap + TAIL, width))] * (experts // 2) + [const_spec((experts // 2, cap + TAIL, width))],
        out_shape=[jax.ShapeDtypeStruct((1, cap + TAIL, width), BF)] * (experts // 2)
        + [jax.ShapeDtypeStruct((experts // 2, cap + TAIL, width), BF)],
        scratch_shapes=[pltpu.VMEM((experts, cap, width), F32)],
        cost_estimate=estimate("expert_input_grad"),
        name="expert_input_grad",
    )


def down_kernel(place_a_ref, place_b_ref, hidt_ref, gc_ref, *outs):
    owners = place_a_ref.shape[0]
    shard = 2 * outs[0].shape[0] // owners
    size = int(np.gcd(shard, 32))
    rows = hidt_ref.shape[0]
    step = pl.program_id(0)
    total = dot(hidt_ref[...], gc_ref[...]).astype(BF)
    half = total.shape[1] // 2
    for i in range(rows // size):
        row = step * rows + i * size
        owner = row // shard
        piece = total[i * size : (i + 1) * size]
        for keep_ref, send_ref, place_ref, cols in (
            (outs[0], outs[1], place_a_ref, piece[:, :half]),
            (outs[2], outs[3], place_b_ref, piece[:, half:]),
        ):
            place = place_ref[owner]
            at = pl.multiple_of((place % (owners // 2)) * shard + (row - owner * shard), size)

            @pl.when(place < owners // 2)
            def _(keep_ref=keep_ref, at=at, cols=cols):
                keep_ref[pl.ds(at, size), :] = cols

            @pl.when(place >= owners // 2)
            def _(send_ref=send_ref, at=at, cols=cols):
                send_ref[pl.ds(at, size), :] = cols


def down_grads(hid_t, grad_cots, place_a, place_b):
    rows, width = grad_cots.shape
    ff = hid_t.shape[0]
    table = pl.BlockSpec(memory_space=pltpu.SMEM)
    part = jax.ShapeDtypeStruct((ff // 2, width // 2), BF)
    return call(
        down_kernel,
        (place_a, place_b, hid_t, grad_cots),
        [table, table, pl.BlockSpec((ff // 4, rows), lambda f: (f, 0)), const_spec((rows, width))],
        grid=(4,),
        out_specs=[const_spec(part.shape)] * 4,
        out_shape=[part] * 4,
        cost_estimate=estimate("down_grads"),
        name="down_grads",
    )


def produced_kernel(hid_ref, wd_ref, low_ref, high_ref):
    rows = dot(hid_ref[...], wd_ref[0]).astype(BF)
    lower = pl.program_id(0) < pl.num_programs(0) // 2

    @pl.when(lower)
    def _():
        low_ref[0] = rows

    @pl.when(jnp.logical_not(lower))
    def _():
        high_ref[0] = rows


def produced_rows(hid, w_down, experts):
    rows, ff = hid.shape
    width = w_down.shape[2]
    cap, half = rows // experts, experts // 2
    return call(
        produced_kernel,
        (hid, w_down),
        [pl.BlockSpec((cap, ff), lambda m: (m, 0)), const_spec(w_down.shape)],
        grid=(experts,),
        out_specs=[
            pl.BlockSpec((1, cap, width), lambda m: (jnp.minimum(m, half - 1), 0, 0)),
            pl.BlockSpec((1, cap, width), lambda m: (jnp.maximum(m - half, 0), 0, 0)),
        ],
        out_shape=[jax.ShapeDtypeStruct((half, cap, width), BF)] * 2,
        cost_estimate=estimate("produced_rows"),
        name="produced_rows",
    )


def distinct(slots):
    arrays, found = [], []
    for array, index in slots:
        which = next((i for i, other in enumerate(arrays) if other is array), None)
        if which is None:
            which = len(arrays)
            arrays.append(array)
        found.append((which, index))
    return arrays, found


def layer_out_kernel(mid_ref, ch_ref, code_ref, *refs, slots):
    parts, out_ref = refs[:-1], refs[-1]
    cap = parts[0].shape[1]
    total = mid_ref[...]
    chances = ch_ref[...].T
    for m, (which, index) in enumerate(slots):
        picked = dot(selector_t(code_ref[:, m : m + 1], cap), parts[which][index])
        total = total + chances[:, m : m + 1] * picked
    out_ref[...] = total.astype(BF)


def layer_output(middle, chances, code_t, slots):
    rows, width = middle.shape
    arrays, found = distinct(slots)
    args = (middle, chances, code_t, *arrays)
    return call(
        functools.partial(layer_out_kernel, slots=found),
        args,
        [pl.BlockSpec(memory_space=pltpu.VMEM)] * len(args),
        out_shape=jax.ShapeDtypeStruct((rows, width), BF),
        cost_estimate=estimate("layer_output"),
        name="layer_output",
    )


def moe_bwd_kernel(
    cot_ref, mid_ref, gain_ref, nm_ref, ch_ref, wr_ref, code_ref, codet_ref, wo_ref, *refs, slots
):
    backs, (gmid_ref, branch_ref, ga_ref, gain_o_ref, router_o_ref) = refs[:-5], refs[-5:]
    experts, cap = len(slots), backs[0].shape[1] - TAIL
    rows = cot_ref.shape[0]
    grad = jnp.zeros(mid_ref.shape, F32)
    gate_rows = []
    for m, (which, index) in enumerate(slots):
        grad = grad + dot(selector_t(codet_ref[:, m : m + 1], cap), backs[which][index, 0:cap, :])
        picked = dot(backs[which][index, cap : cap + TAIL, 0:cap], selector(code_ref[m : m + 1, :], cap))
        gate_rows.append(jnp.sum(picked, axis=0, keepdims=True))
    gate_rows.append(jnp.zeros((TAIL - experts, rows), F32))
    grad_chances = jnp.concatenate(gate_rows, axis=0)
    chances = ch_ref[...]
    grad_logits = chances * (grad_chances - jnp.sum(chances * grad_chances, axis=0, keepdims=True))
    pieces = jnp.concatenate(split3(grad_logits), axis=0)
    wr = wr_ref[...]
    grad = grad + dot_tn(pieces, jnp.concatenate([wr, wr, wr], axis=0))
    router = dot(pieces, nm_ref[...])
    router_o_ref[...] = router[0:TAIL] + router[TAIL : 2 * TAIL] + router[2 * TAIL : 3 * TAIL]
    mid = mid_ref[...]
    scale = rms_scale(mid)
    unit = mid * scale
    gain_o_ref[...] = jnp.sum(grad * unit, axis=0, keepdims=True)
    scaled = grad * gain_ref[...]
    grad_mid = cot_ref[...].astype(F32) + scale * (scaled - unit * jnp.mean(scaled * unit, axis=-1, keepdims=True))
    gmid_ref[...] = grad_mid
    branch = grad_mid.astype(BF)
    branch_ref[...] = branch
    ga_ref[...] = dot_nt(branch, wo_ref[...]).astype(BF)


def sort_rows(place_ref, value, out_ref):
    owners = place_ref.shape[0]
    rows = value.shape[0] // owners
    for b in range(owners):
        out_ref[pl.ds(pl.multiple_of(place_ref[b] * rows, rows), rows), :] = value[b * rows : (b + 1) * rows]


def moe_bwd(cot, middle, gain_moe, normed_moe, chances, wr_t, code, code_t, w_out, slots):
    rows, width = cot.shape
    arrays, found = distinct(slots)
    args = (cot, middle, gain_moe[None], normed_moe, chances, wr_t, code, code_t, w_out, *arrays)
    wide = jax.ShapeDtypeStruct((rows, width), BF)
    return call(
        functools.partial(moe_bwd_kernel, slots=found),
        args,
        [pl.BlockSpec(memory_space=pltpu.VMEM)] * len(args),
        out_shape=[
            jax.ShapeDtypeStruct((rows, width), F32),
            wide,
            wide,
            jax.ShapeDtypeStruct((1, width), F32),
            jax.ShapeDtypeStruct((TAIL, width), F32),
        ],
        cost_estimate=estimate("moe_bwd"),
        name="moe_bwd",
    )


def attn_bwd_kernel(
    qs_ref, k_ref, v_ref, ga_ref, lse_ref, woff_ref, seg_ref,
    dq_ref, dk_ref, dv_ref, dwoff_ref, mask_scr, p_scr, ds_scr,
    *, head_dim,
):
    rows = qs_ref.shape[0]
    blocks = rows // LANES

    @pl.when(pl.program_id(0) == 0)
    def _():
        mask_scr[...] = segment_mask(seg_ref, 0, rows)

    scaled, keys, values, grads = qs_ref[...], k_ref[...], v_ref[...], ga_ref[...]
    q_t, g_t, k_t = scaled.T, grads.T, keys.T
    low_half = lax.broadcasted_iota(jnp.int32, (rows, LANES), 1) < head_dim
    dq_t, dk_parts, dv_parts = [], [], []
    lane = lax.broadcasted_iota(jnp.int32, (1, BAND), 1)
    for h in range(HEAD_GROUP):
        row = woff_ref[0, h : h + 1, :]
        band = band_of(row)
        pair = slice(LANES * (h // 2), LANES * (h // 2 + 1))
        k_pair, v_pair = keys[:, pair], values[:, pair]
        q_only, g_only = only_rows(q_t, h, head_dim), only_rows(g_t, h, head_dim)
        tiles = {}
        for b in range(0, blocks, 2):
            lanes = slice(b * LANES, (b + 2) * LANES)
            s = dot(k_pair, q_only[:, lanes]) + bias_block(band, row, b, 2, blocks) + mask_scr[:, lanes]
            p = jnp.exp(s - lse_ref[0, h : h + 1, lanes])
            dp = dot(v_pair, g_only[:, lanes])
            ds = p * (dp - jnp.sum(p * dp, axis=0, keepdims=True))
            p_scr[:, lanes] = p.astype(BF)
            ds_scr[:, lanes] = ds.astype(BF)
            for q_block in range(2):
                for k_block in range(blocks):
                    d = max(-2, min(2, k_block - b - q_block))
                    tile = ds[k_block * LANES : (k_block + 1) * LANES, q_block * LANES : (q_block + 1) * LANES]
                    tiles[d] = tiles[d] + tile if d in tiles else tile
        skewed = jnp.concatenate([tiles[1], tiles[0], tiles[-1], jnp.zeros_like(tiles[0])], axis=1)
        offsets = diagonal_sums(skewed)
        offsets = offsets + jnp.where(lane == FAR_AFTER, jnp.sum(tiles[2]), 0.0)
        offsets = offsets + jnp.where(lane == FAR_BEFORE, jnp.sum(tiles[-2]), 0.0)
        dwoff_ref[0, h : h + 1, :] = offsets
        p_all, ds_all = p_scr[...], ds_scr[...]
        dv_parts.append(dot(p_all, grads[:, pair]))
        dk_parts.append(dot(ds_all, scaled[:, pair]))
        dq_t.append(dot(k_t[h * head_dim : (h + 1) * head_dim], ds_all))
    dq = jnp.concatenate(dq_t, axis=0).T * head_dim ** (-0.5)
    dq_ref[...] = dq.astype(BF)
    for i in range(HEAD_GROUP // 2):
        pair = slice(LANES * i, LANES * (i + 1))
        dk_ref[:, pair] = jnp.where(low_half, dk_parts[2 * i], dk_parts[2 * i + 1]).astype(BF)
        dv_ref[:, pair] = jnp.where(low_half, dv_parts[2 * i], dv_parts[2 * i + 1]).astype(BF)


def attn_bwd(scaled, keys, values, grad_att, lse, woff, seg):
    rows, width = scaled.shape
    groups = woff.shape[0]
    cols = width // groups
    col_block = pl.BlockSpec((rows, cols), lambda g: (0, g))
    wide = jax.ShapeDtypeStruct((rows, width), BF)
    return call(
        functools.partial(attn_bwd_kernel, head_dim=cols // HEAD_GROUP),
        (scaled, keys, values, grad_att, lse, woff, seg),
        [
            col_block,
            col_block,
            col_block,
            col_block,
            pl.BlockSpec((1, HEAD_GROUP, rows), lambda g: (g, 0, 0)),
            pl.BlockSpec((1, HEAD_GROUP, BAND), lambda g: (g, 0, 0)),
            const_spec(seg.shape),
        ],
        grid=(groups,),
        out_specs=[col_block, col_block, col_block, pl.BlockSpec((1, HEAD_GROUP, BAND), lambda g: (g, 0, 0))],
        out_shape=[wide, wide, wide, jax.ShapeDtypeStruct((groups, HEAD_GROUP, BAND), F32)],
        scratch_shapes=[
            pltpu.VMEM((rows, rows), F32),
            pltpu.VMEM((rows, rows), BF),
            pltpu.VMEM((rows, rows), BF),
        ],
        cost_estimate=estimate("attn_bwd"),
        name="attn_bwd",
    )


def sorted_rows_kernel(pq_ref, pk_ref, tok_ref, gain_ref, att_ref, att_o_ref, out_ref, sort_scr):
    start = tok_ref[...].astype(F32)
    normed_t = (start * rms_scale(start) * gain_ref[...]).T
    attended_t = att_ref[...].astype(F32).T
    sort_rows(pq_ref, attended_t, sort_scr)
    att_o_ref[...] = sort_scr[...].astype(BF)
    for i, place_ref in enumerate((pq_ref, pk_ref)):
        sort_rows(place_ref, normed_t, sort_scr)
        out_ref[i] = sort_scr[...].astype(BF)


def sorted_rows(place_q, place_k, tokens, gain_attn, attended):
    rows, width = tokens.shape
    return call(
        sorted_rows_kernel,
        (place_q, place_k, tokens, gain_attn[None], attended),
        [pl.BlockSpec(memory_space=pltpu.SMEM)] * 2 + [pl.BlockSpec(memory_space=pltpu.VMEM)] * 3,
        out_shape=[jax.ShapeDtypeStruct((width, rows), BF), jax.ShapeDtypeStruct((2, width, rows), BF)],
        scratch_shapes=[pltpu.VMEM((width, rows), F32)],
        cost_estimate=estimate("sorted_rows"),
        name="sorted_rows",
    )


def dense_terms_kernel(att_ref, rows_ref, branch_ref, dq_ref, dk_ref, dv_ref, keep_ref, send_ref):
    half = keep_ref.shape[1]
    for i, d_ref in enumerate((branch_ref, dq_ref, dk_ref, dv_ref)):
        lhs = att_ref[...] if i == 0 else rows_ref[min(i - 1, 1)]
        term = dot(lhs, d_ref[...]).astype(BF)
        keep_ref[i] = term[:half]
        send_ref[i] = term[half:]


def dense_terms(att_t, lhs, branch, dq, dk, dv):
    _, width, rows = lhs.shape
    cols = 256
    col_block = pl.BlockSpec((rows, cols), lambda g: (0, g))
    return call(
        dense_terms_kernel,
        (att_t, lhs, branch, dq, dk, dv),
        [const_spec(att_t.shape), const_spec(lhs.shape)] + [col_block] * 4,
        grid=(width // cols,),
        out_specs=[pl.BlockSpec((4, width // 2, cols), lambda g: (0, 0, g))] * 2,
        out_shape=[jax.ShapeDtypeStruct((4, width // 2, width), BF)] * 2,
        cost_estimate=estimate("dense_terms"),
        name="dense_terms",
    )


def norm_bwd_kernel(
    place_ref, tok_ref, gain_ref, gmid_ref, small_ref, dq_ref, dk_ref, dv_ref, wq_ref, wk_ref, wv_ref,
    tg_ref, keep_ref, send_ref, acc, sort_scr, *, gain_row,
):
    step = pl.program_id(0)
    total = dot_nt(dq_ref[...], wq_ref[...]) + dot_nt(dk_ref[...], wk_ref[...]) + dot_nt(dv_ref[...], wv_ref[...])

    @pl.when(step == 0)
    def _():
        acc[...] = total

    @pl.when(step > 0)
    def _():
        acc[...] += total

    @pl.when(step == pl.num_programs(0) - 1)
    def _():
        grad = acc[...]
        start = tok_ref[...].astype(F32)
        scale = rms_scale(start)
        unit = start * scale
        gain_grad = jnp.sum(grad * unit, axis=0, keepdims=True)
        scaled = grad * gain_ref[...]
        tg_ref[...] = gmid_ref[...] + scale * (scaled - unit * jnp.mean(scaled * unit, axis=-1, keepdims=True))
        small = small_ref[...]
        row = lax.broadcasted_iota(jnp.int32, small.shape, 0)
        small = jnp.where(row == gain_row, gain_grad, small)
        small = jnp.concatenate([small, jnp.zeros((LANES - small.shape[0], small.shape[1]), F32)], axis=0)
        sort_rows(place_ref, small.T, sort_scr)
        half = sort_scr.shape[0] // 2
        keep_ref[...] = sort_scr[0:half].astype(BF)
        send_ref[...] = sort_scr[half:].astype(BF)


def norm_bwd(place, tokens, gain_attn, grad_mid, small, gain_row, dq, dk, dv, w_query, w_key, w_value):
    rows, width = tokens.shape
    cols = 256
    col_block = pl.BlockSpec((rows, cols), lambda g: (0, g))
    weight_block = pl.BlockSpec((width, cols), lambda g: (0, g))
    half = jax.ShapeDtypeStruct((width // 2, LANES), BF)
    return call(
        functools.partial(norm_bwd_kernel, gain_row=gain_row),
        (place, tokens, gain_attn[None], grad_mid, small, dq, dk, dv, w_query, w_key, w_value),
        [pl.BlockSpec(memory_space=pltpu.SMEM)]
        + [const_spec((rows, width)), const_spec((1, width)), const_spec((rows, width)), const_spec(small.shape)]
        + [col_block] * 3
        + [weight_block] * 3,
        grid=(width // cols,),
        out_specs=[const_spec((rows, width)), const_spec(half.shape), const_spec(half.shape)],
        out_shape=[jax.ShapeDtypeStruct((rows, width), F32), half, half],
        scratch_shapes=[pltpu.VMEM((rows, width), F32), pltpu.VMEM((width, LANES), F32)],
        cost_estimate=estimate("norm_bwd"),
        name="norm_bwd",
    )


def last_sums_kernel(token_ref, keep_ref, got_ref, *outs, experts, counts):
    total = keep_ref[...].astype(F32) + got_ref[...].astype(F32)
    width = outs[0].shape[1]
    for i in range(2):
        outs[i][...] = total[i, :, 0:width]
        outs[2 + i][...] = total[i, :, width + LANES :]
    small = total[0, :, width : width + LANES] + token_ref[...]
    outs[4][...] = small[:, 0:experts]
    flat = small.T
    for i, count in enumerate(counts):
        outs[5 + i][...] = flat[TAIL // 2 + i : TAIL // 2 + i + 1, 0:count]


def last_sums(token, keep, got, width, experts, counts):
    rows = keep.shape[1]
    return call(
        functools.partial(last_sums_kernel, experts=experts, counts=counts),
        (token, keep, got),
        [pl.BlockSpec(memory_space=pltpu.VMEM)] * 3,
        out_shape=[jax.ShapeDtypeStruct((rows, width), F32)] * 4
        + [jax.ShapeDtypeStruct((rows, experts), F32)]
        + [jax.ShapeDtypeStruct((1, count), F32) for count in counts],
        cost_estimate=estimate("last_sums"),
        name="last_sums",
    )


def bits_of(size):
    return size.bit_length() - 1


def swap(value, axis, size, mask):
    return lax.ppermute(value, axis, [(i, i ^ mask) for i in range(size)])


def pick(value, index, axis):
    return lax.dynamic_index_in_dim(value, index, axis, keepdims=False)


class Order:
    def __init__(self, token):
        self.token = token

    def enter(self, tree):
        tree, self.token = lax.optimization_barrier((tree, self.token))
        return tree

    leave = enter


def places(me, bits, order):
    key = jnp.arange(1 << bits, dtype=jnp.int32) ^ me
    place = jnp.zeros_like(key)
    for bit in order:
        place = place * 2 + ((key >> bit) & 1)
    return place


class Halving:
    def __init__(self, order, keep, send, dim, route, name):
        self.order, self.keep, self.to_send, self.dim, self.route, self.name = order, keep, send, dim, list(route), name
        self.got = None

    def start(self):
        axis, size, bit = self.route[0]
        with jax.named_scope(f"{self.name}_{axis}{1 << bit}"):
            value = self.order.enter(self.keep if self.to_send is None else self.to_send)
            self.got = swap(value, axis, size, 1 << bit)


def arrive(*units):
    for unit in units:
        unit.got = unit.order.leave(unit.got)


def fold_kernel(*refs, cuts, inputs):
    pairs, outs = refs[:inputs], list(refs[inputs:])
    at = 0
    for dim, last, width in cuts:
        total = []
        for _ in range(width):
            total.append(pairs[at][...].astype(F32) + pairs[at + 1][...].astype(F32))
            at += 2
        if last:
            outs.pop(0)[...] = total[0]
            continue
        rows = total[0].shape[dim] // 2
        for start in (0, rows):
            out = outs.pop(0)
            cut = [lax.slice_in_dim(v, start, start + rows, axis=dim).astype(BF) for v in total]
            if len(out.shape) == len(cut[0].shape):
                at_lane = 0
                for part in cut:
                    out[..., at_lane : at_lane + part.shape[-1]] = part
                    at_lane += part.shape[-1]
            else:
                for i in range(width):
                    out[i] = cut[i]


def fold(*units, hold=()):
    groups = [unit if isinstance(unit, tuple) else (unit,) for unit in units]
    order = groups[0][0].order
    args, cuts, shapes = [], [], []
    for group in groups:
        for unit in group:
            unit.route.pop(0)
            got = order.leave(unit.got)
            args += [unit.keep, got]
        unit = group[0]
        last = unit.to_send is None or not unit.route
        cuts.append((unit.dim, last, len(group)))
        if last:
            shapes.append(jax.ShapeDtypeStruct(got.shape, F32))
        else:
            shape = list(got.shape)
            shape[unit.dim] //= 2
            stacked = len(group) > 1 and len(shape) == 2
            if stacked:
                shape = [len(group)] + shape
            else:
                shape[-1] = sum(member.keep.shape[-1] for member in group)
            shapes += [jax.ShapeDtypeStruct(tuple(shape), BF)] * 2
    args = order.enter(args)
    outs = list(
        call(
            functools.partial(fold_kernel, cuts=cuts, inputs=len(args)),
            args,
            [pl.BlockSpec(memory_space=pltpu.VMEM)] * len(args),
            out_shape=shapes,
            cost_estimate=estimate("fold"),
            name="fold",
        )
    )
    outs = order.leave(outs)
    for group, (_, last, width) in zip(groups, cuts):
        unit = group[0]
        unit.keep = outs.pop(0)
        if not last:
            unit.to_send = outs.pop(0)
        if width > 1 and unit.keep.ndim > group[1].keep.ndim:
            unit.dim += 1
        if unit.route and unit not in hold:
            unit.start()


def fold_first_kernel(keep_ref, got_ref, small_keep_ref, small_got_ref, *outs):
    width = keep_ref.shape[2]
    small = (small_keep_ref[...] + small_got_ref[...]).astype(F32)
    for i in range(keep_ref.shape[0]):
        total = keep_ref[i].astype(F32) + got_ref[i].astype(F32)
        rows = total.shape[0] // 2
        for j in range(2):
            out = outs[i // 2 * 2 + j]
            out[i % 2, :, 0:width] = total[j * rows : (j + 1) * rows].astype(BF)
            if i < 2:
                extra = small[j * rows : (j + 1) * rows] if i == 0 else jnp.zeros((rows, LANES), F32)
                out[i, :, width:] = extra.astype(BF)


def fold_first(keep, got, small_keep, small_got):
    _, rows, width = keep.shape
    shapes = [jax.ShapeDtypeStruct((2, rows // 2, width + extra), BF) for extra in (LANES, LANES, 0, 0)]
    return call(
        fold_first_kernel,
        (keep, got, small_keep, small_got),
        [pl.BlockSpec(memory_space=pltpu.VMEM)] * 4,
        out_shape=shapes,
        cost_estimate=estimate("fold_first"),
        name="fold_first",
    )


class Return:
    def __init__(self, order, low, high, axis, size, name, pieces=False):
        self.order, self.axis, self.size, self.name = order, axis, size, name
        half = high.shape[0]
        low = [(value, 0) for value in low] if isinstance(low, list) else [(low, i) for i in range(half)]
        self.slots = low + [(high, i) for i in range(half)]
        self.bit = bits_of(size) - 1
        if pieces:
            self.start_pieces()
        else:
            with jax.named_scope(f"{self.name}{1 << self.bit}"):
                self.got = swap(self.order.enter(high), self.axis, self.size, 1 << self.bit)

    def moving(self):
        return [m for m in range(self.size) if (m >> self.bit) & 1]

    def start_pieces(self):
        self.got = []
        for m in self.moving():
            array, index = self.slots[m]
            with jax.named_scope(f"{self.name}{1 << self.bit}_{m}"):
                piece = array if array.shape[0] == 1 else array[index][None]
                self.got.append(swap(self.order.enter(piece), self.axis, self.size, 1 << self.bit))

    def fold(self):
        got = self.order.leave(self.got)
        for i, m in enumerate(self.moving()):
            self.slots[m] = (got[i], 0) if isinstance(got, list) else (got, i)
        self.bit -= 1
        if self.bit >= 0:
            self.start_pieces()

    def finish(self):
        while self.bit >= 0:
            self.fold()


class Gather:
    def __init__(self, order, value, axis, size, name):
        self.order, self.axis, self.size, self.name = order, axis, size, name
        self.blocks = {0: value}
        self.send(0, size // 2)
        if size > 2:
            self.send(0, 1)

    def send(self, m, bit):
        with jax.named_scope(f"{self.name}{m}_{bit}"):
            self.blocks[m ^ bit] = swap(self.blocks[m], self.axis, self.size, bit)

    def settle(self):
        self.blocks[1] = self.order.leave(self.blocks[1])

    def relay(self):
        self.blocks[self.size // 2] = self.order.leave(self.blocks[self.size // 2])
        bit = self.size // 2
        while bit:
            for m in range(0, self.size, 2 * bit):
                if m ^ bit not in self.blocks:
                    self.send(m, bit)
            bit //= 2

    def finish(self):
        self.blocks = self.order.leave(self.blocks)
        return [self.blocks[m] for m in range(self.size)]


def body(
    tokens,
    cotangent,
    gain_attn,
    w_query,
    w_key,
    w_value,
    w_out,
    rel_bias,
    gain_moe,
    w_router,
    w_gate,
    w_up,
    w_down,
    segments,
    routes,
    *,
    dp_size,
    ep_size,
):
    TURNS.clear()
    rows, width = tokens.shape
    buckets, heads = rel_bias.shape
    experts = w_router.shape[1]
    cap = 10 * rows // (4 * experts)
    ff = w_gate.shape[2]
    me = lax.axis_index("expert")

    cots = Gather(None, cotangent, "expert", ep_size, "cot")
    scaled, keys, values, woff, token, code, *filled, payload = attn_first(
        tokens, gain_attn, w_query, w_key, w_value, w_out, rel_bias.T, segments, gain_moe, w_router.T, routes.T
    )
    order = Order(token)
    cots.order = order
    me_ref = me.reshape(1).astype(jnp.int32)

    dp_bits, ep_bits = bits_of(dp_size), bits_of(ep_size)
    dp_me = lax.axis_index("dp")
    dp_order = list(range(dp_bits))
    z_order = [1, 0] + dp_order[2:]
    place_x = places(dp_me, dp_bits, dp_order)
    place_z = places(dp_me, dp_bits, z_order)

    def dp_route(bits):
        return [("dp", dp_size, b) for b in bits]

    dp_part = [ep_bits + b for b in dp_order]
    ep_part = list(range(1, ep_bits))
    q_bits = [0] + ep_part + dp_part
    k_bits = [0] + dp_part[:2] + ep_part + dp_part[2:]
    whole_me = dp_me * ep_size + me

    def route(bits):
        return [("expert", ep_size, b) if b < ep_bits else ("dp", dp_size, b - ep_bits) for b in bits]

    place_q, place_k = [places(whole_me, dp_bits + ep_bits, bits) for bits in (q_bits, k_bits)]

    first_half = Gather(order, order.enter(payload), "expert", ep_size, "rows_a")
    attended, lse, middle, normed_moe, chances, payload = order.leave(
        attn_second(tokens, order.enter(scaled), keys, values, w_out, woff, segments, gain_moe, w_router.T, filled)
    )
    cots.settle()
    first_half.settle()
    second_half = Gather(order, order.enter(payload), "expert", ep_size, "rows_b")
    first_half.relay()
    cots.relay()
    cots, heads_rows = cots.finish(), first_half.finish()
    blocks = ff // FF_BLOCK
    counts = [blocks - blocks // 2, blocks // 2]
    starts = [sum(counts[:i]) for i in range(len(counts))]
    gh_first, cot_rows = order.leave(cot_hidden(order.enter(me_ref), heads_rows, cots, w_down, cap, starts[1]))
    second_half.relay()
    payloads = [v for pair in zip(heads_rows, second_half.finish()) for v in pair]
    scs, units = [], []

    def expert_part(i, source, filled=()):
        *shared, gate_keep, gate_send, up_keep, up_send, sc, hid, hid_t, gg, gu = order.leave(
            expert_a(
                order.enter(source), gh_second if i else gh_first, starts[i], w_gate, w_up, starts[i], counts[i], filled
            )
        )
        scs.append(sc)
        gate = Halving(order, gate_keep, gate_send, 0, dp_route(z_order), f"gate{i}")
        units.append((gate, Halving(order, up_keep, up_send, 0, dp_route(dp_order), f"up{i}")))
        return shared, (hid, hid_t, gg, gu)

    def by_xor(value):
        return jnp.stack([pick(value, me ^ m, 0) for m in range(experts)])

    def padded(value):
        return jnp.pad(value, ((0, TAIL - experts), (0, 0)))

    (x_all, x_t, gate_all, grad_cots), filled = expert_part(0, (me_ref, place_x, payloads, cot_rows))
    for unit in units[0]:
        unit.start()
    gh_second = order.leave(cot_hidden_more(order.enter(cot_rows), w_down, starts[1]))
    _, (hid, hid_t, gg, gu) = expert_part(1, (x_all, x_t, gate_all), filled)
    for unit in units[1]:
        unit.start()
    *back_low, back_high = order.leave(expert_b(order.enter(gg), gu, scs, w_gate, w_up, experts))
    backs = Return(order, back_low, back_high, "expert", ep_size, "grad_rows")
    first, second = units[0][0], units[1][0]
    fold(*units[0])
    down_parts = order.leave(down_grads(order.enter(hid_t), grad_cots, place_z, place_x))
    down_units = tuple(
        Halving(order, down_parts[2 * i], down_parts[2 * i + 1], 0, dp_route(bits), f"down{i}")
        for i, bits in enumerate((z_order, dp_order))
    )
    down = down_units[0]
    fold(*units[1], units[0], hold=units[0])
    code_xor, chances_xor, wr_xor = order.enter((by_xor(code), padded(by_xor(chances)), padded(by_xor(w_router.T))))
    backs.fold()
    att_t, normed_t = order.leave(sorted_rows(place_q, place_k, tokens, gain_attn, order.enter(attended)))
    backs.finish()
    for unit in down_units:
        unit.start()
    grad_mid, branch, grad_att, gain_moe_term, router_term = order.leave(
        moe_bwd(
            cotangent, middle, gain_moe, normed_moe, chances_xor, wr_xor, code_xor, code_xor.T, w_out,
            backs.slots,
        )
    )
    dq, dk, dv, dwoff = order.leave(attn_bwd(scaled, keys, values, order.enter(grad_att), lse, woff, segments))
    arrive(*units[1])
    dense_keep, dense_send = order.leave(dense_terms(att_t, normed_t, branch, order.enter(dq), dk, dv))
    arrive(*down_units)
    core = Halving(order, dense_keep, dense_send, 1, route(q_bits)[:1], "dense")
    core.start()
    first.start()
    fold(*down_units, units[1], hold=units[1])
    devices = dp_size * ep_size
    share = width // devices
    onehot = jnp.asarray(band_onehot(rows, buckets))
    bias_term = jnp.dot(onehot, dwoff.reshape(heads, BAND).T, precision=HIGHEST).reshape(devices, -1)
    bias_share = bias_term.shape[1]
    bias_row = jnp.pad(bias_term, ((0, 0), (0, share - bias_share))).reshape(1, width)
    small = jnp.concatenate(
        [
            jnp.pad(by_xor(router_term), ((0, TAIL // 2 - experts), (0, 0))),
            jnp.zeros((1, width), F32),
            gain_moe_term,
            bias_row,
            jnp.zeros((TAIL // 2 - 3, width), F32),
        ],
        axis=0,
    )
    token_grad, small_keep, small_send = order.leave(
        norm_bwd(
            place_q, tokens, gain_attn, grad_mid, order.enter(small), TAIL // 2, dq, dk, dv, w_query, w_key, w_value
        )
    )
    with jax.named_scope("small_expert1"):
        small_got = swap(order.enter(small_send), "expert", ep_size, 1)
    core_got = order.leave(core.got)
    halves = order.leave(fold_first(order.enter(dense_keep), core_got, small_keep, order.leave(small_got)))
    dense = [
        Halving(order, halves[2 * i], halves[2 * i + 1], 1, route(bits)[1:], name)
        for i, (bits, name) in enumerate(((q_bits, "out_q"), (k_bits, "k_v")))
    ]
    out_q, k_v = dense
    arrive(down, first)
    k_v.start()
    out_q.start()
    second.start()
    prod_low, prod_high = order.leave(produced_rows(order.enter(hid), w_down, experts))
    returned = Return(order, prod_low, prod_high, "expert", ep_size, "produced_rows")
    fold(k_v, out_q, down_units, first, second)
    fold(k_v, out_q)
    while first.route or second.route:
        fold(*[unit for unit in (first, second) if unit.route])
    terms = [first.keep, second.keep]
    gate_grad = order.leave(jnp.concatenate([term[0] for term in terms], axis=1)[None])
    up_grad = order.leave(jnp.concatenate([term[1] for term in terms], axis=1)[None])
    returned.fold()
    returned.finish()
    layer_out = order.leave(layer_output(middle, chances_xor, code_xor.T, returned.slots))
    while len(out_q.route) > 2:
        fold(*[unit for unit in (out_q, k_v, down) if unit.route])
    fold(*[(out_q, k_v)] + ([down] if down.route else []))
    down_grad = order.leave(jnp.concatenate([down.keep[0], down.keep[1]], axis=1)[None])
    pairs = order.leave([out_q.keep, out_q.got])
    out_grad, query_grad, key_grad, value_grad, router_grad, *gains = last_sums(
        order.token, *pairs, width, experts, (share, share, bias_share)
    )
    gain_attn_grad, gain_moe_grad, bias_grad = [value.reshape(-1) for value in gains]
    return (
        layer_out,
        token_grad,
        query_grad,
        key_grad,
        value_grad,
        out_grad,
        gain_attn_grad,
        gain_moe_grad,
        bias_grad,
        router_grad,
        gate_grad,
        up_grad,
        down_grad,
    )


def solution(mesh):
    in_specs = (
        P(("dp", "expert"), None),
        P(("dp", "expert"), None),
        P(),
        P(),
        P(),
        P(),
        P(),
        P(),
        P(),
        P(),
        P("expert", None, None),
        P("expert", None, None),
        P("expert", None, None),
        P(("dp", "expert"), None),
        P(("dp", "expert"), None),
    )
    out_specs = (
        P(("dp", "expert"), None),
        P(("dp", "expert"), None),
        P(("dp", "expert"), None),
        P(("dp", "expert"), None),
        P(("dp", "expert"), None),
        P(("dp", "expert"), None),
        P(("dp", "expert")),
        P(("dp", "expert")),
        P(("dp", "expert")),
        P(("dp", "expert"), None),
        P("expert", "dp", None),
        P("expert", "dp", None),
        P("expert", "dp", None),
    )
    run = functools.partial(body, dp_size=mesh.shape["dp"], ep_size=mesh.shape["expert"])
    return jax.shard_map(run, mesh=mesh, in_specs=in_specs, out_specs=out_specs, check_vma=False)
```

```python
import functools

import jax
import jax.numpy as jnp
import numpy as np
from jax import lax
from jax.experimental import pallas as pl
from jax.experimental.pallas import tpu as pltpu
from jax.sharding import PartitionSpec as P

EPS = 1e-06
HIGHEST = lax.Precision.HIGHEST
LANES = 128
BAND = 4 * LANES
HEAD_GROUP = 4
TAIL = 16
FAR = -1e30
BF = jnp.bfloat16
F32 = jnp.float32
VMEM_LIMIT = 56 * 1024 * 1024


def bucket_of(relative, buckets):
    halfway = buckets // 2
    exact_span = halfway // 2
    distance = np.abs(relative)
    beyond = exact_span + (
        np.log(np.maximum(distance, 1) / exact_span)
        / np.log(128.0 / exact_span)
        * (halfway - exact_span)
    ).astype(np.int64)
    beyond = np.minimum(beyond, halfway - 1)
    return (
        (relative > 0).astype(np.int64) * halfway
        + np.where(distance < exact_span, distance, beyond)
    ).astype(np.int32)


def band_onehot(length, buckets):
    place = np.arange(BAND)
    relative = np.where(place <= 3 * LANES, LANES - place, BAND + LANES - place)
    table = (bucket_of(relative, buckets)[None, :] == np.arange(buckets)[:, None]).astype(np.float32)
    table[:, 3 * LANES] = 0.0
    far = np.arange(LANES, length)
    assert np.all(bucket_of(far, buckets) == bucket_of(far, buckets)[0])
    assert np.all(bucket_of(-far, buckets) == bucket_of(-far, buckets)[0])
    return table


FAR_AFTER = 3 * LANES + 1
FAR_BEFORE = 3 * LANES - 1


def dot(a, b):
    return lax.dot_general(a, b, (((1,), (0,)), ((), ())), preferred_element_type=F32)


def dot_nt(a, b):
    return lax.dot_general(a, b, (((1,), (1,)), ((), ())), preferred_element_type=F32)


def dot_tn(a, b):
    return lax.dot_general(a, b, (((0,), (0,)), ((), ())), preferred_element_type=F32)


def split3(value):
    hi = value.astype(BF)
    rest = value - hi.astype(F32)
    mid = rest.astype(BF)
    low = (rest - mid.astype(F32)).astype(BF)
    return hi, mid, low


def rms_scale(value):
    return lax.rsqrt(jnp.mean(value * value, axis=-1, keepdims=True) + EPS)


def params(**kw):
    return pltpu.CompilerParams(vmem_limit_bytes=VMEM_LIMIT, **kw)


TIMES = {
    ("down_grads", 0): 10.0,
    ("dense_terms", 0): 13.1,
    ("fold", 1): 2.0,
}


TURNS = {}


def estimate(name):
    turn = TURNS.get(name, 0)
    TURNS[name] = turn + 1
    time = TIMES.get((name, turn), 0.1)
    return pl.CostEstimate(flops=int(time * 1.15e9), bytes_accessed=100000, transcendentals=0)


def call(kernel, args, in_specs, **kw):
    return pl.pallas_call(kernel, in_specs=list(in_specs), compiler_params=params(), **kw)(*args)


def whole_specs(args):
    return [const_spec(a.shape) for a in args]


def const_spec(shape):
    return pl.BlockSpec(shape, lambda *_: (0,) * len(shape))


def selector(code_row, rows):
    place = lax.broadcasted_iota(jnp.int32, (rows, code_row.shape[1]), 0)
    return jnp.where(place == code_row, 1.0, 0.0).astype(BF)


def selector_t(code_column, rows):
    place = lax.broadcasted_iota(jnp.int32, (code_column.shape[0], rows), 1)
    return jnp.where(place == code_column, 1.0, 0.0).astype(BF)


def band_of(row):
    return pltpu.roll(jnp.broadcast_to(row, (LANES, BAND)), 0, 1, stride=1, stride_axis=0)


def diagonal_sums(skewed):
    eight = skewed[0:8]
    for start in range(8, LANES, 8):
        eight = eight + pltpu.roll(skewed[start : start + 8], BAND - start, 1)
    total = eight[0:1]
    for row in range(1, 8):
        total = total + pltpu.roll(eight[row : row + 1], BAND - row, 1)
    return total


def bias_block(band, row, first, count, k_blocks):
    far = [jnp.broadcast_to(row[:, at : at + 1], (LANES, LANES)) for at in (FAR_BEFORE, FAR_AFTER)]
    columns = []
    for q_block in range(first, first + count):
        pieces = []
        for k_block in range(k_blocks):
            d = k_block - q_block
            pieces.append(far[1] if d > 1 else far[0] if d < -1 else band[:, LANES * (1 - d) : LANES * (2 - d)])
        columns.append(jnp.concatenate(pieces, axis=0))
    return jnp.concatenate(columns, axis=1)


def only_rows(value, h, head_dim):
    mine = value[h * head_dim : (h + 1) * head_dim]
    none = jnp.zeros_like(mine)
    return jnp.concatenate([mine, none] if h % 2 == 0 else [none, mine], axis=0)


def attend(scaled, keys, values, woff_ref, mask, first, head_dim):
    count = scaled.shape[0] // LANES
    q_t, v_t = scaled.T, values.T
    heads_t, totals = [], []
    for h in range(HEAD_GROUP):
        row = woff_ref[0, h : h + 1, :]
        bias = bias_block(band_of(row), row, first, count, keys.shape[0] // LANES)
        k_pair = keys[:, LANES * (h // 2) : LANES * (h // 2 + 1)]
        s = dot(k_pair, only_rows(q_t, h, head_dim)) + bias + mask
        peak = jnp.max(s, axis=0, keepdims=True)
        p = jnp.exp(s - peak)
        total = jnp.sum(p, axis=0, keepdims=True)
        heads_t.append(dot(v_t[h * head_dim : (h + 1) * head_dim], p.astype(BF)) * (1.0 / total))
        totals.append(peak + jnp.log(total))
    return jnp.concatenate(heads_t, axis=0).T.astype(BF), jnp.concatenate(totals, axis=0)


def slot_codes(routes):
    chosen = routes.astype(F32)
    tokens = chosen.shape[1]
    numbers = lax.broadcasted_iota(jnp.int32, (TAIL // 2, tokens), 0).astype(F32)
    named = jnp.logical_or(numbers == chosen[0:1], numbers == chosen[1:2])
    row = lax.broadcasted_iota(jnp.int32, (tokens, tokens), 0)
    lane = lax.broadcasted_iota(jnp.int32, (tokens, tokens), 1)
    before = jnp.where(row < lane, 1.0, 0.0).astype(BF)
    return jnp.where(named, dot(jnp.where(named, 1.0, 0.0).astype(BF), before), -1.0)


def packed_codes(codes):
    upper = jnp.floor((codes + 1.0) * (1.0 / 16.0))
    return jnp.concatenate([upper, codes + 1.0 - 16.0 * upper], axis=0)


def own_code(me, packed):
    row = lax.broadcasted_iota(jnp.int32, packed.shape, 0)
    weight = jnp.where(row == me, 16.0, jnp.where(row == me + TAIL // 2, 1.0, 0.0))
    return (jnp.sum(packed.astype(F32) * weight, axis=0, keepdims=True) - 1.0).astype(jnp.int32)


def route_rows(mid, gain_ref, wr_ref, experts, nm_ref, ch_ref, payload_ref, codes=None):
    rows = mid.shape[0]
    nm = (mid * rms_scale(mid) * gain_ref[...]).astype(BF)
    nm_ref[...] = nm
    router = jnp.concatenate([wr_ref[...].astype(F32), jnp.zeros((TAIL - experts, nm.shape[1]), F32)], axis=0)
    logits = dot_nt(router.astype(BF), nm)
    live = lax.broadcasted_iota(jnp.int32, logits.shape, 0) < experts
    logits = jnp.where(live, logits, FAR)
    raised = jnp.exp(logits - jnp.max(logits, axis=0, keepdims=True))
    chances = raised / jnp.sum(raised, axis=0, keepdims=True)
    ch_ref[...] = chances
    hi = chances.astype(BF).astype(F32)
    both = jnp.concatenate([hi[: TAIL // 2], (chances - hi)[: TAIL // 2]], axis=0)
    payload_ref[0:rows, :] = nm
    tail = [both] if codes is None else [both, packed_codes(codes)]
    used = sum(v.shape[1] for v in tail)
    tail.append(jnp.zeros((TAIL, nm.shape[1] - used), F32))
    payload_ref[rows:, :] = jnp.concatenate(tail, axis=1).astype(BF)


def segment_mask(seg_ref, first, count):
    seg = seg_ref[...].astype(F32)
    column = jnp.broadcast_to(seg, (8, seg.shape[1])).T[:, 0:1]
    return jnp.where(column == seg[:, first : first + count], 0.0, FAR)


def attn_first_kernel(
    tok_ref, gain_a_ref, wq_ref, wk_ref, wv_ref, wo_ref, bias_ref, onehot_ref, seg_ref, gain_m_ref, wr_ref, routes_ref,
    qs_ref, k_ref, v_ref, woff_ref, token_ref, code_ref, att_ref, lse_ref, mid_ref, nm_ref, ch_ref, payload_ref,
    n_scr, mask_scr, woff_scr, code_scr,
    *, experts, head_dim,
):
    step = pl.program_id(0)
    rows = att_ref.shape[0]

    @pl.when(step == 0)
    def _():
        start = tok_ref[...].astype(F32)
        n_scr[...] = (start * rms_scale(start) * gain_a_ref[...]).astype(BF)
        mid_ref[...] = start[:rows]
        mask_scr[...] = segment_mask(seg_ref, 0, rows)
        token_ref[...] = jnp.where(seg_ref[:, 0:LANES] < 0, 1.0, 0.0)
        codes = slot_codes(routes_ref[...])
        code_scr[...] = codes
        code_ref[...] = codes[:experts].astype(jnp.int32)
        table = onehot_ref[...]
        offsets = sum(dot(part, table) for part in split3(bias_ref[...]))
        for g in range(woff_scr.shape[0]):
            woff_scr[g] = offsets[g * HEAD_GROUP : (g + 1) * HEAD_GROUP]

    woff_ref[0] = woff_scr[step]

    normed = n_scr[...]
    scaled = (dot(normed, wq_ref[...]).astype(BF).astype(F32) * head_dim ** (-0.5)).astype(BF)
    keys = dot(normed, wk_ref[...]).astype(BF)
    values = dot(normed, wv_ref[...]).astype(BF)
    qs_ref[...] = scaled
    k_ref[...] = keys
    v_ref[...] = values
    att, totals = attend(scaled[:rows], keys, values, woff_ref, mask_scr[...], 0, head_dim)
    att_ref[...] = att
    lse_ref[0] = totals
    mid_ref[...] += dot(att, wo_ref[...])

    @pl.when(step == pl.num_programs(0) - 1)
    def _():
        route_rows(mid_ref[...], gain_m_ref, wr_ref, experts, nm_ref, ch_ref, payload_ref, code_scr[...])


def attn_second_kernel(
    tok_ref, qs_ref, k_ref, v_ref, wo_ref, woff_ref, seg_ref, gain_m_ref, wr_ref, *refs, experts, head_dim
):
    att_ref, lse_ref, mid_ref, nm_ref, ch_ref, payload_ref, mask_scr = refs[-7:]
    step = pl.program_id(0)
    rows = att_ref.shape[0]

    @pl.when(step == 0)
    def _():
        mid_ref[...] = tok_ref[...].astype(F32)
        mask_scr[...] = segment_mask(seg_ref, rows, rows)

    att, totals = attend(qs_ref[...], k_ref[...], v_ref[...], woff_ref, mask_scr[...], rows // LANES, head_dim)
    att_ref[...] = att
    lse_ref[0] = totals
    mid_ref[...] += dot(att, wo_ref[...])

    @pl.when(step == pl.num_programs(0) - 1)
    def _():
        route_rows(mid_ref[...], gain_m_ref, wr_ref, experts, nm_ref, ch_ref, payload_ref)


def attn_halves(rows, width, groups, half):
    cols, part = width // groups, rows // 2
    wide = jax.ShapeDtypeStruct((rows, width), BF)
    shapes = [
        wide,
        jax.ShapeDtypeStruct((groups, HEAD_GROUP, rows), F32),
        jax.ShapeDtypeStruct((rows, width), F32),
        wide,
        jax.ShapeDtypeStruct((TAIL, rows), F32),
        jax.ShapeDtypeStruct((part + TAIL, width), BF),
    ]
    specs = [
        pl.BlockSpec((part, cols), lambda g: (half, g)),
        pl.BlockSpec((1, HEAD_GROUP, part), lambda g: (g, 0, half)),
        pl.BlockSpec((part, width), lambda g: (half, 0)),
        pl.BlockSpec((part, width), lambda g: (half, 0)),
        pl.BlockSpec((TAIL, part), lambda g: (0, half)),
        const_spec((part + TAIL, width)),
    ]
    return shapes, specs


def attn_first(tokens, gain_attn, w_query, w_key, w_value, w_out, rel_bias, seg, gain_moe, w_router, routes):
    rows, width = tokens.shape
    heads, buckets = rel_bias.shape
    experts = w_router.shape[0]
    groups = heads // HEAD_GROUP
    cols, part = width // groups, rows // 2
    weight_block = pl.BlockSpec((width, cols), lambda g: (0, g))
    shapes, specs = attn_halves(rows, width, groups, 0)
    wide = jax.ShapeDtypeStruct((rows, width), BF)
    return call(
        functools.partial(attn_first_kernel, experts=experts, head_dim=cols // HEAD_GROUP),
        (tokens, gain_attn[None], w_query, w_key, w_value, w_out, rel_bias, jnp.asarray(band_onehot(rows, buckets)).astype(BF),
         seg, gain_moe[None], w_router, routes),
        [
            const_spec((rows, width)),
            const_spec((1, width)),
            weight_block,
            weight_block,
            weight_block,
            pl.BlockSpec((cols, width), lambda g: (g, 0)),
            const_spec(rel_bias.shape),
            const_spec((buckets, BAND)),
            const_spec(seg.shape),
            const_spec((1, width)),
            const_spec(w_router.shape),
            const_spec(routes.shape),
        ],
        grid=(groups,),
        out_specs=[pl.BlockSpec((rows, cols), lambda g: (0, g))] * 3
        + [pl.BlockSpec((1, HEAD_GROUP, BAND), lambda g: (g, 0, 0)), const_spec((1, LANES)), const_spec((experts, rows))]
        + specs,
        out_shape=[wide] * 3
        + [jax.ShapeDtypeStruct((groups, HEAD_GROUP, BAND), F32), jax.ShapeDtypeStruct((1, LANES), F32)]
        + [jax.ShapeDtypeStruct((experts, rows), jnp.int32)]
        + shapes,
        scratch_shapes=[
            pltpu.VMEM((rows, width), BF),
            pltpu.VMEM((rows, part), F32),
            pltpu.VMEM((groups, HEAD_GROUP, BAND), F32),
            pltpu.VMEM((TAIL // 2, rows), F32),
        ],
        cost_estimate=estimate("attn_first"),
        name="attn_first",
    )


def attn_second(tokens, scaled, keys, values, w_out, woff, seg, gain_moe, w_router, filled):
    rows, width = tokens.shape
    experts = w_router.shape[0]
    groups = woff.shape[0]
    cols, part = width // groups, rows // 2
    col_block = pl.BlockSpec((rows, cols), lambda g: (0, g))
    shapes, specs = attn_halves(rows, width, groups, 1)
    args = (tokens, scaled, keys, values, w_out, woff, seg, gain_moe[None], w_router)
    return call(
        functools.partial(attn_second_kernel, experts=experts, head_dim=cols // HEAD_GROUP),
        (*args, *filled),
        [
            pl.BlockSpec((part, width), lambda g: (1, 0)),
            pl.BlockSpec((part, cols), lambda g: (1, g)),
            col_block,
            col_block,
            pl.BlockSpec((cols, width), lambda g: (g, 0)),
            pl.BlockSpec((1, HEAD_GROUP, BAND), lambda g: (g, 0, 0)),
            const_spec(seg.shape),
            const_spec((1, width)),
            const_spec(w_router.shape),
        ]
        + [pl.BlockSpec(memory_space=pl.ANY)] * len(filled),
        grid=(groups,),
        out_specs=specs,
        out_shape=shapes,
        scratch_shapes=[pltpu.VMEM((rows, part), F32)],
        input_output_aliases={len(args) + i: i for i in range(len(filled))},
        cost_estimate=estimate("attn_second"),
        name="attn_second",
    )


def gelu_parts(gate):
    c0 = np.float32(np.sqrt(2.0 / np.pi))
    c1 = np.float32(0.044715)
    square = gate * gate
    t = jnp.tanh(c0 * gate * (1.0 + c1 * square))
    half = 0.5 * (1.0 + t)
    value = gate * half
    slope = half + 0.5 * gate * (1.0 - t * t) * (c0 * (1.0 + 3.0 * c1 * square))
    return value, slope


FF_BLOCK = 256


def cot_hidden_kernel(me_ref, *refs, experts):
    tail_refs, cot_refs, wd_ref = refs[:experts], refs[experts : 2 * experts], refs[2 * experts]
    out_ref, rows_ref = refs[2 * experts + 1 :]

    @pl.when(pl.program_id(0) == 0)
    def _():
        cap = rows_ref.shape[0] // experts
        tokens = cot_refs[0].shape[0]
        for m, (tail_ref, cot_ref) in enumerate(zip(tail_refs, cot_refs)):
            code = own_code(me_ref[0], tail_ref[:, tokens // 2 : tokens // 2 + tokens])
            rows_ref[m * cap : (m + 1) * cap, :] = dot(selector(code, cap), cot_ref[...]).astype(BF)

    out_ref[...] = dot_nt(rows_ref[...], wd_ref[0]).astype(BF)


def cot_hidden(me, payloads, cots, w_down, cap, count):
    experts = len(cots)
    width = cots[0].shape[1]
    rows = experts * cap
    last = payloads[0].shape[0] // TAIL - 1
    return call(
        functools.partial(cot_hidden_kernel, experts=experts),
        (me, *payloads, *cots, w_down),
        [pl.BlockSpec(memory_space=pltpu.SMEM)]
        + [pl.BlockSpec((TAIL, width), lambda f: (last, 0))] * experts
        + whole_specs(cots)
        + [pl.BlockSpec((1, FF_BLOCK, width), lambda f: (0, f, 0))],
        grid=(count,),
        out_specs=[pl.BlockSpec((rows, FF_BLOCK), lambda f: (0, f)), const_spec((rows, width))],
        out_shape=[jax.ShapeDtypeStruct((rows, count * FF_BLOCK), BF), jax.ShapeDtypeStruct((rows, width), BF)],
        cost_estimate=estimate("cot_hidden"),
        name="cot_hidden",
    )


ROW_BLOCK = 320


def expert_first(me_ref, place_ref, payloads, cot_ref, x_ref, xt_ref, gate_ref, gc_ref):
    experts = len(payloads) // 2
    cap = x_ref.shape[0] // experts
    part = payloads[0].shape[0] - TAIL
    row = lax.broadcasted_iota(jnp.int32, (TAIL, part), 0)
    mine = jnp.logical_or(row == me_ref[0], row == me_ref[0] + TAIL // 2)
    for m in range(experts):
        code = own_code(me_ref[0], payloads[2 * m][part:, part : 3 * part])
        chosen = selector(code, cap)
        place = slice(m * cap, (m + 1) * cap)
        total = jnp.zeros((cap, x_ref.shape[1]), F32)
        gate = jnp.zeros((cap, 1), F32)
        for i in range(2):
            payload = payloads[2 * m + i]
            part_chosen = chosen[:, i * part : (i + 1) * part]
            total = total + dot(part_chosen, payload[0:part, :])
            chances = jnp.sum(jnp.where(mine, payload[part:, 0:part].astype(F32), 0.0), axis=0, keepdims=True)
            gate = gate + jnp.sum(part_chosen.astype(F32) * chances, axis=1, keepdims=True)
        x_ref[place, :] = total.astype(BF)
        gate_ref[place, :] = jnp.broadcast_to(gate, (cap, LANES))
        gc_ref[place, :] = (cot_ref[place, :].astype(F32) * gate).astype(BF)
    flipped = x_ref[...].T
    owners = place_ref.shape[0]
    rows = flipped.shape[0] // owners
    for b in range(owners):
        at = pl.multiple_of(place_ref[b] * rows, rows)
        xt_ref[pl.ds(at, rows), :] = flipped[b * rows : (b + 1) * rows]


def expert_a_kernel(*refs, experts):
    step = pl.program_id(0)
    if experts:
        me_ref, place_ref = refs[:2]
        payloads = refs[2 : 2 + 2 * experts]
        cot_ref, gh_ref, wg_ref, wu_ref, x_ref, xt_ref, gate_ref, gc_ref = refs[2 + 2 * experts : 10 + 2 * experts]

        @pl.when(step == 0)
        def _():
            expert_first(me_ref, place_ref, payloads, cot_ref, x_ref, xt_ref, gate_ref, gc_ref)

    else:
        x_ref, xt_ref, gate_ref, gh_ref, wg_ref, wu_ref = refs[:6]
    gate_keep_ref, gate_send_ref, up_keep_ref, up_send_ref, sc_ref, hid_ref, hidt_ref, gg_ref, gu_ref = refs[-9:]

    @pl.when(step == 0)
    def _():
        sc_ref[...] = jnp.zeros_like(sc_ref)

    wg, wu = wg_ref[0], wu_ref[0]
    width = wg.shape[1]
    for start in range(0, x_ref.shape[0], ROW_BLOCK):
        part = slice(start, start + ROW_BLOCK)
        x = x_ref[part, :]
        gate_pre = dot(x, wg)
        up_pre = dot(x, wu)
        grad = gh_ref[part, :].astype(F32)
        act, slope = gelu_parts(gate_pre)
        hidden = act * up_pre
        hid_ref[part, :] = hidden.astype(BF)
        product = hidden * grad
        folded = product[:, 0:LANES]
        for i in range(1, width // LANES):
            folded = folded + product[:, i * LANES : (i + 1) * LANES]
        sc_ref[part, :] += folded
        grad = grad * gate_ref[part, 0:1]
        gg_ref[part, :] = (slope * up_pre * grad).astype(BF)
        gu_ref[part, :] = (act * grad).astype(BF)
    hidt_ref[...] = hid_ref[...].T
    xt = xt_ref[...]
    cut = xt.shape[0] // 4
    for grad_ref, keep_ref, send_ref, second in ((gg_ref, gate_keep_ref, gate_send_ref, 1), (gu_ref, up_keep_ref, up_send_ref, 0)):
        term = dot(xt, grad_ref[...]).astype(BF)
        for q in range(4):
            upper, lower = (q % 2, q // 2) if second else (q // 2, q % 2)
            (send_ref if upper else keep_ref)[lower * cut : (lower + 1) * cut] = term[q * cut : (q + 1) * cut]


def expert_a(source, gh, gh_first, w_gate, w_up, first, count, filled=()):
    opening = 0 if filled else len(source[2]) // 2
    rows = gh.shape[0]
    width, ff = w_gate.shape[1:]
    span = count * FF_BLOCK
    col_weight = pl.BlockSpec((1, width, FF_BLOCK), lambda f: (0, 0, first + f))
    out_block = pl.BlockSpec((rows, FF_BLOCK), lambda f: (0, first + f))
    wide = jax.ShapeDtypeStruct((rows, ff), BF)
    tall = jax.ShapeDtypeStruct((ff, rows), BF)
    term = jax.ShapeDtypeStruct((width // 2, span), BF)
    term_block = pl.BlockSpec((width // 2, FF_BLOCK), lambda f: (0, f))
    if opening:
        me, place, payloads, cot_rows = source
        args = (me, place, *payloads, cot_rows)
        specs = [pl.BlockSpec(memory_space=pltpu.SMEM)] * 2 + whole_specs((*payloads, cot_rows))
        shared = [
            jax.ShapeDtypeStruct((rows, width), BF),
            jax.ShapeDtypeStruct((width, rows), BF),
            jax.ShapeDtypeStruct((rows, LANES), F32),
            jax.ShapeDtypeStruct((rows, width), BF),
        ]
    else:
        args = tuple(source)
        specs = whole_specs(source)
        shared = []
    args = (*args, gh, w_gate, w_up)
    used = len(args)
    first_filled = len(shared) + 5

    def run(*refs):
        expert_a_kernel(*refs[:used], *refs[used + len(filled) :], experts=opening)

    return call(
        run,
        (*args, *filled),
        specs
        + [pl.BlockSpec((rows, FF_BLOCK), lambda f: (0, first - gh_first + f)), col_weight, col_weight]
        + [pl.BlockSpec(memory_space=pl.ANY)] * len(filled),
        grid=(count,),
        out_specs=whole_specs(shared)
        + [term_block] * 4
        + [const_spec((rows, LANES)), out_block]
        + [pl.BlockSpec((FF_BLOCK, rows), lambda f: (first + f, 0)), out_block, out_block],
        out_shape=shared + [term] * 4 + [jax.ShapeDtypeStruct((rows, LANES), F32), wide, tall, wide, wide],
        input_output_aliases={used + i: first_filled + i for i in range(len(filled))},
        cost_estimate=estimate("expert_grads"),
        name="expert_grads",
    )


def expert_b_kernel(gg_ref, gu_ref, *refs, cap, experts):
    count = experts // 2 + 4
    sc_refs, (wg_ref, wu_ref, *outs, acc) = refs[:-count], refs[-count:]
    part_sum = dot_nt(gg_ref[...], wg_ref[0]) + dot_nt(gu_ref[...], wu_ref[0])
    step, block = pl.program_id(0), pl.program_id(1)

    @pl.when(step == 0)
    def _():
        acc[block] = part_sum

    def finish(out_ref, at):
        total = acc[block] + part_sum
        row = lax.broadcasted_iota(jnp.int32, (cap, cap), 0)
        lane = lax.broadcasted_iota(jnp.int32, (cap, cap), 1)
        place = lax.broadcasted_iota(jnp.int32, (TAIL, cap), 0)
        out_ref[at, 0:cap, :] = total.astype(BF)
        folded = sc_refs[0][...]
        for other in sc_refs[1:]:
            folded = folded + other[...]
        column = jnp.sum(folded, axis=1, keepdims=True)
        flat = jnp.sum(jnp.where(row == lane, column, 0.0), axis=0, keepdims=True)
        hi, mid, low = split3(flat)
        packed = jnp.where(
            place == 0, hi.astype(F32), jnp.where(place == 1, mid.astype(F32), jnp.where(place == 2, low.astype(F32), 0.0))
        )
        out_ref[at, cap : cap + TAIL, :] = jnp.zeros((TAIL, total.shape[1]), BF)
        out_ref[at, cap : cap + TAIL, 0:cap] = packed.astype(BF)

    last = step == pl.num_programs(0) - 1
    half = experts // 2
    for m in range(experts):

        @pl.when(jnp.logical_and(last, block == m))
        def _(m=m):
            finish(outs[m] if m < half else outs[half], 0 if m < half else m - half)


def expert_b(gg, gu, scs, w_gate, w_up, experts):
    rows, ff = gg.shape
    width = w_gate.shape[1]
    cap = rows // experts
    cut = ff // 2
    grads = pl.BlockSpec((cap, cut), lambda k, m: (m, k))
    sums = pl.BlockSpec((cap, LANES), lambda k, m: (m, 0))
    weight = pl.BlockSpec((1, width, cut), lambda k, m: (0, 0, k))
    return call(
        functools.partial(expert_b_kernel, cap=cap, experts=experts),
        (gg, gu, *scs, w_gate, w_up),
        [grads, grads] + [sums] * len(scs) + [weight, weight],
        grid=(2, experts),
        out_specs=[const_spec((1, cap + TAIL, width))] * (experts // 2) + [const_spec((experts // 2, cap + TAIL, width))],
        out_shape=[jax.ShapeDtypeStruct((1, cap + TAIL, width), BF)] * (experts // 2)
        + [jax.ShapeDtypeStruct((experts // 2, cap + TAIL, width), BF)],
        scratch_shapes=[pltpu.VMEM((experts, cap, width), F32)],
        cost_estimate=estimate("expert_input_grad"),
        name="expert_input_grad",
    )


def down_kernel(place_a_ref, place_b_ref, hidt_ref, gc_ref, *outs):
    owners = place_a_ref.shape[0]
    shard = 2 * outs[0].shape[0] // owners
    size = int(np.gcd(shard, 32))
    rows = hidt_ref.shape[0]
    step = pl.program_id(0)
    total = dot(hidt_ref[...], gc_ref[...]).astype(BF)
    half = total.shape[1] // 2
    for i in range(rows // size):
        row = step * rows + i * size
        owner = row // shard
        piece = total[i * size : (i + 1) * size]
        for keep_ref, send_ref, place_ref, cols in (
            (outs[0], outs[1], place_a_ref, piece[:, :half]),
            (outs[2], outs[3], place_b_ref, piece[:, half:]),
        ):
            place = place_ref[owner]
            at = pl.multiple_of((place % (owners // 2)) * shard + (row - owner * shard), size)

            @pl.when(place < owners // 2)
            def _(keep_ref=keep_ref, at=at, cols=cols):
                keep_ref[pl.ds(at, size), :] = cols

            @pl.when(place >= owners // 2)
            def _(send_ref=send_ref, at=at, cols=cols):
                send_ref[pl.ds(at, size), :] = cols


def down_grads(hid_t, grad_cots, place_a, place_b):
    rows, width = grad_cots.shape
    ff = hid_t.shape[0]
    table = pl.BlockSpec(memory_space=pltpu.SMEM)
    part = jax.ShapeDtypeStruct((ff // 2, width // 2), BF)
    return call(
        down_kernel,
        (place_a, place_b, hid_t, grad_cots),
        [table, table, pl.BlockSpec((ff // 4, rows), lambda f: (f, 0)), const_spec((rows, width))],
        grid=(4,),
        out_specs=[const_spec(part.shape)] * 4,
        out_shape=[part] * 4,
        cost_estimate=estimate("down_grads"),
        name="down_grads",
    )


def produced_kernel(hid_ref, wd_ref, low_ref, high_ref):
    rows = dot(hid_ref[...], wd_ref[0]).astype(BF)
    lower = pl.program_id(0) < pl.num_programs(0) // 2

    @pl.when(lower)
    def _():
        low_ref[0] = rows

    @pl.when(jnp.logical_not(lower))
    def _():
        high_ref[0] = rows


def produced_rows(hid, w_down, experts):
    rows, ff = hid.shape
    width = w_down.shape[2]
    cap, half = rows // experts, experts // 2
    return call(
        produced_kernel,
        (hid, w_down),
        [pl.BlockSpec((cap, ff), lambda m: (m, 0)), const_spec(w_down.shape)],
        grid=(experts,),
        out_specs=[
            pl.BlockSpec((1, cap, width), lambda m: (jnp.minimum(m, half - 1), 0, 0)),
            pl.BlockSpec((1, cap, width), lambda m: (jnp.maximum(m - half, 0), 0, 0)),
        ],
        out_shape=[jax.ShapeDtypeStruct((half, cap, width), BF)] * 2,
        cost_estimate=estimate("produced_rows"),
        name="produced_rows",
    )


def distinct(slots):
    arrays, found = [], []
    for array, index in slots:
        which = next((i for i, other in enumerate(arrays) if other is array), None)
        if which is None:
            which = len(arrays)
            arrays.append(array)
        found.append((which, index))
    return arrays, found


def layer_out_kernel(mid_ref, ch_ref, code_ref, *refs, slots):
    parts, out_ref = refs[:-1], refs[-1]
    cap = parts[0].shape[1]
    total = mid_ref[...]
    chances = ch_ref[...].T
    for m, (which, index) in enumerate(slots):
        picked = dot(selector_t(code_ref[:, m : m + 1], cap), parts[which][index])
        total = total + chances[:, m : m + 1] * picked
    out_ref[...] = total.astype(BF)


def layer_output(middle, chances, code_t, slots):
    rows, width = middle.shape
    arrays, found = distinct(slots)
    args = (middle, chances, code_t, *arrays)
    return call(
        functools.partial(layer_out_kernel, slots=found),
        args,
        [pl.BlockSpec(memory_space=pltpu.VMEM)] * len(args),
        out_shape=jax.ShapeDtypeStruct((rows, width), BF),
        cost_estimate=estimate("layer_output"),
        name="layer_output",
    )


def moe_bwd_kernel(
    cot_ref, mid_ref, gain_ref, nm_ref, ch_ref, wr_ref, code_ref, codet_ref, wo_ref, *refs, slots
):
    backs, (gmid_ref, branch_ref, ga_ref, gain_o_ref, router_o_ref) = refs[:-5], refs[-5:]
    experts, cap = len(slots), backs[0].shape[1] - TAIL
    rows = cot_ref.shape[0]
    grad = jnp.zeros(mid_ref.shape, F32)
    gate_rows = []
    for m, (which, index) in enumerate(slots):
        grad = grad + dot(selector_t(codet_ref[:, m : m + 1], cap), backs[which][index, 0:cap, :])
        picked = dot(backs[which][index, cap : cap + TAIL, 0:cap], selector(code_ref[m : m + 1, :], cap))
        gate_rows.append(jnp.sum(picked, axis=0, keepdims=True))
    gate_rows.append(jnp.zeros((TAIL - experts, rows), F32))
    grad_chances = jnp.concatenate(gate_rows, axis=0)
    chances = ch_ref[...]
    grad_logits = chances * (grad_chances - jnp.sum(chances * grad_chances, axis=0, keepdims=True))
    pieces = jnp.concatenate(split3(grad_logits), axis=0)
    wr = wr_ref[...]
    grad = grad + dot_tn(pieces, jnp.concatenate([wr, wr, wr], axis=0))
    router = dot(pieces, nm_ref[...])
    router_o_ref[...] = router[0:TAIL] + router[TAIL : 2 * TAIL] + router[2 * TAIL : 3 * TAIL]
    mid = mid_ref[...]
    scale = rms_scale(mid)
    unit = mid * scale
    gain_o_ref[...] = jnp.sum(grad * unit, axis=0, keepdims=True)
    scaled = grad * gain_ref[...]
    grad_mid = cot_ref[...].astype(F32) + scale * (scaled - unit * jnp.mean(scaled * unit, axis=-1, keepdims=True))
    gmid_ref[...] = grad_mid
    branch = grad_mid.astype(BF)
    branch_ref[...] = branch
    ga_ref[...] = dot_nt(branch, wo_ref[...]).astype(BF)


def sort_rows(place_ref, value, out_ref):
    owners = place_ref.shape[0]
    rows = value.shape[0] // owners
    for b in range(owners):
        out_ref[pl.ds(pl.multiple_of(place_ref[b] * rows, rows), rows), :] = value[b * rows : (b + 1) * rows]


def moe_bwd(cot, middle, gain_moe, normed_moe, chances, wr_t, code, code_t, w_out, slots):
    rows, width = cot.shape
    arrays, found = distinct(slots)
    args = (cot, middle, gain_moe[None], normed_moe, chances, wr_t, code, code_t, w_out, *arrays)
    wide = jax.ShapeDtypeStruct((rows, width), BF)
    return call(
        functools.partial(moe_bwd_kernel, slots=found),
        args,
        [pl.BlockSpec(memory_space=pltpu.VMEM)] * len(args),
        out_shape=[
            jax.ShapeDtypeStruct((rows, width), F32),
            wide,
            wide,
            jax.ShapeDtypeStruct((1, width), F32),
            jax.ShapeDtypeStruct((TAIL, width), F32),
        ],
        cost_estimate=estimate("moe_bwd"),
        name="moe_bwd",
    )


def attn_bwd_kernel(
    qs_ref, k_ref, v_ref, ga_ref, lse_ref, woff_ref, seg_ref,
    dq_ref, dk_ref, dv_ref, dwoff_ref, mask_scr, p_scr, ds_scr,
    *, head_dim,
):
    rows = qs_ref.shape[0]
    blocks = rows // LANES

    @pl.when(pl.program_id(0) == 0)
    def _():
        mask_scr[...] = segment_mask(seg_ref, 0, rows)

    scaled, keys, values, grads = qs_ref[...], k_ref[...], v_ref[...], ga_ref[...]
    q_t, g_t, k_t = scaled.T, grads.T, keys.T
    low_half = lax.broadcasted_iota(jnp.int32, (rows, LANES), 1) < head_dim
    dq_t, dk_parts, dv_parts = [], [], []
    lane = lax.broadcasted_iota(jnp.int32, (1, BAND), 1)
    for h in range(HEAD_GROUP):
        row = woff_ref[0, h : h + 1, :]
        band = band_of(row)
        pair = slice(LANES * (h // 2), LANES * (h // 2 + 1))
        k_pair, v_pair = keys[:, pair], values[:, pair]
        q_only, g_only = only_rows(q_t, h, head_dim), only_rows(g_t, h, head_dim)
        tiles = {}
        for b in range(0, blocks, 2):
            lanes = slice(b * LANES, (b + 2) * LANES)
            s = dot(k_pair, q_only[:, lanes]) + bias_block(band, row, b, 2, blocks) + mask_scr[:, lanes]
            p = jnp.exp(s - lse_ref[0, h : h + 1, lanes])
            dp = dot(v_pair, g_only[:, lanes])
            ds = p * (dp - jnp.sum(p * dp, axis=0, keepdims=True))
            p_scr[:, lanes] = p.astype(BF)
            ds_scr[:, lanes] = ds.astype(BF)
            for q_block in range(2):
                for k_block in range(blocks):
                    d = max(-2, min(2, k_block - b - q_block))
                    tile = ds[k_block * LANES : (k_block + 1) * LANES, q_block * LANES : (q_block + 1) * LANES]
                    tiles[d] = tiles[d] + tile if d in tiles else tile
        skewed = jnp.concatenate([tiles[1], tiles[0], tiles[-1], jnp.zeros_like(tiles[0])], axis=1)
        offsets = diagonal_sums(skewed)
        offsets = offsets + jnp.where(lane == FAR_AFTER, jnp.sum(tiles[2]), 0.0)
        offsets = offsets + jnp.where(lane == FAR_BEFORE, jnp.sum(tiles[-2]), 0.0)
        dwoff_ref[0, h : h + 1, :] = offsets
        p_all, ds_all = p_scr[...], ds_scr[...]
        dv_parts.append(dot(p_all, grads[:, pair]))
        dk_parts.append(dot(ds_all, scaled[:, pair]))
        dq_t.append(dot(k_t[h * head_dim : (h + 1) * head_dim], ds_all))
    dq = jnp.concatenate(dq_t, axis=0).T * head_dim ** (-0.5)
    dq_ref[...] = dq.astype(BF)
    for i in range(HEAD_GROUP // 2):
        pair = slice(LANES * i, LANES * (i + 1))
        dk_ref[:, pair] = jnp.where(low_half, dk_parts[2 * i], dk_parts[2 * i + 1]).astype(BF)
        dv_ref[:, pair] = jnp.where(low_half, dv_parts[2 * i], dv_parts[2 * i + 1]).astype(BF)


def attn_bwd(scaled, keys, values, grad_att, lse, woff, seg):
    rows, width = scaled.shape
    groups = woff.shape[0]
    cols = width // groups
    col_block = pl.BlockSpec((rows, cols), lambda g: (0, g))
    wide = jax.ShapeDtypeStruct((rows, width), BF)
    return call(
        functools.partial(attn_bwd_kernel, head_dim=cols // HEAD_GROUP),
        (scaled, keys, values, grad_att, lse, woff, seg),
        [
            col_block,
            col_block,
            col_block,
            col_block,
            pl.BlockSpec((1, HEAD_GROUP, rows), lambda g: (g, 0, 0)),
            pl.BlockSpec((1, HEAD_GROUP, BAND), lambda g: (g, 0, 0)),
            const_spec(seg.shape),
        ],
        grid=(groups,),
        out_specs=[col_block, col_block, col_block, pl.BlockSpec((1, HEAD_GROUP, BAND), lambda g: (g, 0, 0))],
        out_shape=[wide, wide, wide, jax.ShapeDtypeStruct((groups, HEAD_GROUP, BAND), F32)],
        scratch_shapes=[
            pltpu.VMEM((rows, rows), F32),
            pltpu.VMEM((rows, rows), BF),
            pltpu.VMEM((rows, rows), BF),
        ],
        cost_estimate=estimate("attn_bwd"),
        name="attn_bwd",
    )


def sorted_rows_kernel(pq_ref, pk_ref, tok_ref, gain_ref, att_ref, att_o_ref, out_ref, sort_scr):
    start = tok_ref[...].astype(F32)
    normed_t = (start * rms_scale(start) * gain_ref[...]).T
    attended_t = att_ref[...].astype(F32).T
    sort_rows(pq_ref, attended_t, sort_scr)
    att_o_ref[...] = sort_scr[...].astype(BF)
    for i, place_ref in enumerate((pq_ref, pk_ref)):
        sort_rows(place_ref, normed_t, sort_scr)
        out_ref[i] = sort_scr[...].astype(BF)


def sorted_rows(place_q, place_k, tokens, gain_attn, attended):
    rows, width = tokens.shape
    return call(
        sorted_rows_kernel,
        (place_q, place_k, tokens, gain_attn[None], attended),
        [pl.BlockSpec(memory_space=pltpu.SMEM)] * 2 + [pl.BlockSpec(memory_space=pltpu.VMEM)] * 3,
        out_shape=[jax.ShapeDtypeStruct((width, rows), BF), jax.ShapeDtypeStruct((2, width, rows), BF)],
        scratch_shapes=[pltpu.VMEM((width, rows), F32)],
        cost_estimate=estimate("sorted_rows"),
        name="sorted_rows",
    )


def dense_terms_kernel(att_ref, rows_ref, branch_ref, dq_ref, dk_ref, dv_ref, keep_ref, send_ref):
    half = keep_ref.shape[1]
    for i, d_ref in enumerate((branch_ref, dq_ref, dk_ref, dv_ref)):
        lhs = att_ref[...] if i == 0 else rows_ref[min(i - 1, 1)]
        term = dot(lhs, d_ref[...]).astype(BF)
        keep_ref[i] = term[:half]
        send_ref[i] = term[half:]


def dense_terms(att_t, lhs, branch, dq, dk, dv):
    _, width, rows = lhs.shape
    cols = 256
    col_block = pl.BlockSpec((rows, cols), lambda g: (0, g))
    return call(
        dense_terms_kernel,
        (att_t, lhs, branch, dq, dk, dv),
        [const_spec(att_t.shape), const_spec(lhs.shape)] + [col_block] * 4,
        grid=(width // cols,),
        out_specs=[pl.BlockSpec((4, width // 2, cols), lambda g: (0, 0, g))] * 2,
        out_shape=[jax.ShapeDtypeStruct((4, width // 2, width), BF)] * 2,
        cost_estimate=estimate("dense_terms"),
        name="dense_terms",
    )


def norm_bwd_kernel(
    place_ref, tok_ref, gain_ref, gmid_ref, small_ref, dq_ref, dk_ref, dv_ref, wq_ref, wk_ref, wv_ref,
    tg_ref, keep_ref, send_ref, acc, sort_scr, *, gain_row,
):
    step = pl.program_id(0)
    total = dot_nt(dq_ref[...], wq_ref[...]) + dot_nt(dk_ref[...], wk_ref[...]) + dot_nt(dv_ref[...], wv_ref[...])

    @pl.when(step == 0)
    def _():
        acc[...] = total

    @pl.when(step > 0)
    def _():
        acc[...] += total

    @pl.when(step == pl.num_programs(0) - 1)
    def _():
        grad = acc[...]
        start = tok_ref[...].astype(F32)
        scale = rms_scale(start)
        unit = start * scale
        gain_grad = jnp.sum(grad * unit, axis=0, keepdims=True)
        scaled = grad * gain_ref[...]
        tg_ref[...] = gmid_ref[...] + scale * (scaled - unit * jnp.mean(scaled * unit, axis=-1, keepdims=True))
        small = small_ref[...]
        row = lax.broadcasted_iota(jnp.int32, small.shape, 0)
        small = jnp.where(row == gain_row, gain_grad, small)
        small = jnp.concatenate([small, jnp.zeros((LANES - small.shape[0], small.shape[1]), F32)], axis=0)
        sort_rows(place_ref, small.T, sort_scr)
        half = sort_scr.shape[0] // 2
        keep_ref[...] = sort_scr[0:half].astype(BF)
        send_ref[...] = sort_scr[half:].astype(BF)


def norm_bwd(place, tokens, gain_attn, grad_mid, small, gain_row, dq, dk, dv, w_query, w_key, w_value):
    rows, width = tokens.shape
    cols = 256
    col_block = pl.BlockSpec((rows, cols), lambda g: (0, g))
    weight_block = pl.BlockSpec((width, cols), lambda g: (0, g))
    half = jax.ShapeDtypeStruct((width // 2, LANES), BF)
    return call(
        functools.partial(norm_bwd_kernel, gain_row=gain_row),
        (place, tokens, gain_attn[None], grad_mid, small, dq, dk, dv, w_query, w_key, w_value),
        [pl.BlockSpec(memory_space=pltpu.SMEM)]
        + [const_spec((rows, width)), const_spec((1, width)), const_spec((rows, width)), const_spec(small.shape)]
        + [col_block] * 3
        + [weight_block] * 3,
        grid=(width // cols,),
        out_specs=[const_spec((rows, width)), const_spec(half.shape), const_spec(half.shape)],
        out_shape=[jax.ShapeDtypeStruct((rows, width), F32), half, half],
        scratch_shapes=[pltpu.VMEM((rows, width), F32), pltpu.VMEM((width, LANES), F32)],
        cost_estimate=estimate("norm_bwd"),
        name="norm_bwd",
    )


def last_sums_kernel(token_ref, keep_ref, got_ref, *outs, experts, counts):
    total = keep_ref[...].astype(F32) + got_ref[...].astype(F32)
    width = outs[0].shape[1]
    for i in range(2):
        outs[i][...] = total[i, :, 0:width]
        outs[2 + i][...] = total[i, :, width + LANES :]
    small = total[0, :, width : width + LANES] + token_ref[...]
    outs[4][...] = small[:, 0:experts]
    flat = small.T
    for i, count in enumerate(counts):
        outs[5 + i][...] = flat[TAIL // 2 + i : TAIL // 2 + i + 1, 0:count]


def last_sums(token, keep, got, width, experts, counts):
    rows = keep.shape[1]
    return call(
        functools.partial(last_sums_kernel, experts=experts, counts=counts),
        (token, keep, got),
        [pl.BlockSpec(memory_space=pltpu.VMEM)] * 3,
        out_shape=[jax.ShapeDtypeStruct((rows, width), F32)] * 4
        + [jax.ShapeDtypeStruct((rows, experts), F32)]
        + [jax.ShapeDtypeStruct((1, count), F32) for count in counts],
        cost_estimate=estimate("last_sums"),
        name="last_sums",
    )


def bits_of(size):
    return size.bit_length() - 1


def swap(value, axis, size, mask):
    return lax.ppermute(value, axis, [(i, i ^ mask) for i in range(size)])


def pick(value, index, axis):
    return lax.dynamic_index_in_dim(value, index, axis, keepdims=False)


class Order:
    def __init__(self, token):
        self.token = token

    def enter(self, tree):
        tree, self.token = lax.optimization_barrier((tree, self.token))
        return tree

    leave = enter


def places(me, bits, order):
    key = jnp.arange(1 << bits, dtype=jnp.int32) ^ me
    place = jnp.zeros_like(key)
    for bit in order:
        place = place * 2 + ((key >> bit) & 1)
    return place


class Halving:
    def __init__(self, order, keep, send, dim, route, name):
        self.order, self.keep, self.to_send, self.dim, self.route, self.name = order, keep, send, dim, list(route), name
        self.got = None

    def start(self):
        axis, size, bit = self.route[0]
        with jax.named_scope(f"{self.name}_{axis}{1 << bit}"):
            value = self.order.enter(self.keep if self.to_send is None else self.to_send)
            self.got = swap(value, axis, size, 1 << bit)


def arrive(*units):
    for unit in units:
        unit.got = unit.order.leave(unit.got)


def fold_kernel(*refs, cuts, inputs):
    pairs, outs = refs[:inputs], list(refs[inputs:])
    at = 0
    for dim, last, width in cuts:
        total = []
        for _ in range(width):
            total.append(pairs[at][...].astype(F32) + pairs[at + 1][...].astype(F32))
            at += 2
        if last:
            outs.pop(0)[...] = total[0]
            continue
        rows = total[0].shape[dim] // 2
        for start in (0, rows):
            out = outs.pop(0)
            cut = [lax.slice_in_dim(v, start, start + rows, axis=dim).astype(BF) for v in total]
            if len(out.shape) == len(cut[0].shape):
                at_lane = 0
                for part in cut:
                    out[..., at_lane : at_lane + part.shape[-1]] = part
                    at_lane += part.shape[-1]
            else:
                for i in range(width):
                    out[i] = cut[i]


def fold(*units, hold=()):
    groups = [unit if isinstance(unit, tuple) else (unit,) for unit in units]
    order = groups[0][0].order
    args, cuts, shapes = [], [], []
    for group in groups:
        for unit in group:
            unit.route.pop(0)
            got = order.leave(unit.got)
            args += [unit.keep, got]
        unit = group[0]
        last = unit.to_send is None or not unit.route
        cuts.append((unit.dim, last, len(group)))
        if last:
            shapes.append(jax.ShapeDtypeStruct(got.shape, F32))
        else:
            shape = list(got.shape)
            shape[unit.dim] //= 2
            stacked = len(group) > 1 and len(shape) == 2
            if stacked:
                shape = [len(group)] + shape
            else:
                shape[-1] = sum(member.keep.shape[-1] for member in group)
            shapes += [jax.ShapeDtypeStruct(tuple(shape), BF)] * 2
    args = order.enter(args)
    outs = list(
        call(
            functools.partial(fold_kernel, cuts=cuts, inputs=len(args)),
            args,
            [pl.BlockSpec(memory_space=pltpu.VMEM)] * len(args),
            out_shape=shapes,
            cost_estimate=estimate("fold"),
            name="fold",
        )
    )
    outs = order.leave(outs)
    for group, (_, last, width) in zip(groups, cuts):
        unit = group[0]
        unit.keep = outs.pop(0)
        if not last:
            unit.to_send = outs.pop(0)
        if width > 1 and unit.keep.ndim > group[1].keep.ndim:
            unit.dim += 1
        if unit.route and unit not in hold:
            unit.start()


def fold_first_kernel(keep_ref, got_ref, small_keep_ref, small_got_ref, *outs):
    width = keep_ref.shape[2]
    small = (small_keep_ref[...] + small_got_ref[...]).astype(F32)
    for i in range(keep_ref.shape[0]):
        total = keep_ref[i].astype(F32) + got_ref[i].astype(F32)
        rows = total.shape[0] // 2
        for j in range(2):
            out = outs[i // 2 * 2 + j]
            out[i % 2, :, 0:width] = total[j * rows : (j + 1) * rows].astype(BF)
            if i < 2:
                extra = small[j * rows : (j + 1) * rows] if i == 0 else jnp.zeros((rows, LANES), F32)
                out[i, :, width:] = extra.astype(BF)


def fold_first(keep, got, small_keep, small_got):
    _, rows, width = keep.shape
    shapes = [jax.ShapeDtypeStruct((2, rows // 2, width + extra), BF) for extra in (LANES, LANES, 0, 0)]
    return call(
        fold_first_kernel,
        (keep, got, small_keep, small_got),
        [pl.BlockSpec(memory_space=pltpu.VMEM)] * 4,
        out_shape=shapes,
        cost_estimate=estimate("fold_first"),
        name="fold_first",
    )


class Return:
    def __init__(self, order, low, high, axis, size, name, pieces=False):
        self.order, self.axis, self.size, self.name = order, axis, size, name
        half = high.shape[0]
        low = [(value, 0) for value in low] if isinstance(low, list) else [(low, i) for i in range(half)]
        self.slots = low + [(high, i) for i in range(half)]
        self.bit = bits_of(size) - 1
        if pieces:
            self.start_pieces()
        else:
            with jax.named_scope(f"{self.name}{1 << self.bit}"):
                self.got = swap(self.order.enter(high), self.axis, self.size, 1 << self.bit)

    def moving(self):
        return [m for m in range(self.size) if (m >> self.bit) & 1]

    def start_pieces(self):
        self.got = []
        for m in self.moving():
            array, index = self.slots[m]
            with jax.named_scope(f"{self.name}{1 << self.bit}_{m}"):
                piece = array if array.shape[0] == 1 else array[index][None]
                self.got.append(swap(self.order.enter(piece), self.axis, self.size, 1 << self.bit))

    def fold(self):
        got = self.order.leave(self.got)
        for i, m in enumerate(self.moving()):
            self.slots[m] = (got[i], 0) if isinstance(got, list) else (got, i)
        self.bit -= 1
        if self.bit >= 0:
            self.start_pieces()

    def finish(self):
        while self.bit >= 0:
            self.fold()


class Gather:
    def __init__(self, order, value, axis, size, name):
        self.order, self.axis, self.size, self.name = order, axis, size, name
        self.blocks = {0: value}
        self.send(0, size // 2)
        if size > 2:
            self.send(0, 1)

    def send(self, m, bit):
        with jax.named_scope(f"{self.name}{m}_{bit}"):
            self.blocks[m ^ bit] = swap(self.blocks[m], self.axis, self.size, bit)

    def settle(self):
        self.blocks[1] = self.order.leave(self.blocks[1])

    def relay(self):
        self.blocks[self.size // 2] = self.order.leave(self.blocks[self.size // 2])
        bit = self.size // 2
        while bit:
            for m in range(0, self.size, 2 * bit):
                if m ^ bit not in self.blocks:
                    self.send(m, bit)
            bit //= 2

    def finish(self):
        self.blocks = self.order.leave(self.blocks)
        return [self.blocks[m] for m in range(self.size)]


def body(
    tokens,
    cotangent,
    gain_attn,
    w_query,
    w_key,
    w_value,
    w_out,
    rel_bias,
    gain_moe,
    w_router,
    w_gate,
    w_up,
    w_down,
    segments,
    routes,
    *,
    dp_size,
    ep_size,
):
    TURNS.clear()
    rows, width = tokens.shape
    buckets, heads = rel_bias.shape
    experts = w_router.shape[1]
    cap = 10 * rows // (4 * experts)
    ff = w_gate.shape[2]
    me = lax.axis_index("expert")

    cots = Gather(None, cotangent, "expert", ep_size, "cot")
    scaled, keys, values, woff, token, code, *filled, payload = attn_first(
        tokens, gain_attn, w_query, w_key, w_value, w_out, rel_bias.T, segments, gain_moe, w_router.T, routes.T
    )
    order = Order(token)
    cots.order = order
    me_ref = me.reshape(1).astype(jnp.int32)

    dp_bits, ep_bits = bits_of(dp_size), bits_of(ep_size)
    dp_me = lax.axis_index("dp")
    dp_order = list(range(dp_bits))
    z_order = [1, 0] + dp_order[2:]
    place_x = places(dp_me, dp_bits, dp_order)
    place_z = places(dp_me, dp_bits, z_order)

    def dp_route(bits):
        return [("dp", dp_size, b) for b in bits]

    dp_part = [ep_bits + b for b in dp_order]
    ep_part = list(range(1, ep_bits))
    q_bits = [0] + ep_part + dp_part
    k_bits = [0] + dp_part[:2] + ep_part + dp_part[2:]
    whole_me = dp_me * ep_size + me

    def route(bits):
        return [("expert", ep_size, b) if b < ep_bits else ("dp", dp_size, b - ep_bits) for b in bits]

    place_q, place_k = [places(whole_me, dp_bits + ep_bits, bits) for bits in (q_bits, k_bits)]

    first_half = Gather(order, order.enter(payload), "expert", ep_size, "rows_a")
    attended, lse, middle, normed_moe, chances, payload = order.leave(
        attn_second(tokens, order.enter(scaled), keys, values, w_out, woff, segments, gain_moe, w_router.T, filled)
    )
    cots.settle()
    first_half.settle()
    second_half = Gather(order, order.enter(payload), "expert", ep_size, "rows_b")
    first_half.relay()
    cots.relay()
    cots, heads_rows = cots.finish(), first_half.finish()
    blocks = ff // FF_BLOCK
    counts = [blocks - blocks // 2, blocks // 2]
    starts = [sum(counts[:i]) for i in range(len(counts))]
    grad_hidden, cot_rows = order.leave(cot_hidden(order.enter(me_ref), heads_rows, cots, w_down, cap, blocks))
    second_half.relay()
    payloads = [v for pair in zip(heads_rows, second_half.finish()) for v in pair]
    scs, units = [], []

    def expert_part(i, source, filled=()):
        *shared, gate_keep, gate_send, up_keep, up_send, sc, hid, hid_t, gg, gu = order.leave(
            expert_a(
                order.enter(source), grad_hidden, 0, w_gate, w_up, starts[i], counts[i], filled
            )
        )
        scs.append(sc)
        gate = Halving(order, gate_keep, gate_send, 0, dp_route(z_order), f"gate{i}")
        units.append((gate, Halving(order, up_keep, up_send, 0, dp_route(dp_order), f"up{i}")))
        return shared, (hid, hid_t, gg, gu)

    def by_xor(value):
        return jnp.stack([pick(value, me ^ m, 0) for m in range(experts)])

    def padded(value):
        return jnp.pad(value, ((0, TAIL - experts), (0, 0)))

    (x_all, x_t, gate_all, grad_cots), filled = expert_part(0, (me_ref, place_x, payloads, cot_rows))
    for unit in units[0]:
        unit.start()
    _, (hid, hid_t, gg, gu) = expert_part(1, (x_all, x_t, gate_all), filled)
    for unit in units[1]:
        unit.start()
    *back_low, back_high = order.leave(expert_b(order.enter(gg), gu, scs, w_gate, w_up, experts))
    backs = Return(order, back_low, back_high, "expert", ep_size, "grad_rows")
    first, second = units[0][0], units[1][0]
    fold(*units[0])
    down_parts = order.leave(down_grads(order.enter(hid_t), grad_cots, place_z, place_x))
    down_units = tuple(
        Halving(order, down_parts[2 * i], down_parts[2 * i + 1], 0, dp_route(bits), f"down{i}")
        for i, bits in enumerate((z_order, dp_order))
    )
    down = down_units[0]
    fold(*units[1], units[0], hold=units[0])
    code_xor, chances_xor, wr_xor = order.enter((by_xor(code), padded(by_xor(chances)), padded(by_xor(w_router.T))))
    backs.fold()
    att_t, normed_t = order.leave(sorted_rows(place_q, place_k, tokens, gain_attn, order.enter(attended)))
    backs.finish()
    for unit in down_units:
        unit.start()
    grad_mid, branch, grad_att, gain_moe_term, router_term = order.leave(
        moe_bwd(
            cotangent, middle, gain_moe, normed_moe, chances_xor, wr_xor, code_xor, code_xor.T, w_out,
            backs.slots,
        )
    )
    dq, dk, dv, dwoff = order.leave(attn_bwd(scaled, keys, values, order.enter(grad_att), lse, woff, segments))
    arrive(*units[1])
    dense_keep, dense_send = order.leave(dense_terms(att_t, normed_t, branch, order.enter(dq), dk, dv))
    arrive(*down_units)
    core = Halving(order, dense_keep, dense_send, 1, route(q_bits)[:1], "dense")
    core.start()
    first.start()
    fold(*down_units, units[1], hold=units[1])
    devices = dp_size * ep_size
    share = width // devices
    onehot = jnp.asarray(band_onehot(rows, buckets))
    bias_term = jnp.dot(onehot, dwoff.reshape(heads, BAND).T, precision=HIGHEST).reshape(devices, -1)
    bias_share = bias_term.shape[1]
    bias_row = jnp.pad(bias_term, ((0, 0), (0, share - bias_share))).reshape(1, width)
    small = jnp.concatenate(
        [
            jnp.pad(by_xor(router_term), ((0, TAIL // 2 - experts), (0, 0))),
            jnp.zeros((1, width), F32),
            gain_moe_term,
            bias_row,
            jnp.zeros((TAIL // 2 - 3, width), F32),
        ],
        axis=0,
    )
    token_grad, small_keep, small_send = order.leave(
        norm_bwd(
            place_q, tokens, gain_attn, grad_mid, order.enter(small), TAIL // 2, dq, dk, dv, w_query, w_key, w_value
        )
    )
    with jax.named_scope("small_expert1"):
        small_got = swap(order.enter(small_send), "expert", ep_size, 1)
    core_got = order.leave(core.got)
    halves = order.leave(fold_first(order.enter(dense_keep), core_got, small_keep, order.leave(small_got)))
    dense = [
        Halving(order, halves[2 * i], halves[2 * i + 1], 1, route(bits)[1:], name)
        for i, (bits, name) in enumerate(((q_bits, "out_q"), (k_bits, "k_v")))
    ]
    out_q, k_v = dense
    arrive(down, first)
    k_v.start()
    out_q.start()
    second.start()
    prod_low, prod_high = order.leave(produced_rows(order.enter(hid), w_down, experts))
    returned = Return(order, prod_low, prod_high, "expert", ep_size, "produced_rows")
    fold(k_v, out_q, down_units, first, second)
    fold(k_v, out_q)
    while first.route or second.route:
        fold(*[unit for unit in (first, second) if unit.route])
    terms = [first.keep, second.keep]
    gate_grad = order.leave(jnp.concatenate([term[0] for term in terms], axis=1)[None])
    up_grad = order.leave(jnp.concatenate([term[1] for term in terms], axis=1)[None])
    returned.fold()
    returned.finish()
    layer_out = order.leave(layer_output(middle, chances_xor, code_xor.T, returned.slots))
    while len(out_q.route) > 2:
        fold(*[unit for unit in (out_q, k_v, down) if unit.route])
    fold(*[(out_q, k_v)] + ([down] if down.route else []))
    down_grad = order.leave(jnp.concatenate([down.keep[0], down.keep[1]], axis=1)[None])
    pairs = order.leave([out_q.keep, out_q.got])
    out_grad, query_grad, key_grad, value_grad, router_grad, *gains = last_sums(
        order.token, *pairs, width, experts, (share, share, bias_share)
    )
    gain_attn_grad, gain_moe_grad, bias_grad = [value.reshape(-1) for value in gains]
    return (
        layer_out,
        token_grad,
        query_grad,
        key_grad,
        value_grad,
        out_grad,
        gain_attn_grad,
        gain_moe_grad,
        bias_grad,
        router_grad,
        gate_grad,
        up_grad,
        down_grad,
    )


def solution(mesh):
    in_specs = (
        P(("dp", "expert"), None),
        P(("dp", "expert"), None),
        P(),
        P(),
        P(),
        P(),
        P(),
        P(),
        P(),
        P(),
        P("expert", None, None),
        P("expert", None, None),
        P("expert", None, None),
        P(("dp", "expert"), None),
        P(("dp", "expert"), None),
    )
    out_specs = (
        P(("dp", "expert"), None),
        P(("dp", "expert"), None),
        P(("dp", "expert"), None),
        P(("dp", "expert"), None),
        P(("dp", "expert"), None),
        P(("dp", "expert"), None),
        P(("dp", "expert")),
        P(("dp", "expert")),
        P(("dp", "expert")),
        P(("dp", "expert"), None),
        P("expert", "dp", None),
        P("expert", "dp", None),
        P("expert", "dp", None),
    )
    run = functools.partial(body, dp_size=mesh.shape["dp"], ep_size=mesh.shape["expert"])
    return jax.shard_map(run, mesh=mesh, in_specs=in_specs, out_specs=out_specs, check_vma=False)
```

```python
import functools

import jax
import jax.numpy as jnp
import numpy as np
from jax import lax
from jax.experimental import pallas as pl
from jax.experimental.pallas import tpu as pltpu
from jax.sharding import PartitionSpec as P

EPS = 1e-06
HIGHEST = lax.Precision.HIGHEST
LANES = 128
BAND = 4 * LANES
HEAD_GROUP = 4
TAIL = 16
FAR = -1e30
BF = jnp.bfloat16
F32 = jnp.float32
VMEM_LIMIT = 56 * 1024 * 1024


def bucket_of(relative, buckets):
    halfway = buckets // 2
    exact_span = halfway // 2
    distance = np.abs(relative)
    beyond = exact_span + (
        np.log(np.maximum(distance, 1) / exact_span)
        / np.log(128.0 / exact_span)
        * (halfway - exact_span)
    ).astype(np.int64)
    beyond = np.minimum(beyond, halfway - 1)
    return (
        (relative > 0).astype(np.int64) * halfway
        + np.where(distance < exact_span, distance, beyond)
    ).astype(np.int32)


def band_onehot(length, buckets):
    place = np.arange(BAND)
    relative = np.where(place <= 3 * LANES, LANES - place, BAND + LANES - place)
    table = (bucket_of(relative, buckets)[None, :] == np.arange(buckets)[:, None]).astype(np.float32)
    table[:, 3 * LANES] = 0.0
    far = np.arange(LANES, length)
    assert np.all(bucket_of(far, buckets) == bucket_of(far, buckets)[0])
    assert np.all(bucket_of(-far, buckets) == bucket_of(-far, buckets)[0])
    return table


FAR_AFTER = 3 * LANES + 1
FAR_BEFORE = 3 * LANES - 1


def dot(a, b):
    return lax.dot_general(a, b, (((1,), (0,)), ((), ())), preferred_element_type=F32)


def dot_nt(a, b):
    return lax.dot_general(a, b, (((1,), (1,)), ((), ())), preferred_element_type=F32)


def dot_tn(a, b):
    return lax.dot_general(a, b, (((0,), (0,)), ((), ())), preferred_element_type=F32)


def split3(value):
    hi = value.astype(BF)
    rest = value - hi.astype(F32)
    mid = rest.astype(BF)
    low = (rest - mid.astype(F32)).astype(BF)
    return hi, mid, low


def rms_scale(value):
    return lax.rsqrt(jnp.mean(value * value, axis=-1, keepdims=True) + EPS)


def params(**kw):
    return pltpu.CompilerParams(vmem_limit_bytes=VMEM_LIMIT, **kw)


TIMES = {
    ("down_grads", 0): 10.0,
    ("dense_terms", 0): 13.1,
    ("fold", 1): 2.0,
}


TURNS = {}


def estimate(name):
    turn = TURNS.get(name, 0)
    TURNS[name] = turn + 1
    time = TIMES.get((name, turn), 0.1)
    return pl.CostEstimate(flops=int(time * 1.15e9), bytes_accessed=100000, transcendentals=0)


def call(kernel, args, in_specs, **kw):
    return pl.pallas_call(kernel, in_specs=list(in_specs), compiler_params=params(), **kw)(*args)


def whole_specs(args):
    return [const_spec(a.shape) for a in args]


def const_spec(shape):
    return pl.BlockSpec(shape, lambda *_: (0,) * len(shape))


def selector(code_row, rows):
    place = lax.broadcasted_iota(jnp.int32, (rows, code_row.shape[1]), 0)
    return jnp.where(place == code_row, 1.0, 0.0).astype(BF)


def selector_t(code_column, rows):
    place = lax.broadcasted_iota(jnp.int32, (code_column.shape[0], rows), 1)
    return jnp.where(place == code_column, 1.0, 0.0).astype(BF)


def band_of(row):
    return pltpu.roll(jnp.broadcast_to(row, (LANES, BAND)), 0, 1, stride=1, stride_axis=0)


def diagonal_sums(skewed):
    eight = skewed[0:8]
    for start in range(8, LANES, 8):
        eight = eight + pltpu.roll(skewed[start : start + 8], BAND - start, 1)
    total = eight[0:1]
    for row in range(1, 8):
        total = total + pltpu.roll(eight[row : row + 1], BAND - row, 1)
    return total


def bias_block(band, row, first, count, k_blocks):
    far = [jnp.broadcast_to(row[:, at : at + 1], (LANES, LANES)) for at in (FAR_BEFORE, FAR_AFTER)]
    columns = []
    for q_block in range(first, first + count):
        pieces = []
        for k_block in range(k_blocks):
            d = k_block - q_block
            pieces.append(far[1] if d > 1 else far[0] if d < -1 else band[:, LANES * (1 - d) : LANES * (2 - d)])
        columns.append(jnp.concatenate(pieces, axis=0))
    return jnp.concatenate(columns, axis=1)


def only_rows(value, h, head_dim):
    mine = value[h * head_dim : (h + 1) * head_dim]
    none = jnp.zeros_like(mine)
    return jnp.concatenate([mine, none] if h % 2 == 0 else [none, mine], axis=0)


def attend(scaled, keys, values, woff_ref, mask, first, head_dim):
    count = scaled.shape[0] // LANES
    q_t, v_t = scaled.T, values.T
    heads_t, totals = [], []
    for h in range(HEAD_GROUP):
        row = woff_ref[0, h : h + 1, :]
        bias = bias_block(band_of(row), row, first, count, keys.shape[0] // LANES)
        k_pair = keys[:, LANES * (h // 2) : LANES * (h // 2 + 1)]
        s = dot(k_pair, only_rows(q_t, h, head_dim)) + bias + mask
        peak = jnp.max(s, axis=0, keepdims=True)
        p = jnp.exp(s - peak)
        total = jnp.sum(p, axis=0, keepdims=True)
        heads_t.append(dot(v_t[h * head_dim : (h + 1) * head_dim], p.astype(BF)) * (1.0 / total))
        totals.append(peak + jnp.log(total))
    return jnp.concatenate(heads_t, axis=0).T.astype(BF), jnp.concatenate(totals, axis=0)


def slot_codes(routes):
    chosen = routes.astype(F32)
    tokens = chosen.shape[1]
    numbers = lax.broadcasted_iota(jnp.int32, (TAIL // 2, tokens), 0).astype(F32)
    named = jnp.logical_or(numbers == chosen[0:1], numbers == chosen[1:2])
    row = lax.broadcasted_iota(jnp.int32, (tokens, tokens), 0)
    lane = lax.broadcasted_iota(jnp.int32, (tokens, tokens), 1)
    before = jnp.where(row < lane, 1.0, 0.0).astype(BF)
    return jnp.where(named, dot(jnp.where(named, 1.0, 0.0).astype(BF), before), -1.0)


def packed_codes(codes):
    upper = jnp.floor((codes + 1.0) * (1.0 / 16.0))
    return jnp.concatenate([upper, codes + 1.0 - 16.0 * upper], axis=0)


def own_code(me, packed):
    row = lax.broadcasted_iota(jnp.int32, packed.shape, 0)
    weight = jnp.where(row == me, 16.0, jnp.where(row == me + TAIL // 2, 1.0, 0.0))
    return (jnp.sum(packed.astype(F32) * weight, axis=0, keepdims=True) - 1.0).astype(jnp.int32)


def route_rows(mid, gain_ref, wr_ref, experts, nm_ref, ch_ref, payload_ref, codes=None):
    rows = mid.shape[0]
    nm = (mid * rms_scale(mid) * gain_ref[...]).astype(BF)
    nm_ref[...] = nm
    router = jnp.concatenate([wr_ref[...].astype(F32), jnp.zeros((TAIL - experts, nm.shape[1]), F32)], axis=0)
    logits = dot_nt(router.astype(BF), nm)
    live = lax.broadcasted_iota(jnp.int32, logits.shape, 0) < experts
    logits = jnp.where(live, logits, FAR)
    raised = jnp.exp(logits - jnp.max(logits, axis=0, keepdims=True))
    chances = raised / jnp.sum(raised, axis=0, keepdims=True)
    ch_ref[...] = chances
    hi = chances.astype(BF).astype(F32)
    both = jnp.concatenate([hi[: TAIL // 2], (chances - hi)[: TAIL // 2]], axis=0)
    payload_ref[0:rows, :] = nm
    tail = [both] if codes is None else [both, packed_codes(codes)]
    used = sum(v.shape[1] for v in tail)
    tail.append(jnp.zeros((TAIL, nm.shape[1] - used), F32))
    payload_ref[rows:, :] = jnp.concatenate(tail, axis=1).astype(BF)


def segment_mask(seg_ref, first, count):
    seg = seg_ref[...].astype(F32)
    column = jnp.broadcast_to(seg, (8, seg.shape[1])).T[:, 0:1]
    return jnp.where(column == seg[:, first : first + count], 0.0, FAR)


def attn_first_kernel(
    tok_ref, gain_a_ref, wq_ref, wk_ref, wv_ref, wo_ref, bias_ref, onehot_ref, seg_ref, gain_m_ref, wr_ref, routes_ref,
    qs_ref, k_ref, v_ref, woff_ref, token_ref, code_ref, att_ref, lse_ref, mid_ref, nm_ref, ch_ref, payload_ref,
    n_scr, mask_scr, woff_scr, code_scr,
    *, experts, head_dim,
):
    step = pl.program_id(0)
    rows = att_ref.shape[0]

    @pl.when(step == 0)
    def _():
        start = tok_ref[...].astype(F32)
        n_scr[...] = (start * rms_scale(start) * gain_a_ref[...]).astype(BF)
        mid_ref[...] = start[:rows]
        mask_scr[...] = segment_mask(seg_ref, 0, rows)
        token_ref[...] = jnp.where(seg_ref[:, 0:LANES] < 0, 1.0, 0.0)
        codes = slot_codes(routes_ref[...])
        code_scr[...] = codes
        code_ref[...] = codes[:experts].astype(jnp.int32)
        table = onehot_ref[...]
        offsets = sum(dot(part, table) for part in split3(bias_ref[...]))
        for g in range(woff_scr.shape[0]):
            woff_scr[g] = offsets[g * HEAD_GROUP : (g + 1) * HEAD_GROUP]

    woff_ref[0] = woff_scr[step]

    normed = n_scr[...]
    scaled = (dot(normed, wq_ref[...]).astype(BF).astype(F32) * head_dim ** (-0.5)).astype(BF)
    keys = dot(normed, wk_ref[...]).astype(BF)
    values = dot(normed, wv_ref[...]).astype(BF)
    qs_ref[...] = scaled
    k_ref[...] = keys
    v_ref[...] = values
    att, totals = attend(scaled[:rows], keys, values, woff_ref, mask_scr[...], 0, head_dim)
    att_ref[...] = att
    lse_ref[0] = totals
    mid_ref[...] += dot(att, wo_ref[...])

    @pl.when(step == pl.num_programs(0) - 1)
    def _():
        route_rows(mid_ref[...], gain_m_ref, wr_ref, experts, nm_ref, ch_ref, payload_ref, code_scr[...])


def attn_second_kernel(
    tok_ref, qs_ref, k_ref, v_ref, wo_ref, woff_ref, seg_ref, gain_m_ref, wr_ref, *refs, experts, head_dim
):
    att_ref, lse_ref, mid_ref, nm_ref, ch_ref, payload_ref, mask_scr = refs[-7:]
    step = pl.program_id(0)
    rows = att_ref.shape[0]

    @pl.when(step == 0)
    def _():
        mid_ref[...] = tok_ref[...].astype(F32)
        mask_scr[...] = segment_mask(seg_ref, rows, rows)

    att, totals = attend(qs_ref[...], k_ref[...], v_ref[...], woff_ref, mask_scr[...], rows // LANES, head_dim)
    att_ref[...] = att
    lse_ref[0] = totals
    mid_ref[...] += dot(att, wo_ref[...])

    @pl.when(step == pl.num_programs(0) - 1)
    def _():
        route_rows(mid_ref[...], gain_m_ref, wr_ref, experts, nm_ref, ch_ref, payload_ref)


def attn_halves(rows, width, groups, half):
    cols, part = width // groups, rows // 2
    wide = jax.ShapeDtypeStruct((rows, width), BF)
    shapes = [
        wide,
        jax.ShapeDtypeStruct((groups, HEAD_GROUP, rows), F32),
        jax.ShapeDtypeStruct((rows, width), F32),
        wide,
        jax.ShapeDtypeStruct((TAIL, rows), F32),
        jax.ShapeDtypeStruct((part + TAIL, width), BF),
    ]
    specs = [
        pl.BlockSpec((part, cols), lambda g: (half, g)),
        pl.BlockSpec((1, HEAD_GROUP, part), lambda g: (g, 0, half)),
        pl.BlockSpec((part, width), lambda g: (half, 0)),
        pl.BlockSpec((part, width), lambda g: (half, 0)),
        pl.BlockSpec((TAIL, part), lambda g: (0, half)),
        const_spec((part + TAIL, width)),
    ]
    return shapes, specs


def attn_first(tokens, gain_attn, w_query, w_key, w_value, w_out, rel_bias, seg, gain_moe, w_router, routes):
    rows, width = tokens.shape
    heads, buckets = rel_bias.shape
    experts = w_router.shape[0]
    groups = heads // HEAD_GROUP
    cols, part = width // groups, rows // 2
    weight_block = pl.BlockSpec((width, cols), lambda g: (0, g))
    shapes, specs = attn_halves(rows, width, groups, 0)
    wide = jax.ShapeDtypeStruct((rows, width), BF)
    return call(
        functools.partial(attn_first_kernel, experts=experts, head_dim=cols // HEAD_GROUP),
        (tokens, gain_attn[None], w_query, w_key, w_value, w_out, rel_bias, jnp.asarray(band_onehot(rows, buckets)).astype(BF),
         seg, gain_moe[None], w_router, routes),
        [
            const_spec((rows, width)),
            const_spec((1, width)),
            weight_block,
            weight_block,
            weight_block,
            pl.BlockSpec((cols, width), lambda g: (g, 0)),
            const_spec(rel_bias.shape),
            const_spec((buckets, BAND)),
            const_spec(seg.shape),
            const_spec((1, width)),
            const_spec(w_router.shape),
            const_spec(routes.shape),
        ],
        grid=(groups,),
        out_specs=[pl.BlockSpec((rows, cols), lambda g: (0, g))] * 3
        + [pl.BlockSpec((1, HEAD_GROUP, BAND), lambda g: (g, 0, 0)), const_spec((1, LANES)), const_spec((experts, rows))]
        + specs,
        out_shape=[wide] * 3
        + [jax.ShapeDtypeStruct((groups, HEAD_GROUP, BAND), F32), jax.ShapeDtypeStruct((1, LANES), F32)]
        + [jax.ShapeDtypeStruct((experts, rows), jnp.int32)]
        + shapes,
        scratch_shapes=[
            pltpu.VMEM((rows, width), BF),
            pltpu.VMEM((rows, part), F32),
            pltpu.VMEM((groups, HEAD_GROUP, BAND), F32),
            pltpu.VMEM((TAIL // 2, rows), F32),
        ],
        cost_estimate=estimate("attn_first"),
        name="attn_first",
    )


def attn_second(tokens, scaled, keys, values, w_out, woff, seg, gain_moe, w_router, filled):
    rows, width = tokens.shape
    experts = w_router.shape[0]
    groups = woff.shape[0]
    cols, part = width // groups, rows // 2
    col_block = pl.BlockSpec((rows, cols), lambda g: (0, g))
    shapes, specs = attn_halves(rows, width, groups, 1)
    args = (tokens, scaled, keys, values, w_out, woff, seg, gain_moe[None], w_router)
    return call(
        functools.partial(attn_second_kernel, experts=experts, head_dim=cols // HEAD_GROUP),
        (*args, *filled),
        [
            pl.BlockSpec((part, width), lambda g: (1, 0)),
            pl.BlockSpec((part, cols), lambda g: (1, g)),
            col_block,
            col_block,
            pl.BlockSpec((cols, width), lambda g: (g, 0)),
            pl.BlockSpec((1, HEAD_GROUP, BAND), lambda g: (g, 0, 0)),
            const_spec(seg.shape),
            const_spec((1, width)),
            const_spec(w_router.shape),
        ]
        + [pl.BlockSpec(memory_space=pl.ANY)] * len(filled),
        grid=(groups,),
        out_specs=specs,
        out_shape=shapes,
        scratch_shapes=[pltpu.VMEM((rows, part), F32)],
        input_output_aliases={len(args) + i: i for i in range(len(filled))},
        cost_estimate=estimate("attn_second"),
        name="attn_second",
    )


def gelu_parts(gate):
    c0 = np.float32(np.sqrt(2.0 / np.pi))
    c1 = np.float32(0.044715)
    square = gate * gate
    t = jnp.tanh(c0 * gate * (1.0 + c1 * square))
    half = 0.5 * (1.0 + t)
    value = gate * half
    slope = half + 0.5 * gate * (1.0 - t * t) * (c0 * (1.0 + 3.0 * c1 * square))
    return value, slope


FF_BLOCK = 256


def cot_hidden_kernel(me_ref, *refs, experts):
    tail_refs, cot_refs, wd_ref = refs[:experts], refs[experts : 2 * experts], refs[2 * experts]
    out_ref, rows_ref = refs[2 * experts + 1 :]

    @pl.when(pl.program_id(0) == 0)
    def _():
        cap = rows_ref.shape[0] // experts
        tokens = cot_refs[0].shape[0]
        for m, (tail_ref, cot_ref) in enumerate(zip(tail_refs, cot_refs)):
            code = own_code(me_ref[0], tail_ref[:, tokens // 2 : tokens // 2 + tokens])
            rows_ref[m * cap : (m + 1) * cap, :] = dot(selector(code, cap), cot_ref[...]).astype(BF)

    out_ref[...] = dot_nt(rows_ref[...], wd_ref[0]).astype(BF)


def cot_hidden(me, payloads, cots, w_down, cap, count):
    experts = len(cots)
    width = cots[0].shape[1]
    rows = experts * cap
    span = count * FF_BLOCK // 2
    last = payloads[0].shape[0] // TAIL - 1
    return call(
        functools.partial(cot_hidden_kernel, experts=experts),
        (me, *payloads, *cots, w_down),
        [pl.BlockSpec(memory_space=pltpu.SMEM)]
        + [pl.BlockSpec((TAIL, width), lambda f: (last, 0))] * experts
        + whole_specs(cots)
        + [pl.BlockSpec((1, span, width), lambda f: (0, f, 0))],
        grid=(2,),
        out_specs=[pl.BlockSpec((rows, span), lambda f: (0, f)), const_spec((rows, width))],
        out_shape=[jax.ShapeDtypeStruct((rows, count * FF_BLOCK), BF), jax.ShapeDtypeStruct((rows, width), BF)],
        cost_estimate=estimate("cot_hidden"),
        name="cot_hidden",
    )


ROW_BLOCK = 320


def expert_first(me_ref, place_ref, payloads, cot_ref, x_ref, xt_ref, gate_ref, gc_ref):
    experts = len(payloads) // 2
    cap = x_ref.shape[0] // experts
    part = payloads[0].shape[0] - TAIL
    row = lax.broadcasted_iota(jnp.int32, (TAIL, part), 0)
    mine = jnp.logical_or(row == me_ref[0], row == me_ref[0] + TAIL // 2)
    for m in range(experts):
        code = own_code(me_ref[0], payloads[2 * m][part:, part : 3 * part])
        chosen = selector(code, cap)
        place = slice(m * cap, (m + 1) * cap)
        total = jnp.zeros((cap, x_ref.shape[1]), F32)
        gate = jnp.zeros((cap, 1), F32)
        for i in range(2):
            payload = payloads[2 * m + i]
            part_chosen = chosen[:, i * part : (i + 1) * part]
            total = total + dot(part_chosen, payload[0:part, :])
            chances = jnp.sum(jnp.where(mine, payload[part:, 0:part].astype(F32), 0.0), axis=0, keepdims=True)
            gate = gate + jnp.sum(part_chosen.astype(F32) * chances, axis=1, keepdims=True)
        x_ref[place, :] = total.astype(BF)
        gate_ref[place, :] = jnp.broadcast_to(gate, (cap, LANES))
        gc_ref[place, :] = (cot_ref[place, :].astype(F32) * gate).astype(BF)
    flipped = x_ref[...].T
    owners = place_ref.shape[0]
    rows = flipped.shape[0] // owners
    for b in range(owners):
        at = pl.multiple_of(place_ref[b] * rows, rows)
        xt_ref[pl.ds(at, rows), :] = flipped[b * rows : (b + 1) * rows]


def expert_a_kernel(*refs, experts):
    step = pl.program_id(0)
    if experts:
        me_ref, place_ref = refs[:2]
        payloads = refs[2 : 2 + 2 * experts]
        cot_ref, gh_ref, wg_ref, wu_ref, x_ref, xt_ref, gate_ref, gc_ref = refs[2 + 2 * experts : 10 + 2 * experts]

        @pl.when(step == 0)
        def _():
            expert_first(me_ref, place_ref, payloads, cot_ref, x_ref, xt_ref, gate_ref, gc_ref)

    else:
        x_ref, xt_ref, gate_ref, gh_ref, wg_ref, wu_ref = refs[:6]
    gate_keep_ref, gate_send_ref, up_keep_ref, up_send_ref, sc_ref, hid_ref, hidt_ref, gg_ref, gu_ref = refs[-9:]

    @pl.when(step == 0)
    def _():
        sc_ref[...] = jnp.zeros_like(sc_ref)

    wg, wu = wg_ref[0], wu_ref[0]
    width = wg.shape[1]
    for start in range(0, x_ref.shape[0], ROW_BLOCK):
        part = slice(start, start + ROW_BLOCK)
        x = x_ref[part, :]
        gate_pre = dot(x, wg)
        up_pre = dot(x, wu)
        grad = gh_ref[part, :].astype(F32)
        act, slope = gelu_parts(gate_pre)
        hidden = act * up_pre
        hid_ref[part, :] = hidden.astype(BF)
        product = hidden * grad
        folded = product[:, 0:LANES]
        for i in range(1, width // LANES):
            folded = folded + product[:, i * LANES : (i + 1) * LANES]
        sc_ref[part, :] += folded
        grad = grad * gate_ref[part, 0:1]
        gg_ref[part, :] = (slope * up_pre * grad).astype(BF)
        gu_ref[part, :] = (act * grad).astype(BF)
    hidt_ref[...] = hid_ref[...].T
    xt = xt_ref[...]
    cut = xt.shape[0] // 4
    for grad_ref, keep_ref, send_ref, second in ((gg_ref, gate_keep_ref, gate_send_ref, 1), (gu_ref, up_keep_ref, up_send_ref, 0)):
        term = dot(xt, grad_ref[...]).astype(BF)
        for q in range(4):
            upper, lower = (q % 2, q // 2) if second else (q // 2, q % 2)
            (send_ref if upper else keep_ref)[lower * cut : (lower + 1) * cut] = term[q * cut : (q + 1) * cut]


def expert_a(source, gh, gh_first, w_gate, w_up, first, count, filled=()):
    opening = 0 if filled else len(source[2]) // 2
    rows = gh.shape[0]
    width, ff = w_gate.shape[1:]
    span = count * FF_BLOCK
    col_weight = pl.BlockSpec((1, width, FF_BLOCK), lambda f: (0, 0, first + f))
    out_block = pl.BlockSpec((rows, FF_BLOCK), lambda f: (0, first + f))
    wide = jax.ShapeDtypeStruct((rows, ff), BF)
    tall = jax.ShapeDtypeStruct((ff, rows), BF)
    term = jax.ShapeDtypeStruct((width // 2, span), BF)
    term_block = pl.BlockSpec((width // 2, FF_BLOCK), lambda f: (0, f))
    if opening:
        me, place, payloads, cot_rows = source
        args = (me, place, *payloads, cot_rows)
        specs = [pl.BlockSpec(memory_space=pltpu.SMEM)] * 2 + whole_specs((*payloads, cot_rows))
        shared = [
            jax.ShapeDtypeStruct((rows, width), BF),
            jax.ShapeDtypeStruct((width, rows), BF),
            jax.ShapeDtypeStruct((rows, LANES), F32),
            jax.ShapeDtypeStruct((rows, width), BF),
        ]
    else:
        args = tuple(source)
        specs = whole_specs(source)
        shared = []
    args = (*args, gh, w_gate, w_up)
    used = len(args)
    first_filled = len(shared) + 5

    def run(*refs):
        expert_a_kernel(*refs[:used], *refs[used + len(filled) :], experts=opening)

    return call(
        run,
        (*args, *filled),
        specs
        + [pl.BlockSpec((rows, FF_BLOCK), lambda f: (0, first - gh_first + f)), col_weight, col_weight]
        + [pl.BlockSpec(memory_space=pl.ANY)] * len(filled),
        grid=(count,),
        out_specs=whole_specs(shared)
        + [term_block] * 4
        + [const_spec((rows, LANES)), out_block]
        + [pl.BlockSpec((FF_BLOCK, rows), lambda f: (first + f, 0)), out_block, out_block],
        out_shape=shared + [term] * 4 + [jax.ShapeDtypeStruct((rows, LANES), F32), wide, tall, wide, wide],
        input_output_aliases={used + i: first_filled + i for i in range(len(filled))},
        cost_estimate=estimate("expert_grads"),
        name="expert_grads",
    )


def expert_b_kernel(gg_ref, gu_ref, *refs, cap, experts):
    count = experts // 2 + 4
    sc_refs, (wg_ref, wu_ref, *outs, acc) = refs[:-count], refs[-count:]
    part_sum = dot_nt(gg_ref[...], wg_ref[0]) + dot_nt(gu_ref[...], wu_ref[0])
    step, block = pl.program_id(0), pl.program_id(1)

    @pl.when(step == 0)
    def _():
        acc[block] = part_sum

    def finish(out_ref, at):
        total = acc[block] + part_sum
        row = lax.broadcasted_iota(jnp.int32, (cap, cap), 0)
        lane = lax.broadcasted_iota(jnp.int32, (cap, cap), 1)
        place = lax.broadcasted_iota(jnp.int32, (TAIL, cap), 0)
        out_ref[at, 0:cap, :] = total.astype(BF)
        folded = sc_refs[0][...]
        for other in sc_refs[1:]:
            folded = folded + other[...]
        column = jnp.sum(folded, axis=1, keepdims=True)
        flat = jnp.sum(jnp.where(row == lane, column, 0.0), axis=0, keepdims=True)
        hi, mid, low = split3(flat)
        packed = jnp.where(
            place == 0, hi.astype(F32), jnp.where(place == 1, mid.astype(F32), jnp.where(place == 2, low.astype(F32), 0.0))
        )
        out_ref[at, cap : cap + TAIL, :] = jnp.zeros((TAIL, total.shape[1]), BF)
        out_ref[at, cap : cap + TAIL, 0:cap] = packed.astype(BF)

    last = step == pl.num_programs(0) - 1
    half = experts // 2
    for m in range(experts):

        @pl.when(jnp.logical_and(last, block == m))
        def _(m=m):
            finish(outs[m] if m < half else outs[half], 0 if m < half else m - half)


def expert_b(gg, gu, scs, w_gate, w_up, experts):
    rows, ff = gg.shape
    width = w_gate.shape[1]
    cap = rows // experts
    cut = ff // 2
    grads = pl.BlockSpec((cap, cut), lambda k, m: (m, k))
    sums = pl.BlockSpec((cap, LANES), lambda k, m: (m, 0))
    weight = pl.BlockSpec((1, width, cut), lambda k, m: (0, 0, k))
    return call(
        functools.partial(expert_b_kernel, cap=cap, experts=experts),
        (gg, gu, *scs, w_gate, w_up),
        [grads, grads] + [sums] * len(scs) + [weight, weight],
        grid=(2, experts),
        out_specs=[const_spec((1, cap + TAIL, width))] * (experts // 2) + [const_spec((experts // 2, cap + TAIL, width))],
        out_shape=[jax.ShapeDtypeStruct((1, cap + TAIL, width), BF)] * (experts // 2)
        + [jax.ShapeDtypeStruct((experts // 2, cap + TAIL, width), BF)],
        scratch_shapes=[pltpu.VMEM((experts, cap, width), F32)],
        cost_estimate=estimate("expert_input_grad"),
        name="expert_input_grad",
    )


def down_kernel(place_a_ref, place_b_ref, hidt_ref, gc_ref, *outs):
    owners = place_a_ref.shape[0]
    shard = 2 * outs[0].shape[0] // owners
    size = int(np.gcd(shard, 32))
    rows = hidt_ref.shape[0]
    step = pl.program_id(0)
    total = dot(hidt_ref[...], gc_ref[...]).astype(BF)
    half = total.shape[1] // 2
    for i in range(rows // size):
        row = step * rows + i * size
        owner = row // shard
        piece = total[i * size : (i + 1) * size]
        for keep_ref, send_ref, place_ref, cols in (
            (outs[0], outs[1], place_a_ref, piece[:, :half]),
            (outs[2], outs[3], place_b_ref, piece[:, half:]),
        ):
            place = place_ref[owner]
            at = pl.multiple_of((place % (owners // 2)) * shard + (row - owner * shard), size)

            @pl.when(place < owners // 2)
            def _(keep_ref=keep_ref, at=at, cols=cols):
                keep_ref[pl.ds(at, size), :] = cols

            @pl.when(place >= owners // 2)
            def _(send_ref=send_ref, at=at, cols=cols):
                send_ref[pl.ds(at, size), :] = cols


def down_grads(hid_t, grad_cots, place_a, place_b):
    rows, width = grad_cots.shape
    ff = hid_t.shape[0]
    table = pl.BlockSpec(memory_space=pltpu.SMEM)
    part = jax.ShapeDtypeStruct((ff // 2, width // 2), BF)
    return call(
        down_kernel,
        (place_a, place_b, hid_t, grad_cots),
        [table, table, pl.BlockSpec((ff // 4, rows), lambda f: (f, 0)), const_spec((rows, width))],
        grid=(4,),
        out_specs=[const_spec(part.shape)] * 4,
        out_shape=[part] * 4,
        cost_estimate=estimate("down_grads"),
        name="down_grads",
    )


def produced_kernel(hid_ref, wd_ref, low_ref, high_ref):
    rows = dot(hid_ref[...], wd_ref[0]).astype(BF)
    lower = pl.program_id(0) < pl.num_programs(0) // 2

    @pl.when(lower)
    def _():
        low_ref[0] = rows

    @pl.when(jnp.logical_not(lower))
    def _():
        high_ref[0] = rows


def produced_rows(hid, w_down, experts):
    rows, ff = hid.shape
    width = w_down.shape[2]
    cap, half = rows // experts, experts // 2
    return call(
        produced_kernel,
        (hid, w_down),
        [pl.BlockSpec((cap, ff), lambda m: (m, 0)), const_spec(w_down.shape)],
        grid=(experts,),
        out_specs=[
            pl.BlockSpec((1, cap, width), lambda m: (jnp.minimum(m, half - 1), 0, 0)),
            pl.BlockSpec((1, cap, width), lambda m: (jnp.maximum(m - half, 0), 0, 0)),
        ],
        out_shape=[jax.ShapeDtypeStruct((half, cap, width), BF)] * 2,
        cost_estimate=estimate("produced_rows"),
        name="produced_rows",
    )


def distinct(slots):
    arrays, found = [], []
    for array, index in slots:
        which = next((i for i, other in enumerate(arrays) if other is array), None)
        if which is None:
            which = len(arrays)
            arrays.append(array)
        found.append((which, index))
    return arrays, found


def layer_out_kernel(mid_ref, ch_ref, code_ref, *refs, slots):
    parts, out_ref = refs[:-1], refs[-1]
    cap = parts[0].shape[1]
    total = mid_ref[...]
    chances = ch_ref[...].T
    for m, (which, index) in enumerate(slots):
        picked = dot(selector_t(code_ref[:, m : m + 1], cap), parts[which][index])
        total = total + chances[:, m : m + 1] * picked
    out_ref[...] = total.astype(BF)


def layer_output(middle, chances, code_t, slots):
    rows, width = middle.shape
    arrays, found = distinct(slots)
    args = (middle, chances, code_t, *arrays)
    return call(
        functools.partial(layer_out_kernel, slots=found),
        args,
        [pl.BlockSpec(memory_space=pltpu.VMEM)] * len(args),
        out_shape=jax.ShapeDtypeStruct((rows, width), BF),
        cost_estimate=estimate("layer_output"),
        name="layer_output",
    )


def moe_bwd_kernel(
    cot_ref, mid_ref, gain_ref, nm_ref, ch_ref, wr_ref, code_ref, codet_ref, wo_ref, *refs, slots
):
    backs, (gmid_ref, branch_ref, ga_ref, gain_o_ref, router_o_ref) = refs[:-5], refs[-5:]
    experts, cap = len(slots), backs[0].shape[1] - TAIL
    rows = cot_ref.shape[0]
    grad = jnp.zeros(mid_ref.shape, F32)
    gate_rows = []
    for m, (which, index) in enumerate(slots):
        grad = grad + dot(selector_t(codet_ref[:, m : m + 1], cap), backs[which][index, 0:cap, :])
        picked = dot(backs[which][index, cap : cap + TAIL, 0:cap], selector(code_ref[m : m + 1, :], cap))
        gate_rows.append(jnp.sum(picked, axis=0, keepdims=True))
    gate_rows.append(jnp.zeros((TAIL - experts, rows), F32))
    grad_chances = jnp.concatenate(gate_rows, axis=0)
    chances = ch_ref[...]
    grad_logits = chances * (grad_chances - jnp.sum(chances * grad_chances, axis=0, keepdims=True))
    pieces = jnp.concatenate(split3(grad_logits), axis=0)
    wr = wr_ref[...]
    grad = grad + dot_tn(pieces, jnp.concatenate([wr, wr, wr], axis=0))
    router = dot(pieces, nm_ref[...])
    router_o_ref[...] = router[0:TAIL] + router[TAIL : 2 * TAIL] + router[2 * TAIL : 3 * TAIL]
    mid = mid_ref[...]
    scale = rms_scale(mid)
    unit = mid * scale
    gain_o_ref[...] = jnp.sum(grad * unit, axis=0, keepdims=True)
    scaled = grad * gain_ref[...]
    grad_mid = cot_ref[...].astype(F32) + scale * (scaled - unit * jnp.mean(scaled * unit, axis=-1, keepdims=True))
    gmid_ref[...] = grad_mid
    branch = grad_mid.astype(BF)
    branch_ref[...] = branch
    ga_ref[...] = dot_nt(branch, wo_ref[...]).astype(BF)


def sort_rows(place_ref, value, out_ref):
    owners = place_ref.shape[0]
    rows = value.shape[0] // owners
    for b in range(owners):
        out_ref[pl.ds(pl.multiple_of(place_ref[b] * rows, rows), rows), :] = value[b * rows : (b + 1) * rows]


def moe_bwd(cot, middle, gain_moe, normed_moe, chances, wr_t, code, code_t, w_out, slots):
    rows, width = cot.shape
    arrays, found = distinct(slots)
    args = (cot, middle, gain_moe[None], normed_moe, chances, wr_t, code, code_t, w_out, *arrays)
    wide = jax.ShapeDtypeStruct((rows, width), BF)
    return call(
        functools.partial(moe_bwd_kernel, slots=found),
        args,
        [pl.BlockSpec(memory_space=pltpu.VMEM)] * len(args),
        out_shape=[
            jax.ShapeDtypeStruct((rows, width), F32),
            wide,
            wide,
            jax.ShapeDtypeStruct((1, width), F32),
            jax.ShapeDtypeStruct((TAIL, width), F32),
        ],
        cost_estimate=estimate("moe_bwd"),
        name="moe_bwd",
    )


def attn_bwd_kernel(
    qs_ref, k_ref, v_ref, ga_ref, lse_ref, woff_ref, seg_ref,
    dq_ref, dk_ref, dv_ref, dwoff_ref, mask_scr, p_scr, ds_scr,
    *, head_dim,
):
    rows = qs_ref.shape[0]
    blocks = rows // LANES

    @pl.when(pl.program_id(0) == 0)
    def _():
        mask_scr[...] = segment_mask(seg_ref, 0, rows)

    scaled, keys, values, grads = qs_ref[...], k_ref[...], v_ref[...], ga_ref[...]
    q_t, g_t, k_t = scaled.T, grads.T, keys.T
    low_half = lax.broadcasted_iota(jnp.int32, (rows, LANES), 1) < head_dim
    dq_t, dk_parts, dv_parts = [], [], []
    lane = lax.broadcasted_iota(jnp.int32, (1, BAND), 1)
    for h in range(HEAD_GROUP):
        row = woff_ref[0, h : h + 1, :]
        band = band_of(row)
        pair = slice(LANES * (h // 2), LANES * (h // 2 + 1))
        k_pair, v_pair = keys[:, pair], values[:, pair]
        q_only, g_only = only_rows(q_t, h, head_dim), only_rows(g_t, h, head_dim)
        tiles = {}
        for b in range(0, blocks, 2):
            lanes = slice(b * LANES, (b + 2) * LANES)
            s = dot(k_pair, q_only[:, lanes]) + bias_block(band, row, b, 2, blocks) + mask_scr[:, lanes]
            p = jnp.exp(s - lse_ref[0, h : h + 1, lanes])
            dp = dot(v_pair, g_only[:, lanes])
            ds = p * (dp - jnp.sum(p * dp, axis=0, keepdims=True))
            p_scr[:, lanes] = p.astype(BF)
            ds_scr[:, lanes] = ds.astype(BF)
            for q_block in range(2):
                for k_block in range(blocks):
                    d = max(-2, min(2, k_block - b - q_block))
                    tile = ds[k_block * LANES : (k_block + 1) * LANES, q_block * LANES : (q_block + 1) * LANES]
                    tiles[d] = tiles[d] + tile if d in tiles else tile
        skewed = jnp.concatenate([tiles[1], tiles[0], tiles[-1], jnp.zeros_like(tiles[0])], axis=1)
        offsets = diagonal_sums(skewed)
        offsets = offsets + jnp.where(lane == FAR_AFTER, jnp.sum(tiles[2]), 0.0)
        offsets = offsets + jnp.where(lane == FAR_BEFORE, jnp.sum(tiles[-2]), 0.0)
        dwoff_ref[0, h : h + 1, :] = offsets
        p_all, ds_all = p_scr[...], ds_scr[...]
        dv_parts.append(dot(p_all, grads[:, pair]))
        dk_parts.append(dot(ds_all, scaled[:, pair]))
        dq_t.append(dot(k_t[h * head_dim : (h + 1) * head_dim], ds_all))
    dq = jnp.concatenate(dq_t, axis=0).T * head_dim ** (-0.5)
    dq_ref[...] = dq.astype(BF)
    for i in range(HEAD_GROUP // 2):
        pair = slice(LANES * i, LANES * (i + 1))
        dk_ref[:, pair] = jnp.where(low_half, dk_parts[2 * i], dk_parts[2 * i + 1]).astype(BF)
        dv_ref[:, pair] = jnp.where(low_half, dv_parts[2 * i], dv_parts[2 * i + 1]).astype(BF)


def attn_bwd(scaled, keys, values, grad_att, lse, woff, seg):
    rows, width = scaled.shape
    groups = woff.shape[0]
    cols = width // groups
    col_block = pl.BlockSpec((rows, cols), lambda g: (0, g))
    wide = jax.ShapeDtypeStruct((rows, width), BF)
    return call(
        functools.partial(attn_bwd_kernel, head_dim=cols // HEAD_GROUP),
        (scaled, keys, values, grad_att, lse, woff, seg),
        [
            col_block,
            col_block,
            col_block,
            col_block,
            pl.BlockSpec((1, HEAD_GROUP, rows), lambda g: (g, 0, 0)),
            pl.BlockSpec((1, HEAD_GROUP, BAND), lambda g: (g, 0, 0)),
            const_spec(seg.shape),
        ],
        grid=(groups,),
        out_specs=[col_block, col_block, col_block, pl.BlockSpec((1, HEAD_GROUP, BAND), lambda g: (g, 0, 0))],
        out_shape=[wide, wide, wide, jax.ShapeDtypeStruct((groups, HEAD_GROUP, BAND), F32)],
        scratch_shapes=[
            pltpu.VMEM((rows, rows), F32),
            pltpu.VMEM((rows, rows), BF),
            pltpu.VMEM((rows, rows), BF),
        ],
        cost_estimate=estimate("attn_bwd"),
        name="attn_bwd",
    )


def sorted_rows_kernel(pq_ref, pk_ref, tok_ref, gain_ref, att_ref, att_o_ref, out_ref, sort_scr):
    start = tok_ref[...].astype(F32)
    normed_t = (start * rms_scale(start) * gain_ref[...]).T
    attended_t = att_ref[...].astype(F32).T
    sort_rows(pq_ref, attended_t, sort_scr)
    att_o_ref[...] = sort_scr[...].astype(BF)
    for i, place_ref in enumerate((pq_ref, pk_ref)):
        sort_rows(place_ref, normed_t, sort_scr)
        out_ref[i] = sort_scr[...].astype(BF)


def sorted_rows(place_q, place_k, tokens, gain_attn, attended):
    rows, width = tokens.shape
    return call(
        sorted_rows_kernel,
        (place_q, place_k, tokens, gain_attn[None], attended),
        [pl.BlockSpec(memory_space=pltpu.SMEM)] * 2 + [pl.BlockSpec(memory_space=pltpu.VMEM)] * 3,
        out_shape=[jax.ShapeDtypeStruct((width, rows), BF), jax.ShapeDtypeStruct((2, width, rows), BF)],
        scratch_shapes=[pltpu.VMEM((width, rows), F32)],
        cost_estimate=estimate("sorted_rows"),
        name="sorted_rows",
    )


def dense_terms_kernel(att_ref, rows_ref, branch_ref, dq_ref, dk_ref, dv_ref, keep_ref, send_ref):
    half = keep_ref.shape[1]
    for i, d_ref in enumerate((branch_ref, dq_ref, dk_ref, dv_ref)):
        lhs = att_ref[...] if i == 0 else rows_ref[min(i - 1, 1)]
        term = dot(lhs, d_ref[...]).astype(BF)
        keep_ref[i] = term[:half]
        send_ref[i] = term[half:]


def dense_terms(att_t, lhs, branch, dq, dk, dv):
    _, width, rows = lhs.shape
    cols = 256
    col_block = pl.BlockSpec((rows, cols), lambda g: (0, g))
    return call(
        dense_terms_kernel,
        (att_t, lhs, branch, dq, dk, dv),
        [const_spec(att_t.shape), const_spec(lhs.shape)] + [col_block] * 4,
        grid=(width // cols,),
        out_specs=[pl.BlockSpec((4, width // 2, cols), lambda g: (0, 0, g))] * 2,
        out_shape=[jax.ShapeDtypeStruct((4, width // 2, width), BF)] * 2,
        cost_estimate=estimate("dense_terms"),
        name="dense_terms",
    )


def norm_bwd_kernel(
    place_ref, tok_ref, gain_ref, gmid_ref, small_ref, dq_ref, dk_ref, dv_ref, wq_ref, wk_ref, wv_ref,
    tg_ref, keep_ref, send_ref, acc, sort_scr, *, gain_row,
):
    step = pl.program_id(0)
    total = dot_nt(dq_ref[...], wq_ref[...]) + dot_nt(dk_ref[...], wk_ref[...]) + dot_nt(dv_ref[...], wv_ref[...])

    @pl.when(step == 0)
    def _():
        acc[...] = total

    @pl.when(step > 0)
    def _():
        acc[...] += total

    @pl.when(step == pl.num_programs(0) - 1)
    def _():
        grad = acc[...]
        start = tok_ref[...].astype(F32)
        scale = rms_scale(start)
        unit = start * scale
        gain_grad = jnp.sum(grad * unit, axis=0, keepdims=True)
        scaled = grad * gain_ref[...]
        tg_ref[...] = gmid_ref[...] + scale * (scaled - unit * jnp.mean(scaled * unit, axis=-1, keepdims=True))
        small = small_ref[...]
        row = lax.broadcasted_iota(jnp.int32, small.shape, 0)
        small = jnp.where(row == gain_row, gain_grad, small)
        small = jnp.concatenate([small, jnp.zeros((LANES - small.shape[0], small.shape[1]), F32)], axis=0)
        sort_rows(place_ref, small.T, sort_scr)
        half = sort_scr.shape[0] // 2
        keep_ref[...] = sort_scr[0:half].astype(BF)
        send_ref[...] = sort_scr[half:].astype(BF)


def norm_bwd(place, tokens, gain_attn, grad_mid, small, gain_row, dq, dk, dv, w_query, w_key, w_value):
    rows, width = tokens.shape
    cols = 256
    col_block = pl.BlockSpec((rows, cols), lambda g: (0, g))
    weight_block = pl.BlockSpec((width, cols), lambda g: (0, g))
    half = jax.ShapeDtypeStruct((width // 2, LANES), BF)
    return call(
        functools.partial(norm_bwd_kernel, gain_row=gain_row),
        (place, tokens, gain_attn[None], grad_mid, small, dq, dk, dv, w_query, w_key, w_value),
        [pl.BlockSpec(memory_space=pltpu.SMEM)]
        + [const_spec((rows, width)), const_spec((1, width)), const_spec((rows, width)), const_spec(small.shape)]
        + [col_block] * 3
        + [weight_block] * 3,
        grid=(width // cols,),
        out_specs=[const_spec((rows, width)), const_spec(half.shape), const_spec(half.shape)],
        out_shape=[jax.ShapeDtypeStruct((rows, width), F32), half, half],
        scratch_shapes=[pltpu.VMEM((rows, width), F32), pltpu.VMEM((width, LANES), F32)],
        cost_estimate=estimate("norm_bwd"),
        name="norm_bwd",
    )


def last_sums_kernel(token_ref, keep_ref, got_ref, *outs, experts, counts):
    total = keep_ref[...].astype(F32) + got_ref[...].astype(F32)
    width = outs[0].shape[1]
    for i in range(2):
        outs[i][...] = total[i, :, 0:width]
        outs[2 + i][...] = total[i, :, width + LANES :]
    small = total[0, :, width : width + LANES] + token_ref[...]
    outs[4][...] = small[:, 0:experts]
    flat = small.T
    for i, count in enumerate(counts):
        outs[5 + i][...] = flat[TAIL // 2 + i : TAIL // 2 + i + 1, 0:count]


def last_sums(token, keep, got, width, experts, counts):
    rows = keep.shape[1]
    return call(
        functools.partial(last_sums_kernel, experts=experts, counts=counts),
        (token, keep, got),
        [pl.BlockSpec(memory_space=pltpu.VMEM)] * 3,
        out_shape=[jax.ShapeDtypeStruct((rows, width), F32)] * 4
        + [jax.ShapeDtypeStruct((rows, experts), F32)]
        + [jax.ShapeDtypeStruct((1, count), F32) for count in counts],
        cost_estimate=estimate("last_sums"),
        name="last_sums",
    )


def bits_of(size):
    return size.bit_length() - 1


def swap(value, axis, size, mask):
    return lax.ppermute(value, axis, [(i, i ^ mask) for i in range(size)])


def pick(value, index, axis):
    return lax.dynamic_index_in_dim(value, index, axis, keepdims=False)


class Order:
    def __init__(self, token):
        self.token = token

    def enter(self, tree):
        tree, self.token = lax.optimization_barrier((tree, self.token))
        return tree

    leave = enter


def places(me, bits, order):
    key = jnp.arange(1 << bits, dtype=jnp.int32) ^ me
    place = jnp.zeros_like(key)
    for bit in order:
        place = place * 2 + ((key >> bit) & 1)
    return place


class Halving:
    def __init__(self, order, keep, send, dim, route, name):
        self.order, self.keep, self.to_send, self.dim, self.route, self.name = order, keep, send, dim, list(route), name
        self.got = None

    def start(self):
        axis, size, bit = self.route[0]
        with jax.named_scope(f"{self.name}_{axis}{1 << bit}"):
            value = self.order.enter(self.keep if self.to_send is None else self.to_send)
            self.got = swap(value, axis, size, 1 << bit)


def arrive(*units):
    for unit in units:
        unit.got = unit.order.leave(unit.got)


def fold_kernel(*refs, cuts, inputs):
    pairs, outs = refs[:inputs], list(refs[inputs:])
    at = 0
    for dim, last, width in cuts:
        total = []
        for _ in range(width):
            total.append(pairs[at][...].astype(F32) + pairs[at + 1][...].astype(F32))
            at += 2
        if last:
            outs.pop(0)[...] = total[0]
            continue
        rows = total[0].shape[dim] // 2
        for start in (0, rows):
            out = outs.pop(0)
            cut = [lax.slice_in_dim(v, start, start + rows, axis=dim).astype(BF) for v in total]
            if len(out.shape) == len(cut[0].shape):
                at_lane = 0
                for part in cut:
                    out[..., at_lane : at_lane + part.shape[-1]] = part
                    at_lane += part.shape[-1]
            else:
                for i in range(width):
                    out[i] = cut[i]


def fold(*units, hold=()):
    groups = [unit if isinstance(unit, tuple) else (unit,) for unit in units]
    order = groups[0][0].order
    args, cuts, shapes = [], [], []
    for group in groups:
        for unit in group:
            unit.route.pop(0)
            got = order.leave(unit.got)
            args += [unit.keep, got]
        unit = group[0]
        last = unit.to_send is None or not unit.route
        cuts.append((unit.dim, last, len(group)))
        if last:
            shapes.append(jax.ShapeDtypeStruct(got.shape, F32))
        else:
            shape = list(got.shape)
            shape[unit.dim] //= 2
            stacked = len(group) > 1 and len(shape) == 2
            if stacked:
                shape = [len(group)] + shape
            else:
                shape[-1] = sum(member.keep.shape[-1] for member in group)
            shapes += [jax.ShapeDtypeStruct(tuple(shape), BF)] * 2
    args = order.enter(args)
    outs = list(
        call(
            functools.partial(fold_kernel, cuts=cuts, inputs=len(args)),
            args,
            [pl.BlockSpec(memory_space=pltpu.VMEM)] * len(args),
            out_shape=shapes,
            cost_estimate=estimate("fold"),
            name="fold",
        )
    )
    outs = order.leave(outs)
    for group, (_, last, width) in zip(groups, cuts):
        unit = group[0]
        unit.keep = outs.pop(0)
        if not last:
            unit.to_send = outs.pop(0)
        if width > 1 and unit.keep.ndim > group[1].keep.ndim:
            unit.dim += 1
        if unit.route and unit not in hold:
            unit.start()


def fold_first_kernel(keep_ref, got_ref, small_keep_ref, small_got_ref, *outs):
    width = keep_ref.shape[2]
    small = (small_keep_ref[...] + small_got_ref[...]).astype(F32)
    for i in range(keep_ref.shape[0]):
        total = keep_ref[i].astype(F32) + got_ref[i].astype(F32)
        rows = total.shape[0] // 2
        for j in range(2):
            out = outs[i // 2 * 2 + j]
            out[i % 2, :, 0:width] = total[j * rows : (j + 1) * rows].astype(BF)
            if i < 2:
                extra = small[j * rows : (j + 1) * rows] if i == 0 else jnp.zeros((rows, LANES), F32)
                out[i, :, width:] = extra.astype(BF)


def fold_first(keep, got, small_keep, small_got):
    _, rows, width = keep.shape
    shapes = [jax.ShapeDtypeStruct((2, rows // 2, width + extra), BF) for extra in (LANES, LANES, 0, 0)]
    return call(
        fold_first_kernel,
        (keep, got, small_keep, small_got),
        [pl.BlockSpec(memory_space=pltpu.VMEM)] * 4,
        out_shape=shapes,
        cost_estimate=estimate("fold_first"),
        name="fold_first",
    )


class Return:
    def __init__(self, order, low, high, axis, size, name, pieces=False):
        self.order, self.axis, self.size, self.name = order, axis, size, name
        half = high.shape[0]
        low = [(value, 0) for value in low] if isinstance(low, list) else [(low, i) for i in range(half)]
        self.slots = low + [(high, i) for i in range(half)]
        self.bit = bits_of(size) - 1
        if pieces:
            self.start_pieces()
        else:
            with jax.named_scope(f"{self.name}{1 << self.bit}"):
                self.got = swap(self.order.enter(high), self.axis, self.size, 1 << self.bit)

    def moving(self):
        return [m for m in range(self.size) if (m >> self.bit) & 1]

    def start_pieces(self):
        self.got = []
        for m in self.moving():
            array, index = self.slots[m]
            with jax.named_scope(f"{self.name}{1 << self.bit}_{m}"):
                piece = array if array.shape[0] == 1 else array[index][None]
                self.got.append(swap(self.order.enter(piece), self.axis, self.size, 1 << self.bit))

    def fold(self):
        got = self.order.leave(self.got)
        for i, m in enumerate(self.moving()):
            self.slots[m] = (got[i], 0) if isinstance(got, list) else (got, i)
        self.bit -= 1
        if self.bit >= 0:
            self.start_pieces()

    def finish(self):
        while self.bit >= 0:
            self.fold()


class Gather:
    def __init__(self, order, value, axis, size, name):
        self.order, self.axis, self.size, self.name = order, axis, size, name
        self.blocks = {0: value}
        self.send(0, size // 2)
        if size > 2:
            self.send(0, 1)

    def send(self, m, bit):
        with jax.named_scope(f"{self.name}{m}_{bit}"):
            self.blocks[m ^ bit] = swap(self.blocks[m], self.axis, self.size, bit)

    def settle(self):
        self.blocks[1] = self.order.leave(self.blocks[1])

    def relay(self):
        self.blocks[self.size // 2] = self.order.leave(self.blocks[self.size // 2])
        bit = self.size // 2
        while bit:
            for m in range(0, self.size, 2 * bit):
                if m ^ bit not in self.blocks:
                    self.send(m, bit)
            bit //= 2

    def finish(self):
        self.blocks = self.order.leave(self.blocks)
        return [self.blocks[m] for m in range(self.size)]


def body(
    tokens,
    cotangent,
    gain_attn,
    w_query,
    w_key,
    w_value,
    w_out,
    rel_bias,
    gain_moe,
    w_router,
    w_gate,
    w_up,
    w_down,
    segments,
    routes,
    *,
    dp_size,
    ep_size,
):
    TURNS.clear()
    rows, width = tokens.shape
    buckets, heads = rel_bias.shape
    experts = w_router.shape[1]
    cap = 10 * rows // (4 * experts)
    ff = w_gate.shape[2]
    me = lax.axis_index("expert")

    cots = Gather(None, cotangent, "expert", ep_size, "cot")
    scaled, keys, values, woff, token, code, *filled, payload = attn_first(
        tokens, gain_attn, w_query, w_key, w_value, w_out, rel_bias.T, segments, gain_moe, w_router.T, routes.T
    )
    order = Order(token)
    cots.order = order
    me_ref = me.reshape(1).astype(jnp.int32)

    dp_bits, ep_bits = bits_of(dp_size), bits_of(ep_size)
    dp_me = lax.axis_index("dp")
    dp_order = list(range(dp_bits))
    z_order = [1, 0] + dp_order[2:]
    place_x = places(dp_me, dp_bits, dp_order)
    place_z = places(dp_me, dp_bits, z_order)

    def dp_route(bits):
        return [("dp", dp_size, b) for b in bits]

    dp_part = [ep_bits + b for b in dp_order]
    ep_part = list(range(1, ep_bits))
    q_bits = [0] + ep_part + dp_part
    k_bits = [0] + dp_part[:2] + ep_part + dp_part[2:]
    whole_me = dp_me * ep_size + me

    def route(bits):
        return [("expert", ep_size, b) if b < ep_bits else ("dp", dp_size, b - ep_bits) for b in bits]

    place_q, place_k = [places(whole_me, dp_bits + ep_bits, bits) for bits in (q_bits, k_bits)]

    first_half = Gather(order, order.enter(payload), "expert", ep_size, "rows_a")
    attended, lse, middle, normed_moe, chances, payload = order.leave(
        attn_second(tokens, order.enter(scaled), keys, values, w_out, woff, segments, gain_moe, w_router.T, filled)
    )
    cots.settle()
    first_half.settle()
    second_half = Gather(order, order.enter(payload), "expert", ep_size, "rows_b")
    first_half.relay()
    cots.relay()
    cots, heads_rows = cots.finish(), first_half.finish()
    blocks = ff // FF_BLOCK
    counts = [blocks - blocks // 2, blocks // 2]
    starts = [sum(counts[:i]) for i in range(len(counts))]
    grad_hidden, cot_rows = order.leave(cot_hidden(order.enter(me_ref), heads_rows, cots, w_down, cap, blocks))
    second_half.relay()
    payloads = [v for pair in zip(heads_rows, second_half.finish()) for v in pair]
    scs, units = [], []

    def expert_part(i, source, filled=()):
        *shared, gate_keep, gate_send, up_keep, up_send, sc, hid, hid_t, gg, gu = order.leave(
            expert_a(
                order.enter(source), grad_hidden, 0, w_gate, w_up, starts[i], counts[i], filled
            )
        )
        scs.append(sc)
        gate = Halving(order, gate_keep, gate_send, 0, dp_route(z_order), f"gate{i}")
        units.append((gate, Halving(order, up_keep, up_send, 0, dp_route(dp_order), f"up{i}")))
        return shared, (hid, hid_t, gg, gu)

    def by_xor(value):
        return jnp.stack([pick(value, me ^ m, 0) for m in range(experts)])

    def padded(value):
        return jnp.pad(value, ((0, TAIL - experts), (0, 0)))

    (x_all, x_t, gate_all, grad_cots), filled = expert_part(0, (me_ref, place_x, payloads, cot_rows))
    for unit in units[0]:
        unit.start()
    _, (hid, hid_t, gg, gu) = expert_part(1, (x_all, x_t, gate_all), filled)
    for unit in units[1]:
        unit.start()
    *back_low, back_high = order.leave(expert_b(order.enter(gg), gu, scs, w_gate, w_up, experts))
    backs = Return(order, back_low, back_high, "expert", ep_size, "grad_rows")
    first, second = units[0][0], units[1][0]
    fold(*units[0])
    down_parts = order.leave(down_grads(order.enter(hid_t), grad_cots, place_z, place_x))
    down_units = tuple(
        Halving(order, down_parts[2 * i], down_parts[2 * i + 1], 0, dp_route(bits), f"down{i}")
        for i, bits in enumerate((z_order, dp_order))
    )
    down = down_units[0]
    fold(*units[1], units[0], hold=units[0])
    code_xor, chances_xor, wr_xor = order.enter((by_xor(code), padded(by_xor(chances)), padded(by_xor(w_router.T))))
    backs.fold()
    att_t, normed_t = order.leave(sorted_rows(place_q, place_k, tokens, gain_attn, order.enter(attended)))
    backs.finish()
    for unit in down_units:
        unit.start()
    grad_mid, branch, grad_att, gain_moe_term, router_term = order.leave(
        moe_bwd(
            cotangent, middle, gain_moe, normed_moe, chances_xor, wr_xor, code_xor, code_xor.T, w_out,
            backs.slots,
        )
    )
    dq, dk, dv, dwoff = order.leave(attn_bwd(scaled, keys, values, order.enter(grad_att), lse, woff, segments))
    arrive(*units[1])
    dense_keep, dense_send = order.leave(dense_terms(att_t, normed_t, branch, order.enter(dq), dk, dv))
    arrive(*down_units)
    core = Halving(order, dense_keep, dense_send, 1, route(q_bits)[:1], "dense")
    core.start()
    first.start()
    fold(*down_units, units[1], hold=units[1])
    devices = dp_size * ep_size
    share = width // devices
    onehot = jnp.asarray(band_onehot(rows, buckets))
    bias_term = jnp.dot(onehot, dwoff.reshape(heads, BAND).T, precision=HIGHEST).reshape(devices, -1)
    bias_share = bias_term.shape[1]
    bias_row = jnp.pad(bias_term, ((0, 0), (0, share - bias_share))).reshape(1, width)
    small = jnp.concatenate(
        [
            jnp.pad(by_xor(router_term), ((0, TAIL // 2 - experts), (0, 0))),
            jnp.zeros((1, width), F32),
            gain_moe_term,
            bias_row,
            jnp.zeros((TAIL // 2 - 3, width), F32),
        ],
        axis=0,
    )
    token_grad, small_keep, small_send = order.leave(
        norm_bwd(
            place_q, tokens, gain_attn, grad_mid, order.enter(small), TAIL // 2, dq, dk, dv, w_query, w_key, w_value
        )
    )
    with jax.named_scope("small_expert1"):
        small_got = swap(order.enter(small_send), "expert", ep_size, 1)
    core_got = order.leave(core.got)
    halves = order.leave(fold_first(order.enter(dense_keep), core_got, small_keep, order.leave(small_got)))
    dense = [
        Halving(order, halves[2 * i], halves[2 * i + 1], 1, route(bits)[1:], name)
        for i, (bits, name) in enumerate(((q_bits, "out_q"), (k_bits, "k_v")))
    ]
    out_q, k_v = dense
    arrive(down, first)
    k_v.start()
    out_q.start()
    second.start()
    prod_low, prod_high = order.leave(produced_rows(order.enter(hid), w_down, experts))
    returned = Return(order, prod_low, prod_high, "expert", ep_size, "produced_rows")
    fold(k_v, out_q, down_units, first, second)
    fold(k_v, out_q)
    while first.route or second.route:
        fold(*[unit for unit in (first, second) if unit.route])
    terms = [first.keep, second.keep]
    gate_grad = order.leave(jnp.concatenate([term[0] for term in terms], axis=1)[None])
    up_grad = order.leave(jnp.concatenate([term[1] for term in terms], axis=1)[None])
    returned.fold()
    returned.finish()
    layer_out = order.leave(layer_output(middle, chances_xor, code_xor.T, returned.slots))
    while len(out_q.route) > 2:
        fold(*[unit for unit in (out_q, k_v, down) if unit.route])
    fold(*[(out_q, k_v)] + ([down] if down.route else []))
    down_grad = order.leave(jnp.concatenate([down.keep[0], down.keep[1]], axis=1)[None])
    pairs = order.leave([out_q.keep, out_q.got])
    out_grad, query_grad, key_grad, value_grad, router_grad, *gains = last_sums(
        order.token, *pairs, width, experts, (share, share, bias_share)
    )
    gain_attn_grad, gain_moe_grad, bias_grad = [value.reshape(-1) for value in gains]
    return (
        layer_out,
        token_grad,
        query_grad,
        key_grad,
        value_grad,
        out_grad,
        gain_attn_grad,
        gain_moe_grad,
        bias_grad,
        router_grad,
        gate_grad,
        up_grad,
        down_grad,
    )


def solution(mesh):
    in_specs = (
        P(("dp", "expert"), None),
        P(("dp", "expert"), None),
        P(),
        P(),
        P(),
        P(),
        P(),
        P(),
        P(),
        P(),
        P("expert", None, None),
        P("expert", None, None),
        P("expert", None, None),
        P(("dp", "expert"), None),
        P(("dp", "expert"), None),
    )
    out_specs = (
        P(("dp", "expert"), None),
        P(("dp", "expert"), None),
        P(("dp", "expert"), None),
        P(("dp", "expert"), None),
        P(("dp", "expert"), None),
        P(("dp", "expert"), None),
        P(("dp", "expert")),
        P(("dp", "expert")),
        P(("dp", "expert")),
        P(("dp", "expert"), None),
        P("expert", "dp", None),
        P("expert", "dp", None),
        P("expert", "dp", None),
    )
    run = functools.partial(body, dp_size=mesh.shape["dp"], ep_size=mesh.shape["expert"])
    return jax.shard_map(run, mesh=mesh, in_specs=in_specs, out_specs=out_specs, check_vma=False)
```
